32 devices in a mesh: dp: 2 (over y), hid: 4 (over x, core), dm: 4 (over z).
Axes of the slice: x: 2, y: 2, z: 4, core: 2. Of those that a mesh axis runs over, the one named last changes fastest.
Arguments:
- tokens: bfloat16 [10240, 768], P(('dp', 'dm'))
- clusters: int32 [10240], P(('dp', 'dm')), may hold values from 0 to 99, as said below
- top_keys: int32 [200, 32], P('dp'), may hold values from 0 to 5119, as said below
- lengths: int32 [4], P('dp'), may hold values from 1024 to 4096, as said below
- qkv_weight: bfloat16 [3, 768, 768], P(None, None, 'hid')
- out_weight: bfloat16 [768, 768], P('hid'), may hold values from -0.21875 to 0.21875
- first_gain: float32 [768], replicated, may hold values from 0.5 to 1.5
- first_bias: float32 [768], replicated, may hold values from -1.5 to 1.5
- second_gain: float32 [768], replicated, may hold values from 0.5 to 1.5
- second_bias: float32 [768], replicated, may hold values from -1.5 to 1.5
- expand_weight: bfloat16 [768, 3072], P(('dp', 'dm'), 'hid'), may hold values from -0.21875 to 0.21875
- shrink_weight: bfloat16 [3072, 768], P('hid', ('dp', 'dm')), may hold values from -0.109375 to 0.109375
- cotangent: bfloat16 [10240, 768], P(('dp', 'dm')), may hold values from -6 to 6
Outputs:
- result: bfloat16 [10240, 768], P(('dp', 'dm'))
- tokens_grad: bfloat16 [10240, 768], P(('dp', 'dm'))
- qkv_grad: float32 [3, 768, 768], P(None, None, 'hid')
- out_grad: float32 [768, 768], P('hid')
- first_gain_grad: float32 [768], replicated
- first_bias_grad: float32 [768], replicated
- second_gain_grad: float32 [768], replicated
- second_bias_grad: float32 [768], replicated
- expand_grad: float32 [768, 3072], P(('dp', 'dm'), 'hid')
- shrink_grad: float32 [3072, 768], P('hid', ('dp', 'dm'))
The draws below stay inside these ranges and needn't reach their ends.
Inputs may be any that keep to these rules, and one draw needn't show every extreme that they name: Entries 2p and 2p + 1 are the lengths of the two sequences of pack p, laid end to end in that order; they sum to 5120. `clusters`: cluster numbers count within a pack; every cluster of every pack has 32 queries or more, all in one sequence. `top_keys`: row p * 100 + c lists 32 different positions within pack p, all in the sequence of cluster c's queries.
All inputs are finite; a program needn't handle non-finite values.
Results may differ from the reference program's by a relative error of at most 0.015.
Values may be sent and summed in bfloat16 or wider, within the bound.
A program may use at most 256 MiB of HBM per device.

```python
import math
import jax
import jax.numpy as jnp
from jax import lax

D = 768
HEAD_DIM = 64
FF = 3072
CL = 100
TOPK = 32
TOK_DP = 5120
MIN_LEN = 1024
TOKENS = 10240
SEQS = 4
N_DP = 2
N_HID = 4
N_DM = 4


def pack_layout(key):
    shard_rows = TOK_DP // N_DM

    def one_pack(pack_key, leading):
        key_short, key_order, key_shuffle, key_extra = jax.random.split(pack_key, 4)
        short_length = jax.random.randint(key_short, (), MIN_LEN, shard_rows)
        short_length = jnp.where(leading, MIN_LEN, short_length)
        long_first = jax.random.randint(key_order, (), 0, 2)
        first_length = jnp.where(long_first == 1, TOK_DP - short_length, short_length)
        pack_lengths = jnp.stack([first_length, TOK_DP - first_length]).astype(jnp.int32)
        places = jnp.arange(TOK_DP, dtype=jnp.int32)
        segment = (places >= first_length).astype(jnp.int32)
        shuffle = jax.random.permutation(key_shuffle, TOK_DP).astype(jnp.int32)
        ordering = jnp.argsort(segment * TOK_DP + shuffle, stable=True).astype(jnp.int32)
        ranking = jnp.zeros(TOK_DP, jnp.int32).at[ordering].set(places)
        within = ranking - segment * first_length
        first_clusters = jnp.maximum(1, first_length * CL // TOK_DP)
        cluster_count = jnp.where(segment == 0, first_clusters, CL - first_clusters)
        cluster_base = jnp.where(segment == 0, 0, first_clusters)
        spare_cluster = jax.random.randint(key_extra, (TOK_DP,), 0, 1 << 20) % cluster_count
        assigned = cluster_base + jnp.where(within < cluster_count * TOPK, within % cluster_count, spare_cluster)
        numbers = jnp.arange(CL, dtype=jnp.int32)
        in_second = (numbers >= first_clusters).astype(jnp.int32)
        offset = jnp.where(in_second == 1, numbers - first_clusters, numbers)
        per_sequence = jnp.where(in_second == 1, CL - first_clusters, first_clusters)
        slot_rank = in_second[:, None] * first_length + offset[:, None] + per_sequence[:, None] * jnp.arange(TOPK, dtype=jnp.int32)[None, :]
        chosen = ordering[slot_rank]
        return (pack_lengths, assigned.astype(jnp.int32), chosen.astype(jnp.int32))
    pack_keys = jax.random.split(key, N_DP)
    leading = jnp.arange(N_DP) == 0
    return jax.vmap(one_pack)(pack_keys, leading)


def pick_rows(table, picked):
    return table[picked]


def draw_lengths(key, part):
    pack_lengths, assigned, chosen = pack_layout(key)
    return pack_lengths.reshape(SEQS)


def draw_clusters(key, part):
    pack_lengths, assigned, chosen = pack_layout(key)
    return assigned.reshape(TOKENS)


def draw_top_keys(key, part):
    pack_lengths, assigned, chosen = pack_layout(key)
    return chosen.reshape(N_DP * CL, TOPK)


def draw_tokens(key, part):
    pack_lengths, assigned, chosen = pack_layout(key)
    key = jax.random.fold_in(key, 5)
    key_centre, key_noise, key_scale = jax.random.split(key, 3)
    centres = jax.random.normal(key_centre, (N_DP, CL, D), jnp.float32)
    noise = jax.random.normal(key_noise, (N_DP, TOK_DP, D), jnp.float32)
    column_scale = jnp.exp(jax.random.uniform(key_scale, (D,), jnp.float32, math.log(0.3), math.log(3.0)))
    picked = jax.vmap(pick_rows)(centres, assigned)
    mixed = column_scale * (0.8 * picked + 0.6 * noise)
    return mixed.reshape(TOKENS, D).astype(jnp.bfloat16)


def draw_qkv_weight(key, part):
    key = jax.random.fold_in(key, 9)
    key_query, key_key, key_value = jax.random.split(key, 3)
    spread = 1.2 / math.sqrt(D)
    query_part = spread * jax.random.normal(key_query, (D, D), jnp.float32)
    key_part = 0.8 * query_part + 0.6 * spread * jax.random.normal(key_key, (D, D), jnp.float32)
    value_part = jax.random.normal(key_value, (D, D), jnp.float32) / math.sqrt(D)
    return jnp.stack([query_part, key_part, value_part]).astype(jnp.bfloat16)


def levels(rng, dims, cuts, smallest, high):
    loudness, own = 1.0, jax.random.fold_in(rng, 6)
    for position, blocks in cuts:
        steps = jnp.exp(jax.random.uniform(jax.random.fold_in(own, position), (blocks,), jnp.float32, smallest / len(cuts), high / len(cuts)))
        loudness = loudness * jnp.repeat(steps, dims[position] // blocks).reshape([-1 if axis == position else 1 for axis in range(len(dims))])
    return loudness


def scatter_about(rng, shape, scale, most, shards=(), kind=jnp.bfloat16):
    drawn = jax.random.normal(rng, shape, jnp.float32) * scale
    if len(shards) > 0:
        drawn = levels(rng, shape, shards, -0.22, 0.18) * drawn
    return jnp.clip(drawn, min=-most, max=most).astype(kind)


def setup_inputs(seed: int = 0) -> dict:
    splits = jax.random.split(jax.random.key(seed), 14)
    tokens = draw_tokens(jax.random.fold_in(splits[13], 71), 0)
    clusters = draw_clusters(jax.random.fold_in(splits[13], 71), 0)
    top_keys = draw_top_keys(jax.random.fold_in(splits[13], 71), 0)
    lengths = draw_lengths(jax.random.fold_in(splits[13], 71), 0)
    qkv_weight = draw_qkv_weight(jax.random.fold_in(splits[13], 71), 0)
    out_weight = scatter_about(splits[5], (D, D), D ** -0.5, 0.21875, ((0, 4),))
    first_gain = jnp.clip(1.0 + 0.1 * jax.random.normal(splits[6], (D,), jnp.float32), 0.5, 1.5)
    first_bias = scatter_about(splits[7], (D,), 0.3, 1.5, (), jnp.float32)
    second_gain = jnp.clip(1.0 + 0.1 * jax.random.normal(splits[8], (D,), jnp.float32), 0.5, 1.5)
    second_bias = scatter_about(splits[9], (D,), 0.3, 1.5, (), jnp.float32)
    expand_weight = scatter_about(splits[10], (D, FF), D ** -0.5, 0.21875, ((0, 8), (1, 4)))
    shrink_weight = scatter_about(splits[11], (FF, D), FF ** -0.5, 0.109375, ((0, 4), (1, 8)))
    cotangent = scatter_about(splits[12], (TOKENS, D), 1.0, 6.0, ((0, 8),))
    return dict(tokens=tokens, clusters=clusters, top_keys=top_keys, lengths=lengths, qkv_weight=qkv_weight, out_weight=out_weight, first_gain=first_gain, first_bias=first_bias, second_gain=second_gain, second_bias=second_bias, expand_weight=expand_weight, shrink_weight=shrink_weight, cotangent=cotangent)


EPSILON = 1e-05
NEGATIVE = -1e+30
HIGHEST = lax.Precision.HIGHEST

@jax.custom_vjp
def low(v):
    return lax.optimization_barrier(v.astype(jnp.bfloat16)).astype(jnp.float32)

@jax.custom_vjp
def low_back(v):
    return v

def low_keep(v):
    return (low(v), None)

def low_pass(kept, grad):
    return (grad,)

def back_keep(v):
    return (v, None)

def back_low(kept, grad):
    return (low(grad),)
low.defvjp(low_keep, low_pass)
low_back.defvjp(back_keep, back_low)

def layer_norm(values, norm_gain, norm_bias):
    centred = values - lax.optimization_barrier(jnp.mean(values, -1, keepdims=True))
    variance = lax.optimization_barrier(jnp.mean(centred * centred, -1, keepdims=True))
    return centred * lax.rsqrt(variance + EPSILON) * norm_gain + norm_bias

def softmax_last(scores):
    largest = lax.optimization_barrier(jnp.max(scores, -1, keepdims=True))
    raised = jnp.exp(scores - largest)
    return raised / lax.optimization_barrier(jnp.sum(raised, -1, keepdims=True))

def clustered(queries, keys, values, segment, cluster, chosen_keys):
    pack_size = queries.shape[0]
    head_count = queries.shape[1]
    score_scale = HEAD_DIM ** (-0.5)
    member = (cluster[:, None] == jnp.arange(CL)[None, :]).astype(jnp.float32)
    counts = lax.optimization_barrier(jnp.sum(member, 0))
    member_sums = jnp.einsum('pc,phe->che', member, queries, precision=HIGHEST)
    centres = low_back(low(member_sums / counts[:, None, None]))
    same_sequence = segment[chosen_keys[:, 0]][:, None] == segment[None, :]
    top_mask = jnp.zeros((CL, pack_size), jnp.float32).at[jnp.arange(CL)[:, None], chosen_keys].set(1.0)
    raw_scores = low_back(jnp.einsum('che,phe->hcp', centres, keys, precision=HIGHEST) * score_scale)
    centre_probs = softmax_last(jnp.where(same_sequence[None], raw_scores, NEGATIVE))
    top_mass = lax.optimization_barrier(jnp.sum(centre_probs * top_mask[None], -1))
    rest_part = low_back(jnp.einsum('hcp,phe->che', low(centre_probs) * (1.0 - top_mask)[None], values, precision=HIGHEST))
    block_rows = 512 if pack_size % 512 == 0 else pack_size
    block_count = pack_size // block_rows

    def exact_block(carried):
        query_block, cluster_block = carried
        picked = chosen_keys[cluster_block]
        key_block = keys[picked]
        value_block = values[picked]
        scores = low_back(jnp.einsum('bhe,bjhe->bhj', query_block, key_block, precision=HIGHEST) * score_scale)
        weights = low(softmax_last(scores))
        exact_out = low_back(jnp.einsum('bhj,bjhe->bhe', weights, value_block, precision=HIGHEST))
        return top_mass.T[cluster_block][:, :, None] * exact_out + rest_part[cluster_block]
    outputs = lax.map(jax.checkpoint(exact_block), (queries.reshape(block_count, block_rows, head_count, HEAD_DIM), cluster.reshape(block_count, block_rows)))
    return outputs.reshape(pack_size, head_count * HEAD_DIM)

def pack_forward(inputs, qkv_matrix, out_matrix, gain_first, bias_first, gain_second, bias_second, expand_matrix, shrink_matrix, segment, cluster, chosen_keys):
    pack_size = inputs.shape[0]
    head_count = qkv_matrix.shape[2] // HEAD_DIM
    first_normed = low(layer_norm(inputs, gain_first, bias_first))
    projected = low_back(low(jnp.einsum('pd,kde->kpe', first_normed, qkv_matrix, precision=HIGHEST)))
    shaped = projected.reshape(3, pack_size, head_count, HEAD_DIM)
    attended = low(clustered(shaped[0], shaped[1], shaped[2], segment, cluster, chosen_keys))
    group_width = D // N_HID
    pieces = [low(jnp.dot(attended[:, column * group_width:(column + 1) * group_width], out_matrix[column * group_width:(column + 1) * group_width], precision=HIGHEST)) for column in range(N_HID)]
    middle = inputs + low_back(sum(pieces))
    second_normed = low(layer_norm(middle, gain_second, bias_second))
    hidden = low_back(jnp.dot(second_normed, expand_matrix, precision=HIGHEST))
    activated = low(jax.nn.gelu(hidden))
    unit_width = FF // N_HID
    parts_out = [low(jnp.dot(activated[:, column * unit_width:(column + 1) * unit_width], shrink_matrix[column * unit_width:(column + 1) * unit_width], precision=HIGHEST)) for column in range(N_HID)]
    return middle + sum(parts_out)

def reference(tokens, clusters, top_keys, lengths, qkv_weight, out_weight, first_gain, first_bias, second_gain, second_bias, expand_weight, shrink_weight, cotangent):
    weights = (qkv_weight.astype(jnp.float32), out_weight.astype(jnp.float32), first_gain.astype(jnp.float32), first_bias.astype(jnp.float32), second_gain.astype(jnp.float32), second_bias.astype(jnp.float32), expand_weight.astype(jnp.float32), shrink_weight.astype(jnp.float32))
    stacked = (tokens.astype(jnp.float32).reshape(N_DP, TOK_DP, D), cotangent.astype(jnp.float32).reshape(N_DP, TOK_DP, D), lengths.reshape(N_DP, 2), clusters.reshape(N_DP, TOK_DP), top_keys.reshape(N_DP, CL, TOPK))

    def one_pack(totals, carried):
        inputs, upstream, pack_lengths, cluster, chosen_keys = carried
        segment = (jnp.arange(TOK_DP) >= pack_lengths[0]).astype(jnp.int32)

        def forward(inputs, qkv_matrix, out_matrix, gain_first, bias_first, gain_second, bias_second, expand_matrix, shrink_matrix):
            return pack_forward(inputs, qkv_matrix, out_matrix, gain_first, bias_first, gain_second, bias_second, expand_matrix, shrink_matrix, segment, cluster, chosen_keys)
        output, pullback = jax.vjp(forward, inputs, weights[0], weights[1], weights[2], weights[3], weights[4], weights[5], weights[6], weights[7])
        gradients = pullback(upstream)
        totals = tuple((running + gradient for running, gradient in zip(totals, gradients[1:])))
        return (totals, (output.astype(jnp.bfloat16), gradients[0].astype(jnp.bfloat16)))
    starting = tuple((jnp.zeros_like(weight) for weight in weights))
    totals, (results, input_grads) = lax.scan(one_pack, starting, stacked)
    return (results.reshape(TOKENS, D), input_grads.reshape(TOKENS, D), totals[0], totals[1], totals[2], totals[3], totals[4], totals[5], totals[6], totals[7])
```

```python
import functools

import jax
import jax.numpy as jnp
from jax import lax
from jax.experimental import pallas as pl
from jax.experimental.pallas import tpu as pltpu
from jax.sharding import PartitionSpec as P

HEAD_DIM = 64
CL = 100
TOPK = 32
CLP = 128
SLOTS = 3328
GROUP = 8
GSLOTS = GROUP * TOPK
GROUPS = SLOTS // GSLOTS
WIN = 128
EPSILON = 1e-05
NEGATIVE = -1e30
HIGHEST = lax.Precision.HIGHEST
F32 = jnp.float32
BF16 = jnp.bfloat16
MESH = pl.DeviceIdType.MESH
NT = (((1,), (1,)), ((), ()))
TN = (((0,), (0,)), ((), ()))
SCALE = HEAD_DIM ** (-0.5)


def dot(a, b):
    return jnp.dot(a, b, preferred_element_type=F32)


def dot_nt(a, b):
    return lax.dot_general(a, b, NT, preferred_element_type=F32)


def dot_tn(a, b):
    return lax.dot_general(a, b, TN, preferred_element_type=F32)


def iota(shape, dim):
    return lax.broadcasted_iota(jnp.int32, shape, dim)


def norm_parts(values):
    centred = values - jnp.mean(values, -1, keepdims=True)
    spread = lax.rsqrt(jnp.mean(centred * centred, -1, keepdims=True) + EPSILON)
    return (centred * spread, spread)


def norm_back(upstream, normed, spread, norm_gain):
    through = upstream * norm_gain
    inner = (
        through
        - jnp.mean(through, -1, keepdims=True)
        - normed * jnp.mean(through * normed, -1, keepdims=True)
    )
    return (spread * inner, jnp.sum(upstream * normed, 0), jnp.sum(upstream, 0))


def head_lanes(width, head):
    lane = iota((1, width), 1)
    return lane // HEAD_DIM == head


def block_diagonal(rows, heads):
    width = rows.shape[1]
    zero = jnp.zeros_like(rows)
    return jnp.concatenate(
        [jnp.where(head_lanes(width, h), rows, zero) for h in range(heads)], axis=0
    )


def diagonal_blocks(full, heads):
    rows, width = full.shape[0] // heads, full.shape[1]
    out = full[:rows]
    for h in range(1, heads):
        out = jnp.where(head_lanes(width, h), full[h * rows : (h + 1) * rows], out)
    return out


def front_kernel(
    tok, ccol, crow, weight, gain, bias,
    fn_out, qs_out, k_out, v_out, csum_out, starts_out, rcol_out, rrow_out, cls_out,
    q_ref, member_ref,
):
    rows = tok.shape[0]
    width = weight.shape[2]
    tiles = rows // 128
    lower = (iota((128, 128), 0) > iota((128, 128), 1)).astype(BF16)
    lane = iota((128, 128), 1)
    csum_out[...] = jnp.zeros_like(csum_out)

    def tile(i, running):
        at = pl.ds(pl.multiple_of(i * 128, 128), 128)
        normed, _ = norm_parts(tok[at, :].astype(F32))
        first = (normed * gain[...] + bias[...]).astype(BF16)
        fn_out[at, :] = first
        q = dot(first, weight[0]).astype(BF16)
        q_ref[at, :] = q
        k_out[at, :] = dot(first, weight[1]).astype(BF16)
        v_out[at, :] = dot(first, weight[2]).astype(BF16)
        member = (ccol[at, :] == lane).astype(F32)
        low = member.astype(BF16)
        member_ref[at, :] = low
        extended = jnp.concatenate([q, jnp.ones((128, 256 - width), BF16)], axis=1)
        csum_out[...] += dot_tn(low, extended)
        earlier = dot(lower, low) + running
        rcol_out[at, :] = jnp.sum(member * earlier, 1, keepdims=True)
        return running + jnp.sum(member, 0, keepdims=True)

    counts = lax.fori_loop(0, tiles, tile, jnp.zeros((1, 128), F32))
    before = (iota((128, 128), 0) < iota((128, 128), 1)).astype(F32)
    starts = jnp.dot(
        jnp.broadcast_to(counts, (8, 128)), before, precision=HIGHEST, preferred_element_type=F32
    )
    starts_out[...] = starts.astype(jnp.int32)

    def ranks(i, carry):
        at = pl.ds(pl.multiple_of(i * 128, 128), 128)
        member = member_ref[at, :].astype(F32)
        rank = rcol_out[at, :] + jnp.sum(member * starts[:1], 1, keepdims=True)
        rcol_out[at, :] = rank
        turned = jnp.transpose(jnp.broadcast_to(rank, (128, 128)))
        rrow_out[:, at] = turned[:8]
        return carry

    lax.fori_loop(0, tiles, ranks, 0)
    rank_row = rrow_out[:1, :].astype(jnp.int32)

    def place(i, carry):
        at = pl.ds(pl.multiple_of(i * 128, 128), 128)
        chosen = (iota((128, rows), 0) + i * 128 == rank_row).astype(BF16)
        qs_out[at, :] = dot(chosen, q_ref[...]).astype(BF16)
        sorted_member = dot(chosen, member_ref[...])
        cls_out[at, :] = jnp.sum(sorted_member * lane.astype(F32), 1, keepdims=True).astype(
            jnp.int32
        )
        return carry

    lax.fori_loop(0, tiles, place, 0)
    qs_out[rows:, :] = jnp.zeros((WIN, width), BF16)
    cls_out[rows:, :] = jnp.full((WIN, 1), -1, jnp.int32)


def vmem(n):
    return [pl.BlockSpec(memory_space=pltpu.VMEM)] * n


def front(tokens, clusters, qkv_weight, gain, bias):
    rows = tokens.shape[0]
    width = qkv_weight.shape[2]
    shape = jax.ShapeDtypeStruct
    return pl.pallas_call(
        front_kernel,
        out_shape=(
            shape(tokens.shape, BF16),
            shape((rows + WIN, width), BF16),
            shape((rows, width), BF16),
            shape((rows, width), BF16),
            shape((CLP, 256), F32),
            shape((8, 128), jnp.int32),
            shape((rows, 1), F32),
            shape((8, rows), F32),
            shape((rows + WIN, 1), jnp.int32),
        ),
        in_specs=vmem(6),
        out_specs=tuple(vmem(9)),
        scratch_shapes=[pltpu.VMEM((rows, width), BF16), pltpu.VMEM((rows, 128), BF16)],
        compiler_params=pltpu.CompilerParams(vmem_limit_bytes=40 << 20),
        name="front",
    )(tokens, clusters.reshape(rows, 1), clusters.reshape(1, rows), qkv_weight, gain[None], bias[None])


def sequence_masks(lengths, topk, rows):
    own_start = lax.axis_index("dm") * rows
    key_second = iota((1, rows), 1) + own_start >= lengths[0]
    centre_second = topk[:, :1] >= lengths[0]
    return key_second == centre_second


def centre_forward_kernel(lengths, csum, k, v, topk, centre_out, tm_out, stat_out):
    rows, width = k.shape
    heads = width // HEAD_DIM
    own_start = lax.axis_index("dm") * rows
    count = jnp.maximum(csum[:, width : width + 1], 1.0)
    centre = (csum[:, :width] / count).astype(BF16)
    centre_out[...] = centre
    here = iota((CLP, rows), 1) + own_start
    hit = topk[:, :1] == here
    for t in range(1, TOPK):
        hit = hit | (topk[:, t : t + 1] == here)
    top = hit.astype(F32)
    tm_out[...] = top.astype(BF16)
    outside = 1.0 - top
    same = sequence_masks(lengths, topk, rows)
    full = dot_nt(block_diagonal(centre, heads), k[...]) * SCALE
    lane = iota((CLP, 128), 1)
    stats = jnp.zeros((CLP, 128), F32)
    weights = []
    for h in range(heads):
        scores = jnp.where(same, full[h * CLP : (h + 1) * CLP], NEGATIVE)
        largest = jnp.max(scores, 1, keepdims=True)
        raised = jnp.exp(scores - largest)
        total = jnp.sum(raised, 1, keepdims=True)
        mass = jnp.sum(raised * top, 1, keepdims=True)
        weights.append((raised * outside).astype(BF16))
        stats = jnp.where(lane == h, largest, stats)
        stats = jnp.where(lane == 8 + h, total, stats)
        stats = jnp.where(lane == 16 + h, mass, stats)
    rest = diagonal_blocks(dot(jnp.concatenate(weights, axis=0), v[...]), heads)
    stat_out[:, :256] = jnp.concatenate([rest, jnp.zeros((CLP, 256 - width), F32)], axis=1)
    stat_out[:, 256:] = stats


def centre_forward(lengths, csum, k, v, topk):
    rows, width = k.shape
    shape = jax.ShapeDtypeStruct
    return pl.pallas_call(
        centre_forward_kernel,
        out_shape=(
            shape((CLP, width), BF16),
            shape((CLP, rows), BF16),
            shape((CLP, 384), F32),
        ),
        in_specs=[pl.BlockSpec(memory_space=pltpu.SMEM)] + vmem(4),
        out_specs=tuple(vmem(3)),
        compiler_params=pltpu.CompilerParams(vmem_limit_bytes=40 << 20),
        name="centre_forward",
    )(lengths, csum, k, v, topk)


def merge_stats(stats, heads, width):
    parts = stats.shape[0]
    largest = stats[0][:, 256:]
    for d in range(1, parts):
        largest = jnp.maximum(largest, stats[d][:, 256:])
    total = jnp.zeros((CLP, 1), F32)
    mass_rows = jnp.zeros((CLP, width), F32)
    rest_rows = jnp.zeros((CLP, width), F32)
    lane = iota((CLP, 128), 1)
    merged = jnp.zeros((CLP, 128), F32)
    for h in range(heads):
        top = largest[:, h : h + 1]
        total = jnp.zeros((CLP, 1), F32)
        mass = jnp.zeros((CLP, 1), F32)
        rest = jnp.zeros((CLP, width), F32)
        for d in range(parts):
            block = stats[d]
            factor = jnp.exp(block[:, 256 + h : 257 + h] - top)
            total += factor * block[:, 264 + h : 265 + h]
            mass += factor * block[:, 272 + h : 273 + h]
            rest += factor * block[:, :width]
        mine = head_lanes(width, h)
        mass = mass / total
        mass_rows = jnp.where(mine, mass, mass_rows)
        rest_rows = jnp.where(mine, rest / total, rest_rows)
        merged = jnp.where(lane == h, top, merged)
        merged = jnp.where(lane == 8 + h, total, merged)
        merged = jnp.where(lane == 16 + h, mass, merged)
    return mass_rows, rest_rows, merged


def exact_forward_kernel(
    starts, qs, cls, ks, vs, stats, rcol, att_out, rows_out, merged_out, att_s, mix_s
):
    rows, width = rcol.shape[0], qs.shape[1]
    heads = width // HEAD_DIM
    tiles = rows // 128
    mass_rows, rest_rows, merged = merge_stats(stats, heads, width)
    rows_out[:, :width] = mass_rows
    rows_out[:, width:] = rest_rows
    merged_out[...] = merged
    both = jnp.concatenate([mass_rows, rest_rows], axis=1)
    high = both.astype(BF16)
    low = (both - high.astype(F32)).astype(BF16)
    lane = iota((128, 128), 1)

    def spread(i, carry):
        at = pl.ds(pl.multiple_of(i * 128, 128), 128)
        member = (cls[at, :] == lane).astype(BF16)
        mix_s[at, :] = dot(member, high) + dot(member, low)
        return carry

    lax.fori_loop(0, tiles + 1, spread, 0)
    slot_cluster = iota((WIN, GSLOTS), 1) // TOPK

    def group(g, carry):
        at = pl.ds(pl.multiple_of(g * GSLOTS, GSLOTS), GSLOTS)
        keys = block_diagonal(ks[at, :], heads)
        values = block_diagonal(vs[at, :], heads)
        first, last = starts[0, g * GROUP], starts[0, g * GROUP + GROUP]
        base = first // 16 * 16
        windows = jnp.where(last > first, (last - base + WIN - 1) // WIN, 0)

        def window(w, carry):
            row = pl.multiple_of(base + w * WIN, 16)
            here = pl.ds(row, WIN)
            mine = cls[here, :] == slot_cluster + g * GROUP
            scores = dot_nt(qs[here, :], keys) * SCALE
            weights = []
            for h in range(heads):
                part = jnp.where(mine, scores[:, h * GSLOTS : (h + 1) * GSLOTS], NEGATIVE)
                raised = jnp.where(mine, jnp.exp(part - jnp.max(part, 1, keepdims=True)), 0.0)
                total = jnp.maximum(jnp.sum(raised, 1, keepdims=True), 0.5)
                weights.append((raised / total).astype(BF16))
            out = dot(jnp.concatenate(weights, axis=1), values)
            mix = mix_s[here, :]
            place = iota((WIN, 1), 0) + row
            inside = (place >= first) & (place < last)
            att_s[here, :] = jnp.where(inside, mix[:, :width] * out + mix[:, width:], att_s[here, :])
            return carry

        return lax.fori_loop(0, windows, window, carry)

    lax.fori_loop(0, GROUPS, group, 0)

    def unplace(i, carry):
        at = pl.ds(pl.multiple_of(i * 128, 128), 128)
        chosen = (iota((128, rows), 1) == rcol[at, :].astype(jnp.int32)).astype(BF16)
        att_out[at, :] = dot(chosen, att_s[:rows, :].astype(BF16)).astype(BF16)
        return carry

    lax.fori_loop(0, tiles, unplace, 0)


def exact_forward(starts, qs, cls, ks, vs, stats, rcol):
    rows, width = rcol.shape[0], qs.shape[1]
    shape = jax.ShapeDtypeStruct
    return pl.pallas_call(
        exact_forward_kernel,
        out_shape=(
            shape((rows, width), BF16),
            shape((CLP, 2 * width), F32),
            shape((CLP, 128), F32),
        ),
        in_specs=[pl.BlockSpec(memory_space=pltpu.SMEM)] + vmem(6),
        out_specs=tuple(vmem(3)),
        scratch_shapes=[
            pltpu.VMEM((rows + WIN, width), F32),
            pltpu.VMEM((rows + WIN, 2 * width), F32),
        ],
        compiler_params=pltpu.CompilerParams(vmem_limit_bytes=40 << 20),
        name="exact_forward",
    )(starts, qs, cls, ks, vs, stats, rcol)


def exact_backward_kernel(
    starts, qs, cls, ks, vs, rows_in, rcol, rrow, grad,
    dq_out, dk_out, dv_out, centre_out,
    grad_s, mass_s, dq_s, part_s, dk_s, dv_s,
):
    rows, width = rcol.shape[0], qs.shape[1]
    heads = width // HEAD_DIM
    tiles = rows // 128
    mass_rows = rows_in[:, :width]
    high = mass_rows.astype(BF16)
    low = (mass_rows - high.astype(F32)).astype(BF16)
    lane = iota((128, 128), 1)
    rank_row = rrow[:1, :].astype(jnp.int32)

    def place(i, carry):
        at = pl.ds(pl.multiple_of(i * 128, 128), 128)
        chosen = (iota((128, rows), 0) + i * 128 == rank_row).astype(BF16)
        grad_s[at, :] = dot(chosen, grad[...]).astype(BF16)
        member = (cls[at, :] == lane).astype(BF16)
        mass_s[at, :] = dot(member, high) + dot(member, low)
        return carry

    lax.fori_loop(0, tiles, place, 0)
    grad_s[rows:, :] = jnp.zeros((WIN, width), BF16)
    mass_s[rows:, :] = jnp.zeros((WIN, width), F32)
    slot_cluster = iota((WIN, GSLOTS), 1) // TOPK

    def group(g, carry):
        at = pl.ds(pl.multiple_of(g * GSLOTS, GSLOTS), GSLOTS)
        keys = block_diagonal(ks[at, :], heads)
        values = block_diagonal(vs[at, :], heads)
        first, last = starts[0, g * GROUP], starts[0, g * GROUP + GROUP]
        base = first // 16 * 16
        windows = jnp.where(last > first, (last - base + WIN - 1) // WIN, 0)
        dk_s[...] = jnp.zeros_like(dk_s)
        dv_s[...] = jnp.zeros_like(dv_s)

        def window(w, carry):
            row = pl.multiple_of(base + w * WIN, 16)
            here = pl.ds(row, WIN)
            mine = cls[here, :] == slot_cluster + g * GROUP
            query, upstream = qs[here, :], grad_s[here, :]
            scores = dot_nt(query, keys) * SCALE
            against = dot_nt(upstream, values)
            mass = mass_s[here, :]
            weights, score_grads = [], []
            mass_part = jnp.zeros((WIN, width), F32)
            for h in range(heads):
                cut = slice(h * GSLOTS, (h + 1) * GSLOTS)
                part = jnp.where(mine, scores[:, cut], NEGATIVE)
                raised = jnp.where(mine, jnp.exp(part - jnp.max(part, 1, keepdims=True)), 0.0)
                total = jnp.maximum(jnp.sum(raised, 1, keepdims=True), 0.5)
                probs = raised / total
                meeting = jnp.sum(probs * against[:, cut], 1, keepdims=True)
                weighted = probs * mass[:, h * HEAD_DIM : h * HEAD_DIM + 1]
                weights.append(weighted.astype(BF16))
                score_grads.append((weighted * (against[:, cut] - meeting)).astype(BF16))
                mass_part = jnp.where(head_lanes(width, h), meeting, mass_part)
            score_grad = jnp.concatenate(score_grads, axis=1)
            weight = jnp.concatenate(weights, axis=1)
            place = iota((WIN, 1), 0) + row
            inside = (place >= first) & (place < last)
            dq = dot(score_grad, keys) * SCALE
            dq_s[here, :] = jnp.where(inside, dq, dq_s[here, :])
            part_s[here, :] = jnp.where(inside, mass_part, part_s[here, :])
            dk_s[...] += diagonal_blocks(dot_tn(score_grad, query), heads) * SCALE
            dv_s[...] += diagonal_blocks(dot_tn(weight, upstream), heads)
            return carry

        lax.fori_loop(0, windows, window, 0)
        dk_out[at, :] = dk_s[...].astype(BF16)
        dv_out[at, :] = dv_s[...].astype(BF16)
        return carry

    lax.fori_loop(0, GROUPS, group, 0)
    centre_out[...] = jnp.zeros_like(centre_out)

    def unplace(i, carry):
        at = pl.ds(pl.multiple_of(i * 128, 128), 128)
        chosen = (iota((128, rows), 1) == rcol[at, :].astype(jnp.int32)).astype(BF16)
        dq_out[at, :] = dot(chosen, dq_s[:rows, :].astype(BF16))
        member = (cls[at, :] == lane).astype(BF16)
        pair = jnp.concatenate([part_s[at, :].astype(BF16), grad_s[at, :]], axis=1)
        centre_out[...] += dot_tn(member, pair)
        return carry

    lax.fori_loop(0, tiles, unplace, 0)


def exact_backward(starts, qs, cls, ks, vs, rows_in, rcol, rrow, grad):
    rows, width = rcol.shape[0], qs.shape[1]
    shape = jax.ShapeDtypeStruct
    return pl.pallas_call(
        exact_backward_kernel,
        out_shape=(
            shape((rows, width), F32),
            shape((SLOTS, width), BF16),
            shape((SLOTS, width), BF16),
            shape((CLP, 2 * width), F32),
        ),
        in_specs=[pl.BlockSpec(memory_space=pltpu.SMEM)] + vmem(8),
        out_specs=tuple(vmem(4)),
        scratch_shapes=[
            pltpu.VMEM((rows + WIN, width), BF16),
            pltpu.VMEM((rows + WIN, width), F32),
            pltpu.VMEM((rows + WIN, width), F32),
            pltpu.VMEM((rows + WIN, width), F32),
            pltpu.VMEM((GSLOTS, width), F32),
            pltpu.VMEM((GSLOTS, width), F32),
        ],
        compiler_params=pltpu.CompilerParams(vmem_limit_bytes=40 << 20),
        name="exact_backward",
    )(starts, qs, cls, ks, vs, rows_in, rcol, rrow, grad)


def centre_backward_kernel(
    lengths, k, v, centre, topk, tm, merged, rows_in, summed, dk_out, dv_out, part_out
):
    rows, width = k.shape
    heads = width // HEAD_DIM
    top = tm[...].astype(F32)
    outside = 1.0 - top
    same = sequence_masks(lengths, topk, rows)
    centre_blocks = block_diagonal(centre[...], heads)
    rest_grad = summed[:, width:].astype(BF16)
    rest_blocks = block_diagonal(rest_grad, heads)
    full = dot_nt(centre_blocks, k[...]) * SCALE
    against = dot_nt(rest_blocks, v[...])
    product = rest_grad.astype(F32) * rows_in[:, width:]
    score_grads, weights = [], []
    for h in range(heads):
        cut = slice(h * CLP, (h + 1) * CLP)
        largest, total = merged[:, h : h + 1], merged[:, 8 + h : 9 + h]
        mass = merged[:, 16 + h : 17 + h]
        mass_grad = summed[:, h * HEAD_DIM : h * HEAD_DIM + 1]
        probs = jnp.where(same, jnp.exp(full[cut] - largest) / total, 0.0)
        mean = mass * mass_grad + jnp.sum(
            jnp.where(head_lanes(width, h), product, 0.0), 1, keepdims=True
        )
        grad = against[cut] * outside + mass_grad * top
        score_grads.append((probs * (grad - mean)).astype(BF16))
        weights.append((probs * outside).astype(BF16))
    score_grad = jnp.concatenate(score_grads, axis=0)
    weight = jnp.concatenate(weights, axis=0)
    part_out[...] = diagonal_blocks(dot(score_grad, k[...]), heads) * SCALE
    dk_out[...] = dot_tn(score_grad, centre_blocks) * SCALE
    dv_out[...] = dot_tn(weight, rest_blocks)


def centre_backward(lengths, k, v, centre, topk, tm, merged, rows_in, summed):
    rows, width = k.shape
    shape = jax.ShapeDtypeStruct
    return pl.pallas_call(
        centre_backward_kernel,
        out_shape=(
            shape((rows, width), F32),
            shape((rows, width), F32),
            shape((CLP, width), F32),
        ),
        in_specs=[pl.BlockSpec(memory_space=pltpu.SMEM)] + vmem(8),
        out_specs=tuple(vmem(3)),
        compiler_params=pltpu.CompilerParams(vmem_limit_bytes=40 << 20),
        name="centre_backward",
    )(lengths, k, v, centre, topk, tm, merged, rows_in, summed)


def gather_kernel(scol, table, out):
    rows = table.shape[0]
    own_start = lax.axis_index("dm") * rows

    def tile(i, carry):
        at = pl.ds(pl.multiple_of(i * 128, 128), 128)
        chosen = (scol[at, :] == iota((128, rows), 1) + own_start).astype(BF16)
        out[at, :] = dot(chosen, table[...]).astype(BF16)
        return carry

    lax.fori_loop(0, SLOTS // 128, tile, 0)


def gather_slots(scol, table):
    return pl.pallas_call(
        gather_kernel,
        out_shape=jax.ShapeDtypeStruct((SLOTS, table.shape[1]), BF16),
        in_specs=vmem(2),
        out_specs=vmem(1)[0],
        compiler_params=pltpu.CompilerParams(vmem_limit_bytes=40 << 20),
        name="gather_slots",
    )(scol, table)


def scatter_kernel(srow, slots, base, out):
    rows = out.shape[0]
    own_start = lax.axis_index("dm") * rows

    def tile(i, carry):
        at = pl.ds(pl.multiple_of(i * 128, 128), 128)
        chosen = (srow[...] == iota((128, SLOTS), 0) + own_start + i * 128).astype(BF16)
        out[at, :] = (base[at, :] + dot(chosen, slots[...])).astype(BF16)
        return carry

    lax.fori_loop(0, rows // 128, tile, 0)


def scatter_slots(srow, slots, base):
    return pl.pallas_call(
        scatter_kernel,
        out_shape=jax.ShapeDtypeStruct(base.shape, BF16),
        in_specs=vmem(3),
        out_specs=vmem(1)[0],
        compiler_params=pltpu.CompilerParams(vmem_limit_bytes=40 << 20),
        name="scatter_slots",
    )(srow, slots, base)


def shards(
    tokens,
    clusters,
    top_keys,
    lengths,
    qkv_weight,
    out_weight,
    first_gain,
    first_bias,
    second_gain,
    second_bias,
    expand_weight,
    shrink_weight,
    cotangent,
):
    row_count = tokens.shape[0]
    width = qkv_weight.shape[2]
    inputs = tokens.astype(F32)
    expand_full, shrink_full = (
        lax.all_gather(expand_weight, ("dp", "dm"), axis=0, tiled=True),
        lax.all_gather(shrink_weight, ("dp", "dm"), axis=1, tiled=True),
    )
    topk = jnp.pad(top_keys, ((0, CLP - CL), (0, 0)), constant_values=-1)
    flat = jnp.pad(top_keys.reshape(-1), (0, SLOTS - CL * TOPK), constant_values=-1)
    scol, srow = flat.reshape(SLOTS, 1), flat.reshape(1, SLOTS)

    first_normed, qs, k, v, csum, starts, rcol, rrow, cls = front(
        tokens, clusters, qkv_weight, first_gain, first_bias
    )
    csum = lax.psum(csum, "dm")
    slot_kv = lax.psum(gather_slots(scol, jnp.concatenate([k, v], axis=1)), "dm")
    ks, vs = slot_kv[:, :width], slot_kv[:, width:]
    centre, tm, stats = centre_forward(lengths, csum, k, v, topk)
    stats = lax.all_gather(stats, "dm", axis=0)
    attended, rows_in, merged = exact_forward(starts, qs, cls, ks, vs, stats, rcol)

    head_part = jnp.dot(attended, out_weight, preferred_element_type=F32)
    attention_sum = lax.psum(head_part.astype(BF16), "hid").astype(F32)
    middle = inputs + attention_sum
    normed_two, spread_two = norm_parts(middle)
    second_normed = (normed_two * second_gain + second_bias).astype(BF16)
    hidden = jnp.dot(second_normed, expand_full, preferred_element_type=F32)
    activated = jax.nn.gelu(hidden).astype(BF16)
    hidden_part = jnp.dot(activated, shrink_full, preferred_element_type=F32)
    hidden_sum = lax.psum(hidden_part.astype(BF16), "hid").astype(F32)
    result = (middle + hidden_sum).astype(BF16)
    upstream = cotangent.astype(F32)
    activated_grad = jnp.dot(cotangent, shrink_full.T, preferred_element_type=F32)
    shrink_local = jnp.dot(activated.T, cotangent, preferred_element_type=F32)
    gelu_value, gelu_pull = jax.vjp(jax.nn.gelu, hidden)
    hidden_grad = gelu_pull(activated_grad)[0].astype(BF16)
    expand_local = jnp.dot(second_normed.T, hidden_grad, preferred_element_type=F32)
    second_part = jnp.dot(hidden_grad, expand_full.T, preferred_element_type=F32)
    second_grad = lax.psum(second_part.astype(BF16), "hid").astype(F32)
    expand_grad, shrink_grad = (
        lax.psum_scatter(expand_local, ("dp", "dm"), scatter_dimension=0, tiled=True),
        lax.psum_scatter(shrink_local, ("dp", "dm"), scatter_dimension=1, tiled=True),
    )
    middle_inner, second_gain_part, second_bias_part = norm_back(
        second_grad, normed_two, spread_two, second_gain
    )
    middle_grad = upstream + middle_inner
    branch_grad = middle_grad.astype(BF16)
    out_grad_part = jnp.dot(attended.T, branch_grad, preferred_element_type=F32)
    attended_grad = jnp.dot(branch_grad, out_weight.T, preferred_element_type=F32).astype(BF16)

    dq, dks, dvs, summed = exact_backward(
        starts, qs, cls, ks, vs, rows_in, rcol, rrow, attended_grad
    )
    summed = lax.psum(summed, "dm")
    dkc, dvc, centre_part = centre_backward(
        lengths, k, v, centre, topk, tm, merged, rows_in, summed
    )
    centre_grad = lax.psum(centre_part, "dm").astype(BF16)
    slot_grads = lax.psum(jnp.concatenate([dks, dvs], axis=1), "dm")
    key_value = scatter_slots(srow, slot_grads, jnp.concatenate([dkc, dvc], axis=1))
    counts = csum[:, width : width + 1]
    member = clusters[:, None] == jnp.arange(CLP, dtype=jnp.int32)[None, :]
    query_centre = jnp.dot(
        member.astype(BF16), centre_grad, preferred_element_type=F32
    ) / jnp.dot(member.astype(F32), counts, precision=HIGHEST)
    query_total = (dq + query_centre).astype(BF16)
    projected_grad = jnp.stack([query_total, key_value[:, :width], key_value[:, width:]])
    projection_part = jnp.einsum(
        "rd,kre->kde", first_normed, projected_grad, preferred_element_type=F32
    )
    first_part = jnp.einsum("kre,kde->rd", projected_grad, qkv_weight, preferred_element_type=F32)
    first_grad = lax.psum(first_part.astype(BF16), "hid").astype(F32)
    normed_one, spread_one = norm_parts(inputs)
    inputs_inner, first_gain_part, first_bias_part = norm_back(
        first_grad, normed_one, spread_one, first_gain
    )
    tokens_grad = (middle_grad + inputs_inner).astype(BF16)
    qkv_grad, out_grad, first_gain_grad, first_bias_grad, second_gain_grad, second_bias_grad = (
        lax.psum(
            (
                projection_part,
                out_grad_part,
                first_gain_part,
                first_bias_part,
                second_gain_part,
                second_bias_part,
            ),
            ("dp", "dm"),
        )
    )
    return (
        result,
        tokens_grad,
        qkv_grad,
        out_grad,
        first_gain_grad,
        first_bias_grad,
        second_gain_grad,
        second_bias_grad,
        expand_grad,
        shrink_grad,
    )


def solution(mesh):
    in_specs = (
        P(("dp", "dm"), None),
        P(("dp", "dm")),
        P("dp", None),
        P("dp"),
        P(None, None, "hid"),
        P("hid", None),
        P(),
        P(),
        P(),
        P(),
        P(("dp", "dm"), "hid"),
        P("hid", ("dp", "dm")),
        P(("dp", "dm"), None),
    )
    out_specs = (
        P(("dp", "dm"), None),
        P(("dp", "dm"), None),
        P(None, None, "hid"),
        P("hid", None),
        P(),
        P(),
        P(),
        P(),
        P(("dp", "dm"), "hid"),
        P("hid", ("dp", "dm")),
    )
    return jax.shard_map(shards, mesh=mesh, in_specs=in_specs, out_specs=out_specs, check_vma=False)
```

```python
import functools

import jax
import jax.numpy as jnp
from jax import lax
from jax.experimental import pallas as pl
from jax.experimental.pallas import tpu as pltpu
from jax.sharding import PartitionSpec as P

HEAD_DIM = 64
CL = 100
TOPK = 32
CLP = 128
SLOTS = 3328
GROUP = 8
GSLOTS = GROUP * TOPK
GROUPS = SLOTS // GSLOTS
WIN = 128
EPSILON = 1e-05
NEGATIVE = -1e30
HIGHEST = lax.Precision.HIGHEST
F32 = jnp.float32
BF16 = jnp.bfloat16
MESH = pl.DeviceIdType.MESH
NT = (((1,), (1,)), ((), ()))
TN = (((0,), (0,)), ((), ()))
SCALE = HEAD_DIM ** (-0.5)


def dot(a, b):
    return jnp.dot(a, b, preferred_element_type=F32)


def dot_nt(a, b):
    return lax.dot_general(a, b, NT, preferred_element_type=F32)


def dot_tn(a, b):
    return lax.dot_general(a, b, TN, preferred_element_type=F32)


def iota(shape, dim):
    return lax.broadcasted_iota(jnp.int32, shape, dim)


def norm_parts(values):
    centred = values - jnp.mean(values, -1, keepdims=True)
    spread = lax.rsqrt(jnp.mean(centred * centred, -1, keepdims=True) + EPSILON)
    return (centred * spread, spread)


def norm_back(upstream, normed, spread, norm_gain):
    through = upstream * norm_gain
    inner = (
        through
        - jnp.mean(through, -1, keepdims=True)
        - normed * jnp.mean(through * normed, -1, keepdims=True)
    )
    return (spread * inner, jnp.sum(upstream * normed, 0), jnp.sum(upstream, 0))


def head_lanes(width, head):
    lane = iota((1, width), 1)
    return lane // HEAD_DIM == head


def block_diagonal(rows, heads):
    width = rows.shape[1]
    zero = jnp.zeros_like(rows)
    return jnp.concatenate(
        [jnp.where(head_lanes(width, h), rows, zero) for h in range(heads)], axis=0
    )


def diagonal_blocks(full, heads):
    rows, width = full.shape[0] // heads, full.shape[1]
    out = full[:rows]
    for h in range(1, heads):
        out = jnp.where(head_lanes(width, h), full[h * rows : (h + 1) * rows], out)
    return out


def vmem(n):
    return [pl.BlockSpec(memory_space=pltpu.VMEM)] * n


HALF = SLOTS // 2
CHUNK = 128
CHUNKS = HALF // CHUNK
LAG = 2


def small_exchange(buf, sends, recvs, me, parts):
    copies = []
    for step in range(1, parts):
        copies.append(
            pltpu.make_async_remote_copy(
                src_ref=buf.at[me],
                dst_ref=buf.at[me],
                send_sem=sends.at[step],
                recv_sem=recvs.at[step],
                device_id={"dm": lax.rem(me + step, parts)},
                device_id_type=MESH,
            )
        )
    return copies


def front_kernel(
    lengths, tok, ccol, weight, gain, bias, scol, topk,
    fn_out, sfn_out, qs_out, k_out, v_out, ks_out, vs_out, starts_out, rcol_out, rrow_out,
    cls_out, centre_out, tm_out, rows_out, merged_out, count_out,
    q_ref, member_ref, csum, cbuf, rbuf, sbuf, own, to_right, to_left, from_left, from_right,
    csend, crecv, rsend, rrecv, ssend, srecv,
    send_right, recv_left, send_left, recv_right, send_x, recv_x, send_core, recv_core,
    send_relay, recv_relay,
):
    rows = tok.shape[0]
    width = weight.shape[2]
    heads = width // HEAD_DIM
    half_width = tok.shape[1] // 2
    tiles = rows // 128
    parts = lax.axis_size("dm")
    me, hid = lax.axis_index("dm"), lax.axis_index("hid")
    core, side = lax.rem(hid, 2), hid // 2
    core_peer = {"hid": hid + 1 - 2 * core}
    x_peer = {"hid": hid + 2 - 4 * side}
    lower = (iota((128, 128), 0) > iota((128, 128), 1)).astype(BF16)
    lane = iota((128, 128), 1)

    barrier = pltpu.get_barrier_semaphore()
    for step in range(1, parts):
        pl.semaphore_signal(
            barrier, inc=1, device_id={"dm": lax.rem(me + step, parts)}, device_id_type=MESH
        )
    for peer in (core_peer, x_peer):
        pl.semaphore_signal(barrier, inc=1, device_id=peer, device_id_type=MESH)

    csum[...] = jnp.zeros_like(csum)

    def tile(i, running):
        at = pl.ds(pl.multiple_of(i * 128, 128), 128)
        normed, _ = norm_parts(tok[at, :].astype(F32))
        first = (normed * gain[...] + bias[...]).astype(BF16)
        fn_out[at, :] = first
        q = dot(first, weight[0]).astype(BF16)
        q_ref[at, :] = q
        k_out[at, :] = dot(first, weight[1]).astype(BF16)
        v_out[at, :] = dot(first, weight[2]).astype(BF16)
        member = (ccol[at, :] == lane).astype(F32)
        low = member.astype(BF16)
        member_ref[at, :] = low
        extended = jnp.concatenate([q, jnp.ones((128, 256 - width), BF16)], axis=1)
        csum[...] += dot_tn(low, extended)
        earlier = dot(lower, low) + running
        rcol_out[at, :] = jnp.sum(member * earlier, 1, keepdims=True)
        return running + jnp.sum(member, 0, keepdims=True)

    counts = lax.fori_loop(0, tiles, tile, jnp.zeros((1, 128), F32))
    sums = csum[...]
    sixteens = jnp.floor(sums * 0.0625)
    wide = iota((CLP, 256), 1)
    packed = jnp.where(wide == width, sixteens, jnp.where(wide == width + 1, sums - 16.0 * sixteens, sums))
    cbuf[me] = packed.astype(BF16)
    pl.semaphore_wait(barrier, parts + 1)
    centre_copies = small_exchange(cbuf, csend, crecv, me, parts)
    for copy in centre_copies:
        copy.start()

    @pl.when(me == 0)
    def _():
        from_left[...] = jnp.zeros_like(from_left)

    @pl.when(me == parts - 1)
    def _():
        from_right[...] = jnp.zeros_like(from_right)

    columns = pl.ds(pl.multiple_of(side * half_width, 128), half_width)
    other_columns = pl.ds(pl.multiple_of((1 - side) * half_width, 128), half_width)
    own_start = me * rows

    def chunk_rows(i, which):
        return pl.ds(pl.multiple_of(which * HALF + i * CHUNK, CHUNK), CHUNK)

    def right_copy(i):
        return pltpu.make_async_remote_copy(
            src_ref=to_right.at[i], dst_ref=from_left.at[i], send_sem=send_right.at[i],
            recv_sem=recv_left.at[i], device_id={"dm": lax.rem(me + 1, parts)}, device_id_type=MESH,
        )

    def left_copy(i):
        return pltpu.make_async_remote_copy(
            src_ref=to_left.at[i], dst_ref=from_right.at[i], send_sem=send_left.at[i],
            recv_sem=recv_right.at[i], device_id={"dm": lax.rem(me + parts - 1, parts)},
            device_id_type=MESH,
        )

    def x_copy(i):
        block = sfn_out.at[chunk_rows(i, core), columns]
        return pltpu.make_async_remote_copy(
            src_ref=block, dst_ref=block, send_sem=send_x.at[i], recv_sem=recv_x.at[i],
            device_id=x_peer, device_id_type=MESH,
        )

    def core_copy(i):
        block = sfn_out.at[chunk_rows(i, core), columns]
        return pltpu.make_async_remote_copy(
            src_ref=block, dst_ref=block, send_sem=send_core.at[i], recv_sem=recv_core.at[i],
            device_id=core_peer, device_id_type=MESH,
        )

    def relay_copy(i):
        block = sfn_out.at[chunk_rows(i, core), other_columns]
        return pltpu.make_async_remote_copy(
            src_ref=block, dst_ref=block, send_sem=send_relay.at[i], recv_sem=recv_relay.at[i],
            device_id=core_peer, device_id_type=MESH,
        )

    def when_chunk(i, work):
        @pl.when((i >= 0) & (i < CHUNKS))
        def _():
            work(i)

    def make_own(i):
        chosen = (scol[chunk_rows(i, core), :] == iota((CHUNK, rows), 1) + own_start).astype(BF16)
        own[i] = dot(chosen, fn_out[:, columns]).astype(BF16)

    def go_right(i):
        @pl.when(me > 0)
        def _():
            right_copy(i).wait_recv()

        @pl.when(me < parts - 1)
        def _():
            to_right[i] = own[i] + from_left[i]
            right_copy(i).start()

    def go_left(i):
        @pl.when(me < parts - 1)
        def _():
            left_copy(i).wait_recv()

        @pl.when(me > 0)
        def _():
            to_left[i] = own[i] + from_right[i]
            left_copy(i).start()

    def finish(i):
        sfn_out[chunk_rows(i, core), columns] = own[i] + from_left[i] + from_right[i]
        x_copy(i).start()
        core_copy(i).start()

    def relay(i):
        x_copy(i).wait_recv()
        relay_copy(i).start()

    far = jnp.maximum(me, parts - 1 - me)

    def ticks(first, last):
        def tick(t, carry):
            when_chunk(t, make_own)
            when_chunk(t - LAG * me, go_right)
            when_chunk(t - LAG * (parts - 1 - me), go_left)
            when_chunk(t - LAG * far, finish)
            when_chunk(t - LAG * far - LAG, relay)
            return carry

        lax.fori_loop(first, last, tick, 0)

    before = (iota((128, 128), 0) < iota((128, 128), 1)).astype(F32)
    starts = jnp.dot(
        jnp.broadcast_to(counts, (8, 128)), before, precision=HIGHEST, preferred_element_type=F32
    )
    starts_out[...] = starts.astype(jnp.int32)

    def ranks(i, carry):
        at = pl.ds(pl.multiple_of(i * 128, 128), 128)
        member = member_ref[at, :].astype(F32)
        rank = rcol_out[at, :] + jnp.sum(member * starts[:1], 1, keepdims=True)
        rcol_out[at, :] = rank
        turned = jnp.transpose(jnp.broadcast_to(rank, (128, 128)))
        rrow_out[:, at] = turned[:8]
        return carry

    def place(i, carry):
        at = pl.ds(pl.multiple_of(i * 128, 128), 128)
        rank_row = rrow_out[:1, :].astype(jnp.int32)
        chosen = (iota((128, rows), 0) + i * 128 == rank_row).astype(BF16)
        qs_out[at, :] = dot(chosen, q_ref[...]).astype(BF16)
        sorted_member = dot(chosen, member_ref[...])
        cls_out[at, :] = jnp.sum(sorted_member * lane.astype(F32), 1, keepdims=True).astype(
            jnp.int32
        )
        return carry

    ticks(0, 3)
    lax.fori_loop(0, tiles, ranks, 0)
    ticks(3, 5)
    lax.fori_loop(0, tiles // 2, place, 0)
    ticks(5, 7)
    lax.fori_loop(tiles // 2, tiles, place, 0)
    qs_out[rows:, :] = jnp.zeros((WIN, width), BF16)
    cls_out[rows:, :] = jnp.full((WIN, 1), -1, jnp.int32)
    ticks(7, 9)

    for copy in centre_copies:
        copy.wait_recv()
    gathered = cbuf[0].astype(F32)
    for d in range(1, parts):
        gathered += cbuf[d].astype(F32)
    count = jnp.maximum(16.0 * gathered[:, width : width + 1] + gathered[:, width + 1 : width + 2], 1.0)
    count_out[...] = jnp.broadcast_to(count, (CLP, 128))
    centre = (gathered[:, :width] / count).astype(BF16)
    centre_out[...] = centre
    here = iota((CLP, rows), 1) + own_start
    hit = topk[:, :1] == here
    for t in range(1, TOPK):
        hit = hit | (topk[:, t : t + 1] == here)
    top = hit.astype(F32)
    tm_out[...] = top.astype(BF16)
    ticks(9, 11)
    outside = 1.0 - top
    same = sequence_masks(lengths, topk, rows)
    full = dot_nt(block_diagonal(centre, heads), k_out[...]) * SCALE
    stats = jnp.zeros((CLP, 128), F32)
    weights = []
    for h in range(heads):
        scores = jnp.where(same, full[h * CLP : (h + 1) * CLP], NEGATIVE)
        largest = jnp.max(scores, 1, keepdims=True)
        raised = jnp.exp(scores - largest)
        total = jnp.sum(raised, 1, keepdims=True)
        mass = jnp.sum(raised * top, 1, keepdims=True)
        weights.append((raised * outside).astype(BF16))
        stats = jnp.where(lane == h, largest, stats)
        stats = jnp.where(lane == 8 + h, total, stats)
        stats = jnp.where(lane == 16 + h, mass, stats)
    rest = diagonal_blocks(dot(jnp.concatenate(weights, axis=0), v_out[...]), heads)
    rbuf[me] = rest.astype(BF16)
    sbuf[me] = jnp.transpose(stats)[:24]
    rest_copies = small_exchange(rbuf, rsend, rrecv, me, parts)
    stat_copies = small_exchange(sbuf, ssend, srecv, me, parts)
    for copy in rest_copies + stat_copies:
        copy.start()
    ticks(11, CHUNKS + LAG * parts)

    for copy in rest_copies + stat_copies:
        copy.wait_recv()
    largest = sbuf[0][:8]
    for d in range(1, parts):
        largest = jnp.maximum(largest, sbuf[d][:8])
    total = jnp.zeros((8, 128), F32)
    mass = jnp.zeros((8, 128), F32)
    factors = []
    for d in range(parts):
        factor = jnp.exp(sbuf[d][:8] - largest)
        total += factor * sbuf[d][8:16]
        mass += factor * sbuf[d][16:24]
        factors.append(factor)
    live = iota((8, 128), 0) < heads
    total = jnp.where(live, total, 1.0)
    mass = mass / total
    table = [largest, total, mass] + [factor / total for factor in factors]
    table.append(jnp.zeros((128 - 8 * len(table), 128), F32))
    columns_table = jnp.transpose(jnp.concatenate(table, axis=0))
    merged_out[...] = columns_table
    mass_rows = jnp.zeros((CLP, width), F32)
    rest_rows = jnp.zeros((CLP, width), F32)
    for h in range(heads):
        mine = head_lanes(width, h)
        mass_rows = jnp.where(mine, columns_table[:, 16 + h : 17 + h], mass_rows)
        rest = jnp.zeros((CLP, width), F32)
        for d in range(parts):
            lane_at = 24 + 8 * d + h
            rest += columns_table[:, lane_at : lane_at + 1] * rbuf[d].astype(F32)
        rest_rows = jnp.where(mine, rest, rest_rows)
    rows_out[:, :width] = mass_rows
    rows_out[:, width:] = rest_rows

    def arrive(i, carry):
        core_copy(i).wait_recv()
        relay_copy(i).wait_recv()
        return carry

    def project(i, carry):
        at = pl.ds(pl.multiple_of(i * GSLOTS, GSLOTS), GSLOTS)
        ks_out[at, :] = dot(sfn_out[at, :], weight[1]).astype(BF16)
        vs_out[at, :] = dot(sfn_out[at, :], weight[2]).astype(BF16)
        return carry

    lax.fori_loop(0, CHUNKS, arrive, 0)
    lax.fori_loop(0, GROUPS, project, 0)

    def drain(i, carry):
        @pl.when(me < parts - 1)
        def _():
            right_copy(i).wait_send()

        @pl.when(me > 0)
        def _():
            left_copy(i).wait_send()

        x_copy(i).wait_send()
        core_copy(i).wait_send()
        relay_copy(i).wait_send()
        return carry

    lax.fori_loop(0, CHUNKS, drain, 0)
    for copy in centre_copies + rest_copies + stat_copies:
        copy.wait_send()


def front(lengths, tokens, clusters, qkv_weight, gain, bias, scol, topk, parts):
    rows, model = tokens.shape
    width = qkv_weight.shape[2]
    shape = jax.ShapeDtypeStruct
    dma = pltpu.SemaphoreType.DMA
    chain = pltpu.VMEM((CHUNKS, CHUNK, model // 2), BF16)
    return pl.pallas_call(
        front_kernel,
        out_shape=(
            shape(tokens.shape, BF16),
            shape((SLOTS, model), BF16),
            shape((rows + WIN, width), BF16),
            shape((rows, width), BF16),
            shape((rows, width), BF16),
            shape((SLOTS, width), BF16),
            shape((SLOTS, width), BF16),
            shape((8, 128), jnp.int32),
            shape((rows, 1), F32),
            shape((8, rows), F32),
            shape((rows + WIN, 1), jnp.int32),
            shape((CLP, width), BF16),
            shape((CLP, rows), BF16),
            shape((CLP, 2 * width), F32),
            shape((CLP, 128), F32),
            shape((CLP, 128), F32),
        ),
        in_specs=[pl.BlockSpec(memory_space=pltpu.SMEM)] + vmem(7),
        out_specs=tuple(vmem(16)),
        scratch_shapes=[
            pltpu.VMEM((rows, width), BF16),
            pltpu.VMEM((rows, 128), BF16),
            pltpu.VMEM((CLP, 256), F32),
            pltpu.VMEM((parts, CLP, 256), BF16),
            pltpu.VMEM((parts, CLP, width), BF16),
            pltpu.VMEM((parts, 24, 128), F32),
            chain, chain, chain, chain, chain,
        ]
        + [dma((parts,))] * 6
        + [dma((CHUNKS,))] * 10,
        compiler_params=pltpu.CompilerParams(
            vmem_limit_bytes=56 << 20, collective_id=0, has_side_effects=True
        ),
        name="front",
    )(
        lengths, tokens, clusters.reshape(rows, 1), qkv_weight, gain[None], bias[None], scol, topk
    )


def sequence_masks(lengths, topk, rows):
    own_start = lax.axis_index("dm") * rows
    key_second = iota((1, rows), 1) + own_start >= lengths[0]
    centre_second = topk[:, :1] >= lengths[0]
    return key_second == centre_second


def exact_forward_kernel(
    starts, qs, cls, ks, vs, both, rcol, att_out, att_s, mix_s
):
    rows, width = rcol.shape[0], qs.shape[1]
    heads = width // HEAD_DIM
    tiles = rows // 128
    high = both[...].astype(BF16)
    low = (both[...] - high.astype(F32)).astype(BF16)
    lane = iota((128, 128), 1)

    def spread(i, carry):
        at = pl.ds(pl.multiple_of(i * 128, 128), 128)
        member = (cls[at, :] == lane).astype(BF16)
        mix_s[at, :] = dot(member, high) + dot(member, low)
        return carry

    lax.fori_loop(0, tiles + 1, spread, 0)
    slot_cluster = iota((WIN, GSLOTS), 1) // TOPK

    def group(g, carry):
        at = pl.ds(pl.multiple_of(g * GSLOTS, GSLOTS), GSLOTS)
        keys = block_diagonal(ks[at, :], heads)
        values = block_diagonal(vs[at, :], heads)
        first, last = starts[0, g * GROUP], starts[0, g * GROUP + GROUP]
        base = first // 16 * 16
        windows = jnp.where(last > first, (last - base + WIN - 1) // WIN, 0)

        def window(w, carry):
            row = pl.multiple_of(base + w * WIN, 16)
            here = pl.ds(row, WIN)
            mine = cls[here, :] == slot_cluster + g * GROUP
            scores = dot_nt(qs[here, :], keys) * SCALE
            weights = []
            for h in range(heads):
                part = jnp.where(mine, scores[:, h * GSLOTS : (h + 1) * GSLOTS], NEGATIVE)
                raised = jnp.where(mine, jnp.exp(part - jnp.max(part, 1, keepdims=True)), 0.0)
                total = jnp.maximum(jnp.sum(raised, 1, keepdims=True), 0.5)
                weights.append((raised / total).astype(BF16))
            out = dot(jnp.concatenate(weights, axis=1), values)
            mix = mix_s[here, :]
            place = iota((WIN, 1), 0) + row
            inside = (place >= first) & (place < last)
            att_s[here, :] = jnp.where(inside, mix[:, :width] * out + mix[:, width:], att_s[here, :])
            return carry

        return lax.fori_loop(0, windows, window, carry)

    lax.fori_loop(0, GROUPS, group, 0)

    def unplace(i, carry):
        at = pl.ds(pl.multiple_of(i * 128, 128), 128)
        chosen = (iota((128, rows), 1) == rcol[at, :].astype(jnp.int32)).astype(BF16)
        att_out[at, :] = dot(chosen, att_s[:rows, :].astype(BF16)).astype(BF16)
        return carry

    lax.fori_loop(0, tiles, unplace, 0)


def exact_forward(starts, qs, cls, ks, vs, both, rcol):
    rows, width = rcol.shape[0], qs.shape[1]
    shape = jax.ShapeDtypeStruct
    return pl.pallas_call(
        exact_forward_kernel,
        out_shape=shape((rows, width), BF16),
        in_specs=[pl.BlockSpec(memory_space=pltpu.SMEM)] + vmem(6),
        out_specs=vmem(1)[0],
        scratch_shapes=[
            pltpu.VMEM((rows + WIN, width), F32),
            pltpu.VMEM((rows + WIN, 2 * width), F32),
        ],
        compiler_params=pltpu.CompilerParams(vmem_limit_bytes=40 << 20),
        name="exact_forward",
    )(starts, qs, cls, ks, vs, both, rcol)


def exact_backward_kernel(
    starts, qs, cls, ks, vs, rows_in, rcol, rrow, grad,
    dq_out, dk_out, dv_out, centre_out,
    grad_s, mass_s, dq_s, part_s, dk_s, dv_s,
):
    rows, width = rcol.shape[0], qs.shape[1]
    heads = width // HEAD_DIM
    tiles = rows // 128
    mass_rows = rows_in[:, :width]
    high = mass_rows.astype(BF16)
    low = (mass_rows - high.astype(F32)).astype(BF16)
    lane = iota((128, 128), 1)
    rank_row = rrow[:1, :].astype(jnp.int32)

    def place(i, carry):
        at = pl.ds(pl.multiple_of(i * 128, 128), 128)
        chosen = (iota((128, rows), 0) + i * 128 == rank_row).astype(BF16)
        grad_s[at, :] = dot(chosen, grad[...]).astype(BF16)
        member = (cls[at, :] == lane).astype(BF16)
        mass_s[at, :] = dot(member, high) + dot(member, low)
        return carry

    lax.fori_loop(0, tiles, place, 0)
    grad_s[rows:, :] = jnp.zeros((WIN, width), BF16)
    mass_s[rows:, :] = jnp.zeros((WIN, width), F32)
    slot_cluster = iota((WIN, GSLOTS), 1) // TOPK

    def group(g, carry):
        at = pl.ds(pl.multiple_of(g * GSLOTS, GSLOTS), GSLOTS)
        keys = block_diagonal(ks[at, :], heads)
        values = block_diagonal(vs[at, :], heads)
        first, last = starts[0, g * GROUP], starts[0, g * GROUP + GROUP]
        base = first // 16 * 16
        windows = jnp.where(last > first, (last - base + WIN - 1) // WIN, 0)
        dk_s[...] = jnp.zeros_like(dk_s)
        dv_s[...] = jnp.zeros_like(dv_s)

        def window(w, carry):
            row = pl.multiple_of(base + w * WIN, 16)
            here = pl.ds(row, WIN)
            mine = cls[here, :] == slot_cluster + g * GROUP
            query, upstream = qs[here, :], grad_s[here, :]
            scores = dot_nt(query, keys) * SCALE
            against = dot_nt(upstream, values)
            mass = mass_s[here, :]
            weights, score_grads = [], []
            mass_part = jnp.zeros((WIN, width), F32)
            for h in range(heads):
                cut = slice(h * GSLOTS, (h + 1) * GSLOTS)
                part = jnp.where(mine, scores[:, cut], NEGATIVE)
                raised = jnp.where(mine, jnp.exp(part - jnp.max(part, 1, keepdims=True)), 0.0)
                total = jnp.maximum(jnp.sum(raised, 1, keepdims=True), 0.5)
                probs = raised / total
                meeting = jnp.sum(probs * against[:, cut], 1, keepdims=True)
                weighted = probs * mass[:, h * HEAD_DIM : h * HEAD_DIM + 1]
                weights.append(weighted.astype(BF16))
                score_grads.append((weighted * (against[:, cut] - meeting)).astype(BF16))
                mass_part = jnp.where(head_lanes(width, h), meeting, mass_part)
            score_grad = jnp.concatenate(score_grads, axis=1)
            weight = jnp.concatenate(weights, axis=1)
            place = iota((WIN, 1), 0) + row
            inside = (place >= first) & (place < last)
            dq = dot(score_grad, keys) * SCALE
            dq_s[here, :] = jnp.where(inside, dq, dq_s[here, :])
            part_s[here, :] = jnp.where(inside, mass_part, part_s[here, :])
            dk_s[...] += diagonal_blocks(dot_tn(score_grad, query), heads) * SCALE
            dv_s[...] += diagonal_blocks(dot_tn(weight, upstream), heads)
            return carry

        lax.fori_loop(0, windows, window, 0)
        dk_out[at, :] = dk_s[...].astype(BF16)
        dv_out[at, :] = dv_s[...].astype(BF16)
        return carry

    lax.fori_loop(0, GROUPS, group, 0)
    centre_out[...] = jnp.zeros_like(centre_out)

    def unplace(i, carry):
        at = pl.ds(pl.multiple_of(i * 128, 128), 128)
        chosen = (iota((128, rows), 1) == rcol[at, :].astype(jnp.int32)).astype(BF16)
        dq_out[at, :] = dot(chosen, dq_s[:rows, :].astype(BF16))
        member = (cls[at, :] == lane).astype(BF16)
        pair = jnp.concatenate([part_s[at, :].astype(BF16), grad_s[at, :]], axis=1)
        centre_out[...] += dot_tn(member, pair)
        return carry

    lax.fori_loop(0, tiles, unplace, 0)


def exact_backward(starts, qs, cls, ks, vs, rows_in, rcol, rrow, grad):
    rows, width = rcol.shape[0], qs.shape[1]
    shape = jax.ShapeDtypeStruct
    return pl.pallas_call(
        exact_backward_kernel,
        out_shape=(
            shape((rows, width), F32),
            shape((SLOTS, width), BF16),
            shape((SLOTS, width), BF16),
            shape((CLP, 2 * width), F32),
        ),
        in_specs=[pl.BlockSpec(memory_space=pltpu.SMEM)] + vmem(8),
        out_specs=tuple(vmem(4)),
        scratch_shapes=[
            pltpu.VMEM((rows + WIN, width), BF16),
            pltpu.VMEM((rows + WIN, width), F32),
            pltpu.VMEM((rows + WIN, width), F32),
            pltpu.VMEM((rows + WIN, width), F32),
            pltpu.VMEM((GSLOTS, width), F32),
            pltpu.VMEM((GSLOTS, width), F32),
        ],
        compiler_params=pltpu.CompilerParams(vmem_limit_bytes=40 << 20),
        name="exact_backward",
    )(starts, qs, cls, ks, vs, rows_in, rcol, rrow, grad)


def centre_backward_kernel(
    lengths, k, v, centre, topk, tm, merged, rows_in, summed, dk_out, dv_out, part_out
):
    rows, width = k.shape
    heads = width // HEAD_DIM
    top = tm[...].astype(F32)
    outside = 1.0 - top
    same = sequence_masks(lengths, topk, rows)
    centre_blocks = block_diagonal(centre[...], heads)
    rest_grad = summed[:, width:].astype(BF16)
    rest_blocks = block_diagonal(rest_grad, heads)
    full = dot_nt(centre_blocks, k[...]) * SCALE
    against = dot_nt(rest_blocks, v[...])
    product = rest_grad.astype(F32) * rows_in[:, width:]
    score_grads, weights = [], []
    for h in range(heads):
        cut = slice(h * CLP, (h + 1) * CLP)
        largest, total = merged[:, h : h + 1], merged[:, 8 + h : 9 + h]
        mass = merged[:, 16 + h : 17 + h]
        mass_grad = summed[:, h * HEAD_DIM : h * HEAD_DIM + 1]
        probs = jnp.where(same, jnp.exp(full[cut] - largest) / total, 0.0)
        mean = mass * mass_grad + jnp.sum(
            jnp.where(head_lanes(width, h), product, 0.0), 1, keepdims=True
        )
        grad = against[cut] * outside + mass_grad * top
        score_grads.append((probs * (grad - mean)).astype(BF16))
        weights.append((probs * outside).astype(BF16))
    score_grad = jnp.concatenate(score_grads, axis=0)
    weight = jnp.concatenate(weights, axis=0)
    part_out[...] = diagonal_blocks(dot(score_grad, k[...]), heads) * SCALE
    dk_out[...] = dot_tn(score_grad, centre_blocks) * SCALE
    dv_out[...] = dot_tn(weight, rest_blocks)


def centre_backward(lengths, k, v, centre, topk, tm, merged, rows_in, summed):
    rows, width = k.shape
    shape = jax.ShapeDtypeStruct
    return pl.pallas_call(
        centre_backward_kernel,
        out_shape=(
            shape((rows, width), F32),
            shape((rows, width), F32),
            shape((CLP, width), F32),
        ),
        in_specs=[pl.BlockSpec(memory_space=pltpu.SMEM)] + vmem(8),
        out_specs=tuple(vmem(3)),
        compiler_params=pltpu.CompilerParams(vmem_limit_bytes=40 << 20),
        name="centre_backward",
    )(lengths, k, v, centre, topk, tm, merged, rows_in, summed)


def scatter_kernel(srow, slots, base, out):
    rows = out.shape[0]
    own_start = lax.axis_index("dm") * rows

    def tile(i, carry):
        at = pl.ds(pl.multiple_of(i * 128, 128), 128)
        chosen = (srow[...] == iota((128, SLOTS), 0) + own_start + i * 128).astype(BF16)
        out[at, :] = (base[at, :] + dot(chosen, slots[...])).astype(BF16)
        return carry

    lax.fori_loop(0, rows // 128, tile, 0)


def scatter_slots(srow, slots, base):
    return pl.pallas_call(
        scatter_kernel,
        out_shape=jax.ShapeDtypeStruct(base.shape, BF16),
        in_specs=vmem(3),
        out_specs=vmem(1)[0],
        compiler_params=pltpu.CompilerParams(vmem_limit_bytes=40 << 20),
        name="scatter_slots",
    )(srow, slots, base)


def shards(
    tokens,
    clusters,
    top_keys,
    lengths,
    qkv_weight,
    out_weight,
    first_gain,
    first_bias,
    second_gain,
    second_bias,
    expand_weight,
    shrink_weight,
    cotangent,
):
    row_count = tokens.shape[0]
    width = qkv_weight.shape[2]
    inputs = tokens.astype(F32)
    expand_full, shrink_full = (
        lax.all_gather(expand_weight, ("dp", "dm"), axis=0, tiled=True),
        lax.all_gather(shrink_weight, ("dp", "dm"), axis=1, tiled=True),
    )
    topk = jnp.pad(top_keys, ((0, CLP - CL), (0, 0)), constant_values=-1)
    flat = jnp.pad(top_keys.reshape(-1), (0, SLOTS - CL * TOPK), constant_values=-1)
    scol, srow = flat.reshape(SLOTS, 1), flat.reshape(1, SLOTS)

    (
        first_normed, slot_normed, qs, k, v, ks, vs, starts, rcol, rrow, cls, centre, tm, rows_in,
        merged, counts,
    ) = front(
        lengths, tokens, clusters, qkv_weight, first_gain, first_bias, scol, topk, lax.axis_size("dm")
    )
    attended = exact_forward(starts, qs, cls, ks, vs, rows_in, rcol)

    head_part = jnp.dot(attended, out_weight, preferred_element_type=F32)
    attention_sum = lax.psum(head_part.astype(BF16), "hid").astype(F32)
    middle = inputs + attention_sum
    normed_two, spread_two = norm_parts(middle)
    second_normed = (normed_two * second_gain + second_bias).astype(BF16)
    hidden = jnp.dot(second_normed, expand_full, preferred_element_type=F32)
    activated = jax.nn.gelu(hidden).astype(BF16)
    hidden_part = jnp.dot(activated, shrink_full, preferred_element_type=F32)
    hidden_sum = lax.psum(hidden_part.astype(BF16), "hid").astype(F32)
    result = (middle + hidden_sum).astype(BF16)
    upstream = cotangent.astype(F32)
    activated_grad = jnp.dot(cotangent, shrink_full.T, preferred_element_type=F32)
    shrink_local = jnp.dot(activated.T, cotangent, preferred_element_type=F32)
    gelu_value, gelu_pull = jax.vjp(jax.nn.gelu, hidden)
    hidden_grad = gelu_pull(activated_grad)[0].astype(BF16)
    expand_local = jnp.dot(second_normed.T, hidden_grad, preferred_element_type=F32)
    second_part = jnp.dot(hidden_grad, expand_full.T, preferred_element_type=F32)
    second_grad = lax.psum(second_part.astype(BF16), "hid").astype(F32)
    expand_grad, shrink_grad = (
        lax.psum_scatter(expand_local, ("dp", "dm"), scatter_dimension=0, tiled=True),
        lax.psum_scatter(shrink_local, ("dp", "dm"), scatter_dimension=1, tiled=True),
    )
    middle_inner, second_gain_part, second_bias_part = norm_back(
        second_grad, normed_two, spread_two, second_gain
    )
    middle_grad = upstream + middle_inner
    branch_grad = middle_grad.astype(BF16)
    out_grad_part = jnp.dot(attended.T, branch_grad, preferred_element_type=F32)
    attended_grad = jnp.dot(branch_grad, out_weight.T, preferred_element_type=F32).astype(BF16)

    dq, dks, dvs, summed = exact_backward(
        starts, qs, cls, ks, vs, rows_in, rcol, rrow, attended_grad
    )
    summed = lax.psum(summed, "dm")
    dkc, dvc, centre_part = centre_backward(
        lengths, k, v, centre, topk, tm, merged, rows_in, summed
    )
    centre_grad = lax.psum(centre_part, "dm").astype(BF16)
    slot_grads = lax.psum(jnp.concatenate([dks, dvs], axis=1), "dm")
    key_value = scatter_slots(srow, slot_grads, jnp.concatenate([dkc, dvc], axis=1))
    member = clusters[:, None] == jnp.arange(CLP, dtype=jnp.int32)[None, :]
    query_centre = jnp.dot(
        member.astype(BF16), centre_grad, preferred_element_type=F32
    ) / jnp.dot(member.astype(F32), counts[:, :1], precision=HIGHEST)
    query_total = (dq + query_centre).astype(BF16)
    projected_grad = jnp.stack([query_total, key_value[:, :width], key_value[:, width:]])
    projection_part = jnp.einsum(
        "rd,kre->kde", first_normed, projected_grad, preferred_element_type=F32
    )
    first_part = jnp.einsum("kre,kde->rd", projected_grad, qkv_weight, preferred_element_type=F32)
    first_grad = lax.psum(first_part.astype(BF16), "hid").astype(F32)
    normed_one, spread_one = norm_parts(inputs)
    inputs_inner, first_gain_part, first_bias_part = norm_back(
        first_grad, normed_one, spread_one, first_gain
    )
    tokens_grad = (middle_grad + inputs_inner).astype(BF16)
    qkv_grad, out_grad, first_gain_grad, first_bias_grad, second_gain_grad, second_bias_grad = (
        lax.psum(
            (
                projection_part,
                out_grad_part,
                first_gain_part,
                first_bias_part,
                second_gain_part,
                second_bias_part,
            ),
            ("dp", "dm"),
        )
    )
    return (
        result,
        tokens_grad,
        qkv_grad,
        out_grad,
        first_gain_grad,
        first_bias_grad,
        second_gain_grad,
        second_bias_grad,
        expand_grad,
        shrink_grad,
    )


def solution(mesh):
    in_specs = (
        P(("dp", "dm"), None),
        P(("dp", "dm")),
        P("dp", None),
        P("dp"),
        P(None, None, "hid"),
        P("hid", None),
        P(),
        P(),
        P(),
        P(),
        P(("dp", "dm"), "hid"),
        P("hid", ("dp", "dm")),
        P(("dp", "dm"), None),
    )
    out_specs = (
        P(("dp", "dm"), None),
        P(("dp", "dm"), None),
        P(None, None, "hid"),
        P("hid", None),
        P(),
        P(),
        P(),
        P(),
        P(("dp", "dm"), "hid"),
        P("hid", ("dp", "dm")),
    )
    return jax.shard_map(shards, mesh=mesh, in_specs=in_specs, out_specs=out_specs, check_vma=False)
```

```python
import functools

import jax
import jax.numpy as jnp
from jax import lax
from jax.experimental import pallas as pl
from jax.experimental.pallas import tpu as pltpu
from jax.sharding import PartitionSpec as P

HEAD_DIM = 64
CL = 100
TOPK = 32
CLP = 128
SLOTS = 3328
GROUP = 8
GSLOTS = GROUP * TOPK
GROUPS = SLOTS // GSLOTS
WIN = 128
HALF = SLOTS // 2
CHUNK = 128
CHUNKS = HALF // CHUNK
LAG = 2
UNITS = 6
EPSILON = 1e-05
NEGATIVE = -1e30
HIGHEST = lax.Precision.HIGHEST
F32 = jnp.float32
BF16 = jnp.bfloat16
MESH = pl.DeviceIdType.MESH
NT = (((1,), (1,)), ((), ()))
TN = (((0,), (0,)), ((), ()))
SCALE = HEAD_DIM ** (-0.5)


def dot(a, b):
    return jnp.dot(a, b, preferred_element_type=F32)


def dot_nt(a, b):
    return lax.dot_general(a, b, NT, preferred_element_type=F32)


def dot_tn(a, b):
    return lax.dot_general(a, b, TN, preferred_element_type=F32)


def iota(shape, dim):
    return lax.broadcasted_iota(jnp.int32, shape, dim)


def norm_parts(values):
    centred = values - jnp.mean(values, -1, keepdims=True)
    spread = lax.rsqrt(jnp.mean(centred * centred, -1, keepdims=True) + EPSILON)
    return (centred * spread, spread)


def norm_back(upstream, normed, spread, norm_gain):
    through = upstream * norm_gain
    inner = (
        through
        - jnp.mean(through, -1, keepdims=True)
        - normed * jnp.mean(through * normed, -1, keepdims=True)
    )
    return (spread * inner, jnp.sum(upstream * normed, 0), jnp.sum(upstream, 0))


def head_lanes(width, head):
    lane = iota((1, width), 1)
    return lane // HEAD_DIM == head


def block_diagonal(rows, heads):
    width = rows.shape[1]
    zero = jnp.zeros_like(rows)
    return jnp.concatenate(
        [jnp.where(head_lanes(width, h), rows, zero) for h in range(heads)], axis=0
    )


def diagonal_blocks(full, heads):
    rows, width = full.shape[0] // heads, full.shape[1]
    out = full[:rows]
    for h in range(1, heads):
        out = jnp.where(head_lanes(width, h), full[h * rows : (h + 1) * rows], out)
    return out


def vmem(n):
    return [pl.BlockSpec(memory_space=pltpu.VMEM)] * n


def remote(src, dst, send, recv, device):
    return pltpu.make_async_remote_copy(
        src_ref=src, dst_ref=dst, send_sem=send, recv_sem=recv, device_id=device,
        device_id_type=MESH,
    )


def greet(devices):
    barrier = pltpu.get_barrier_semaphore()
    for device in devices:
        pl.semaphore_signal(barrier, inc=1, device_id=device, device_id_type=MESH)
    return barrier


def small_exchange(buf, sends, recvs, me, parts):
    return [
        remote(
            buf.at[me], buf.at[me], sends.at[step], recvs.at[step],
            {"dm": lax.rem(me + step, parts)},
        )
        for step in range(1, parts)
    ]


def when_in(i, count, work):
    @pl.when((i >= 0) & (i < count))
    def _():
        work(i)


def aligned(start, size):
    return pl.ds(pl.multiple_of(start, 128), size)


def sequence_masks(lengths, topk, rows):
    own_start = lax.axis_index("dm") * rows
    key_second = iota((1, rows), 1) + own_start >= lengths[0]
    centre_second = topk[:, :1] >= lengths[0]
    return key_second == centre_second


def front_kernel(
    pair, lengths, tok, ccol, weight, gain, bias, scol, topk, wexp, wshr, wout,
    fn_out, sfn_out, qs_out, k_out, v_out, ks_out, vs_out, starts_out, rcol_out, rrow_out,
    cls_out, centre_out, tm_out, rows_out, merged_out, count_out, wall_out, wfull_out,
    q_ref, member_ref, cbuf, rbuf, sbuf, own, to_right, to_left, from_left, from_right,
    csend, crecv, rsend, rrecv, ssend, srecv,
    send_right, recv_left, send_left, recv_right, send_x, recv_x, send_core, recv_core,
    send_relay, recv_relay, osend, orecv, wsend, wrecv, ysend, yrecv,
):
    rows, model = tok.shape
    width = weight.shape[2]
    heads = width // HEAD_DIM
    half_width = model // 2
    tiles = rows // 128
    parts = lax.axis_size("dm")
    me, hid, dp = lax.axis_index("dm"), lax.axis_index("hid"), lax.axis_index("dp")
    core, side = lax.rem(hid, 2), hid // 2
    core_peer = {"hid": hid + 1 - 2 * core}
    x_peer = {"hid": hid + 2 - 4 * side}
    lane = iota((128, 128), 1)
    columns = aligned(side * half_width, half_width)
    other_columns = aligned((1 - side) * half_width, half_width)
    own_start = me * rows

    greeted = [{"dm": lax.rem(me + step, parts)} for step in range(1, parts)]
    greeted += [core_peer, x_peer]
    if pair:
        greeted.append({"dp": 1 - dp})
    barrier = greet(greeted)

    out_rows = pl.ds(pl.multiple_of(hid * width, 64), width)
    wall_out[out_rows, :] = wout[...]
    out_x_rows = pl.ds(pl.multiple_of((hid + 2 - 4 * side) * width, 64), width)
    out_copies = [
        remote(wall_out.at[out_rows, :], wall_out.at[out_rows, :], osend.at[0], orecv.at[0], core_peer),
        remote(wall_out.at[out_rows, :], wall_out.at[out_rows, :], osend.at[1], orecv.at[1], x_peer),
        remote(
            wall_out.at[out_x_rows, :], wall_out.at[out_x_rows, :], osend.at[2], orecv.at[2], core_peer
        ),
    ]
    if pair:
        shard = wexp.shape[0]

        def shard_rows(d, m):
            return pl.ds(pl.multiple_of((d * parts + m) * shard, 32), shard)

        mine = shard_rows(dp, me)
        wfull_out[mine, :] = jnp.concatenate([wexp[...], wshr[...]], axis=1)
        shard_copies = [
            remote(
                wfull_out.at[mine, :], wfull_out.at[mine, :], wsend.at[step], wrecv.at[step],
                {"dm": lax.rem(me + step, parts)},
            )
            for step in range(1, parts)
        ]

        def across(step):
            block = wfull_out.at[shard_rows(dp, lax.rem(me + parts - step, parts)), :]
            return remote(block, block, ysend.at[step], yrecv.at[step], {"dp": 1 - dp})

    pl.semaphore_wait(barrier, len(greeted))
    if pair:
        across(0).start()
        for copy in shard_copies:
            copy.start()
    out_copies[0].start()
    out_copies[1].start()

    def first_norm(i, carry):
        at = aligned(i * 256, 256)
        normed, _ = norm_parts(tok[at, :].astype(F32))
        fn_out[at, :] = (normed * gain[...] + bias[...]).astype(BF16)
        return carry

    lax.fori_loop(0, rows // 256, first_norm, 0)

    @pl.when(me == 0)
    def _():
        from_left[...] = jnp.zeros_like(from_left)

    @pl.when(me == parts - 1)
    def _():
        from_right[...] = jnp.zeros_like(from_right)

    def chunk_rows(i, which):
        return aligned(which * HALF + i * CHUNK, CHUNK)

    def right_copy(i):
        return remote(
            to_right.at[i], from_left.at[i], send_right.at[i], recv_left.at[i],
            {"dm": lax.rem(me + 1, parts)},
        )

    def left_copy(i):
        return remote(
            to_left.at[i], from_right.at[i], send_left.at[i], recv_right.at[i],
            {"dm": lax.rem(me + parts - 1, parts)},
        )

    def x_copy(i):
        block = sfn_out.at[chunk_rows(i, core), columns]
        return remote(block, block, send_x.at[i], recv_x.at[i], x_peer)

    def core_copy(i):
        block = sfn_out.at[chunk_rows(i, core), columns]
        return remote(block, block, send_core.at[i], recv_core.at[i], core_peer)

    def relay_copy(i):
        block = sfn_out.at[chunk_rows(i, core), other_columns]
        return remote(block, block, send_relay.at[i], recv_relay.at[i], core_peer)

    def make_own(first, count):
        at = aligned(core * HALF + first * CHUNK, count * CHUNK)
        chosen = (scol[at, :] == iota((count * CHUNK, rows), 1) + own_start).astype(BF16)
        picked = dot(chosen, fn_out[:, columns]).astype(BF16)
        for i in range(count):
            own[first + i] = picked[i * CHUNK : (i + 1) * CHUNK]

    def go_right(i):
        @pl.when(me > 0)
        def _():
            right_copy(i).wait_recv()

        @pl.when(me < parts - 1)
        def _():
            to_right[i] = own[i] + from_left[i]
            right_copy(i).start()

    def go_left(i):
        @pl.when(me < parts - 1)
        def _():
            left_copy(i).wait_recv()

        @pl.when(me > 0)
        def _():
            to_left[i] = own[i] + from_right[i]
            left_copy(i).start()

    def finish(i):
        sfn_out[chunk_rows(i, core), columns] = own[i] + from_left[i] + from_right[i]
        x_copy(i).start()
        core_copy(i).start()

    def relay(i):
        x_copy(i).wait_recv()
        relay_copy(i).start()

    far = jnp.maximum(me, parts - 1 - me)

    def ticks(first, last):
        def tick(t, carry):
            when_in(t - LAG * me, CHUNKS, go_right)
            when_in(t - LAG * (parts - 1 - me), CHUNKS, go_left)
            when_in(t - LAG * far, CHUNKS, finish)
            when_in(t - LAG * far - LAG, CHUNKS, relay)
            return carry

        lax.fori_loop(first, last, tick, 0)

    def project(part):
        at = aligned(part * (rows // 2), rows // 2)
        first = fn_out[at, :]
        q_ref[at, :] = dot(first, weight[0]).astype(BF16)
        k_out[at, :] = dot(first, weight[1]).astype(BF16)
        v_out[at, :] = dot(first, weight[2]).astype(BF16)

    lower = (iota((128, 128), 0) > iota((128, 128), 1)).astype(BF16)

    def count_tile(i, running):
        at = aligned(i * 128, 128)
        member = (ccol[at, :] == lane).astype(F32)
        low = member.astype(BF16)
        member_ref[at, :] = low
        earlier = dot(lower, low) + running
        rcol_out[at, :] = jnp.sum(member * earlier, 1, keepdims=True)
        return running + jnp.sum(member, 0, keepdims=True)

    def place(i, carry):
        at = aligned(i * 256, 256)
        rank_row = rrow_out[:1, :].astype(jnp.int32)
        chosen = (iota((256, rows), 0) + i * 256 == rank_row).astype(BF16)
        qs_out[at, :] = dot(chosen, q_ref[...]).astype(BF16)
        sorted_member = dot(chosen, member_ref[...])
        cls_out[at, :] = jnp.sum(
            sorted_member * iota((256, 128), 1).astype(F32), 1, keepdims=True
        ).astype(jnp.int32)
        return carry

    make_own(0, 4)
    ticks(0, 1)
    project(0)
    ticks(1, 2)
    make_own(4, 4)
    ticks(2, 4)
    project(1)
    ticks(4, 5)
    counts = lax.fori_loop(0, tiles, count_tile, jnp.zeros((1, 128), F32))
    extended = jnp.concatenate([q_ref[...], jnp.ones((rows, 256 - width), BF16)], axis=1)
    sums = dot_tn(member_ref[...], extended)
    sixteens = jnp.floor(sums * 0.0625)
    wide = iota((CLP, 256), 1)
    packed = jnp.where(
        wide == width, sixteens, jnp.where(wide == width + 1, sums - 16.0 * sixteens, sums)
    )
    cbuf[me] = packed.astype(BF16)
    centre_copies = small_exchange(cbuf, csend, crecv, me, parts)
    for copy in centre_copies:
        copy.start()
    ticks(5, 6)
    make_own(8, CHUNKS - 8)
    ticks(6, 7)
    before = (iota((128, 128), 0) < iota((128, 128), 1)).astype(F32)
    starts = jnp.dot(
        jnp.broadcast_to(counts, (8, 128)), before, precision=HIGHEST, preferred_element_type=F32
    )
    starts_out[...] = starts.astype(jnp.int32)

    def ranks(i, carry):
        at = aligned(i * 128, 128)
        member = member_ref[at, :].astype(F32)
        rank = rcol_out[at, :] + jnp.sum(member * starts[:1], 1, keepdims=True)
        rcol_out[at, :] = rank
        turned = jnp.transpose(jnp.broadcast_to(rank, (128, 128)))
        rrow_out[:, at] = turned[:8]
        return carry

    lax.fori_loop(0, tiles, ranks, 0)
    ticks(7, 8)
    here = iota((CLP, rows), 1) + own_start
    hit = topk[:, :1] == here
    for t in range(1, TOPK):
        hit = hit | (topk[:, t : t + 1] == here)
    tm_out[...] = hit.astype(F32).astype(BF16)
    ticks(8, 9)

    for copy in centre_copies:
        copy.wait_recv()
    gathered = cbuf[0].astype(F32)
    for d in range(1, parts):
        gathered += cbuf[d].astype(F32)
    count = jnp.maximum(
        16.0 * gathered[:, width : width + 1] + gathered[:, width + 1 : width + 2], 1.0
    )
    count_out[...] = jnp.broadcast_to(count, (CLP, 128))
    centre = (gathered[:, :width] / count).astype(BF16)
    centre_out[...] = centre
    same = sequence_masks(lengths, topk, rows)
    stats = jnp.zeros((CLP, 128), F32)
    rest = jnp.zeros((CLP, width), F32)
    for h in range(heads):
        top = tm_out[...].astype(F32)
        mine_lanes = head_lanes(width, h)
        scores = dot_nt(jnp.where(mine_lanes, centre, jnp.zeros_like(centre)), k_out[...]) * SCALE
        scores = jnp.where(same, scores, NEGATIVE)
        largest = jnp.max(scores, 1, keepdims=True)
        raised = jnp.exp(scores - largest)
        total = jnp.sum(raised, 1, keepdims=True)
        within = raised * top
        mass = jnp.sum(within, 1, keepdims=True)
        rest = jnp.where(mine_lanes, dot((raised - within).astype(BF16), v_out[...]), rest)
        stats = jnp.where(lane == h, largest, stats)
        stats = jnp.where(lane == 8 + h, total, stats)
        stats = jnp.where(lane == 16 + h, mass, stats)
    rbuf[me] = rest.astype(BF16)
    sbuf[me] = jnp.transpose(stats)[:24]
    rest_copies = small_exchange(rbuf, rsend, rrecv, me, parts)
    stat_copies = small_exchange(sbuf, ssend, srecv, me, parts)
    for copy in rest_copies + stat_copies:
        copy.start()
    ticks(9, 11)
    lax.fori_loop(0, rows // 512, place, 0)
    ticks(11, 13)
    out_copies[1].wait_recv()
    out_copies[2].start()
    lax.fori_loop(rows // 512, rows // 256, place, 0)
    qs_out[rows:, :] = jnp.zeros((WIN, width), BF16)
    cls_out[rows:, :] = jnp.full((WIN, 1), -1, jnp.int32)
    ticks(13, 15)
    if pair:
        for step in range(1, parts):
            shard_copies[step - 1].wait_recv()
            across(step).start()
    ticks(15, 18)

    for copy in rest_copies + stat_copies:
        copy.wait_recv()
    largest = sbuf[0][:8]
    for d in range(1, parts):
        largest = jnp.maximum(largest, sbuf[d][:8])
    total = jnp.zeros((8, 128), F32)
    mass = jnp.zeros((8, 128), F32)
    factors = []
    for d in range(parts):
        factor = jnp.exp(sbuf[d][:8] - largest)
        total += factor * sbuf[d][8:16]
        mass += factor * sbuf[d][16:24]
        factors.append(factor)
    live = iota((8, 128), 0) < heads
    total = jnp.where(live, total, 1.0)
    mass = mass / total
    table = [largest, total, mass] + [factor / total for factor in factors]
    table.append(jnp.zeros((128 - 8 * len(table), 128), F32))
    columns_table = jnp.transpose(jnp.concatenate(table, axis=0))
    merged_out[...] = columns_table
    mass_rows = jnp.zeros((CLP, width), F32)
    rest_rows = jnp.zeros((CLP, width), F32)
    for h in range(heads):
        mine_lanes = head_lanes(width, h)
        mass_rows = jnp.where(mine_lanes, columns_table[:, 16 + h : 17 + h], mass_rows)
        rest = jnp.zeros((CLP, width), F32)
        for d in range(parts):
            lane_at = 24 + 8 * d + h
            rest += columns_table[:, lane_at : lane_at + 1] * rbuf[d].astype(F32)
        rest_rows = jnp.where(mine_lanes, rest, rest_rows)
    rows_out[:, :width] = mass_rows
    rows_out[:, width:] = rest_rows

    def arrive(i, carry):
        core_copy(i).wait_recv()
        relay_copy(i).wait_recv()
        return carry

    def project_slots(first, count):
        for which in range(2):
            at = pl.ds(which * HALF + first * CHUNK, count * CHUNK)
            block = sfn_out[at, :]
            ks_out[at, :] = dot(block, weight[1]).astype(BF16)
            vs_out[at, :] = dot(block, weight[2]).astype(BF16)

    early = CHUNKS // 2
    lax.fori_loop(0, early, arrive, 0)
    project_slots(0, early)
    ticks(18, CHUNKS + LAG * parts)
    lax.fori_loop(early, CHUNKS, arrive, 0)
    project_slots(early, CHUNKS - early)

    def drain(i, carry):
        @pl.when(me < parts - 1)
        def _():
            right_copy(i).wait_send()

        @pl.when(me > 0)
        def _():
            left_copy(i).wait_send()

        x_copy(i).wait_send()
        core_copy(i).wait_send()
        relay_copy(i).wait_send()
        return carry

    lax.fori_loop(0, CHUNKS, drain, 0)
    for copy in centre_copies + rest_copies + stat_copies + out_copies:
        copy.wait_send()
    out_copies[0].wait_recv()
    out_copies[2].wait_recv()
    if pair:
        for copy in shard_copies:
            copy.wait_send()
        for step in range(parts):
            across(step).wait()


def front(pair, lengths, tokens, clusters, weight, gain, bias, scol, topk, wexp, wshr, wout, parts):
    rows, model = tokens.shape
    width = weight.shape[2]
    shape = jax.ShapeDtypeStruct
    dma = pltpu.SemaphoreType.DMA
    chain = pltpu.VMEM((CHUNKS, CHUNK, model // 2), BF16)
    whole = (model, 2 * wexp.shape[1]) if pair else (16, 128)
    return pl.pallas_call(
        functools.partial(front_kernel, pair),
        out_shape=(
            shape(tokens.shape, BF16),
            shape((SLOTS, model), BF16),
            shape((rows + WIN, width), BF16),
            shape((rows, width), BF16),
            shape((rows, width), BF16),
            shape((SLOTS, width), BF16),
            shape((SLOTS, width), BF16),
            shape((8, 128), jnp.int32),
            shape((rows, 1), F32),
            shape((8, rows), F32),
            shape((rows + WIN, 1), jnp.int32),
            shape((CLP, width), BF16),
            shape((CLP, rows), BF16),
            shape((CLP, 2 * width), F32),
            shape((CLP, 128), F32),
            shape((CLP, 128), F32),
            shape((lax.axis_size("hid") * width, model), BF16),
            shape(whole, BF16),
        ),
        in_specs=[pl.BlockSpec(memory_space=pltpu.SMEM)] + vmem(10),
        out_specs=tuple(vmem(18)),
        scratch_shapes=[
            pltpu.VMEM((rows, width), BF16),
            pltpu.VMEM((rows, 128), BF16),
            pltpu.VMEM((parts, CLP, 256), BF16),
            pltpu.VMEM((parts, CLP, width), BF16),
            pltpu.VMEM((parts, 24, 128), F32),
            chain, chain, chain, chain, chain,
        ]
        + [dma((parts,))] * 6
        + [dma((CHUNKS,))] * 10
        + [dma((3,))] * 2
        + [dma((parts,))] * 4,
        compiler_params=pltpu.CompilerParams(
            vmem_limit_bytes=56 << 20, collective_id=0, has_side_effects=True
        ),
        name="front",
    )(
        lengths, tokens, clusters.reshape(rows, 1), weight, gain[None], bias[None], scol, topk,
        wexp, wshr, wout,
    )


def exact_forward_kernel(
    starts, qs, cls, ks, vs, both, rcol, att_out, att_s, mix_s
):
    rows, width = rcol.shape[0], qs.shape[1]
    heads = width // HEAD_DIM
    tiles = rows // 128
    high = both[...].astype(BF16)
    low = (both[...] - high.astype(F32)).astype(BF16)
    lane = iota((128, 128), 1)

    def spread(i, carry):
        at = pl.ds(pl.multiple_of(i * 128, 128), 128)
        member = (cls[at, :] == lane).astype(BF16)
        mix_s[at, :] = dot(member, high) + dot(member, low)
        return carry

    lax.fori_loop(0, tiles + 1, spread, 0)
    slot_cluster = iota((WIN, GSLOTS), 1) // TOPK

    def group(g, carry):
        at = pl.ds(pl.multiple_of(g * GSLOTS, GSLOTS), GSLOTS)
        keys = block_diagonal(ks[at, :], heads)
        values = block_diagonal(vs[at, :], heads)
        first, last = starts[0, g * GROUP], starts[0, g * GROUP + GROUP]
        base = first // 16 * 16
        windows = jnp.where(last > first, (last - base + WIN - 1) // WIN, 0)

        def window(w, carry):
            row = pl.multiple_of(base + w * WIN, 16)
            here = pl.ds(row, WIN)
            mine = cls[here, :] == slot_cluster + g * GROUP
            scores = dot_nt(qs[here, :], keys) * SCALE
            weights = []
            for h in range(heads):
                part = jnp.where(mine, scores[:, h * GSLOTS : (h + 1) * GSLOTS], NEGATIVE)
                raised = jnp.where(mine, jnp.exp(part - jnp.max(part, 1, keepdims=True)), 0.0)
                total = jnp.maximum(jnp.sum(raised, 1, keepdims=True), 0.5)
                weights.append((raised / total).astype(BF16))
            out = dot(jnp.concatenate(weights, axis=1), values)
            mix = mix_s[here, :]
            place = iota((WIN, 1), 0) + row
            inside = (place >= first) & (place < last)
            att_s[here, :] = jnp.where(inside, mix[:, :width] * out + mix[:, width:], att_s[here, :])
            return carry

        return lax.fori_loop(0, windows, window, carry)

    lax.fori_loop(0, GROUPS, group, 0)

    def unplace(i, carry):
        at = pl.ds(pl.multiple_of(i * 256, 256), 256)
        chosen = (iota((256, rows), 1) == rcol[at, :].astype(jnp.int32)).astype(BF16)
        att_out[at, :] = dot(chosen, att_s[:rows, :].astype(BF16)).astype(BF16)
        return carry

    lax.fori_loop(0, tiles // 2, unplace, 0)


def exact_forward(starts, qs, cls, ks, vs, both, rcol):
    rows, width = rcol.shape[0], qs.shape[1]
    shape = jax.ShapeDtypeStruct
    return pl.pallas_call(
        exact_forward_kernel,
        out_shape=shape((rows, width), BF16),
        in_specs=[pl.BlockSpec(memory_space=pltpu.SMEM)] + vmem(6),
        out_specs=vmem(1)[0],
        scratch_shapes=[
            pltpu.VMEM((rows + WIN, width), F32),
            pltpu.VMEM((rows + WIN, 2 * width), F32),
        ],
        compiler_params=pltpu.CompilerParams(vmem_limit_bytes=40 << 20),
        name="exact_forward",
    )(starts, qs, cls, ks, vs, both, rcol)


def exact_backward_kernel(
    starts, qs, cls, ks, vs, rows_in, rcol, rrow, grad,
    dq_out, dkv_out, centre_out,
    grad_s, mass_s, dq_s, part_s, dk_s, dv_s,
):
    rows, width = rcol.shape[0], qs.shape[1]
    heads = width // HEAD_DIM
    tiles = rows // 128
    mass_rows = rows_in[:, :width]
    high = mass_rows.astype(BF16)
    low = (mass_rows - high.astype(F32)).astype(BF16)
    lane = iota((128, 128), 1)
    rank_row = rrow[:1, :].astype(jnp.int32)

    def place(i, carry):
        at = pl.ds(pl.multiple_of(i * 256, 256), 256)
        chosen = (iota((256, rows), 0) + i * 256 == rank_row).astype(BF16)
        grad_s[at, :] = dot(chosen, grad[...]).astype(BF16)
        member = (cls[at, :] == iota((256, 128), 1)).astype(BF16)
        mass_s[at, :] = dot(member, high) + dot(member, low)
        return carry

    lax.fori_loop(0, tiles // 2, place, 0)
    grad_s[rows:, :] = jnp.zeros((WIN, width), BF16)
    mass_s[rows:, :] = jnp.zeros((WIN, width), F32)
    slot_cluster = iota((WIN, GSLOTS), 1) // TOPK

    def group(g, carry):
        at = pl.ds(pl.multiple_of(g * GSLOTS, GSLOTS), GSLOTS)
        keys = block_diagonal(ks[at, :], heads)
        values = block_diagonal(vs[at, :], heads)
        first, last = starts[0, g * GROUP], starts[0, g * GROUP + GROUP]
        base = first // 16 * 16
        windows = jnp.where(last > first, (last - base + WIN - 1) // WIN, 0)
        dk_s[...] = jnp.zeros_like(dk_s)
        dv_s[...] = jnp.zeros_like(dv_s)

        def window(w, carry):
            row = pl.multiple_of(base + w * WIN, 16)
            here = pl.ds(row, WIN)
            mine = cls[here, :] == slot_cluster + g * GROUP
            query, upstream = qs[here, :], grad_s[here, :]
            scores = dot_nt(query, keys) * SCALE
            against = dot_nt(upstream, values)
            mass = mass_s[here, :]
            weights, score_grads = [], []
            mass_part = jnp.zeros((WIN, width), F32)
            for h in range(heads):
                cut = slice(h * GSLOTS, (h + 1) * GSLOTS)
                part = jnp.where(mine, scores[:, cut], NEGATIVE)
                raised = jnp.where(mine, jnp.exp(part - jnp.max(part, 1, keepdims=True)), 0.0)
                total = jnp.maximum(jnp.sum(raised, 1, keepdims=True), 0.5)
                probs = raised / total
                meeting = jnp.sum(probs * against[:, cut], 1, keepdims=True)
                weighted = probs * mass[:, h * HEAD_DIM : h * HEAD_DIM + 1]
                weights.append(weighted.astype(BF16))
                score_grads.append((weighted * (against[:, cut] - meeting)).astype(BF16))
                mass_part = jnp.where(head_lanes(width, h), meeting, mass_part)
            score_grad = jnp.concatenate(score_grads, axis=1)
            weight = jnp.concatenate(weights, axis=1)
            place = iota((WIN, 1), 0) + row
            inside = (place >= first) & (place < last)
            dq = dot(score_grad, keys) * SCALE
            dq_s[here, :] = jnp.where(inside, dq, dq_s[here, :])
            part_s[here, :] = jnp.where(inside, mass_part, part_s[here, :])
            dk_s[...] += diagonal_blocks(dot_tn(score_grad, query), heads) * SCALE
            dv_s[...] += diagonal_blocks(dot_tn(weight, upstream), heads)
            return carry

        lax.fori_loop(0, windows, window, 0)
        dkv_out[at, :] = jnp.concatenate([dk_s[...], dv_s[...]], axis=1).astype(BF16)
        return carry

    lax.fori_loop(0, GROUPS, group, 0)
    centre_out[...] = jnp.zeros_like(centre_out)

    def unplace(i, carry):
        at = pl.ds(pl.multiple_of(i * 256, 256), 256)
        chosen = (iota((256, rows), 1) == rcol[at, :].astype(jnp.int32)).astype(BF16)
        dq_out[at, :] = dot(chosen, dq_s[:rows, :].astype(BF16)).astype(BF16)
        member = (cls[at, :] == iota((256, 128), 1)).astype(BF16)
        pair = jnp.concatenate([part_s[at, :].astype(BF16), grad_s[at, :]], axis=1)
        centre_out[...] += dot_tn(member, pair)
        return carry

    lax.fori_loop(0, tiles // 2, unplace, 0)


def exact_backward(starts, qs, cls, ks, vs, rows_in, rcol, rrow, grad):
    rows, width = rcol.shape[0], qs.shape[1]
    shape = jax.ShapeDtypeStruct
    return pl.pallas_call(
        exact_backward_kernel,
        out_shape=(
            shape((rows, width), BF16),
            shape((SLOTS, 2 * width), BF16),
            shape((CLP, 2 * width), F32),
        ),
        in_specs=[pl.BlockSpec(memory_space=pltpu.SMEM)] + vmem(8),
        out_specs=tuple(vmem(3)),
        scratch_shapes=[
            pltpu.VMEM((rows + WIN, width), BF16),
            pltpu.VMEM((rows + WIN, width), F32),
            pltpu.VMEM((rows + WIN, width), F32),
            pltpu.VMEM((rows + WIN, width), F32),
            pltpu.VMEM((GSLOTS, width), F32),
            pltpu.VMEM((GSLOTS, width), F32),
        ],
        compiler_params=pltpu.CompilerParams(vmem_limit_bytes=40 << 20),
        name="exact_backward",
    )(starts, qs, cls, ks, vs, rows_in, rcol, rrow, grad)


def gelu_parts(values):
    slope = 0.7978845608028654
    squared = values * values
    turned = jnp.tanh(slope * values * (1.0 + 0.044715 * squared))
    half = 0.5 * (1.0 + turned)
    rise = half + 0.5 * slope * values * (1.0 - turned * turned) * (1.0 + 0.134145 * squared)
    return (values * half, rise)


def middle_kernel(
    pair, tok, cot, att, wout_own, wout, wboth, gain, bias,
    mid_out, mgrad_out, agrad_out, hsum_out, grads_out, wo_out, gains_out,
    att_peer, cat, xcat, sn, act, hg, sp_own, sp_send, sp_recv, hp_own, hp_send, hp_recv,
    sx_send, sx_recv, branch, give, given,
    asend, arecv, xsend, xrecv, rsend, rrecv, ssend, srecv, hsend, hrecv, sxs, sxr, bsend, brecv,
    gsend, grecv,
):
    rows, width = att.shape
    model = tok.shape[1]
    half_width = 2 * width
    half_rows = rows // 2
    blocks = half_rows // 128
    hid = lax.axis_index("hid")
    core, side = lax.rem(hid, 2), hid // 2
    core_peer = {"hid": hid + 1 - 2 * core}
    x_peer = {"hid": hid + 2 - 4 * side}

    dp = lax.axis_index("dp")
    greeted = [core_peer, x_peer] + ([{"dp": 1 - dp}] if pair else [])
    barrier = greet(greeted)
    gains_out[...] = jnp.zeros_like(gains_out)
    pl.semaphore_wait(barrier, len(greeted))

    units = wboth.shape[1] // 2
    wexp, wshr = wboth.at[:, :units], wboth.at[:, units:]

    def block_rows(j, which):
        return pl.ds(pl.multiple_of(which * half_rows + j * 128, 128), 128)

    def own_rows(j):
        return pl.ds(pl.multiple_of(j * 128, 128), 128)

    att_copy = remote(att, att_peer, asend, arecv, core_peer)
    att_copy.start()

    def x_copy(j):
        block = block_rows(j, core)
        return remote(cat.at[block, :], xcat.at[block, :], xsend.at[j], xrecv.at[j], x_peer)

    def relay_copy(j):
        block = xcat.at[block_rows(j, core), :]
        return remote(block, block, rsend.at[j], rrecv.at[j], core_peer)

    def sp_copy(j):
        return remote(sp_send.at[j], sp_recv.at[j], ssend.at[j], srecv.at[j], core_peer)

    def hp_copy(j):
        return remote(hp_send.at[j], hp_recv.at[j], hsend.at[j], hrecv.at[j], core_peer)

    def sx_copy(j):
        return remote(sx_send.at[j], sx_recv.at[j], sxs.at[j], sxr.at[j], x_peer)

    def branch_copy(j):
        block = branch.at[block_rows(j, core), :]
        return remote(block, block, bsend.at[j], brecv.at[j], core_peer)

    def join(at):
        mine, other = att[at, :], att_peer[at, :]
        cat[at, :] = jnp.where(
            core == 0,
            jnp.concatenate([mine, other], axis=1),
            jnp.concatenate([other, mine], axis=1),
        )

    att_copy.wait_recv()

    def spread(j, carry):
        join(block_rows(j, core))
        x_copy(j).start()
        return carry

    lax.fori_loop(0, blocks, spread, 0)

    def join_other(j, carry):
        join(block_rows(j, 1 - core))
        return carry

    lax.fori_loop(0, blocks, join_other, 0)

    def both(ref, j):
        return jnp.concatenate([ref[block_rows(j, core), :], ref[block_rows(j, 1 - core), :]], axis=0)

    def store_both(ref, j, values):
        ref[block_rows(j, core), :] = values[:128]
        ref[block_rows(j, 1 - core), :] = values[128:]

    own_half = pl.ds(pl.multiple_of(side * half_width, 128), half_width)
    other_half = pl.ds(pl.multiple_of((1 - side) * half_width, 128), half_width)

    def forward(j):
        x_copy(j).wait_recv()
        relay_copy(j).start()
        relay_copy(j).wait_recv()
        attention = dot(both(cat, j), wout[own_half, :]) + dot(both(xcat, j), wout[other_half, :])
        middle = both(tok, j).astype(F32) + attention
        mid_out[own_rows(j), :] = middle[:128]
        normed, _ = norm_parts(middle)
        second = (normed * gain[...] + bias[...]).astype(BF16)
        store_both(sn, j, second)
        hidden = dot(second, wexp[...])
        value, rise = gelu_parts(hidden)
        value = value.astype(BF16)
        store_both(act, j, value)
        grad = (dot(both(cot, j), wshr[...]) * rise).astype(BF16)
        store_both(hg, j, grad)
        part = dot_nt(grad, wexp[...])
        sp_own[j] = part[:128]
        sp_send[j] = part[128:].astype(BF16)
        sp_copy(j).start()
        part = dot_nt(value, wshr[...])
        hp_own[j] = part[:128]
        hp_send[j] = part[128:].astype(BF16)
        hp_copy(j).start()

    def chip_sum(j):
        sp_copy(j).wait_recv()
        total = sp_own[j] + sp_recv[j].astype(F32)
        sx_send[j] = total.astype(BF16)
        sx_copy(j).start()
        hp_copy(j).wait_recv()
        hsum_out[own_rows(j), :] = (hp_own[j] + hp_recv[j].astype(F32)).astype(BF16)

    def norm_grad(j):
        sx_copy(j).wait_recv()
        second_grad = sx_send[j].astype(F32) + sx_recv[j].astype(F32)
        normed, spread_two = norm_parts(mid_out[own_rows(j), :])
        inner, gain_part, bias_part = norm_back(second_grad, normed, spread_two, gain[...])
        gains_out[0:1, :] += gain_part[None]
        gains_out[1:2, :] += bias_part[None]
        middle_grad = cot[block_rows(j, core), :].astype(F32) + inner
        mgrad_out[own_rows(j), :] = middle_grad
        branch[block_rows(j, core), :] = middle_grad.astype(BF16)
        branch_copy(j).start()

    def attended_grad(j):
        branch_copy(j).wait_recv()
        for which in range(2):
            at = block_rows(j, which)
            agrad_out[at, :] = dot_nt(branch[at, :], wout_own[...]).astype(BF16)

    def when_block(j, work):
        @pl.when((j >= 0) & (j < blocks))
        def _():
            work(j)

    def ticks(first, last):
        def tick(t, carry):
            when_block(t, forward)
            when_block(t - 1, chip_sum)
            when_block(t - 3, norm_grad)
            when_block(t - 4, attended_grad)
            return carry

        lax.fori_loop(first, last, tick, 0)

    half = model // 2
    part_rows = half if pair else model

    def weight_grad(left, right, which):
        return dot_tn(left[:, aligned(which * half, part_rows)], right[...]).astype(BF16)

    if pair:
        give_copies = [
            remote(give.at[i], given.at[i], gsend.at[i], grecv.at[i], {"dp": 1 - dp})
            for i in range(2)
        ]
        keep = dp
    else:
        keep = 0
    ticks(0, blocks)
    if pair:
        give[0] = weight_grad(cot, act, 1 - dp)
        give_copies[0].start()
    ticks(blocks, blocks + 1)
    if pair:
        give[1] = weight_grad(sn, hg, 1 - dp)
        give_copies[1].start()
    ticks(blocks + 1, blocks + 2)
    shrink_keep = weight_grad(cot, act, keep)
    grads_out[:, units:] = shrink_keep
    ticks(blocks + 2, blocks + 3)
    expand_keep = weight_grad(sn, hg, keep)
    grads_out[:, :units] = expand_keep
    ticks(blocks + 3, blocks + 4)
    wo_out[...] = dot_tn(att[...], branch[...]).astype(BF16)

    def drain(j, carry):
        x_copy(j).wait_send()
        relay_copy(j).wait_send()
        sp_copy(j).wait_send()
        hp_copy(j).wait_send()
        sx_copy(j).wait_send()
        branch_copy(j).wait_send()
        return carry

    lax.fori_loop(0, blocks, drain, 0)
    att_copy.wait_send()
    if pair:
        for i, cut in ((0, slice(units, 2 * units)), (1, slice(0, units))):
            give_copies[i].wait()
            grads_out[:, cut] = grads_out[:, cut] + given[i]


def middle(pair, tokens, cotangent, attended, wout_own, wout, wboth, gain, bias):
    rows, model = tokens.shape
    width = attended.shape[1]
    units = wboth.shape[1] // 2
    part_rows = model // 2 if pair else model
    spare = (2, part_rows, units) if pair else (2, 16, 128)
    blocks = rows // 256
    shape = jax.ShapeDtypeStruct
    dma = pltpu.SemaphoreType.DMA
    low = pltpu.VMEM((blocks, 128, model), BF16)
    full = pltpu.VMEM((blocks, 128, model), F32)
    return pl.pallas_call(
        functools.partial(middle_kernel, pair),
        out_shape=(
            shape((rows // 2, model), F32),
            shape((rows // 2, model), F32),
            shape((rows, width), BF16),
            shape((rows // 2, model), BF16),
            shape((part_rows, 2 * units), BF16),
            shape((width, model), BF16),
            shape((8, model), F32),
        ),
        in_specs=vmem(8),
        out_specs=tuple(vmem(7)),
        scratch_shapes=[
            pltpu.VMEM((rows, width), BF16),
            pltpu.VMEM((rows, 2 * width), BF16),
            pltpu.VMEM((rows, 2 * width), BF16),
            pltpu.VMEM((rows, model), BF16),
            pltpu.VMEM((rows, units), BF16),
            pltpu.VMEM((rows, units), BF16),
            full, low, low, full, low, low, low, low,
            pltpu.VMEM((rows, model), BF16),
            pltpu.VMEM(spare, BF16),
            pltpu.VMEM(spare, BF16),
            dma, dma,
        ]
        + [dma((blocks,))] * 12
        + [dma((2,))] * 2,
        compiler_params=pltpu.CompilerParams(
            vmem_limit_bytes=60 << 20, collective_id=2, has_side_effects=True
        ),
        name="middle",
    )(tokens, cotangent, attended, wout_own, wout, wboth, gain[None], bias[None])


def tail_kernel(
    pair, lengths, dkv, dq, summed, k, v, centre, topk, tm, merged, rows_in, counts, ccol, weight,
    fn, sfn, tok, gain, mgrad, srow, mid, hsum, hsum_x, wo_part, second_gains,
    result_out, tokens_out, qkv_out, out_out, gains_out,
    sbuf, cbuf, wkv, fgm, to_core, from_core, to_x, from_x, to_right, to_left, from_left,
    from_right, from_fin, pq, pkv, dense, dense_to_core, dense_from_core, dense_to_x, dense_from_x,
    dense_own, first, sfn_tile, grad_all, grad_from_y, grad_back, g_own, g_right, g_left, g_from_left,
    g_from_right, gain_core, gain_dm, gain_dp, tile_sem, mid_sem, hsum_sem,
    ssend, srecv, csend, crecv,
    send_core, recv_core, send_x, recv_x, send_right, recv_left, send_left, recv_right, send_fin,
    recv_fin,
    dsend_core, drecv_core, dsend_x, drecv_x, fsend, frecv, tsend, trecv, osend, orecv,
    ysend, yrecv, gsend_right, grecv_left, gsend_left, grecv_right, asend, arecv,
    gcsend, gcrecv, gmsend, gmrecv, gpsend, gprecv,
):
    rows, width = k.shape
    model = tok.shape[1]
    heads = width // HEAD_DIM
    half_width = model // 2
    half_rows = rows // 2
    blocks = half_rows // 128
    parts = lax.axis_size("dm")
    me, hid, dp = lax.axis_index("dm"), lax.axis_index("hid"), lax.axis_index("dp")
    core, side = lax.rem(hid, 2), hid // 2
    core_peer = {"hid": hid + 1 - 2 * core}
    x_peer = {"hid": hid + 2 - 4 * side}
    y_peer = {"dp": 1 - dp}
    own_start = me * rows
    columns = aligned(side * half_width, half_width)
    other_columns = aligned((1 - side) * half_width, half_width)

    greeted = [{"dm": lax.rem(me + step, parts)} for step in range(1, parts)]
    greeted += [core_peer, x_peer] + ([y_peer] if pair else [])
    barrier = greet(greeted)

    wide = iota((CLP, 256), 1)
    packed = jnp.concatenate([summed[:, width:], jnp.zeros((CLP, 256 - width), F32)], axis=1)
    for h in range(heads):
        packed = jnp.where(wide == width + h, summed[:, h * HEAD_DIM : h * HEAD_DIM + 1], packed)
    sbuf[me] = packed.astype(BF16)
    wkv[...] = jnp.concatenate([weight[1], weight[2]], axis=1)
    dense_own[...] = jnp.zeros_like(dense_own)
    mid_copy = pltpu.make_async_copy(mid, dense, mid_sem)
    mid_copy.start()
    hsum_copy = pltpu.make_async_copy(hsum, dense_to_core, hsum_sem)
    hsum_copy.start()

    @pl.when(me == 0)
    def _():
        from_left[...] = jnp.zeros_like(from_left)
        g_from_left[...] = jnp.zeros_like(g_from_left)

    @pl.when(me == parts - 1)
    def _():
        from_right[...] = jnp.zeros_like(from_right)

    pl.semaphore_wait(barrier, len(greeted))
    sum_copies = small_exchange(sbuf, ssend, srecv, me, parts)
    for copy in sum_copies:
        copy.start()

    def chunk_rows(i, which):
        return aligned(which * HALF + i * CHUNK, CHUNK)

    def block_rows(j, which):
        return aligned(which * half_rows + j * 128, 128)

    def own_rows(j):
        return aligned(j * 128, 128)

    def core_copy(i):
        return remote(to_core.at[i], from_core.at[i], send_core.at[i], recv_core.at[i], core_peer)

    def x_copy(i):
        return remote(to_x.at[i], from_x.at[i], send_x.at[i], recv_x.at[i], x_peer)

    right = {"dm": lax.rem(me + 1, parts)}
    left = {"dm": lax.rem(me + parts - 1, parts)}

    def right_copy(i):
        return remote(to_right.at[i], from_left.at[i], send_right.at[i], recv_left.at[i], right)

    def left_copy(i):
        return remote(to_left.at[i], from_right.at[i], send_left.at[i], recv_right.at[i], left)

    def fin_copy(i):
        return remote(from_x.at[i], from_fin.at[i], send_fin.at[i], recv_fin.at[i], core_peer)

    def dense_core_copy(j):
        return remote(
            dense_to_core.at[j], dense_from_core.at[j], dsend_core.at[j], drecv_core.at[j], core_peer
        )

    def dense_x_copy(j):
        return remote(dense_to_x.at[j], dense_from_x.at[j], dsend_x.at[j], drecv_x.at[j], x_peer)

    def first_copy(j):
        block = first.at[j, :, columns]
        return remote(block, block, fsend.at[j], frecv.at[j], x_peer)

    def tokens_copy(j):
        block = tokens_out.at[block_rows(j, core), :]
        return remote(block, block, tsend.at[j], trecv.at[j], core_peer)

    def result_copy(j):
        block = result_out.at[block_rows(j, core), :]
        return remote(block, block, osend.at[j], orecv.at[j], core_peer)

    def spread_back(start, count):
        other = dot_nt(dkv[aligned((1 - core) * HALF + start * CHUNK, count * CHUNK), :], wkv[...])
        other = other.astype(BF16)
        for i in range(count):
            to_core[start + i] = other[i * CHUNK : (i + 1) * CHUNK]
            core_copy(start + i).start()
        mine = dot_nt(dkv[aligned(core * HALF + start * CHUNK, count * CHUNK), :], wkv[...])
        mine = mine.astype(BF16)
        for i in range(count):
            fgm[start + i] = mine[i * CHUNK : (i + 1) * CHUNK]

    def chip_sum(i):
        core_copy(i).wait_recv()
        to_x[i] = fgm[i, :, other_columns] + from_core[i, :, other_columns]
        x_copy(i).start()

    def hid_sum(i):
        x_copy(i).wait_recv()
        fgm[i, :, columns] = (
            fgm[i, :, columns].astype(F32)
            + from_core[i, :, columns].astype(F32)
            + from_x[i].astype(F32)
        ).astype(BF16)

    def go_right(i):
        @pl.when(me > 0)
        def _():
            right_copy(i).wait_recv()

        @pl.when(me < parts - 1)
        def _():
            to_right[i] = fgm[i, :, columns] + from_left[i]
            right_copy(i).start()

    def go_left(i):
        @pl.when(me < parts - 1)
        def _():
            left_copy(i).wait_recv()

        @pl.when(me > 0)
        def _():
            to_left[i] = fgm[i, :, columns] + from_right[i]
            left_copy(i).start()

    def finish(i):
        from_x[i] = (
            fgm[i, :, columns].astype(F32) + from_left[i].astype(F32) + from_right[i].astype(F32)
        ).astype(BF16)
        fin_copy(i).start()

    def scatter(i):
        fin_copy(i).wait_recv()
        here = iota((half_rows, CHUNK), 0) + own_start + core * half_rows
        chosen = [
            (srow[:, chunk_rows(i, which)] == here).astype(BF16) for which in (core, 1 - core)
        ]
        picked = jnp.concatenate([from_x[i], from_fin[i]], axis=0)
        dense_own[...] += dot(jnp.concatenate(chosen, axis=1), picked)

    far = jnp.maximum(me, parts - 1 - me)

    def ticks(start, last):
        def tick(t, carry):
            when_in(t, CHUNKS, chip_sum)
            ready = t - LAG
            when_in(ready, CHUNKS, hid_sum)
            when_in(ready - LAG * me, CHUNKS, go_right)
            when_in(ready - LAG * (parts - 1 - me), CHUNKS, go_left)
            when_in(ready - LAG * far, CHUNKS, finish)
            when_in(ready - LAG * far - 1, CHUNKS, scatter)
            return carry

        lax.fori_loop(start, last, tick, 0)

    spread_back(0, 4)
    ticks(0, 3)
    spread_back(4, 4)
    ticks(3, 5)
    spread_back(8, CHUNKS - 8)

    def result_rows(j, carry):
        total = dense_to_core[j].astype(F32) + hsum_x[j].astype(F32)
        result_out[block_rows(j, core), :] = (dense[j] + total).astype(BF16)
        result_copy(j).start()
        return carry

    for copy in sum_copies:
        copy.wait_recv()
    total = sbuf[0].astype(F32)
    for d in range(1, parts):
        total += sbuf[d].astype(F32)
    same = sequence_masks(lengths, topk, rows)
    rest_grad = total[:, :width].astype(BF16)
    product = rest_grad.astype(F32) * rows_in[:, width:]
    score_grads, weights = [], []
    centre_part = jnp.zeros((CLP, width), F32)
    for h in range(heads):
        lanes = head_lanes(width, h)
        top = tm[...].astype(F32)
        zero = jnp.zeros((CLP, width), BF16)
        full = dot_nt(jnp.where(lanes, centre[...], zero), k[...]) * SCALE
        against = dot_nt(jnp.where(lanes, rest_grad, zero), v[...])
        largest, denominator = merged[:, h : h + 1], merged[:, 8 + h : 9 + h]
        mass = merged[:, 16 + h : 17 + h]
        mass_grad = total[:, width + h : width + h + 1]
        probs = jnp.where(same, jnp.exp(full - largest) / denominator, 0.0)
        mean = mass * mass_grad + jnp.sum(jnp.where(lanes, product, 0.0), 1, keepdims=True)
        grad = jnp.where(top > 0.5, mass_grad, against)
        score_grad = (probs * (grad - mean)).astype(BF16)
        centre_part = jnp.where(lanes, dot(score_grad, k[...]), centre_part)
        score_grads.append(score_grad)
        weights.append(jnp.where(top > 0.5, 0.0, probs).astype(BF16))
    cbuf[me] = (centre_part * SCALE).astype(BF16)
    centre_copies = small_exchange(cbuf, csend, crecv, me, parts)
    for copy in centre_copies:
        copy.start()
    ticks(5, 6)
    score_grad = jnp.concatenate(score_grads, axis=0)
    rest_weight = jnp.concatenate(weights, axis=0)
    pkv[...] = jnp.concatenate(
        [
            (dot_tn(score_grad, block_diagonal(centre[...], heads)) * SCALE).astype(BF16),
            dot_tn(rest_weight, block_diagonal(rest_grad, heads)).astype(BF16),
        ],
        axis=1,
    )
    ticks(6, 7)
    mid_copy.wait()
    hsum_copy.wait()
    lax.fori_loop(0, blocks, result_rows, 0)
    ticks(7, 8)
    for copy in centre_copies:
        copy.wait_recv()
    centre_grad = cbuf[0].astype(F32)
    for d in range(1, parts):
        centre_grad += cbuf[d].astype(F32)
    centre_grad = centre_grad / counts[:, :1]
    high = centre_grad.astype(BF16)
    low = (centre_grad - high.astype(F32)).astype(BF16)

    def queries(i, carry):
        at = aligned(i * 256, 256)
        member = (ccol[at, :] == iota((256, 128), 1)).astype(BF16)
        pq[at, :] = (dq[at, :].astype(F32) + dot(member, high) + dot(member, low)).astype(BF16)
        return carry

    lax.fori_loop(0, rows // 256, queries, 0)
    ticks(8, 9)

    def dense_rows(which):
        at = aligned(which * half_rows, half_rows)
        return dot_nt(pq[at, :], weight[0]) + dot_nt(pkv[at, :], wkv[...])

    other_dense = dense_rows(1 - core).astype(BF16)
    for j in range(blocks):
        dense_to_core[j] = other_dense[j * 128 : (j + 1) * 128]
        dense_core_copy(j).start()
    own_dense = dense_rows(core)
    for j in range(blocks):
        dense[j] = own_dense[j * 128 : (j + 1) * 128]
    ticks(9, 10)

    grad_all[: width, :] = dot_tn(pq[...], fn[...]).astype(BF16)
    ticks(10, 11)

    def slot_tile(c, carry):
        cut = aligned(c * 256, 256)
        fetch = pltpu.make_async_copy(sfn.at[:, cut], sfn_tile, tile_sem)
        fetch.start()
        dense_part = dot_tn(pkv[...], fn[:, cut])
        fetch.wait()
        grad_all[width : 3 * width, cut] = (dense_part + dot_tn(dkv[...], sfn_tile[...])).astype(BF16)
        return carry

    lax.fori_loop(0, 1, slot_tile, 0)
    ticks(11, 12)
    lax.fori_loop(1, 2, slot_tile, 0)
    ticks(12, 13)
    lax.fori_loop(2, model // 256, slot_tile, 0)
    grad_all[3 * width :, :] = wo_part[...]

    if pair:
        y_half = model // 2

        def y_rows(b, d):
            return aligned(d * y_half + b * 128, 128)

        def y_copy(b):
            return remote(
                grad_all.at[y_rows(b, 1 - dp), :], grad_from_y.at[b], ysend.at[b], yrecv.at[b], y_peer
            )

        def y_back(b):
            return remote(
                grad_all.at[y_rows(b, dp), :], grad_back.at[b], asend.at[b], arecv.at[b], y_peer
            )

        def unit_right(u):
            return remote(g_right.at[u], g_from_left.at[u], gsend_right.at[u], grecv_left.at[u], right)

        def unit_left(u):
            return remote(g_left.at[u], g_from_right.at[u], gsend_left.at[u], grecv_right.at[u], left)

        for b in range(3):
            y_copy(b).start()

        def y_sum(b):
            y_copy(b).wait_recv()
            both = grad_all[y_rows(b, dp), :] + grad_from_y[b]
            g_own[2 * b] = both[:, :half_width]
            g_own[2 * b + 1] = both[:, half_width:]

        def unit_go_right(u):
            @pl.when(me > 0)
            def _():
                unit_right(u).wait_recv()

            @pl.when(me < parts - 1)
            def _():
                g_right[u] = g_own[u] + g_from_left[u]
                unit_right(u).start()

            @pl.when(me == parts - 1)
            def _():
                g_from_right[u] = g_own[u] + g_from_left[u]

        def unit_go_left(u):
            @pl.when(me < parts - 1)
            def _():
                unit_left(u).wait_recv()

            @pl.when(me > 0)
            def _():
                g_left[u] = g_from_right[u]
                unit_left(u).start()

        def y_return(b):
            grad_all[y_rows(b, dp), :half_width] = g_from_right[2 * b]
            grad_all[y_rows(b, dp), half_width:] = g_from_right[2 * b + 1]
            y_back(b).start()

        def gticks(start, last):
            def tick(t, carry):
                @pl.when(lax.rem(t, 2) == 0)
                def _():
                    when_in(t // 2, 3, y_sum)

                when_in(t - 1 - LAG * me, UNITS, unit_go_right)
                back = t - 1 - LAG * (parts - 1) - LAG * (parts - 1 - me)
                when_in(back, UNITS, unit_go_left)

                @pl.when((back >= 0) & (lax.rem(back + 1, 2) == 0))
                def _():
                    when_in((back - 1) // 2, 3, y_return)

                return carry

            lax.fori_loop(start, last, tick, 0)
    else:

        def gticks(start, last):
            pass

    ticks(13, 15)
    gticks(0, 1)

    def dense_chip(j, carry):
        dense_core_copy(j).wait_recv()
        dense_to_x[j] = (
            dense[j, :, other_columns] + dense_from_core[j, :, other_columns].astype(F32)
        ).astype(BF16)
        dense_x_copy(j).start()
        return carry

    def dense_hid(j, carry):
        dense_x_copy(j).wait_recv()
        dense_own[own_rows(j), :] += (
            dense[j, :, columns]
            + dense_from_core[j, :, columns].astype(F32)
            + dense_from_x[j].astype(F32)
        )
        return carry

    lax.fori_loop(0, blocks, dense_chip, 0)
    for t in range(15, CHUNKS + LAG * parts + 1):
        ticks(t, t + 1)
        gticks(t - 14, t - 13)
    done = CHUNKS + LAG * parts + 1 - 14
    lax.fori_loop(0, blocks, dense_hid, 0)
    mgrad_copy = pltpu.make_async_copy(mgrad, dense, mid_sem)
    mgrad_copy.start()

    def first_send(j, carry):
        first[j, :, columns] = dense_own[own_rows(j), :].astype(BF16)
        first_copy(j).start()
        return carry

    lax.fori_loop(0, blocks, first_send, 0)
    gticks(done, done + 2)
    gains_out[...] = jnp.zeros_like(gains_out)
    gains_out[2:4, :] = second_gains[0:2, :]

    def first_back(j, carry):
        first_copy(j).wait_recv()
        at = block_rows(j, core)
        normed, spread = norm_parts(tok[at, :].astype(F32))
        inner, gain_part, bias_part = norm_back(first[j].astype(F32), normed, spread, gain[...])
        tokens_out[at, :] = (dense[j] + inner).astype(BF16)
        tokens_copy(j).start()
        gains_out[0:1, :] += gain_part[None]
        gains_out[1:2, :] += bias_part[None]
        return carry

    mgrad_copy.wait()
    lax.fori_loop(0, blocks, first_back, 0)
    if pair:
        last_tick = 1 + LAG * 2 * (parts - 1) + UNITS
        core_gain = remote(gains_out, gain_core, gcsend, gcrecv, core_peer)
        core_gain.start()
        gticks(done + 2, last_tick)
        core_gain.wait_recv()
        gain_dm[me] = gains_out[...] + gain_core[...]
        dm_gains = small_exchange(gain_dm, gmsend, gmrecv, me, parts)
        for copy in dm_gains:
            copy.start()
        for copy in dm_gains:
            copy.wait_recv()
        line = gain_dm[0]
        for d in range(1, parts):
            line = line + gain_dm[d]
        gain_dp[0] = line
        dp_gain = remote(gain_dp.at[0], gain_dp.at[1], gpsend, gprecv, y_peer)
        dp_gain.start()
        for b in range(3):
            y_copy(b).wait_send()
            y_back(b).wait_recv()
            grad_all[y_rows(b, 1 - dp), :] = grad_back[b]
    for part in range(3):
        block = grad_all[part * width : (part + 1) * width, :].astype(F32)
        qkv_out[part] = jnp.transpose(block)
    out_out[...] = grad_all[3 * width :, :].astype(F32)
    if pair:
        dp_gain.wait()
        core_gain.wait_send()
        gains_out[...] = gain_dp[0] + gain_dp[1]
        for copy in dm_gains:
            copy.wait_send()
        for b in range(3):
            y_back(b).wait_send()

        def drain_units(u, carry):
            @pl.when(me < parts - 1)
            def _():
                unit_right(u).wait_send()

            @pl.when(me > 0)
            def _():
                unit_left(u).wait_send()

            return carry

        lax.fori_loop(0, UNITS, drain_units, 0)

    def drain_blocks(j, carry):
        dense_core_copy(j).wait_send()
        dense_x_copy(j).wait_send()
        first_copy(j).wait_send()
        result_copy(j).wait()
        tokens_copy(j).wait()
        return carry

    def drain(i, carry):
        @pl.when(me < parts - 1)
        def _():
            right_copy(i).wait_send()

        @pl.when(me > 0)
        def _():
            left_copy(i).wait_send()

        core_copy(i).wait_send()
        x_copy(i).wait_send()
        fin_copy(i).wait_send()
        return carry

    lax.fori_loop(0, CHUNKS, drain, 0)
    for copy in sum_copies + centre_copies:
        copy.wait_send()
    lax.fori_loop(0, blocks, drain_blocks, 0)


def tail(
    pair, lengths, dkv, dq, summed, k, v, centre, topk, tm, merged, rows_in, counts, clusters,
    weight, fn, sfn, tokens, gain, mgrad, srow, mid, hsum, hsum_x, wo_part, second_gains, parts,
):
    rows, width = k.shape
    model = tokens.shape[1]
    shape = jax.ShapeDtypeStruct
    dma = pltpu.SemaphoreType.DMA
    blocks = rows // 256
    chain = pltpu.VMEM((CHUNKS, CHUNK, model // 2), BF16)
    whole = pltpu.VMEM((CHUNKS, CHUNK, model), BF16)
    unit = pltpu.VMEM((UNITS, 128, model // 2) if pair else (UNITS, 16, 128), BF16)
    return pl.pallas_call(
        functools.partial(tail_kernel, pair),
        out_shape=(
            shape((rows, model), BF16),
            shape((rows, model), BF16),
            shape((3, model, width), F32),
            shape((width, model), F32),
            shape((8, model), F32),
        ),
        in_specs=[pl.BlockSpec(memory_space=pltpu.SMEM)]
        + vmem(14)
        + [pl.BlockSpec(memory_space=pl.ANY)]
        + vmem(2)
        + [pl.BlockSpec(memory_space=pl.ANY)]
        + vmem(1)
        + [pl.BlockSpec(memory_space=pl.ANY)] * 2
        + vmem(3),
        out_specs=tuple(vmem(5)),
        scratch_shapes=[
            pltpu.VMEM((parts, CLP, 256), BF16),
            pltpu.VMEM((parts, CLP, width), BF16),
            pltpu.VMEM((model, 2 * width), BF16),
            whole, whole, whole,
            chain, chain, chain, chain, chain, chain,
            chain,
            pltpu.VMEM((rows, width), BF16),
            pltpu.VMEM((rows, 2 * width), BF16),
            pltpu.VMEM((blocks, 128, model), F32),
            pltpu.VMEM((blocks, 128, model), BF16),
            pltpu.VMEM((blocks, 128, model), BF16),
            pltpu.VMEM((blocks, 128, model // 2), BF16),
            pltpu.VMEM((blocks, 128, model // 2), BF16),
            pltpu.VMEM((rows // 2, model // 2), F32),
            pltpu.VMEM((blocks, 128, model), BF16),
            pltpu.VMEM((SLOTS, 256), BF16),
            pltpu.VMEM((4 * width, model), BF16),
            pltpu.VMEM((3, 128, model), BF16),
            pltpu.VMEM((3, 128, model), BF16),
            unit, unit, unit, unit, unit,
            pltpu.VMEM((8, model), F32),
            pltpu.VMEM((parts, 8, model), F32),
            pltpu.VMEM((2, 8, model), F32),
            dma, dma, dma,
        ]
        + [dma((parts,))] * 4
        + [dma((CHUNKS,))] * 10
        + [dma((blocks,))] * 10
        + [dma((3,))] * 2
        + [dma((UNITS,))] * 4
        + [dma((3,))] * 2
        + [dma, dma, dma((parts,)), dma((parts,)), dma, dma],
        compiler_params=pltpu.CompilerParams(
            vmem_limit_bytes=58 << 20, collective_id=1, has_side_effects=True
        ),
        name="tail",
    )(
        lengths, dkv, dq, summed, k, v, centre, topk, tm, merged, rows_in, counts,
        clusters.reshape(rows, 1), weight, fn, sfn, tokens, gain[None],
        mgrad.reshape(blocks, 128, model), srow, mid.reshape(blocks, 128, model),
        hsum.reshape(blocks, 128, model), hsum_x.reshape(blocks, 128, model), wo_part, second_gains,
    )


def shards(
    tokens,
    clusters,
    top_keys,
    lengths,
    qkv_weight,
    out_weight,
    first_gain,
    first_bias,
    second_gain,
    second_bias,
    expand_weight,
    shrink_weight,
    cotangent,
):
    parts, n_dp = lax.axis_size("dm"), lax.axis_size("dp")
    pair = n_dp == 2
    topk = jnp.pad(top_keys, ((0, CLP - CL), (0, 0)), constant_values=-1)
    flat = jnp.pad(top_keys.reshape(-1), (0, SLOTS - CL * TOPK), constant_values=-1)
    (
        first_normed, slot_normed, qs, k, v, ks, vs, starts, rcol, rrow, cls, centre, tm, rows_in,
        merged, counts, out_full, both_full,
    ) = front(
        pair, lengths, tokens, clusters, qkv_weight, first_gain, first_bias,
        flat.reshape(SLOTS, 1), topk, expand_weight, shrink_weight.T, out_weight, parts,
    )
    if not pair:
        both_full = jnp.concatenate(
            [
                lax.all_gather(expand_weight, ("dp", "dm"), axis=0, tiled=True),
                lax.all_gather(shrink_weight.T, ("dp", "dm"), axis=0, tiled=True),
            ],
            axis=1,
        )
    attended = exact_forward(starts, qs, cls, ks, vs, rows_in, rcol)
    (
        mid, middle_grad, attended_grad, hidden_sum, weight_grads, out_grad_part, second_parts,
    ) = middle(
        pair, tokens, cotangent, attended, out_weight, out_full, both_full, second_gain, second_bias
    )
    hidden_sum_x = lax.ppermute(hidden_sum, "hid", [(i, i ^ 2) for i in range(lax.axis_size("hid"))])
    units = expand_weight.shape[1]
    if pair:
        shard = expand_weight.shape[0]
        me = lax.axis_index("dm")
        summed_grads = lax.dynamic_slice_in_dim(weight_grads, me * shard, shard, 0).astype(F32)
        arrived = []
        for step in range(1, parts):
            block = lax.dynamic_slice_in_dim(
                weight_grads, lax.rem(me + step, parts) * shard, shard, 0
            )
            arrived.append(
                lax.ppermute(block, "dm", [(i, (i + step) % parts) for i in range(parts)])
            )
        for block in arrived:
            summed_grads = summed_grads + block.astype(F32)
    else:
        summed_grads = lax.psum_scatter(
            weight_grads, ("dp", "dm"), scatter_dimension=0, tiled=True
        ).astype(F32)
    expand_grad, shrink_grad = summed_grads[:, :units], summed_grads[:, units:].T
    dq, dkv, summed = exact_backward(
        starts, qs, cls, ks, vs, rows_in, rcol, rrow, attended_grad
    )
    result, tokens_grad, qkv_grad, out_grad, gains = tail(
        pair, lengths, dkv, dq, summed, k, v, centre, topk, tm, merged, rows_in, counts, clusters,
        qkv_weight, first_normed, slot_normed, tokens, first_gain, middle_grad,
        flat.reshape(1, SLOTS), mid, hidden_sum, hidden_sum_x, out_grad_part, second_parts, parts,
    )
    if not pair:
        qkv_grad, out_grad = [
            grad.astype(F32)
            for grad in lax.psum((qkv_grad.astype(BF16), out_grad.astype(BF16)), ("dp", "dm"))
        ]
        gains = 0.5 * lax.psum(gains, ("dp", "dm", "hid"))
    return (
        result,
        tokens_grad,
        qkv_grad,
        out_grad,
        gains[0],
        gains[1],
        gains[2],
        gains[3],
        expand_grad,
        shrink_grad,
    )


def solution(mesh):
    in_specs = (
        P(("dp", "dm"), None),
        P(("dp", "dm")),
        P("dp", None),
        P("dp"),
        P(None, None, "hid"),
        P("hid", None),
        P(),
        P(),
        P(),
        P(),
        P(("dp", "dm"), "hid"),
        P("hid", ("dp", "dm")),
        P(("dp", "dm"), None),
    )
    out_specs = (
        P(("dp", "dm"), None),
        P(("dp", "dm"), None),
        P(None, None, "hid"),
        P("hid", None),
        P(),
        P(),
        P(),
        P(),
        P(("dp", "dm"), "hid"),
        P("hid", ("dp", "dm")),
    )
    return jax.shard_map(shards, mesh=mesh, in_specs=in_specs, out_specs=out_specs, check_vma=False)
```

```python
import functools

import jax
import jax.numpy as jnp
from jax import lax
from jax.experimental import pallas as pl
from jax.experimental.pallas import tpu as pltpu
from jax.sharding import PartitionSpec as P

HEAD_DIM = 64
CL = 100
TOPK = 32
CLP = 128
SLOTS = 3328
GROUP = 8
GSLOTS = GROUP * TOPK
GROUPS = SLOTS // GSLOTS
WIN = 160
HALF = SLOTS // 2
CHUNK = 128
CHUNKS = HALF // CHUNK
LAG = 2
UNITS = 6
EPSILON = 1e-05
NEGATIVE = -1e30
HIGHEST = lax.Precision.HIGHEST
F32 = jnp.float32
BF16 = jnp.bfloat16
MESH = pl.DeviceIdType.MESH
NT = (((1,), (1,)), ((), ()))
TN = (((0,), (0,)), ((), ()))
SCALE = HEAD_DIM ** (-0.5)


def dot(a, b):
    return jnp.dot(a, b, preferred_element_type=F32)


def dot_nt(a, b):
    return lax.dot_general(a, b, NT, preferred_element_type=F32)


def dot_tn(a, b):
    return lax.dot_general(a, b, TN, preferred_element_type=F32)


def iota(shape, dim):
    return lax.broadcasted_iota(jnp.int32, shape, dim)


def norm_parts(values):
    centred = values - jnp.mean(values, -1, keepdims=True)
    spread = lax.rsqrt(jnp.mean(centred * centred, -1, keepdims=True) + EPSILON)
    return (centred * spread, spread)


def norm_back(upstream, normed, spread, norm_gain):
    through = upstream * norm_gain
    inner = (
        through
        - jnp.mean(through, -1, keepdims=True)
        - normed * jnp.mean(through * normed, -1, keepdims=True)
    )
    return (spread * inner, jnp.sum(upstream * normed, 0), jnp.sum(upstream, 0))


def head_lanes(width, head):
    lane = iota((1, width), 1)
    return lane // HEAD_DIM == head


def block_diagonal(rows, heads):
    width = rows.shape[1]
    zero = jnp.zeros_like(rows)
    return jnp.concatenate(
        [jnp.where(head_lanes(width, h), rows, zero) for h in range(heads)], axis=0
    )


def block_diagonal_turned(turned, heads):
    zero = jnp.zeros((HEAD_DIM, turned.shape[1]), turned.dtype)
    columns = []
    for h in range(heads):
        mine = turned[h * HEAD_DIM : (h + 1) * HEAD_DIM]
        columns.append(jnp.concatenate([mine if i == h else zero for i in range(heads)], axis=0))
    return jnp.concatenate(columns, axis=1)


def diagonal_blocks_turned(full, heads):
    rows, size = full.shape[0] // heads, full.shape[1] // heads
    return jnp.concatenate(
        [full[h * rows : (h + 1) * rows, h * size : (h + 1) * size] for h in range(heads)], axis=0
    )


def diagonal_blocks(full, heads):
    rows, width = full.shape[0] // heads, full.shape[1]
    out = full[:rows]
    for h in range(1, heads):
        out = jnp.where(head_lanes(width, h), full[h * rows : (h + 1) * rows], out)
    return out


def vmem(n):
    return [pl.BlockSpec(memory_space=pltpu.VMEM)] * n


def remote(src, dst, send, recv, device):
    return pltpu.make_async_remote_copy(
        src_ref=src, dst_ref=dst, send_sem=send, recv_sem=recv, device_id=device,
        device_id_type=MESH,
    )


def greet(devices):
    barrier = pltpu.get_barrier_semaphore()
    for device in devices:
        pl.semaphore_signal(barrier, inc=1, device_id=device, device_id_type=MESH)
    return barrier


def small_exchange(buf, sends, recvs, me, parts):
    return [
        remote(
            buf.at[me], buf.at[me], sends.at[step], recvs.at[step],
            {"dm": lax.rem(me + step, parts)},
        )
        for step in range(1, parts)
    ]


def when_in(i, count, work):
    @pl.when((i >= 0) & (i < count))
    def _():
        work(i)


def aligned(start, size):
    return pl.ds(pl.multiple_of(start, 128), size)


def sequence_masks(lengths, topk, rows):
    own_start = lax.axis_index("dm") * rows
    key_second = iota((1, rows), 1) + own_start >= lengths[0]
    centre_second = topk[:, :1] >= lengths[0]
    return key_second == centre_second


def front_kernel(
    pair, lengths, tok, ccol, weight, gain, bias, scol, topk, wexp, wshr, wout,
    fn_hbm, sfn_hbm, qs_out, k_out, v_out, ks_out, vs_out, kst_out, vst_out, starts_out, rcol_out, rrow_out,
    cls_out, centre_out, tm_out, rows_out, merged_out, count_out, wall_out, wfull_out, shr_peer_out,
    fn_out, sfn_out, q_ref, member_ref, cbuf, rbuf, sbuf, own, to_right, to_left, from_left, from_right,
    csend, crecv, rsend, rrecv, ssend, srecv,
    send_right, recv_left, send_left, recv_right, send_x, recv_x, send_core, recv_core,
    send_relay, recv_relay, osend, orecv, wsend, wrecv, ysend, yrecv, psend, precv, local_sems,
):
    rows, model = tok.shape
    width = weight.shape[1]
    heads = width // HEAD_DIM
    half_width = model // 2
    tiles = rows // 128
    parts = lax.axis_size("dm")
    me, hid, dp = lax.axis_index("dm"), lax.axis_index("hid"), lax.axis_index("dp")
    core, side = lax.rem(hid, 2), hid // 2
    core_peer = {"hid": hid + 1 - 2 * core}
    x_peer = {"hid": hid + 2 - 4 * side}
    lane = iota((128, 128), 1)
    columns = aligned(side * half_width, half_width)
    other_columns = aligned((1 - side) * half_width, half_width)
    own_start = me * rows

    greeted = [{"dm": lax.rem(me + step, parts)} for step in range(1, parts)]
    greeted += [core_peer, x_peer]
    if pair:
        greeted.append({"dp": 1 - dp})
    barrier = greet(greeted)

    out_rows = pl.ds(pl.multiple_of(hid * width, 64), width)
    out_own = pltpu.make_async_copy(wout, wall_out.at[out_rows, :], local_sems.at[0])
    out_own.start()
    out_x_rows = pl.ds(pl.multiple_of((hid + 2 - 4 * side) * width, 64), width)
    out_copies = [
        remote(wout, wall_out.at[out_rows, :], osend.at[0], orecv.at[0], core_peer),
        remote(wout, wall_out.at[out_rows, :], osend.at[1], orecv.at[1], x_peer),
        remote(
            wall_out.at[out_x_rows, :], wall_out.at[out_x_rows, :], osend.at[2], orecv.at[2], core_peer
        ),
    ]
    if pair:
        shard = wexp.shape[0]

        def shard_rows(d, m):
            return pl.ds(pl.multiple_of((d * parts + m) * shard, 32), shard)

        mine = shard_rows(dp, me)
        def gather(source, whole, sends, recvs, ysends, yrecvs):
            direct = [
                remote(
                    source, whole.at[mine, :], sends.at[step], recvs.at[step],
                    {"dm": lax.rem(me + step, parts)},
                )
                for step in range(1, parts)
            ]
            across = []
            for step in range(parts):
                block = whole.at[shard_rows(dp, lax.rem(me + parts - step, parts)), :]
                across.append(
                    remote(
                        source if step == 0 else block, block, ysends.at[step], yrecvs.at[step],
                        {"dp": 1 - dp},
                    )
                )
            return direct, across

        shard_own = pltpu.make_async_copy(wexp, wfull_out.at[mine, :], local_sems.at[1])
        shard_own.start()
        expand_direct, expand_across = gather(wexp, wfull_out, wsend, wrecv, ysend, yrecv)
        shrink_peer = remote(wshr, shr_peer_out, psend, precv, {"dp": 1 - dp})

    pl.semaphore_wait(barrier, len(greeted))
    if pair:
        expand_across[0].start()
        shrink_peer.start()
        for copy in expand_direct:
            copy.start()
    out_copies[0].start()
    out_copies[1].start()

    def first_norm(i, carry):
        at = aligned(i * 256, 256)
        normed, _ = norm_parts(tok[at, :].astype(F32))
        fn_out[at, :] = (normed * gain[...][None] + bias[...][None]).astype(BF16)
        return carry

    lax.fori_loop(0, rows // 256, first_norm, 0)
    fn_copy = pltpu.make_async_copy(fn_out, fn_hbm, local_sems.at[2])
    fn_copy.start()

    @pl.when(me == 0)
    def _():
        from_left[...] = jnp.zeros_like(from_left)

    @pl.when(me == parts - 1)
    def _():
        from_right[...] = jnp.zeros_like(from_right)

    def chunk_rows(i, which):
        return aligned(which * HALF + i * CHUNK, CHUNK)

    def right_copy(i):
        return remote(
            to_right.at[i], from_left.at[i], send_right.at[i], recv_left.at[i],
            {"dm": lax.rem(me + 1, parts)},
        )

    def left_copy(i):
        return remote(
            to_left.at[i], from_right.at[i], send_left.at[i], recv_right.at[i],
            {"dm": lax.rem(me + parts - 1, parts)},
        )

    def x_copy(i):
        block = sfn_out.at[chunk_rows(i, core), columns]
        return remote(block, block, send_x.at[i], recv_x.at[i], x_peer)

    def core_copy(i):
        block = sfn_out.at[chunk_rows(i, core), columns]
        return remote(block, block, send_core.at[i], recv_core.at[i], core_peer)

    def relay_copy(i):
        block = sfn_out.at[chunk_rows(i, core), other_columns]
        return remote(block, block, send_relay.at[i], recv_relay.at[i], core_peer)

    def make_own(first, count):
        at = aligned(core * HALF + first * CHUNK, count * CHUNK)
        chosen = (scol[at, :] == iota((count * CHUNK, rows), 1) + own_start).astype(BF16)
        picked = dot(chosen, fn_out[:, columns]).astype(BF16)
        for i in range(count):
            own[first + i] = picked[i * CHUNK : (i + 1) * CHUNK]

    def go_right(i):
        @pl.when(me > 0)
        def _():
            right_copy(i).wait_recv()

        @pl.when(me < parts - 1)
        def _():
            to_right[i] = own[i] + from_left[i]
            right_copy(i).start()

    def go_left(i):
        @pl.when(me < parts - 1)
        def _():
            left_copy(i).wait_recv()

        @pl.when(me > 0)
        def _():
            to_left[i] = own[i] + from_right[i]
            left_copy(i).start()

    def finish(i):
        sfn_out[chunk_rows(i, core), columns] = own[i] + from_left[i] + from_right[i]
        x_copy(i).start()
        core_copy(i).start()

    def relay(i):
        x_copy(i).wait_recv()
        relay_copy(i).start()

    far = jnp.maximum(me, parts - 1 - me)

    def ticks(first, last):
        def tick(t, carry):
            when_in(t - LAG * me, CHUNKS, go_right)
            when_in(t - LAG * (parts - 1 - me), CHUNKS, go_left)
            when_in(t - LAG * far, CHUNKS, finish)
            when_in(t - LAG * far - LAG, CHUNKS, relay)
            return carry

        lax.fori_loop(first, last, tick, 0)

    def project(part):
        at = aligned(part * (rows // 2), rows // 2)
        first = fn_out[at, :]
        q_ref[at, :] = dot_nt(first, weight[0]).astype(BF16)
        k_out[at, :] = dot_nt(first, weight[1]).astype(BF16)
        v_out[at, :] = dot_nt(first, weight[2]).astype(BF16)

    lower = (iota((128, 128), 0) > iota((128, 128), 1)).astype(BF16)

    def count_tile(i, running):
        at = aligned(i * 128, 128)
        member = (ccol[at, :] == lane).astype(F32)
        low = member.astype(BF16)
        member_ref[at, :] = low
        earlier = dot(lower, low) + running
        rcol_out[at, :] = jnp.sum(member * earlier, 1, keepdims=True)
        return running + jnp.sum(member, 0, keepdims=True)

    def place(i, carry):
        at = aligned(i * 256, 256)
        rank_row = rrow_out[:1, :].astype(jnp.int32)
        chosen = (iota((256, rows), 0) + i * 256 == rank_row).astype(BF16)
        qs_out[at, :] = (dot(chosen, q_ref[...]) * SCALE).astype(BF16)
        sorted_member = dot(chosen, member_ref[...])
        cls_out[at, :] = jnp.sum(
            sorted_member * iota((256, 128), 1).astype(F32), 1, keepdims=True
        ).astype(jnp.int32)
        return carry

    make_own(0, 4)
    ticks(0, 1)
    project(0)
    ticks(1, 2)
    make_own(4, 4)
    ticks(2, 4)
    project(1)
    ticks(4, 5)
    counts = lax.fori_loop(0, tiles, count_tile, jnp.zeros((1, 128), F32))
    extended = jnp.concatenate([q_ref[...], jnp.ones((rows, 256 - width), BF16)], axis=1)
    sums = dot_tn(member_ref[...], extended)
    sixteens = jnp.floor(sums * 0.0625)
    wide = iota((CLP, 256), 1)
    packed = jnp.where(
        wide == width, sixteens, jnp.where(wide == width + 1, sums - 16.0 * sixteens, sums)
    )
    cbuf[me] = packed.astype(BF16)
    centre_copies = small_exchange(cbuf, csend, crecv, me, parts)
    for copy in centre_copies:
        copy.start()
    ticks(5, 6)
    make_own(8, CHUNKS - 8)
    ticks(6, 7)
    before = (iota((128, 128), 0) < iota((128, 128), 1)).astype(F32)
    starts = jnp.dot(
        jnp.broadcast_to(counts, (8, 128)), before, precision=HIGHEST, preferred_element_type=F32
    )
    starts_out[...] = starts.astype(jnp.int32)

    def ranks(i, carry):
        at = aligned(i * 128, 128)
        member = member_ref[at, :].astype(F32)
        rank = rcol_out[at, :] + jnp.sum(member * starts[:1], 1, keepdims=True)
        rcol_out[at, :] = rank
        turned = jnp.transpose(jnp.broadcast_to(rank, (128, 128)))
        rrow_out[:, at] = turned[:8]
        return carry

    lax.fori_loop(0, tiles, ranks, 0)
    ticks(7, 8)
    here = iota((CLP, rows), 1) + own_start
    hit = topk[:, :1] == here
    for t in range(1, TOPK):
        hit = hit | (topk[:, t : t + 1] == here)
    tm_out[...] = hit.astype(F32).astype(BF16)
    ticks(8, 9)

    for copy in centre_copies:
        copy.wait_recv()
    gathered = cbuf[0].astype(F32)
    for d in range(1, parts):
        gathered += cbuf[d].astype(F32)
    count = jnp.maximum(
        16.0 * gathered[:, width : width + 1] + gathered[:, width + 1 : width + 2], 1.0
    )
    count_out[...] = jnp.broadcast_to(count, (CLP, 128))
    centre = (gathered[:, :width] / count).astype(BF16)
    centre_out[...] = centre
    same = sequence_masks(lengths, topk, rows)
    stats = jnp.zeros((CLP, 128), F32)
    rest = jnp.zeros((CLP, width), F32)
    for h in range(heads):
        top = tm_out[...].astype(F32)
        mine_lanes = head_lanes(width, h)
        scores = dot_nt(jnp.where(mine_lanes, centre, jnp.zeros_like(centre)), k_out[...]) * SCALE
        scores = jnp.where(same, scores, NEGATIVE)
        largest = jnp.max(scores, 1, keepdims=True)
        raised = jnp.exp(scores - largest)
        total = jnp.sum(raised, 1, keepdims=True)
        within = raised * top
        mass = jnp.sum(within, 1, keepdims=True)
        rest = jnp.where(mine_lanes, dot((raised - within).astype(BF16), v_out[...]), rest)
        stats = jnp.where(lane == h, largest, stats)
        stats = jnp.where(lane == 8 + h, total, stats)
        stats = jnp.where(lane == 16 + h, mass, stats)
    rbuf[me] = rest.astype(BF16)
    sbuf[me] = jnp.transpose(stats)[:24]
    rest_copies = small_exchange(rbuf, rsend, rrecv, me, parts)
    stat_copies = small_exchange(sbuf, ssend, srecv, me, parts)
    for copy in rest_copies + stat_copies:
        copy.start()
    ticks(9, 11)
    lax.fori_loop(0, rows // 512, place, 0)
    ticks(11, 13)
    out_copies[1].wait_recv()
    out_copies[2].start()
    lax.fori_loop(rows // 512, rows // 256, place, 0)
    qs_out[rows:, :] = jnp.zeros((WIN, width), BF16)
    cls_out[rows:, :] = jnp.full((WIN, 1), -1, jnp.int32)
    ticks(13, 15)
    if pair:
        for step in range(1, parts):
            expand_direct[step - 1].wait_recv()
            expand_across[step].start()
    ticks(15, 18)

    for copy in rest_copies + stat_copies:
        copy.wait_recv()
    largest = sbuf[0][:8]
    for d in range(1, parts):
        largest = jnp.maximum(largest, sbuf[d][:8])
    total = jnp.zeros((8, 128), F32)
    mass = jnp.zeros((8, 128), F32)
    factors = []
    for d in range(parts):
        factor = jnp.exp(sbuf[d][:8] - largest)
        total += factor * sbuf[d][8:16]
        mass += factor * sbuf[d][16:24]
        factors.append(factor)
    live = iota((8, 128), 0) < heads
    total = jnp.where(live, total, 1.0)
    mass = mass / total
    table = [largest, total, mass] + [factor / total for factor in factors]
    table.append(jnp.zeros((128 - 8 * len(table), 128), F32))
    columns_table = jnp.transpose(jnp.concatenate(table, axis=0))
    merged_out[...] = columns_table
    mass_rows = jnp.zeros((CLP, width), F32)
    rest_rows = jnp.zeros((CLP, width), F32)
    for h in range(heads):
        mine_lanes = head_lanes(width, h)
        mass_rows = jnp.where(mine_lanes, columns_table[:, 16 + h : 17 + h], mass_rows)
        rest = jnp.zeros((CLP, width), F32)
        for d in range(parts):
            lane_at = 24 + 8 * d + h
            rest += columns_table[:, lane_at : lane_at + 1] * rbuf[d].astype(F32)
        rest_rows = jnp.where(mine_lanes, rest, rest_rows)
    rows_out[:, :width] = mass_rows
    rows_out[:, width:] = rest_rows

    def arrive(i, carry):
        core_copy(i).wait_recv()
        relay_copy(i).wait_recv()
        return carry

    def project_slots(first, count):
        for which in range(2):
            at = pl.ds(which * HALF + first * CHUNK, count * CHUNK)
            block = sfn_out[at, :]
            for which_weight, out, turned in ((1, ks_out, kst_out), (2, vs_out, vst_out)):
                product = dot_nt(block, weight[which_weight])
                out[at, :] = product.astype(BF16)
                turned[:, at] = jnp.transpose(product).astype(BF16)

    early = CHUNKS // 2
    lax.fori_loop(0, early, arrive, 0)
    project_slots(0, early)
    ticks(18, CHUNKS + LAG * parts)
    lax.fori_loop(early, CHUNKS, arrive, 0)
    sfn_copy = pltpu.make_async_copy(sfn_out, sfn_hbm, local_sems.at[3])
    sfn_copy.start()
    project_slots(early, CHUNKS - early)

    def drain(i, carry):
        @pl.when(me < parts - 1)
        def _():
            right_copy(i).wait_send()

        @pl.when(me > 0)
        def _():
            left_copy(i).wait_send()

        x_copy(i).wait_send()
        core_copy(i).wait_send()
        relay_copy(i).wait_send()
        return carry

    lax.fori_loop(0, CHUNKS, drain, 0)
    for copy in centre_copies + rest_copies + stat_copies + out_copies:
        copy.wait_send()
    out_copies[0].wait_recv()
    out_copies[2].wait_recv()
    if pair:
        for copy in expand_direct:
            copy.wait_send()
        for copy in expand_across + [shrink_peer]:
            copy.wait()
        shard_own.wait()
    out_own.wait()
    fn_copy.wait()
    sfn_copy.wait()


def front(pair, lengths, tokens, clusters, weight, gain, bias, scol, topk, wexp, wshr, wout, parts):
    rows, model = tokens.shape
    width = weight.shape[1]
    shape = jax.ShapeDtypeStruct
    dma = pltpu.SemaphoreType.DMA
    chain = pltpu.VMEM((CHUNKS, CHUNK, model // 2), BF16)
    whole = (model, wexp.shape[1]) if pair else (16, 128)
    anywhere = [pl.BlockSpec(memory_space=pl.ANY)]
    return pl.pallas_call(
        functools.partial(front_kernel, pair),
        out_shape=(
            shape(tokens.shape, BF16),
            shape((SLOTS, model), BF16),
            shape((rows + WIN, width), BF16),
            shape((rows, width), BF16),
            shape((rows, width), BF16),
            shape((SLOTS, width), BF16),
            shape((SLOTS, width), BF16),
            shape((width, SLOTS), BF16),
            shape((width, SLOTS), BF16),
            shape((8, 128), jnp.int32),
            shape((rows, 1), F32),
            shape((8, rows), F32),
            shape((rows + WIN, 1), jnp.int32),
            shape((CLP, width), BF16),
            shape((CLP, rows), BF16),
            shape((CLP, 2 * width), F32),
            shape((CLP, 128), F32),
            shape((CLP, 128), F32),
            shape((lax.axis_size("hid") * width, model), BF16),
            shape(whole, BF16),
            shape(wshr.shape, BF16),
        ),
        in_specs=[pl.BlockSpec(memory_space=pltpu.SMEM)] + vmem(7) + anywhere * 3,
        out_specs=tuple(anywhere * 2 + vmem(16) + anywhere * 3),
        scratch_shapes=[
            pltpu.VMEM((rows, model), BF16),
            pltpu.VMEM((SLOTS, model), BF16),
            pltpu.VMEM((rows, width), BF16),
            pltpu.VMEM((rows, 128), BF16),
            pltpu.VMEM((parts, CLP, 256), BF16),
            pltpu.VMEM((parts, CLP, width), BF16),
            pltpu.VMEM((parts, 24, 128), F32),
            chain, chain, chain, chain, chain,
        ]
        + [dma((parts,))] * 6
        + [dma((CHUNKS,))] * 10
        + [dma((3,))] * 2
        + [dma((parts,))] * 4
        + [dma, dma, dma((4,))],
        compiler_params=pltpu.CompilerParams(
            vmem_limit_bytes=56 << 20, collective_id=0, has_side_effects=True
        ),
        name="front",
    )(
        lengths, tokens, clusters.reshape(rows, 1), weight, gain, bias, scol, topk,
        wexp, wshr, wout,
    )


UNROLL = 4


def list_windows(starts, rows, group_at, row_at):
    def one_group(g, count):
        first, last = starts[0, g * GROUP], starts[0, g * GROUP + GROUP]
        base = first // 16 * 16
        windows = jnp.where(last > first, (last - base + WIN - 1) // WIN, 0)

        def one(w, carry):
            group_at[count + w] = g
            row_at[count + w] = base + w * WIN
            return carry

        lax.fori_loop(0, windows, one, 0)
        return count + windows

    count = lax.fori_loop(0, GROUPS, one_group, 0)
    for i in range(UNROLL - 1):
        group_at[count + i] = 0
        row_at[count + i] = rows
    return count


def window_probs(scores, mine, inside, h):
    part = jnp.where(mine, scores[:, h * GSLOTS : (h + 1) * GSLOTS], NEGATIVE)
    raised = jnp.exp(part - jnp.max(part, 1, keepdims=True))
    inverse = jnp.where(inside, 1.0 / jnp.sum(raised, 1, keepdims=True), 0.0)
    return raised * inverse


def window_at(starts, group_at, row_at, i):
    g = group_at[i]
    row = pl.multiple_of(row_at[i], 16)
    at = pl.ds(pl.multiple_of(g * GSLOTS, GSLOTS), GSLOTS)
    place = iota((WIN, 1), 0) + row
    inside = (place >= starts[0, g * GROUP]) & (place < starts[0, g * GROUP + GROUP])
    return g, pl.ds(row, WIN), at, inside


def exact_forward_kernel(
    starts, qs, cls, kt_hbm, vs_hbm, both, rcol, att_out, att_s, mix_s, kt, vs, group_at, row_at, sems
):
    rows, width = rcol.shape[0], qs.shape[1]
    heads = width // HEAD_DIM
    copies = [
        pltpu.make_async_copy(kt_hbm, kt, sems.at[0]),
        pltpu.make_async_copy(vs_hbm, vs, sems.at[1]),
    ]
    for copy in copies:
        copy.start()
    high = both[...].astype(BF16)
    low = (both[...] - high.astype(F32)).astype(BF16)
    step = (rows + WIN) // 5

    def spread(i, carry):
        at = pl.ds(pl.multiple_of(i * step, 16), step)
        member = (cls[at, :] == iota((step, 128), 1)).astype(BF16)
        mix_s[at, :] = dot(member, high) + dot(member, low)
        return carry

    lax.fori_loop(0, 5, spread, 0)
    count = list_windows(starts, rows, group_at, row_at)
    for copy in copies:
        copy.wait()
    slot_cluster = iota((WIN, GSLOTS), 1) // TOPK

    def windows(n, carry):
        for i in range(UNROLL):
            g, here, at, inside = window_at(starts, group_at, row_at, n * UNROLL + i)
            keys = block_diagonal_turned(kt[:, at], heads)
            values = block_diagonal(vs[at, :], heads)
            mine = cls[here, :] == slot_cluster + g * GROUP
            scores = dot(qs[here, :], keys)
            weights = [window_probs(scores, mine, inside, h).astype(BF16) for h in range(heads)]
            out = dot(jnp.concatenate(weights, axis=1), values)
            mix = mix_s[here, :]
            att_s[here, :] = jnp.where(inside, mix[:, :width] * out + mix[:, width:], att_s[here, :])
        return carry

    lax.fori_loop(0, (count + UNROLL - 1) // UNROLL, windows, 0)

    def unplace(i, carry):
        at = pl.ds(pl.multiple_of(i * 256, 256), 256)
        chosen = (iota((256, rows), 1) == rcol[at, :].astype(jnp.int32)).astype(BF16)
        att_out[at, :] = dot(chosen, att_s[:rows, :].astype(BF16)).astype(BF16)
        return carry

    lax.fori_loop(0, rows // 256, unplace, 0)


ANYWHERE = pl.BlockSpec(memory_space=pl.ANY)
LISTED = 64


def exact_forward(starts, qs, cls, ks, vs, both, rcol):
    rows, width = rcol.shape[0], qs.shape[1]
    shape = jax.ShapeDtypeStruct
    return pl.pallas_call(
        exact_forward_kernel,
        out_shape=shape((rows, width), BF16),
        in_specs=[pl.BlockSpec(memory_space=pltpu.SMEM)] + vmem(2) + [ANYWHERE] * 2 + vmem(2),
        out_specs=vmem(1)[0],
        scratch_shapes=[
            pltpu.VMEM((rows + WIN, width), F32),
            pltpu.VMEM((rows + WIN, 2 * width), F32),
            pltpu.VMEM((width, SLOTS), BF16),
            pltpu.VMEM((SLOTS, width), BF16),
            pltpu.SMEM((LISTED,), jnp.int32),
            pltpu.SMEM((LISTED,), jnp.int32),
            pltpu.SemaphoreType.DMA((2,)),
        ],
        compiler_params=pltpu.CompilerParams(vmem_limit_bytes=62 << 20),
        name="exact_forward",
    )(starts, qs, cls, ks, vs, both, rcol)


def exact_backward_kernel(
    starts, qs, cls, ks_hbm, kt_hbm, vt_hbm, rows_in, rcol, rrow, grad,
    dq_out, dkv_out, dkvt_out, centre_out,
    grad_s, mass_s, dq_s, part_s, dkv_s, ks, kt, vt, group_at, row_at, sems,
):
    rows, width = rcol.shape[0], qs.shape[1]
    heads = width // HEAD_DIM
    copies = [
        pltpu.make_async_copy(ks_hbm, ks, sems.at[0]),
        pltpu.make_async_copy(kt_hbm, kt, sems.at[1]),
        pltpu.make_async_copy(vt_hbm, vt, sems.at[2]),
    ]
    for copy in copies:
        copy.start()
    mass_rows = rows_in[:, :width]
    high = mass_rows.astype(BF16)
    low = (mass_rows - high.astype(F32)).astype(BF16)
    rank_row = rrow[:1, :].astype(jnp.int32)

    def place(i, carry):
        at = pl.ds(pl.multiple_of(i * 256, 256), 256)
        chosen = (iota((256, rows), 0) + i * 256 == rank_row).astype(BF16)
        grad_s[at, :] = dot(chosen, grad[...]).astype(BF16)
        member = (cls[at, :] == iota((256, 128), 1)).astype(BF16)
        mass_s[at, :] = dot(member, high) + dot(member, low)
        return carry

    lax.fori_loop(0, rows // 256, place, 0)
    grad_s[rows:, :] = jnp.zeros((WIN, width), BF16)
    mass_s[rows:, :] = jnp.zeros((WIN, width), F32)
    dkv_s[...] = jnp.zeros_like(dkv_s)
    count = list_windows(starts, rows, group_at, row_at)
    for copy in copies:
        copy.wait()
    slot_cluster = iota((WIN, GSLOTS), 1) // TOPK

    def windows(n, carry):
        for i in range(UNROLL):
            g, here, at, inside = window_at(starts, group_at, row_at, n * UNROLL + i)
            keys = block_diagonal(ks[at, :], heads)
            mine = cls[here, :] == slot_cluster + g * GROUP
            query, upstream = qs[here, :], grad_s[here, :]
            scores = dot(query, block_diagonal_turned(kt[:, at], heads))
            against = dot(upstream, block_diagonal_turned(vt[:, at], heads))
            mass = mass_s[here, :]
            weights, score_grads = [], []
            mass_part = jnp.zeros((WIN, width), F32)
            for h in range(heads):
                cut = slice(h * GSLOTS, (h + 1) * GSLOTS)
                probs = window_probs(scores, mine, inside, h)
                meeting = jnp.sum(probs * against[:, cut], 1, keepdims=True)
                weighted = probs * mass[:, h * HEAD_DIM : h * HEAD_DIM + 1]
                weights.append(weighted.astype(BF16))
                score_grads.append((weighted * (against[:, cut] - meeting)).astype(BF16))
                mass_part = jnp.where(head_lanes(width, h), meeting, mass_part)
            score_grad = jnp.concatenate(score_grads, axis=1)
            weight = jnp.concatenate(weights, axis=1)
            dq = dot(score_grad, keys) * SCALE
            dq_s[here, :] = jnp.where(inside, dq, dq_s[here, :])
            part_s[here, :] = jnp.where(inside, mass_part, part_s[here, :])
            pair = jnp.concatenate(
                [
                    diagonal_blocks_turned(dot_tn(query, score_grad), heads),
                    diagonal_blocks_turned(dot_tn(upstream, weight), heads),
                ],
                axis=0,
            )
            dkv_s[:, at] = dkv_s[:, at] + pair
        return carry

    lax.fori_loop(0, (count + UNROLL - 1) // UNROLL, windows, 0)
    centre_out[...] = jnp.zeros_like(centre_out)

    def finish_group(g, carry):
        at = pl.ds(pl.multiple_of(g * GSLOTS, GSLOTS), GSLOTS)
        block = dkv_s[:, at]
        dkvt_out[:, at] = block.astype(BF16)
        dkv_out[at, :] = jnp.transpose(block).astype(BF16)
        return carry

    lax.fori_loop(0, GROUPS, finish_group, 0)

    def unplace(i, carry):
        at = pl.ds(pl.multiple_of(i * 256, 256), 256)
        chosen = (iota((256, rows), 1) == rcol[at, :].astype(jnp.int32)).astype(BF16)
        dq_out[at, :] = dot(chosen, dq_s[:rows, :].astype(BF16)).astype(BF16)
        member = (cls[at, :] == iota((256, 128), 1)).astype(BF16)
        pair = jnp.concatenate([part_s[at, :].astype(BF16), grad_s[at, :]], axis=1)
        centre_out[...] += dot_tn(member, pair)
        return carry

    lax.fori_loop(0, rows // 256, unplace, 0)


def exact_backward(starts, qs, cls, ks, kt, vt, rows_in, rcol, rrow, grad):
    rows, width = rcol.shape[0], qs.shape[1]
    shape = jax.ShapeDtypeStruct
    return pl.pallas_call(
        exact_backward_kernel,
        out_shape=(
            shape((rows, width), BF16),
            shape((SLOTS, 2 * width), BF16),
            shape((2 * width, SLOTS), BF16),
            shape((CLP, 2 * width), F32),
        ),
        in_specs=[pl.BlockSpec(memory_space=pltpu.SMEM)] + vmem(2) + [ANYWHERE] * 3 + vmem(4),
        out_specs=tuple(vmem(4)),
        scratch_shapes=[
            pltpu.VMEM((rows + WIN, width), BF16),
            pltpu.VMEM((rows + WIN, width), F32),
            pltpu.VMEM((rows + WIN, width), F32),
            pltpu.VMEM((rows + WIN, width), F32),
            pltpu.VMEM((2 * width, SLOTS), F32),
            pltpu.VMEM((SLOTS, width), BF16),
            pltpu.VMEM((width, SLOTS), BF16),
            pltpu.VMEM((width, SLOTS), BF16),
            pltpu.SMEM((LISTED,), jnp.int32),
            pltpu.SMEM((LISTED,), jnp.int32),
            pltpu.SemaphoreType.DMA((3,)),
        ],
        compiler_params=pltpu.CompilerParams(vmem_limit_bytes=62 << 20),
        name="exact_backward",
    )(starts, qs, cls, ks, kt, vt, rows_in, rcol, rrow, grad)


def gelu_parts(values):
    slope = 0.7978845608028654
    squared = values * values
    turned = jnp.tanh(slope * values * (1.0 + 0.044715 * squared))
    half = 0.5 * (1.0 + turned)
    rise = half + 0.5 * slope * values * (1.0 - turned * turned) * (1.0 + 0.134145 * squared)
    return (values * half, rise)


def middle_kernel(
    pair, parts, tok, cot, att, wout_own, wout, wexp, gain, bias, shr_own, shr_one, shr_two, shr_three, shr_peer,
    mid_out, mgrad_out, agrad_out, hsum_out, wo_out, gains_out, *refs,
):
    grad_outs, refs = refs[: 2 + parts if pair else 1], refs[2 + parts if pair else 1 :]
    middle_body(
        pair, tok, cot, att, wout_own, wout, wexp, gain, bias,
        (shr_own, shr_one, shr_two, shr_three), shr_peer, mid_out, mgrad_out, agrad_out, hsum_out, wo_out, gains_out, grad_outs, *refs,
    )


def middle_body(
    pair, tok, cot, att, wout_own, wout, wexp, gain, bias, shards, shr_peer,
    mid_out, mgrad_out, agrad_out, hsum_out, wo_out, gains_out, grad_outs,
    wshr_ref, att_peer, cat, xcat, sn, act, hg, sp_own, sp_send, sp_recv, hp_own, hp_send, hp_recv,
    sx_send, sx_recv, branch, give, given, kept,
    asend, arecv, xsend, xrecv, rsend, rrecv, ssend, srecv, hsend, hrecv, sxs, sxr, bsend, brecv,
    gsend, grecv, wysend, wyrecv,
):
    rows, width = att.shape
    model = tok.shape[1]
    half_width = 2 * width
    half_rows = rows // 2
    blocks = half_rows // 128
    hid = lax.axis_index("hid")
    core, side = lax.rem(hid, 2), hid // 2
    core_peer = {"hid": hid + 1 - 2 * core}
    x_peer = {"hid": hid + 2 - 4 * side}

    dp = lax.axis_index("dp")
    greeted = [core_peer, x_peer] + ([{"dp": 1 - dp}] if pair else [])
    barrier = greet(greeted)
    gains_out[...] = jnp.zeros_like(gains_out)
    pl.semaphore_wait(barrier, len(greeted))

    units = wexp.shape[1]
    if pair:
        wshr = wshr_ref
        n_dm, my_dm = lax.axis_size("dm"), lax.axis_index("dm")
        shard = model // (2 * n_dm)

        def shard_rows(d, step):
            owner = lax.rem(my_dm + n_dm - step, n_dm)
            return pl.ds(pl.multiple_of((d * n_dm + owner) * shard, 32), shard)

        shard_copies = [
            remote(
                shards[step], wshr.at[shard_rows(dp, step), :], wysend.at[step], wyrecv.at[step],
                {"dp": 1 - dp},
            )
            for step in range(1, n_dm)
        ]
    else:
        wshr = shards[0]

    def block_rows(j, which):
        return pl.ds(pl.multiple_of(which * half_rows + j * 128, 128), 128)

    def own_rows(j):
        return pl.ds(pl.multiple_of(j * 128, 128), 128)

    att_copy = remote(att, att_peer, asend, arecv, core_peer)
    att_copy.start()
    if pair:
        for copy in shard_copies:
            copy.start()
        for step in range(n_dm):
            wshr[shard_rows(dp, step), :] = shards[step][...]
        wshr[shard_rows(1 - dp, 0), :] = shr_peer[...]

    def x_copy(j):
        block = block_rows(j, core)
        return remote(cat.at[block, :], xcat.at[block, :], xsend.at[j], xrecv.at[j], x_peer)

    def relay_copy(j):
        block = xcat.at[block_rows(j, core), :]
        return remote(block, block, rsend.at[j], rrecv.at[j], core_peer)

    def sp_copy(j):
        return remote(sp_send.at[j], sp_recv.at[j], ssend.at[j], srecv.at[j], core_peer)

    def hp_copy(j):
        return remote(hp_send.at[j], hp_recv.at[j], hsend.at[j], hrecv.at[j], core_peer)

    def sx_copy(j):
        return remote(sx_send.at[j], sx_recv.at[j], sxs.at[j], sxr.at[j], x_peer)

    def branch_copy(j):
        block = branch.at[block_rows(j, core), :]
        return remote(block, block, bsend.at[j], brecv.at[j], core_peer)

    def join(at):
        mine, other = att[at, :], att_peer[at, :]
        cat[at, :] = jnp.where(
            core == 0,
            jnp.concatenate([mine, other], axis=1),
            jnp.concatenate([other, mine], axis=1),
        )

    att_copy.wait_recv()

    def spread(j, carry):
        join(block_rows(j, core))
        x_copy(j).start()
        return carry

    lax.fori_loop(0, blocks, spread, 0)

    def join_other(j, carry):
        join(block_rows(j, 1 - core))
        return carry

    lax.fori_loop(0, blocks, join_other, 0)

    def both(ref, j):
        return jnp.concatenate([ref[block_rows(j, core), :], ref[block_rows(j, 1 - core), :]], axis=0)

    def store_both(ref, j, values):
        ref[block_rows(j, core), :] = values[:128]
        ref[block_rows(j, 1 - core), :] = values[128:]

    own_half = pl.ds(pl.multiple_of(side * half_width, 128), half_width)
    other_half = pl.ds(pl.multiple_of((1 - side) * half_width, 128), half_width)

    def forward(j):
        x_copy(j).wait_recv()
        relay_copy(j).start()
        relay_copy(j).wait_recv()
        attention = dot(both(cat, j), wout[own_half, :]) + dot(both(xcat, j), wout[other_half, :])
        middle = both(tok, j).astype(F32) + attention
        mid_out[own_rows(j), :] = middle[:128]
        normed, _ = norm_parts(middle)
        second = (normed * gain[...][None] + bias[...][None]).astype(BF16)
        store_both(sn, j, second)
        hidden = dot(second, wexp[...])
        value, rise = gelu_parts(hidden)
        value = value.astype(BF16)
        store_both(act, j, value)
        if pair:

            @pl.when(j == 0)
            def _():
                for copy in shard_copies:
                    copy.wait_recv()

        grad = (dot(both(cot, j), wshr[...]) * rise).astype(BF16)
        store_both(hg, j, grad)
        part = dot_nt(grad, wexp[...])
        sp_own[j] = part[:128]
        sp_send[j] = part[128:].astype(BF16)
        sp_copy(j).start()
        part = dot_nt(value, wshr[...])
        hp_own[j] = part[:128]
        hp_send[j] = part[128:].astype(BF16)
        hp_copy(j).start()

    def chip_sum(j):
        sp_copy(j).wait_recv()
        total = sp_own[j] + sp_recv[j].astype(F32)
        sx_send[j] = total.astype(BF16)
        sx_copy(j).start()
        hp_copy(j).wait_recv()
        hsum_out[own_rows(j), :] = (hp_own[j] + hp_recv[j].astype(F32)).astype(BF16)

    def norm_grad(j):
        sx_copy(j).wait_recv()
        second_grad = sx_send[j].astype(F32) + sx_recv[j].astype(F32)
        normed, spread_two = norm_parts(mid_out[own_rows(j), :])
        inner, gain_part, bias_part = norm_back(second_grad, normed, spread_two, gain[...][None])
        gains_out[0:1, :] += gain_part[None]
        gains_out[1:2, :] += bias_part[None]
        middle_grad = cot[block_rows(j, core), :].astype(F32) + inner
        mgrad_out[own_rows(j), :] = middle_grad
        branch[block_rows(j, core), :] = middle_grad.astype(BF16)
        branch_copy(j).start()

    def attended_grad(j):
        branch_copy(j).wait_recv()
        for which in range(2):
            at = block_rows(j, which)
            agrad_out[at, :] = dot_nt(branch[at, :], wout_own[...]).astype(BF16)

    def when_block(j, work):
        @pl.when((j >= 0) & (j < blocks))
        def _():
            work(j)

    def ticks(first, last):
        def tick(t, carry):
            when_block(t - 1, chip_sum)
            when_block(t, forward)
            when_block(t - 2, norm_grad)
            when_block(t - 3, attended_grad)
            return carry

        lax.fori_loop(first, last, tick, 0)

    half = model // 2
    part_rows = half if pair else model

    def weight_grad(left, right, which):
        return dot_tn(left[:, aligned(which * half, part_rows)], right[...]).astype(BF16)

    if pair:
        give_copy = remote(give, given, gsend, grecv, {"dp": 1 - dp})
        keep_out, give_out = grad_outs[0], grad_outs[1]
    ticks(0, blocks)
    if pair:
        give[...] = weight_grad(cot, act, 1 - dp)
        give_copy.start()
    ticks(blocks, blocks + 1)
    if pair:
        give_out[...] = weight_grad(sn, hg, 1 - dp)
    else:
        grad_outs[0][:, :units] = weight_grad(sn, hg, 0)
    ticks(blocks + 1, blocks + 2)
    if pair:
        keep_out[...] = weight_grad(sn, hg, dp)
        kept[...] = weight_grad(cot, act, dp)
    else:
        grad_outs[0][:, units:] = weight_grad(cot, act, 0)
    ticks(blocks + 2, blocks + 3)
    wo_out[...] = dot_tn(att[...], branch[...]).astype(BF16)

    def drain(j, carry):
        x_copy(j).wait_send()
        relay_copy(j).wait_send()
        sp_copy(j).wait_send()
        hp_copy(j).wait_send()
        sx_copy(j).wait_send()
        branch_copy(j).wait_send()
        return carry

    lax.fori_loop(0, blocks, drain, 0)
    att_copy.wait_send()
    if pair:
        for copy in shard_copies:
            copy.wait_send()
        give_copy.wait()
        parts, me = lax.axis_size("dm"), lax.axis_index("dm")
        shard = half // parts
        for step in range(parts):
            quarter = pl.ds(pl.multiple_of(lax.rem(me + step, parts) * shard, 32), shard)
            grad_outs[2 + step][...] = kept[quarter, :] + given[quarter, :]


def middle(pair, tokens, cotangent, attended, wout_own, wout, wexp, gain, bias, shards, shr_peer):
    rows, model = tokens.shape
    width = attended.shape[1]
    units = wexp.shape[1]
    part_rows = model // 2 if pair else model
    spare = (part_rows, units) if pair else (16, 128)
    parts = lax.axis_size("dm")
    if pair:
        grads = [(part_rows, units)] * 2 + [(part_rows // parts, units)] * parts
    else:
        grads = [(model, 2 * units)]
    blocks = rows // 256
    shape = jax.ShapeDtypeStruct
    dma = pltpu.SemaphoreType.DMA
    low = pltpu.VMEM((blocks, 128, model), BF16)
    full = pltpu.VMEM((blocks, 128, model), F32)
    return pl.pallas_call(
        functools.partial(middle_kernel, pair, parts),
        out_shape=(
            shape((rows // 2, model), F32),
            shape((rows // 2, model), F32),
            shape((rows, width), BF16),
            shape((rows // 2, model), BF16),
            shape((width, model), BF16),
            shape((8, model), F32),
        )
        + tuple(shape(dims, BF16) for dims in grads),
        in_specs=vmem(13),
        out_specs=tuple(vmem(6 + len(grads))),
        scratch_shapes=[
            pltpu.VMEM((model, units) if pair else (16, 128), BF16),
            pltpu.VMEM((rows, width), BF16),
            pltpu.VMEM((rows, 2 * width), BF16),
            pltpu.VMEM((rows, 2 * width), BF16),
            pltpu.VMEM((rows, model), BF16),
            pltpu.VMEM((rows, units), BF16),
            pltpu.VMEM((rows, units), BF16),
            full, low, low, full, low, low, low, low,
            pltpu.VMEM((rows, model), BF16),
            pltpu.VMEM(spare, BF16),
            pltpu.VMEM(spare, BF16),
            pltpu.VMEM(spare, BF16),
            dma, dma,
        ]
        + [dma((blocks,))] * 12
        + [dma, dma, dma((4,)), dma((4,))],
        compiler_params=pltpu.CompilerParams(
            vmem_limit_bytes=60 << 20, collective_id=2, has_side_effects=True
        ),
        name="middle",
    )(tokens, cotangent, attended, wout_own, wout, wexp, gain, bias, *shards, shr_peer)


def tail_kernel(
    pair, lengths, dkv, dkvt, dq, summed, k, v, centre, topk, tm, merged, rows_in, counts, ccol, weight,
    fn, sfn, tok, gain, mgrad, srow, mid, hsum, hsum_x, second_gains,
    ex_keep, ex_given, sh_own, sh_one, sh_two, sh_three,
    result_out, tokens_out, qkv_out, gain_a, gain_b, gain_c, gain_d, expand_out, shrink_out,
    sbuf, cbuf, fgm, to_core, from_core, to_x, from_x, to_right, to_left, from_left,
    from_right, from_fin, pq, pkv, dense, dense_to_core, dense_from_core, dense_to_x, dense_from_x,
    dense_own, first, sfn_tile, grad_all, grad_from_y, grad_back, g_own, g_right, g_left, g_from_left,
    g_from_right, gain_sum, gain_core, gain_dm, gain_dp, gain_x, expand_send, expand_recv, tile_sem, mid_sem, hsum_sem,
    ssend, srecv, csend, crecv,
    send_core, recv_core, send_x, recv_x, send_right, recv_left, send_left, recv_right, send_fin,
    recv_fin,
    dsend_core, drecv_core, dsend_x, drecv_x, fsend, frecv, tsend, trecv, osend, orecv,
    ysend, yrecv, gsend_right, grecv_left, gsend_left, grecv_right, asend, arecv,
    gcsend, gcrecv, gmsend, gmrecv, gpsend, gprecv, esend, erecv,
):
    gain_outs = (gain_a, gain_b, gain_c, gain_d)
    rows, width = k.shape
    model = tok.shape[1]
    heads = width // HEAD_DIM
    half_width = model // 2
    half_rows = rows // 2
    blocks = half_rows // 128
    parts = lax.axis_size("dm")
    me, hid, dp = lax.axis_index("dm"), lax.axis_index("hid"), lax.axis_index("dp")
    core, side = lax.rem(hid, 2), hid // 2
    core_peer = {"hid": hid + 1 - 2 * core}
    x_peer = {"hid": hid + 2 - 4 * side}
    y_peer = {"dp": 1 - dp}
    own_start = me * rows
    columns = aligned(side * half_width, half_width)
    other_columns = aligned((1 - side) * half_width, half_width)

    greeted = [{"dm": lax.rem(me + step, parts)} for step in range(1, parts)]
    greeted += [core_peer, x_peer] + ([y_peer] if pair else [])
    barrier = greet(greeted)

    wide = iota((CLP, 256), 1)
    packed = jnp.concatenate([summed[:, width:], jnp.zeros((CLP, 256 - width), F32)], axis=1)
    for h in range(heads):
        packed = jnp.where(wide == width + h, summed[:, h * HEAD_DIM : h * HEAD_DIM + 1], packed)
    sbuf[me] = packed.astype(BF16)
    dense_own[...] = jnp.zeros_like(dense_own)
    mid_copy = pltpu.make_async_copy(mid, dense, mid_sem)
    mid_copy.start()
    hsum_copy = pltpu.make_async_copy(hsum, dense_to_core, hsum_sem)
    hsum_copy.start()

    @pl.when(me == 0)
    def _():
        from_left[...] = jnp.zeros_like(from_left)
        g_from_left[...] = jnp.zeros_like(g_from_left)

    @pl.when(me == parts - 1)
    def _():
        from_right[...] = jnp.zeros_like(from_right)

    pl.semaphore_wait(barrier, len(greeted))
    sum_copies = small_exchange(sbuf, ssend, srecv, me, parts)
    for copy in sum_copies:
        copy.start()

    def chunk_rows(i, which):
        return aligned(which * HALF + i * CHUNK, CHUNK)

    def block_rows(j, which):
        return aligned(which * half_rows + j * 128, 128)

    def own_rows(j):
        return aligned(j * 128, 128)

    def core_copy(i):
        return remote(to_core.at[i], from_core.at[i], send_core.at[i], recv_core.at[i], core_peer)

    def x_copy(i):
        return remote(to_x.at[i], from_x.at[i], send_x.at[i], recv_x.at[i], x_peer)

    right = {"dm": lax.rem(me + 1, parts)}
    left = {"dm": lax.rem(me + parts - 1, parts)}

    def right_copy(i):
        return remote(to_right.at[i], from_left.at[i], send_right.at[i], recv_left.at[i], right)

    def left_copy(i):
        return remote(to_left.at[i], from_right.at[i], send_left.at[i], recv_right.at[i], left)

    def fin_copy(i):
        return remote(from_x.at[i], from_fin.at[i], send_fin.at[i], recv_fin.at[i], core_peer)

    def dense_core_copy(j):
        return remote(
            dense_to_core.at[j], dense_from_core.at[j], dsend_core.at[j], drecv_core.at[j], core_peer
        )

    def dense_x_copy(j):
        return remote(dense_to_x.at[j], dense_from_x.at[j], dsend_x.at[j], drecv_x.at[j], x_peer)

    def first_copy(j):
        block = first.at[j, :, columns]
        return remote(block, block, fsend.at[j], frecv.at[j], x_peer)

    def tokens_copy(j):
        block = tokens_out.at[block_rows(j, core), :]
        return remote(block, block, tsend.at[j], trecv.at[j], core_peer)

    def result_copy(j):
        block = result_out.at[block_rows(j, core), :]
        return remote(block, block, osend.at[j], orecv.at[j], core_peer)

    def spread_back(start, count):
        other = dot(dkv[aligned((1 - core) * HALF + start * CHUNK, count * CHUNK), :], weight[width:, :])
        other = other.astype(BF16)
        for i in range(count):
            to_core[start + i] = other[i * CHUNK : (i + 1) * CHUNK]
            core_copy(start + i).start()
        mine = dot(dkv[aligned(core * HALF + start * CHUNK, count * CHUNK), :], weight[width:, :])
        mine = mine.astype(BF16)
        for i in range(count):
            fgm[start + i] = mine[i * CHUNK : (i + 1) * CHUNK]

    def chip_sum(i):
        core_copy(i).wait_recv()
        to_x[i] = fgm[i, :, other_columns] + from_core[i, :, other_columns]
        x_copy(i).start()

    def hid_sum(i):
        x_copy(i).wait_recv()
        fgm[i, :, columns] = (
            fgm[i, :, columns].astype(F32)
            + from_core[i, :, columns].astype(F32)
            + from_x[i].astype(F32)
        ).astype(BF16)

    def go_right(i):
        @pl.when(me > 0)
        def _():
            right_copy(i).wait_recv()

        @pl.when(me < parts - 1)
        def _():
            to_right[i] = fgm[i, :, columns] + from_left[i]
            right_copy(i).start()

    def go_left(i):
        @pl.when(me < parts - 1)
        def _():
            left_copy(i).wait_recv()

        @pl.when(me > 0)
        def _():
            to_left[i] = fgm[i, :, columns] + from_right[i]
            left_copy(i).start()

    def finish(i):
        from_x[i] = (
            fgm[i, :, columns].astype(F32) + from_left[i].astype(F32) + from_right[i].astype(F32)
        ).astype(BF16)
        fin_copy(i).start()

    def scatter(i):
        fin_copy(i).wait_recv()
        here = iota((half_rows, CHUNK), 0) + own_start + core * half_rows
        chosen = [
            (srow[:, chunk_rows(i, which)] == here).astype(BF16) for which in (core, 1 - core)
        ]
        picked = jnp.concatenate([from_x[i], from_fin[i]], axis=0)
        dense_own[...] += dot(jnp.concatenate(chosen, axis=1), picked)

    far = jnp.maximum(me, parts - 1 - me)

    def ticks(start, last):
        def tick(t, carry):
            ready = t
            when_in(ready, CHUNKS, hid_sum)
            when_in(ready - LAG * me, CHUNKS, go_right)
            when_in(ready - LAG * (parts - 1 - me), CHUNKS, go_left)
            when_in(ready - LAG * far, CHUNKS, finish)
            when_in(ready - LAG * far - 1, CHUNKS, scatter)
            return carry

        lax.fori_loop(start, last, tick, 0)

    if pair:
        shard = expand_out.shape[0]

        def shard_rows(m):
            return pl.ds(pl.multiple_of(m * shard, 32), shard)

        expand_copies = []
        for step in range(1, parts):
            target = lax.rem(me + step, parts)
            expand_send[step] = ex_keep[shard_rows(target), :] + ex_given[shard_rows(target), :]
            expand_copies.append(
                remote(
                    expand_send.at[step], expand_recv.at[step], esend.at[step], erecv.at[step],
                    {"dm": target},
                )
            )
        for copy in expand_copies:
            copy.start()

    def chip_sums(first, last):
        def one(i, carry):
            chip_sum(i)
            return carry

        lax.fori_loop(first, last, one, 0)

    spread_back(0, 3)
    chip_sums(0, 3)
    spread_back(3, 5)
    chip_sums(3, 8)
    spread_back(8, CHUNKS - 8)
    chip_sums(8, CHUNKS)

    def result_rows(j, carry):
        total = dense_to_core[j].astype(F32) + hsum_x[j].astype(F32)
        result_out[block_rows(j, core), :] = (dense[j] + total).astype(BF16)
        result_copy(j).start()
        return carry

    for copy in sum_copies:
        copy.wait_recv()
    total = sbuf[0].astype(F32)
    for d in range(1, parts):
        total += sbuf[d].astype(F32)
    same = sequence_masks(lengths, topk, rows)
    rest_grad = total[:, :width].astype(BF16)
    product = rest_grad.astype(F32) * rows_in[:, width:]
    score_grads, weights = [], []
    centre_part = jnp.zeros((CLP, width), F32)
    for h in range(heads):
        lanes = head_lanes(width, h)
        top = tm[...].astype(F32)
        zero = jnp.zeros((CLP, width), BF16)
        full = dot_nt(jnp.where(lanes, centre[...], zero), k[...]) * SCALE
        against = dot_nt(jnp.where(lanes, rest_grad, zero), v[...])
        largest, denominator = merged[:, h : h + 1], merged[:, 8 + h : 9 + h]
        mass = merged[:, 16 + h : 17 + h]
        mass_grad = total[:, width + h : width + h + 1]
        probs = jnp.where(same, jnp.exp(full - largest) / denominator, 0.0)
        mean = mass * mass_grad + jnp.sum(jnp.where(lanes, product, 0.0), 1, keepdims=True)
        grad = jnp.where(top > 0.5, mass_grad, against)
        score_grad = (probs * (grad - mean)).astype(BF16)
        centre_part = jnp.where(lanes, dot(score_grad, k[...]), centre_part)
        score_grads.append(score_grad)
        weights.append(jnp.where(top > 0.5, 0.0, probs).astype(BF16))
    cbuf[me] = (centre_part * SCALE).astype(BF16)
    centre_copies = small_exchange(cbuf, csend, crecv, me, parts)
    for copy in centre_copies:
        copy.start()
    score_grad = jnp.concatenate(score_grads, axis=0)
    rest_weight = jnp.concatenate(weights, axis=0)
    pkv[...] = jnp.concatenate(
        [
            (dot_tn(score_grad, block_diagonal(centre[...], heads)) * SCALE).astype(BF16),
            dot_tn(rest_weight, block_diagonal(rest_grad, heads)).astype(BF16),
        ],
        axis=1,
    )
    if pair:
        part = width // 2

        def y_rows(b, d):
            return pl.ds(pl.multiple_of((d * 3 + b) * part, 32), part)

        def y_copy(b):
            return remote(
                grad_all.at[y_rows(b, 1 - dp), :], grad_from_y.at[b], ysend.at[b], yrecv.at[b], y_peer
            )

        def y_back(b):
            return remote(
                grad_all.at[y_rows(b, dp), :], grad_back.at[b], asend.at[b], arecv.at[b], y_peer
            )

        def unit_right(u):
            return remote(g_right.at[u], g_from_left.at[u], gsend_right.at[u], grecv_left.at[u], right)

        def unit_left(u):
            return remote(g_left.at[u], g_from_right.at[u], gsend_left.at[u], grecv_right.at[u], left)

        def y_sum(b):
            y_copy(b).wait_recv()
            both = grad_all[y_rows(b, dp), :] + grad_from_y[b]
            g_own[2 * b] = both[:, :half_width]
            g_own[2 * b + 1] = both[:, half_width:]

        def unit_go_right(u):
            @pl.when(me > 0)
            def _():
                unit_right(u).wait_recv()

            @pl.when(me < parts - 1)
            def _():
                g_right[u] = g_own[u] + g_from_left[u]
                unit_right(u).start()

            @pl.when(me == parts - 1)
            def _():
                g_from_right[u] = g_own[u] + g_from_left[u]

        def unit_go_left(u):
            @pl.when(me < parts - 1)
            def _():
                unit_left(u).wait_recv()

            @pl.when(me > 0)
            def _():
                g_left[u] = g_from_right[u]
                unit_left(u).start()

        def y_return(b):
            grad_all[y_rows(b, dp), :half_width] = g_from_right[2 * b]
            grad_all[y_rows(b, dp), half_width:] = g_from_right[2 * b + 1]
            y_back(b).start()

        def gticks(start, last):
            def tick(t, carry):
                @pl.when(lax.rem(t, 2) == 0)
                def _():
                    when_in(t // 2, 3, y_sum)

                when_in(t - 1 - LAG * me, UNITS, unit_go_right)
                back = t - 1 - LAG * (parts - 1) - LAG * (parts - 1 - me)
                when_in(back, UNITS, unit_go_left)

                @pl.when((back >= 0) & (lax.rem(back + 1, 2) == 0))
                def _():
                    when_in((back - 1) // 2, 3, y_return)

                return carry

            lax.fori_loop(start, last, tick, 0)
    else:

        def gticks(start, last):
            pass

    def slot_tile(c, carry):
        cut = aligned(c * 256, 256)
        fetch = pltpu.make_async_copy(sfn.at[:, cut], sfn_tile, tile_sem)
        fetch.start()
        grad = dot_tn(pkv[...], fn[:, cut])
        fetch.wait()
        grad = (grad + dot(dkvt[...], sfn_tile[...])).astype(BF16)
        grad_all[:width, cut] = grad[:width]
        grad_all[3 * (width // 2) : 3 * (width // 2) + width, cut] = grad[width:]
        return carry

    ticks(0, 1)
    lax.fori_loop(0, model // 256, slot_tile, 0)
    if pair:
        y_copy(0).start()
        y_copy(1).start()
    ticks(1, 2)
    mid_copy.wait()
    hsum_copy.wait()
    lax.fori_loop(0, blocks, result_rows, 0)
    ticks(2, 4)
    for copy in centre_copies:
        copy.wait_recv()
    centre_grad = cbuf[0].astype(F32)
    for d in range(1, parts):
        centre_grad += cbuf[d].astype(F32)
    centre_grad = centre_grad / counts[:, :1]
    high = centre_grad.astype(BF16)
    low = (centre_grad - high.astype(F32)).astype(BF16)

    def queries(i, carry):
        at = aligned(i * 256, 256)
        member = (ccol[at, :] == iota((256, 128), 1)).astype(BF16)
        pq[at, :] = (dq[at, :].astype(F32) + dot(member, high) + dot(member, low)).astype(BF16)
        return carry

    lax.fori_loop(0, rows // 256, queries, 0)
    query_grad = dot_tn(pq[...], fn[...]).astype(BF16)
    grad_all[width : width + width // 2, :] = query_grad[: width // 2]
    grad_all[5 * (width // 2) :, :] = query_grad[width // 2 :]
    if pair:
        y_copy(2).start()
    ticks(4, 5)

    def dense_rows(which):
        at = aligned(which * half_rows, half_rows)
        return dot(pq[at, :], weight[:width, :]) + dot(pkv[at, :], weight[width:, :])

    other_dense = dense_rows(1 - core).astype(BF16)
    for j in range(blocks):
        dense_to_core[j] = other_dense[j * 128 : (j + 1) * 128]
        dense_core_copy(j).start()
    own_dense = dense_rows(core)
    for j in range(blocks):
        dense[j] = own_dense[j * 128 : (j + 1) * 128]
    ticks(5, 6)

    def dense_chip(j, carry):
        dense_core_copy(j).wait_recv()
        dense_to_x[j] = (
            dense[j, :, other_columns] + dense_from_core[j, :, other_columns].astype(F32)
        ).astype(BF16)
        dense_x_copy(j).start()
        return carry

    def dense_hid(j, carry):
        dense_x_copy(j).wait_recv()
        dense_own[own_rows(j), :] += (
            dense[j, :, columns]
            + dense_from_core[j, :, columns].astype(F32)
            + dense_from_x[j].astype(F32)
        )
        return carry

    lax.fori_loop(0, blocks, dense_chip, 0)
    last = CHUNKS + LAG * (parts - 1) + 1

    def joint(t, carry):
        ticks(t, t + 1)
        gticks(t - 6, t - 5)
        return carry

    lax.fori_loop(6, last, joint, 0)
    done = last - 6
    lax.fori_loop(0, blocks, dense_hid, 0)
    mgrad_copy = pltpu.make_async_copy(mgrad, dense, mid_sem)
    mgrad_copy.start()

    gain_sum[...] = jnp.zeros_like(gain_sum)

    def first_send(j, carry):
        grad = dense_own[own_rows(j), :].astype(BF16)
        first[j, :, columns] = grad
        first_copy(j).start()
        return carry

    lax.fori_loop(0, blocks, first_send, 0)

    def first_gains(j, carry):
        centred = tok[block_rows(j, core), :].astype(F32)
        mean = jnp.mean(centred, -1, keepdims=True)
        variance = jnp.mean(jnp.square(centred - mean), -1, keepdims=True)
        normed = (tok[block_rows(j, core), columns].astype(F32) - mean) * lax.rsqrt(
            variance + EPSILON
        )
        grad = first[j, :, columns].astype(F32)
        gain_sum[0:1, columns] += jnp.sum(grad * normed, 0, keepdims=True)
        gain_sum[1:2, columns] += jnp.sum(grad, 0, keepdims=True)
        return carry

    lax.fori_loop(0, blocks, first_gains, 0)
    gain_sum[2:4, columns] = second_gains[0:2, columns]
    if pair:
        core_gain = remote(gain_sum, gain_core, gcsend, gcrecv, core_peer)
        core_gain.start()
    gticks(done, done + 2)

    def first_back(j, carry):
        first_copy(j).wait_recv()
        at = block_rows(j, core)
        normed, spread = norm_parts(tok[at, :].astype(F32))
        inner, _, _ = norm_back(first[j].astype(F32), normed, spread, gain[...][None])
        tokens_out[at, :] = (dense[j] + inner).astype(BF16)
        tokens_copy(j).start()
        return carry

    mgrad_copy.wait()
    if pair:
        core_gain.wait_recv()
        gain_dm[me] = gain_sum[...] + gain_core[...]
        dm_gains = small_exchange(gain_dm, gmsend, gmrecv, me, parts)
        for copy in dm_gains:
            copy.start()
    lax.fori_loop(0, 1, first_back, 0)
    gticks(done + 2, done + 4)
    lax.fori_loop(1, 2, first_back, 0)
    if pair:
        for copy in dm_gains:
            copy.wait_recv()
        line = gain_dm[0]
        for d in range(1, parts):
            line = line + gain_dm[d]
        gain_dp[0] = line
        dp_gain = remote(gain_dp.at[0], gain_dp.at[1], gpsend.at[0], gprecv.at[0], y_peer)
        dp_gain.start()
    lax.fori_loop(2, 4, first_back, 0)
    if pair:
        dp_gain.wait()
        gain_x[0] = gain_dp[0] + gain_dp[1]
        x_gain = remote(gain_x.at[0], gain_x.at[1], gpsend.at[1], gprecv.at[1], x_peer)
        x_gain.start()
    lax.fori_loop(4, blocks, first_back, 0)
    if pair:
        gticks(done + 4, 1 + LAG * 2 * (parts - 1) + UNITS)
        for b in range(3):
            y_copy(b).wait_send()
            y_back(b).wait_recv()
            grad_all[y_rows(b, 1 - dp), :] = grad_back[b]
    small = width // 2
    qkv_out[0, :small] = grad_all[width : width + small, :]
    qkv_out[0, small:] = grad_all[5 * small :, :]
    qkv_out[1] = grad_all[:width, :]
    qkv_out[2] = grad_all[3 * small : 5 * small, :]
    if pair:
        grad = ex_keep[shard_rows(me), :].astype(F32) + ex_given[shard_rows(me), :].astype(F32)
        for step in range(1, parts):
            expand_copies[step - 1].wait()
            grad = grad + expand_recv[step].astype(F32)
        expand_out[...] = grad
        grad = sh_own[...].astype(F32)
        for block in (sh_one, sh_two, sh_three):
            grad = grad + block[...].astype(F32)
        shrink_out[...] = grad
        x_gain.wait()
        total = gain_x[0] + gain_x[1]
        core_gain.wait_send()
        for copy in dm_gains:
            copy.wait_send()
    else:
        total = gain_sum[...]
    for i, out in enumerate(gain_outs):
        out[...] = total[i]
    if pair:
        for b in range(3):
            y_back(b).wait_send()

        def drain_units(u, carry):
            @pl.when(me < parts - 1)
            def _():
                unit_right(u).wait_send()

            @pl.when(me > 0)
            def _():
                unit_left(u).wait_send()

            return carry

        lax.fori_loop(0, UNITS, drain_units, 0)

    def drain_blocks(j, carry):
        dense_core_copy(j).wait_send()
        dense_x_copy(j).wait_send()
        first_copy(j).wait_send()
        result_copy(j).wait()
        tokens_copy(j).wait()
        return carry

    def drain(i, carry):
        @pl.when(me < parts - 1)
        def _():
            right_copy(i).wait_send()

        @pl.when(me > 0)
        def _():
            left_copy(i).wait_send()

        core_copy(i).wait_send()
        x_copy(i).wait_send()
        fin_copy(i).wait_send()
        return carry

    lax.fori_loop(0, CHUNKS, drain, 0)
    for copy in sum_copies + centre_copies:
        copy.wait_send()
    lax.fori_loop(0, blocks, drain_blocks, 0)


def tail(
    pair, lengths, dkv, dkvt, dq, summed, k, v, centre, topk, tm, merged, rows_in, counts, clusters,
    weight, fn, sfn, tokens, gain, mgrad, srow, mid, hsum, hsum_x, second_gains,
    ex_keep, ex_given, sh_parts, parts,
):
    rows, width = k.shape
    model = tokens.shape[1]
    shape = jax.ShapeDtypeStruct
    dma = pltpu.SemaphoreType.DMA
    blocks = rows // 256
    chain = pltpu.VMEM((CHUNKS, CHUNK, model // 2), BF16)
    whole = pltpu.VMEM((CHUNKS, CHUNK, model), BF16)
    unit = pltpu.VMEM((UNITS, width // 2, model // 2) if pair else (UNITS, 16, 128), BF16)
    return pl.pallas_call(
        functools.partial(tail_kernel, pair),
        out_shape=(
            shape((rows, model), BF16),
            shape((rows, model), BF16),
            shape((3, width, model), BF16),
            shape((model,), F32),
            shape((model,), F32),
            shape((model,), F32),
            shape((model,), F32),
            shape(sh_parts[0].shape, F32),
            shape(sh_parts[0].shape, F32),
        ),
        in_specs=[pl.BlockSpec(memory_space=pltpu.SMEM)]
        + vmem(15)
        + [pl.BlockSpec(memory_space=pl.ANY)]
        + vmem(2)
        + [pl.BlockSpec(memory_space=pl.ANY)]
        + vmem(1)
        + [pl.BlockSpec(memory_space=pl.ANY)] * 2
        + vmem(8),
        out_specs=tuple(vmem(9)),
        scratch_shapes=[
            pltpu.VMEM((parts, CLP, 256), BF16),
            pltpu.VMEM((parts, CLP, width), BF16),
            whole, whole, whole,
            chain, chain, chain, chain, chain, chain,
            chain,
            pltpu.VMEM((rows, width), BF16),
            pltpu.VMEM((rows, 2 * width), BF16),
            pltpu.VMEM((blocks, 128, model), F32),
            pltpu.VMEM((blocks, 128, model), BF16),
            pltpu.VMEM((blocks, 128, model), BF16),
            pltpu.VMEM((blocks, 128, model // 2), BF16),
            pltpu.VMEM((blocks, 128, model // 2), BF16),
            pltpu.VMEM((rows // 2, model // 2), F32),
            pltpu.VMEM((blocks, 128, model), BF16),
            pltpu.VMEM((SLOTS, 256), BF16),
            pltpu.VMEM((3 * width, model), BF16),
            pltpu.VMEM((3, width // 2, model), BF16),
            pltpu.VMEM((3, width // 2, model), BF16),
            unit, unit, unit, unit, unit,
            pltpu.VMEM((8, model), F32),
            pltpu.VMEM((8, model), F32),
            pltpu.VMEM((parts, 8, model), F32),
            pltpu.VMEM((2, 8, model), F32),
            pltpu.VMEM((2, 8, model), F32),
            pltpu.VMEM((parts,) + sh_parts[0].shape, BF16),
            pltpu.VMEM((parts,) + sh_parts[0].shape, BF16),
            dma, dma, dma,
        ]
        + [dma((parts,))] * 4
        + [dma((CHUNKS,))] * 10
        + [dma((blocks,))] * 10
        + [dma((3,))] * 2
        + [dma((UNITS,))] * 4
        + [dma((3,))] * 2
        + [dma, dma, dma((parts,)), dma((parts,)), dma((2,)), dma((2,)), dma((parts,)), dma((parts,))],
        compiler_params=pltpu.CompilerParams(
            vmem_limit_bytes=58 << 20, collective_id=1, has_side_effects=True
        ),
        name="tail",
    )(
        lengths, dkv, dkvt, dq, summed, k, v, centre, topk, tm, merged, rows_in, counts,
        clusters.reshape(rows, 1), weight.reshape(3 * width, model), fn, sfn, tokens, gain,
        mgrad.reshape(blocks, 128, model), srow, mid.reshape(blocks, 128, model),
        hsum.reshape(blocks, 128, model), hsum_x.reshape(blocks, 128, model), second_gains,
        ex_keep, ex_given, *sh_parts,
    )


def shards(
    tokens,
    clusters,
    top_keys,
    lengths,
    qkv_weight,
    out_weight,
    first_gain,
    first_bias,
    second_gain,
    second_bias,
    expand_weight,
    shrink_weight,
    cotangent,
):
    parts, n_dp = lax.axis_size("dm"), lax.axis_size("dp")
    pair = n_dp == 2
    weight = jnp.swapaxes(qkv_weight, 1, 2)
    topk = jnp.pad(top_keys, ((0, CLP - CL), (0, 0)), constant_values=-1)
    flat = jnp.pad(top_keys.reshape(-1), (0, SLOTS - CL * TOPK), constant_values=-1)
    (
        first_normed, slot_normed, qs, k, v, ks, vs, kst, vst, starts, rcol, rrow, cls, centre, tm, rows_in,
        merged, counts, out_full, expand_full, shrink_peer,
    ) = front(
        pair, lengths, tokens, clusters, weight, first_gain, first_bias,
        flat.reshape(SLOTS, 1), topk, expand_weight, shrink_weight.T, out_weight, parts,
    )
    if pair:
        shrink_shards = [shrink_weight.T]
        source, _ = lax.optimization_barrier((shrink_weight.T, starts))
        for step in range(1, parts):
            shrink_shards.append(
                lax.ppermute(source, "dm", [(i, (i + step) % parts) for i in range(parts)])
            )
    else:
        expand_full = lax.all_gather(expand_weight, ("dp", "dm"), axis=0, tiled=True)
        shrink_full = lax.all_gather(shrink_weight.T, ("dp", "dm"), axis=0, tiled=True)
        shrink_shards = [shrink_full] + [jnp.zeros((16, 128), BF16)] * (parts - 1)
    attended = exact_forward(starts, qs, cls, kst, vs, rows_in, rcol)
    mid, middle_grad, attended_grad, hidden_sum, out_grad_part, second_parts, *grads = middle(
        pair, tokens, cotangent, attended, out_weight, out_full, expand_full,
        second_gain, second_bias, shrink_shards, shrink_peer,
    )
    out_grad = lax.psum(out_grad_part, ("dp", "dm"))
    hidden_sum_x = lax.ppermute(hidden_sum, "hid", [(i, i ^ 2) for i in range(lax.axis_size("hid"))])
    units = expand_weight.shape[1]
    if pair:
        expand_keep, expand_give, *shrink_parts = grads
        expand_given = lax.ppermute(expand_give, "dp", [(0, 1), (1, 0)])
        shrink_parts = [shrink_parts[0]] + [
            lax.ppermute(shrink_parts[step], "dm", [(i, (i + step) % parts) for i in range(parts)])
            for step in range(1, parts)
        ]
    else:
        summed_grads = lax.psum_scatter(grads[0], ("dp", "dm"), scatter_dimension=0, tiled=True)
        expand_keep = expand_given = jnp.zeros((16, 128), BF16)
        shrink_parts = [expand_keep] * parts
    dq, dkv, dkvt, summed = exact_backward(
        starts, qs, cls, ks, kst, vst, rows_in, rcol, rrow, attended_grad
    )
    result, tokens_grad, qkv_grad, *gains, expand_grad, shrink_grad = tail(
        pair, lengths, dkv, dkvt, dq, summed, k, v, centre, topk, tm, merged, rows_in, counts, clusters,
        weight, first_normed, slot_normed, tokens, first_gain, middle_grad,
        flat.reshape(1, SLOTS), mid, hidden_sum, hidden_sum_x, second_parts,
        expand_keep, expand_given, shrink_parts, parts,
    )
    out_grad, result = lax.optimization_barrier((out_grad, result))
    if not pair:
        qkv_grad = lax.psum(qkv_grad, ("dp", "dm"))
        gains = lax.psum(jnp.stack(gains), ("dp", "dm", "hid"))
        summed_grads = summed_grads.astype(F32)
        expand_grad, shrink_grad = summed_grads[:, :units], summed_grads[:, units:]
    return (
        result,
        tokens_grad,
        jnp.swapaxes(qkv_grad.astype(F32), 1, 2),
        out_grad.astype(F32),
        gains[0],
        gains[1],
        gains[2],
        gains[3],
        expand_grad,
        shrink_grad.T,
    )


def solution(mesh):
    in_specs = (
        P(("dp", "dm"), None),
        P(("dp", "dm")),
        P("dp", None),
        P("dp"),
        P(None, None, "hid"),
        P("hid", None),
        P(),
        P(),
        P(),
        P(),
        P(("dp", "dm"), "hid"),
        P("hid", ("dp", "dm")),
        P(("dp", "dm"), None),
    )
    out_specs = (
        P(("dp", "dm"), None),
        P(("dp", "dm"), None),
        P(None, None, "hid"),
        P("hid", None),
        P(),
        P(),
        P(),
        P(),
        P(("dp", "dm"), "hid"),
        P("hid", ("dp", "dm")),
    )
    return jax.shard_map(shards, mesh=mesh, in_specs=in_specs, out_specs=out_specs, check_vma=False)
```

```python
import functools

import jax
import jax.numpy as jnp
from jax import lax
from jax.experimental import pallas as pl
from jax.experimental.pallas import tpu as pltpu
from jax.sharding import PartitionSpec as P

HEAD_DIM = 64
CL = 100
TOPK = 32
CLP = 128
SLOTS = 3328
GROUP = 8
GSLOTS = GROUP * TOPK
GROUPS = SLOTS // GSLOTS
WIN = 160
HALF = SLOTS // 2
CHUNK = 128
CHUNKS = HALF // CHUNK
LAG = 2
CENTRE = 6
CENTRE_TICK = 13
UNITS = 6
EPSILON = 1e-05
NEGATIVE = -1e30
HIGHEST = lax.Precision.HIGHEST
F32 = jnp.float32
BF16 = jnp.bfloat16
MESH = pl.DeviceIdType.MESH
NT = (((1,), (1,)), ((), ()))
TN = (((0,), (0,)), ((), ()))
SCALE = HEAD_DIM ** (-0.5)


def dot(a, b):
    return jnp.dot(a, b, preferred_element_type=F32)


def dot_nt(a, b):
    return lax.dot_general(a, b, NT, preferred_element_type=F32)


def dot_tn(a, b):
    return lax.dot_general(a, b, TN, preferred_element_type=F32)


def iota(shape, dim):
    return lax.broadcasted_iota(jnp.int32, shape, dim)


def norm_parts(values):
    centred = values - jnp.mean(values, -1, keepdims=True)
    spread = lax.rsqrt(jnp.mean(centred * centred, -1, keepdims=True) + EPSILON)
    return (centred * spread, spread)


def norm_back(upstream, normed, spread, norm_gain):
    through = upstream * norm_gain
    inner = (
        through
        - jnp.mean(through, -1, keepdims=True)
        - normed * jnp.mean(through * normed, -1, keepdims=True)
    )
    return (spread * inner, jnp.sum(upstream * normed, 0), jnp.sum(upstream, 0))


def head_lanes(width, head):
    lane = iota((1, width), 1)
    return lane // HEAD_DIM == head


def block_diagonal(rows, heads):
    width = rows.shape[1]
    zero = jnp.zeros_like(rows)
    return jnp.concatenate(
        [jnp.where(head_lanes(width, h), rows, zero) for h in range(heads)], axis=0
    )


def block_diagonal_turned(turned, heads):
    zero = jnp.zeros((HEAD_DIM, turned.shape[1]), turned.dtype)
    columns = []
    for h in range(heads):
        mine = turned[h * HEAD_DIM : (h + 1) * HEAD_DIM]
        columns.append(jnp.concatenate([mine if i == h else zero for i in range(heads)], axis=0))
    return jnp.concatenate(columns, axis=1)


def diagonal_blocks_turned(full, heads):
    rows, size = full.shape[0] // heads, full.shape[1] // heads
    return jnp.concatenate(
        [full[h * rows : (h + 1) * rows, h * size : (h + 1) * size] for h in range(heads)], axis=0
    )


def diagonal_blocks(full, heads):
    rows, width = full.shape[0] // heads, full.shape[1]
    out = full[:rows]
    for h in range(1, heads):
        out = jnp.where(head_lanes(width, h), full[h * rows : (h + 1) * rows], out)
    return out


def vmem(n):
    return [pl.BlockSpec(memory_space=pltpu.VMEM)] * n


def remote(src, dst, send, recv, device):
    return pltpu.make_async_remote_copy(
        src_ref=src, dst_ref=dst, send_sem=send, recv_sem=recv, device_id=device,
        device_id_type=MESH,
    )


def greet(devices):
    barrier = pltpu.get_barrier_semaphore()
    for device in devices:
        pl.semaphore_signal(barrier, inc=1, device_id=device, device_id_type=MESH)
    return barrier


def small_exchange(buf, sends, recvs, me, parts):
    return [
        remote(
            buf.at[me], buf.at[me], sends.at[step], recvs.at[step],
            {"dm": lax.rem(me + step, parts)},
        )
        for step in range(1, parts)
    ]


def when_in(i, count, work):
    @pl.when((i >= 0) & (i < count))
    def _():
        work(i)


def aligned(start, size):
    return pl.ds(pl.multiple_of(start, 128), size)


def sequence_masks(lengths, topk, rows):
    own_start = lax.axis_index("dm") * rows
    key_second = iota((1, rows), 1) + own_start >= lengths[0]
    centre_second = topk[:, :1] >= lengths[0]
    return key_second == centre_second


def front_kernel(
    pair, lengths, tok, ccol, weight, gain, bias, scol, topk, wexp, wshr, wout,
    fn_hbm, sfn_hbm, qs_out, k_out, v_out, ks_out, vs_out, kst_out, vst_out, starts_out, rcol_out, rrow_out,
    cls_out, centre_out, tm_out, rows_out, merged_out, count_out, wall_out, wfull_out, shr_peer_out,
    fn_out, sfn_out, q_ref, member_ref, csum, rbuf, sbuf, own, to_right, to_left, from_left, from_right,
    rsend, rrecv, ssend, srecv,
    send_right, recv_left, send_left, recv_right, send_x, recv_x, send_core, recv_core,
    send_relay, recv_relay, osend, orecv, wsend, wsend_left, wrecv, ysend, yrecv, psend, precv, local_sems,
):
    rows, model = tok.shape
    width = weight.shape[1]
    heads = width // HEAD_DIM
    half_width = model // 2
    tiles = rows // 128
    parts = lax.axis_size("dm")
    me, hid, dp = lax.axis_index("dm"), lax.axis_index("hid"), lax.axis_index("dp")
    core, side = lax.rem(hid, 2), hid // 2
    core_peer = {"hid": hid + 1 - 2 * core}
    x_peer = {"hid": hid + 2 - 4 * side}
    lane = iota((128, 128), 1)
    columns = aligned(side * half_width, half_width)
    other_columns = aligned((1 - side) * half_width, half_width)
    own_start = me * rows

    greeted = [{"dm": lax.rem(me + step, parts)} for step in range(1, parts)]
    greeted += [core_peer, x_peer]
    if pair:
        greeted.append({"dp": 1 - dp})
    barrier = greet(greeted)

    out_rows = pl.ds(pl.multiple_of(hid * width, 64), width)
    out_own = pltpu.make_async_copy(wout, wall_out.at[out_rows, :], local_sems.at[0])
    out_own.start()
    out_x_rows = pl.ds(pl.multiple_of((hid + 2 - 4 * side) * width, 64), width)
    out_copies = [
        remote(wout, wall_out.at[out_rows, :], osend.at[0], orecv.at[0], core_peer),
        remote(wout, wall_out.at[out_rows, :], osend.at[1], orecv.at[1], x_peer),
        remote(
            wall_out.at[out_x_rows, :], wall_out.at[out_x_rows, :], osend.at[2], orecv.at[2], core_peer
        ),
    ]
    if pair:
        shard = wexp.shape[0]

        def shard_rows(d, m):
            return pl.ds(pl.multiple_of((d * parts + m) * shard, 32), shard)

        mine = shard_rows(dp, me)
        def whole_shard(origin):
            return wfull_out.at[shard_rows(dp, origin), :]

        def hop(origin, source, sends, neighbour):
            return remote(
                source, whole_shard(origin), sends.at[origin], wrecv.at[origin],
                {"dm": lax.rem(neighbour, parts)},
            )

        def across(origin, source):
            return remote(
                source, whole_shard(origin), ysend.at[origin], yrecv.at[origin], {"dp": 1 - dp}
            )

        def pass_on(step):
            @pl.when(me >= step)
            def _():
                origin = me - step
                block = whole_shard(origin)
                hop(origin, block, wsend, me + 1).wait_recv()
                across(origin, block).start()

                @pl.when(me < parts - 1)
                def _():
                    hop(origin, block, wsend, me + 1).start()

            @pl.when(me + step < parts)
            def _():
                origin = me + step
                block = whole_shard(origin)
                hop(origin, block, wsend_left, me + parts - 1).wait_recv()
                across(origin, block).start()

                @pl.when(me > 0)
                def _():
                    hop(origin, block, wsend_left, me + parts - 1).start()

        shard_own = pltpu.make_async_copy(wexp, wfull_out.at[mine, :], local_sems.at[1])
        shard_own.start()
        shrink_peer = remote(wshr, shr_peer_out, psend, precv, {"dp": 1 - dp})

    pl.semaphore_wait(barrier, len(greeted))
    if pair:
        across(me, wexp).start()
        shrink_peer.start()

        @pl.when(me < parts - 1)
        def _():
            hop(me, wexp, wsend, me + 1).start()

        @pl.when(me > 0)
        def _():
            hop(me, wexp, wsend_left, me + parts - 1).start()

    out_copies[0].start()
    out_copies[1].start()

    def first_norm(i, carry):
        at = aligned(i * 256, 256)
        normed, _ = norm_parts(tok[at, :].astype(F32))
        fn_out[at, :] = (normed * gain[...][None] + bias[...][None]).astype(BF16)
        return carry

    lax.fori_loop(0, rows // 256, first_norm, 0)
    fn_copy = pltpu.make_async_copy(fn_out, fn_hbm, local_sems.at[2])
    fn_copy.start()

    @pl.when(me == 0)
    def _():
        from_left[...] = jnp.zeros_like(from_left)

    @pl.when(me == parts - 1)
    def _():
        from_right[...] = jnp.zeros_like(from_right)

    def chunk_rows(i, which):
        return aligned(which * HALF + i * CHUNK, CHUNK)

    def right_copy(i):
        return remote(
            to_right.at[i], from_left.at[i], send_right.at[i], recv_left.at[i],
            {"dm": lax.rem(me + 1, parts)},
        )

    def left_copy(i):
        return remote(
            to_left.at[i], from_right.at[i], send_left.at[i], recv_right.at[i],
            {"dm": lax.rem(me + parts - 1, parts)},
        )

    def x_copy(i):
        block = sfn_out.at[chunk_rows(i, core), columns]
        return remote(block, block, send_x.at[i], recv_x.at[i], x_peer)

    def core_copy(i):
        block = sfn_out.at[chunk_rows(i, core), columns]
        return remote(block, block, send_core.at[i], recv_core.at[i], core_peer)

    def relay_copy(i):
        block = sfn_out.at[chunk_rows(i, core), other_columns]
        return remote(block, block, send_relay.at[i], recv_relay.at[i], core_peer)

    def make_own(first, count):
        at = aligned(core * HALF + first * CHUNK, count * CHUNK)
        chosen = (scol[at, :] == iota((count * CHUNK, rows), 1) + own_start).astype(BF16)
        picked = dot(chosen, fn_out[:, columns]).astype(BF16)
        for i in range(count):
            own[first + i + (first + i >= CENTRE)] = picked[i * CHUNK : (i + 1) * CHUNK]

    def go_right(i):
        @pl.when(me > 0)
        def _():
            right_copy(i).wait_recv()

        @pl.when(me < parts - 1)
        def _():
            to_right[i] = own[i] + from_left[i]
            right_copy(i).start()

    def go_left(i):
        @pl.when(me < parts - 1)
        def _():
            left_copy(i).wait_recv()

        @pl.when(me > 0)
        def _():
            to_left[i] = own[i] + from_right[i]
            left_copy(i).start()

    def slot_chunk(place):
        return jnp.where(place > CENTRE, place - 1, place)

    def finish(place):
        @pl.when(place == CENTRE)
        def _():
            total = own[place].astype(F32) + from_left[place].astype(F32)
            csum[...] = total + from_right[place].astype(F32)

        @pl.when(place != CENTRE)
        def _():
            i = slot_chunk(place)
            sfn_out[chunk_rows(i, core), columns] = (
                own[place] + from_left[place] + from_right[place]
            )
            x_copy(i).start()
            core_copy(i).start()

    def relay(place):
        @pl.when(place != CENTRE)
        def _():
            i = slot_chunk(place)
            x_copy(i).wait_recv()
            relay_copy(i).start()

    far = jnp.maximum(me, parts - 1 - me)

    def ticks(first, last):
        def tick(t, carry):
            when_in(t - LAG * me, CHUNKS + 1, go_right)
            when_in(t - LAG * (parts - 1 - me), CHUNKS + 1, go_left)
            when_in(t - LAG * far, CHUNKS + 1, finish)
            when_in(t - LAG * far - LAG, CHUNKS + 1, relay)
            return carry

        lax.fori_loop(first, last, tick, 0)

    def project(part):
        at = aligned(part * (rows // 2), rows // 2)
        first = fn_out[at, :]
        q_ref[at, :] = dot_nt(first, weight[0]).astype(BF16)
        k_out[at, :] = dot_nt(first, weight[1]).astype(BF16)
        v_out[at, :] = dot_nt(first, weight[2]).astype(BF16)

    lower = (iota((128, 128), 0) > iota((128, 128), 1)).astype(BF16)

    def count_tile(i, running):
        at = aligned(i * 128, 128)
        member = (ccol[at, :] == lane).astype(F32)
        low = member.astype(BF16)
        member_ref[at, :] = low
        earlier = dot(lower, low) + running
        rcol_out[at, :] = jnp.sum(member * earlier, 1, keepdims=True)
        return running + jnp.sum(member, 0, keepdims=True)

    def place(i, carry):
        at = aligned(i * 256, 256)
        rank_row = rrow_out[:1, :].astype(jnp.int32)
        chosen = (iota((256, rows), 0) + i * 256 == rank_row).astype(BF16)
        qs_out[at, :] = (dot(chosen, q_ref[...]) * SCALE).astype(BF16)
        sorted_member = dot(chosen, member_ref[...])
        cls_out[at, :] = jnp.sum(
            sorted_member * iota((256, 128), 1).astype(F32), 1, keepdims=True
        ).astype(jnp.int32)
        return carry

    make_own(0, 4)
    ticks(0, 1)
    project(0)
    ticks(1, 2)
    make_own(4, 4)
    ticks(2, 4)
    project(1)
    ticks(4, 5)
    if pair:
        pass_on(1)
    counts = lax.fori_loop(0, tiles, count_tile, jnp.zeros((1, 128), F32))
    extended = jnp.concatenate([q_ref[...], jnp.ones((rows, 256 - width), BF16)], axis=1)
    sums = dot_tn(member_ref[...], extended)
    digits = jnp.floor(sums * 0.03125)
    wide = iota((CLP, 256), 1)
    packed = jnp.where(
        wide == width, digits, jnp.where(wide == width + 1, sums - 32.0 * digits, sums)
    )
    own[CENTRE] = jnp.concatenate(
        [packed, jnp.zeros((CLP, half_width - 256), F32)], axis=1
    ).astype(BF16)
    ticks(5, 6)
    make_own(8, CHUNKS - 8)
    ticks(6, 7)
    before = (iota((128, 128), 0) < iota((128, 128), 1)).astype(F32)
    starts = jnp.dot(
        jnp.broadcast_to(counts, (8, 128)), before, precision=HIGHEST, preferred_element_type=F32
    )
    starts_out[...] = starts.astype(jnp.int32)

    def ranks(i, carry):
        at = aligned(i * 128, 128)
        member = member_ref[at, :].astype(F32)
        rank = rcol_out[at, :] + jnp.sum(member * starts[:1], 1, keepdims=True)
        rcol_out[at, :] = rank
        turned = jnp.transpose(jnp.broadcast_to(rank, (128, 128)))
        rrow_out[:, at] = turned[:8]
        return carry

    lax.fori_loop(0, tiles, ranks, 0)
    ticks(7, 8)
    if pair:
        pass_on(2)
    here = iota((CLP, rows), 1) + own_start
    hit = topk[:, :1] == here
    for t in range(1, TOPK):
        hit = hit | (topk[:, t : t + 1] == here)
    tm_out[...] = hit.astype(F32).astype(BF16)
    ticks(8, 9)

    lax.fori_loop(0, rows // 512, place, 0)
    ticks(9, 10)
    lax.fori_loop(rows // 512, rows // 256, place, 0)
    qs_out[rows:, :] = jnp.zeros((WIN, width), BF16)
    cls_out[rows:, :] = jnp.full((WIN, 1), -1, jnp.int32)
    ticks(10, CENTRE_TICK)
    gathered = csum[...]
    count = jnp.maximum(
        32.0 * gathered[:, width : width + 1] + gathered[:, width + 1 : width + 2], 1.0
    )
    count_out[...] = jnp.broadcast_to(count, (CLP, 128))
    centre = (gathered[:, :width] / count).astype(BF16)
    centre_out[...] = centre
    same = sequence_masks(lengths, topk, rows)
    stats = jnp.zeros((CLP, 128), F32)
    rest = jnp.zeros((CLP, width), F32)
    for h in range(heads):
        top = tm_out[...].astype(F32)
        mine_lanes = head_lanes(width, h)
        scores = dot_nt(jnp.where(mine_lanes, centre, jnp.zeros_like(centre)), k_out[...]) * SCALE
        scores = jnp.where(same, scores, NEGATIVE)
        largest = jnp.max(scores, 1, keepdims=True)
        raised = jnp.exp(scores - largest)
        total = jnp.sum(raised, 1, keepdims=True)
        within = raised * top
        mass = jnp.sum(within, 1, keepdims=True)
        rest = jnp.where(mine_lanes, dot((raised - within).astype(BF16), v_out[...]), rest)
        stats = jnp.where(lane == h, largest, stats)
        stats = jnp.where(lane == 8 + h, total, stats)
        stats = jnp.where(lane == 16 + h, mass, stats)
    rbuf[me] = rest.astype(BF16)
    sbuf[me] = jnp.transpose(stats)[:24]
    rest_copies = small_exchange(rbuf, rsend, rrecv, me, parts)
    stat_copies = small_exchange(sbuf, ssend, srecv, me, parts)
    ticks(CENTRE_TICK, CENTRE_TICK + 2)
    out_copies[1].wait_recv()
    out_copies[2].start()
    if pair:
        pass_on(3)
    ticks(CENTRE_TICK + 2, CENTRE_TICK + 3)
    early = CHUNKS // 2
    ticks(CENTRE_TICK + 3, 19)

    def arrive(i, carry):
        core_copy(i).wait_recv()
        relay_copy(i).wait_recv()
        return carry

    def project_slots(first, count):
        for which in range(2):
            at = pl.ds(which * HALF + first * CHUNK, count * CHUNK)
            block = sfn_out[at, :]
            for which_weight, out, turned in ((1, ks_out, kst_out), (2, vs_out, vst_out)):
                product = dot_nt(block, weight[which_weight])
                out[at, :] = product.astype(BF16)
                turned[:, at] = jnp.transpose(product).astype(BF16)

    lax.fori_loop(0, early, arrive, 0)
    project_slots(0, early)
    ticks(19, 20)
    for copy in rest_copies + stat_copies:
        copy.start()
    ticks(20, CHUNKS + 1 + LAG * parts)
    lax.fori_loop(early, CHUNKS, arrive, 0)
    sfn_copy = pltpu.make_async_copy(sfn_out, sfn_hbm, local_sems.at[3])
    sfn_copy.start()
    project_slots(early, CHUNKS - early)
    for copy in rest_copies + stat_copies:
        copy.wait_recv()
    largest = sbuf[0][:8]
    for d in range(1, parts):
        largest = jnp.maximum(largest, sbuf[d][:8])
    total = jnp.zeros((8, 128), F32)
    mass = jnp.zeros((8, 128), F32)
    factors = []
    for d in range(parts):
        factor = jnp.exp(sbuf[d][:8] - largest)
        total += factor * sbuf[d][8:16]
        mass += factor * sbuf[d][16:24]
        factors.append(factor)
    live = iota((8, 128), 0) < heads
    total = jnp.where(live, total, 1.0)
    mass = mass / total
    table = [largest, total, mass] + [factor / total for factor in factors]
    table.append(jnp.zeros((128 - 8 * len(table), 128), F32))
    columns_table = jnp.transpose(jnp.concatenate(table, axis=0))
    merged_out[...] = columns_table
    mass_rows = jnp.zeros((CLP, width), F32)
    rest_rows = jnp.zeros((CLP, width), F32)
    for h in range(heads):
        mine_lanes = head_lanes(width, h)
        mass_rows = jnp.where(mine_lanes, columns_table[:, 16 + h : 17 + h], mass_rows)
        rest = jnp.zeros((CLP, width), F32)
        for d in range(parts):
            lane_at = 24 + 8 * d + h
            rest += columns_table[:, lane_at : lane_at + 1] * rbuf[d].astype(F32)
        rest_rows = jnp.where(mine_lanes, rest, rest_rows)
    rows_out[:, :width] = mass_rows
    rows_out[:, width:] = rest_rows

    def drain(i, carry):
        @pl.when(me < parts - 1)
        def _():
            right_copy(i).wait_send()

        @pl.when(me > 0)
        def _():
            left_copy(i).wait_send()

        return carry

    def drain_slots(i, carry):
        x_copy(i).wait_send()
        core_copy(i).wait_send()
        relay_copy(i).wait_send()
        return carry

    lax.fori_loop(0, CHUNKS + 1, drain, 0)
    lax.fori_loop(0, CHUNKS, drain_slots, 0)
    for copy in rest_copies + stat_copies + out_copies:
        copy.wait_send()
    out_copies[0].wait_recv()
    out_copies[2].wait_recv()
    if pair:
        for origin in range(parts):
            across(origin, wexp).wait()

            @pl.when((me < parts - 1) & (origin <= me))
            def _():
                hop(origin, wexp, wsend, me + 1).wait_send()

            @pl.when((me > 0) & (origin >= me))
            def _():
                hop(origin, wexp, wsend_left, me + parts - 1).wait_send()

        shrink_peer.wait()
        shard_own.wait()
    out_own.wait()
    fn_copy.wait()
    sfn_copy.wait()


def front(pair, lengths, tokens, clusters, weight, gain, bias, scol, topk, wexp, wshr, wout, parts):
    rows, model = tokens.shape
    width = weight.shape[1]
    shape = jax.ShapeDtypeStruct
    dma = pltpu.SemaphoreType.DMA
    chain = pltpu.VMEM((CHUNKS + 1, CHUNK, model // 2), BF16)
    whole = (model, wexp.shape[1]) if pair else (16, 128)
    anywhere = [pl.BlockSpec(memory_space=pl.ANY)]
    return pl.pallas_call(
        functools.partial(front_kernel, pair),
        out_shape=(
            shape(tokens.shape, BF16),
            shape((SLOTS, model), BF16),
            shape((rows + WIN, width), BF16),
            shape((rows, width), BF16),
            shape((rows, width), BF16),
            shape((SLOTS, width), BF16),
            shape((SLOTS, width), BF16),
            shape((width, SLOTS), BF16),
            shape((width, SLOTS), BF16),
            shape((8, 128), jnp.int32),
            shape((rows, 1), F32),
            shape((8, rows), F32),
            shape((rows + WIN, 1), jnp.int32),
            shape((CLP, width), BF16),
            shape((CLP, rows), BF16),
            shape((CLP, 2 * width), F32),
            shape((CLP, 128), F32),
            shape((CLP, 128), F32),
            shape((lax.axis_size("hid") * width, model), BF16),
            shape(whole, BF16),
            shape(wshr.shape, BF16),
        ),
        in_specs=[pl.BlockSpec(memory_space=pltpu.SMEM)] + vmem(7) + anywhere * 3,
        out_specs=tuple(anywhere * 2 + vmem(16) + anywhere * 3),
        scratch_shapes=[
            pltpu.VMEM((rows, model), BF16),
            pltpu.VMEM((SLOTS, model), BF16),
            pltpu.VMEM((rows, width), BF16),
            pltpu.VMEM((rows, 128), BF16),
            pltpu.VMEM((CLP, model // 2), F32),
            pltpu.VMEM((parts, CLP, width), BF16),
            pltpu.VMEM((parts, 24, 128), F32),
            chain, chain, chain, chain, chain,
        ]
        + [dma((parts,))] * 4
        + [dma((CHUNKS + 1,))] * 10
        + [dma((3,))] * 2
        + [dma((parts,))] * 5
        + [dma, dma, dma((4,))],
        compiler_params=pltpu.CompilerParams(
            vmem_limit_bytes=56 << 20, collective_id=0, has_side_effects=True
        ),
        name="front",
    )(
        lengths, tokens, clusters.reshape(rows, 1), weight, gain, bias, scol, topk,
        wexp, wshr, wout,
    )


UNROLL = 4
FORWARD_UNROLL = (4, 2)
BACKWARD_UNROLL = (2, 2)
SMALL = 64


def list_windows(starts, rows, lists):
    big_group, big_row, small_group, small_row = lists

    def one_group(g, counts):
        big, small = counts
        first, last = starts[0, g * GROUP], starts[0, g * GROUP + GROUP]
        base = first // 16 * 16
        span = jnp.where(last > first, last - base, 0)
        short = (span > 0) & (span <= SMALL)
        windows = jnp.where(span > SMALL, (span + WIN - 1) // WIN, 0)

        def one(w, carry):
            big_group[big + w] = g
            big_row[big + w] = base + w * WIN
            return carry

        lax.fori_loop(0, windows, one, 0)
        small_group[small] = g
        small_row[small] = base
        return big + windows, small + jnp.where(short, 1, 0)

    big, small = lax.fori_loop(0, GROUPS, one_group, (0, 0))
    for i in range(UNROLL):
        big_group[big + i] = 0
        big_row[big + i] = rows
        small_group[small + i] = 0
        small_row[small + i] = rows
    return big, small


def each_window(starts, rows, lists, window, unroll):
    big, small = list_windows(starts, rows, lists)
    for count, size, group_at, row_at, times in (
        (big, WIN, lists[0], lists[1], unroll[0]),
        (small, SMALL, lists[2], lists[3], unroll[1]),
    ):

        def several(n, carry):
            for i in range(times):
                window(*window_at(starts, group_at, row_at, n * times + i, size))
            return carry

        lax.fori_loop(0, (count + times - 1) // times, several, 0)


def window_probs(scores, mine, inside, h):
    part = jnp.where(mine, scores[:, h * GSLOTS : (h + 1) * GSLOTS], NEGATIVE)
    raised = jnp.exp(part - jnp.max(part, 1, keepdims=True))
    inverse = jnp.where(inside, 1.0 / jnp.sum(raised, 1, keepdims=True), 0.0)
    return raised * inverse


def window_at(starts, group_at, row_at, i, size):
    g = group_at[i]
    row = pl.multiple_of(row_at[i], 16)
    at = pl.ds(pl.multiple_of(g * GSLOTS, GSLOTS), GSLOTS)
    place = iota((size, 1), 0) + row
    inside = (place >= starts[0, g * GROUP]) & (place < starts[0, g * GROUP + GROUP])
    return size, g, pl.ds(row, size), at, inside


def exact_forward_kernel(
    starts, qs, cls, kt_hbm, vs_hbm, both, rcol, att_out, att_s, mix_s, kt, vs, sems, *lists
):
    rows, width = rcol.shape[0], qs.shape[1]
    heads = width // HEAD_DIM
    copies = [
        pltpu.make_async_copy(kt_hbm, kt, sems.at[0]),
        pltpu.make_async_copy(vs_hbm, vs, sems.at[1]),
    ]
    for copy in copies:
        copy.start()
    high = both[...].astype(BF16)
    low = (both[...] - high.astype(F32)).astype(BF16)
    step = (rows + WIN) // 5

    def spread(i, carry):
        at = pl.ds(pl.multiple_of(i * step, 16), step)
        member = (cls[at, :] == iota((step, 128), 1)).astype(BF16)
        mix_s[at, :] = dot(member, high) + dot(member, low)
        return carry

    lax.fori_loop(0, 5, spread, 0)
    for copy in copies:
        copy.wait()

    def window(size, g, here, at, inside):
        keys = block_diagonal_turned(kt[:, at], heads)
        values = block_diagonal(vs[at, :], heads)
        mine = cls[here, :] == iota((size, GSLOTS), 1) // TOPK + g * GROUP
        scores = dot(qs[here, :], keys)
        weights = [window_probs(scores, mine, inside, h).astype(BF16) for h in range(heads)]
        out = dot(jnp.concatenate(weights, axis=1), values)
        mix = mix_s[here, :]
        att_s[here, :] = jnp.where(inside, mix[:, :width] * out + mix[:, width:], att_s[here, :])

    each_window(starts, rows, lists, window, FORWARD_UNROLL)

    def unplace(i, carry):
        at = pl.ds(pl.multiple_of(i * 256, 256), 256)
        chosen = (iota((256, rows), 1) == rcol[at, :].astype(jnp.int32)).astype(BF16)
        att_out[at, :] = dot(chosen, att_s[:rows, :].astype(BF16)).astype(BF16)
        return carry

    lax.fori_loop(0, rows // 256, unplace, 0)


ANYWHERE = pl.BlockSpec(memory_space=pl.ANY)
LISTED = 64


def exact_forward(starts, qs, cls, ks, vs, both, rcol):
    rows, width = rcol.shape[0], qs.shape[1]
    shape = jax.ShapeDtypeStruct
    return pl.pallas_call(
        exact_forward_kernel,
        out_shape=shape((rows, width), BF16),
        in_specs=[pl.BlockSpec(memory_space=pltpu.SMEM)] + vmem(2) + [ANYWHERE] * 2 + vmem(2),
        out_specs=vmem(1)[0],
        scratch_shapes=[
            pltpu.VMEM((rows + WIN, width), F32),
            pltpu.VMEM((rows + WIN, 2 * width), F32),
            pltpu.VMEM((width, SLOTS), BF16),
            pltpu.VMEM((SLOTS, width), BF16),
            pltpu.SemaphoreType.DMA((2,)),
        ]
        + [pltpu.SMEM((LISTED,), jnp.int32)] * 4,
        compiler_params=pltpu.CompilerParams(vmem_limit_bytes=62 << 20),
        name="exact_forward",
    )(starts, qs, cls, ks, vs, both, rcol)


def exact_backward_kernel(
    starts, qs, cls, ks_hbm, kt_hbm, vt_hbm, rows_in, rcol, rrow, grad,
    dq_out, dkv_out, dkvt_out, centre_out,
    grad_s, mass_s, dq_s, part_s, dkv_s, ks, kt, vt, sems, *lists,
):
    rows, width = rcol.shape[0], qs.shape[1]
    heads = width // HEAD_DIM
    copies = [
        pltpu.make_async_copy(ks_hbm, ks, sems.at[0]),
        pltpu.make_async_copy(kt_hbm, kt, sems.at[1]),
        pltpu.make_async_copy(vt_hbm, vt, sems.at[2]),
    ]
    for copy in copies:
        copy.start()
    mass_rows = rows_in[:, :width]
    high = mass_rows.astype(BF16)
    low = (mass_rows - high.astype(F32)).astype(BF16)
    rank_row = rrow[:1, :].astype(jnp.int32)

    def place(i, carry):
        at = pl.ds(pl.multiple_of(i * 256, 256), 256)
        chosen = (iota((256, rows), 0) + i * 256 == rank_row).astype(BF16)
        grad_s[at, :] = dot(chosen, grad[...]).astype(BF16)
        member = (cls[at, :] == iota((256, 128), 1)).astype(BF16)
        mass_s[at, :] = dot(member, high) + dot(member, low)
        return carry

    lax.fori_loop(0, rows // 256, place, 0)
    grad_s[rows:, :] = jnp.zeros((WIN, width), BF16)
    mass_s[rows:, :] = jnp.zeros((WIN, width), F32)
    dkv_s[...] = jnp.zeros_like(dkv_s)
    for copy in copies:
        copy.wait()

    def window(size, g, here, at, inside):
        keys = block_diagonal(ks[at, :], heads)
        mine = cls[here, :] == iota((size, GSLOTS), 1) // TOPK + g * GROUP
        query, upstream = qs[here, :], grad_s[here, :]
        scores = dot(query, block_diagonal_turned(kt[:, at], heads))
        against = dot(upstream, block_diagonal_turned(vt[:, at], heads))
        mass = mass_s[here, :]
        weights, score_grads = [], []
        mass_part = jnp.zeros((size, width), F32)
        for h in range(heads):
            cut = slice(h * GSLOTS, (h + 1) * GSLOTS)
            probs = window_probs(scores, mine, inside, h)
            meeting = jnp.sum(probs * against[:, cut], 1, keepdims=True)
            weighted = probs * mass[:, h * HEAD_DIM : h * HEAD_DIM + 1]
            weights.append(weighted.astype(BF16))
            score_grads.append((weighted * (against[:, cut] - meeting)).astype(BF16))
            mass_part = jnp.where(head_lanes(width, h), meeting, mass_part)
        score_grad = jnp.concatenate(score_grads, axis=1)
        weight = jnp.concatenate(weights, axis=1)
        dq = dot(score_grad, keys) * SCALE
        dq_s[here, :] = jnp.where(inside, dq, dq_s[here, :])
        part_s[here, :] = jnp.where(inside, mass_part, part_s[here, :])
        pair = jnp.concatenate(
            [
                diagonal_blocks_turned(dot_tn(query, score_grad), heads),
                diagonal_blocks_turned(dot_tn(upstream, weight), heads),
            ],
            axis=0,
        )
        dkv_s[:, at] = dkv_s[:, at] + pair

    each_window(starts, rows, lists, window, BACKWARD_UNROLL)
    centre_out[...] = jnp.zeros_like(centre_out)

    def finish_group(g, carry):
        at = pl.ds(pl.multiple_of(g * GSLOTS, GSLOTS), GSLOTS)
        block = dkv_s[:, at]
        dkvt_out[:, at] = block.astype(BF16)
        dkv_out[at, :] = jnp.transpose(block).astype(BF16)
        return carry

    lax.fori_loop(0, GROUPS, finish_group, 0)

    def unplace(i, carry):
        at = pl.ds(pl.multiple_of(i * 256, 256), 256)
        chosen = (iota((256, rows), 1) == rcol[at, :].astype(jnp.int32)).astype(BF16)
        dq_out[at, :] = dot(chosen, dq_s[:rows, :].astype(BF16)).astype(BF16)
        member = (cls[at, :] == iota((256, 128), 1)).astype(BF16)
        pair = jnp.concatenate([part_s[at, :].astype(BF16), grad_s[at, :]], axis=1)
        centre_out[...] += dot_tn(member, pair)
        return carry

    lax.fori_loop(0, rows // 256, unplace, 0)


def exact_backward(starts, qs, cls, ks, kt, vt, rows_in, rcol, rrow, grad):
    rows, width = rcol.shape[0], qs.shape[1]
    shape = jax.ShapeDtypeStruct
    return pl.pallas_call(
        exact_backward_kernel,
        out_shape=(
            shape((rows, width), BF16),
            shape((SLOTS, 2 * width), BF16),
            shape((2 * width, SLOTS), BF16),
            shape((CLP, 2 * width), F32),
        ),
        in_specs=[pl.BlockSpec(memory_space=pltpu.SMEM)] + vmem(2) + [ANYWHERE] * 3 + vmem(4),
        out_specs=tuple(vmem(4)),
        scratch_shapes=[
            pltpu.VMEM((rows + WIN, width), BF16),
            pltpu.VMEM((rows + WIN, width), F32),
            pltpu.VMEM((rows + WIN, width), F32),
            pltpu.VMEM((rows + WIN, width), F32),
            pltpu.VMEM((2 * width, SLOTS), F32),
            pltpu.VMEM((SLOTS, width), BF16),
            pltpu.VMEM((width, SLOTS), BF16),
            pltpu.VMEM((width, SLOTS), BF16),
            pltpu.SemaphoreType.DMA((3,)),
        ]
        + [pltpu.SMEM((LISTED,), jnp.int32)] * 4,
        compiler_params=pltpu.CompilerParams(vmem_limit_bytes=62 << 20),
        name="exact_backward",
    )(starts, qs, cls, ks, kt, vt, rows_in, rcol, rrow, grad)


def gelu_parts(values):
    slope = 0.7978845608028654
    squared = values * values
    turned = jnp.tanh(slope * values * (1.0 + 0.044715 * squared))
    half = 0.5 * (1.0 + turned)
    rise = half + 0.5 * slope * values * (1.0 - turned * turned) * (1.0 + 0.134145 * squared)
    return (values * half, rise)


def middle_kernel(
    pair, parts, tok, cot, att, wout_own, wout, wexp, gain, bias, shr_own, shr_one, shr_two, shr_three, shr_peer,
    mid_out, mgrad_out, agrad_out, hsum_out, wo_out, gains_out, *refs,
):
    grad_outs, refs = refs[: 2 + parts if pair else 1], refs[2 + parts if pair else 1 :]
    middle_body(
        pair, tok, cot, att, wout_own, wout, wexp, gain, bias,
        (shr_own, shr_one, shr_two, shr_three), shr_peer, mid_out, mgrad_out, agrad_out, hsum_out, wo_out, gains_out, grad_outs, *refs,
    )


def middle_body(
    pair, tok, cot, att, wout_own, wout, wexp, gain, bias, shards, shr_peer,
    mid_out, mgrad_out, agrad_out, hsum_out, wo_out, gains_out, grad_outs,
    wshr_ref, att_peer, cat, xcat, sn, act, hg, sp_own, sp_send, sp_recv, hp_own, hp_send, hp_recv,
    sx_send, sx_recv, branch, kept,
    asend, arecv, xsend, xrecv, rsend, rrecv, ssend, srecv, hsend, hrecv, sxs, sxr, bsend, brecv,
    wysend, wyrecv,
):
    rows, width = att.shape
    model = tok.shape[1]
    half_width = 2 * width
    half_rows = rows // 2
    blocks = half_rows // 128
    hid = lax.axis_index("hid")
    core, side = lax.rem(hid, 2), hid // 2
    core_peer = {"hid": hid + 1 - 2 * core}
    x_peer = {"hid": hid + 2 - 4 * side}

    dp = lax.axis_index("dp")
    greeted = [core_peer, x_peer] + ([{"dp": 1 - dp}] if pair else [])
    barrier = greet(greeted)
    gains_out[...] = jnp.zeros_like(gains_out)
    pl.semaphore_wait(barrier, len(greeted))

    units = wexp.shape[1]
    if pair:
        wshr = wshr_ref
        n_dm, my_dm = lax.axis_size("dm"), lax.axis_index("dm")
        shard = model // (2 * n_dm)

        def shard_rows(d, step):
            owner = lax.rem(my_dm + n_dm - step, n_dm)
            return pl.ds(pl.multiple_of((d * n_dm + owner) * shard, 32), shard)

        shard_copies = [
            remote(
                shards[step], wshr.at[shard_rows(dp, step), :], wysend.at[step], wyrecv.at[step],
                {"dp": 1 - dp},
            )
            for step in range(1, n_dm)
        ]
    else:
        wshr = shards[0]

    def block_rows(j, which):
        return pl.ds(pl.multiple_of(which * half_rows + j * 128, 128), 128)

    def own_rows(j):
        return pl.ds(pl.multiple_of(j * 128, 128), 128)

    att_copy = remote(att, att_peer, asend, arecv, core_peer)
    att_copy.start()
    if pair:
        for copy in shard_copies:
            copy.start()
        for step in range(n_dm):
            wshr[shard_rows(dp, step), :] = shards[step][...]
        wshr[shard_rows(1 - dp, 0), :] = shr_peer[...]

    def x_copy(j):
        block = block_rows(j, core)
        return remote(cat.at[block, :], xcat.at[block, :], xsend.at[j], xrecv.at[j], x_peer)

    def relay_copy(j):
        block = xcat.at[block_rows(j, core), :]
        return remote(block, block, rsend.at[j], rrecv.at[j], core_peer)

    def sp_copy(j):
        return remote(sp_send.at[j], sp_recv.at[j], ssend.at[j], srecv.at[j], core_peer)

    def hp_copy(j):
        return remote(hp_send.at[j], hp_recv.at[j], hsend.at[j], hrecv.at[j], core_peer)

    def sx_copy(j):
        return remote(sx_send.at[j], sx_recv.at[j], sxs.at[j], sxr.at[j], x_peer)

    def branch_copy(j):
        block = branch.at[block_rows(j, core), :]
        return remote(block, block, bsend.at[j], brecv.at[j], core_peer)

    def join(at):
        mine, other = att[at, :], att_peer[at, :]
        cat[at, :] = jnp.where(
            core == 0,
            jnp.concatenate([mine, other], axis=1),
            jnp.concatenate([other, mine], axis=1),
        )

    att_copy.wait_recv()

    def spread(j, carry):
        join(block_rows(j, core))
        x_copy(j).start()
        return carry

    lax.fori_loop(0, blocks, spread, 0)

    def join_other(j, carry):
        join(block_rows(j, 1 - core))
        return carry

    lax.fori_loop(0, blocks, join_other, 0)

    def both(ref, j):
        return jnp.concatenate([ref[block_rows(j, core), :], ref[block_rows(j, 1 - core), :]], axis=0)

    def store_both(ref, j, values):
        ref[block_rows(j, core), :] = values[:128]
        ref[block_rows(j, 1 - core), :] = values[128:]

    own_half = pl.ds(pl.multiple_of(side * half_width, 128), half_width)
    other_half = pl.ds(pl.multiple_of((1 - side) * half_width, 128), half_width)

    def forward(j):
        x_copy(j).wait_recv()
        relay_copy(j).start()
        relay_copy(j).wait_recv()
        attention = dot(both(cat, j), wout[own_half, :]) + dot(both(xcat, j), wout[other_half, :])
        middle = both(tok, j).astype(F32) + attention
        mid_out[own_rows(j), :] = middle[:128]
        normed, _ = norm_parts(middle)
        second = (normed * gain[...][None] + bias[...][None]).astype(BF16)
        store_both(sn, j, second)
        hidden = dot(second, wexp[...])
        value, rise = gelu_parts(hidden)
        value = value.astype(BF16)
        store_both(act, j, value)
        if pair:

            @pl.when(j == 0)
            def _():
                for copy in shard_copies:
                    copy.wait_recv()

        grad = (dot(both(cot, j), wshr[...]) * rise).astype(BF16)
        store_both(hg, j, grad)
        part = dot_nt(grad, wexp[...])
        sp_own[j] = part[:128]
        sp_send[j] = part[128:].astype(BF16)
        sp_copy(j).start()
        part = dot_nt(value, wshr[...])
        hp_own[j] = part[:128]
        hp_send[j] = part[128:].astype(BF16)
        hp_copy(j).start()

    def chip_sum(j):
        sp_copy(j).wait_recv()
        total = sp_own[j] + sp_recv[j].astype(F32)
        sx_send[j] = total.astype(BF16)
        sx_copy(j).start()
        hp_copy(j).wait_recv()
        hsum_out[own_rows(j), :] = (hp_own[j] + hp_recv[j].astype(F32)).astype(BF16)

    def norm_grad(j):
        sx_copy(j).wait_recv()
        second_grad = sx_send[j].astype(F32) + sx_recv[j].astype(F32)
        normed, spread_two = norm_parts(mid_out[own_rows(j), :])
        inner, gain_part, bias_part = norm_back(second_grad, normed, spread_two, gain[...][None])
        gains_out[0:1, :] += gain_part[None]
        gains_out[1:2, :] += bias_part[None]
        middle_grad = cot[block_rows(j, core), :].astype(F32) + inner
        mgrad_out[own_rows(j), :] = middle_grad
        branch[block_rows(j, core), :] = middle_grad.astype(BF16)
        branch_copy(j).start()

    def attended_grad(j):
        branch_copy(j).wait_recv()
        for which in range(2):
            at = block_rows(j, which)
            agrad_out[at, :] = dot_nt(branch[at, :], wout_own[...]).astype(BF16)

    def when_block(j, work):
        @pl.when((j >= 0) & (j < blocks))
        def _():
            work(j)

    def ticks(first, last):
        def tick(t, carry):
            when_block(t - 1, chip_sum)
            when_block(t, forward)
            when_block(t - 2, norm_grad)
            when_block(t - 3, attended_grad)
            return carry

        lax.fori_loop(first, last, tick, 0)

    half = model // 2
    part_rows = half if pair else model

    def weight_grad(left, right, which):
        return dot_tn(left[:, aligned(which * half, part_rows)], right[...]).astype(BF16)

    ticks(0, blocks)
    if pair:
        keep_out, give_out = grad_outs[0], grad_outs[1]
        for d in range(2):
            kept[d] = weight_grad(sn, hg, d)
    else:
        grad_outs[0][:, :units] = weight_grad(sn, hg, 0)
    ticks(blocks, blocks + 1)
    if pair:
        parts, me = lax.axis_size("dm"), lax.axis_index("dm")
        shard = half // parts
        for step in range(parts):
            quarter = pl.ds(pl.multiple_of(lax.rem(me + step, parts) * shard, 32), shard)
            for d in range(2):
                grad_outs[2 + step][d] = kept[d, quarter, :]
        give_out[...] = weight_grad(cot, act, 1 - dp)
    else:
        grad_outs[0][:, units:] = weight_grad(cot, act, 0)
    ticks(blocks + 1, blocks + 2)
    if pair:
        keep_out[...] = weight_grad(cot, act, dp)
    ticks(blocks + 2, blocks + 3)
    wo_out[...] = dot_tn(att[...], branch[...]).astype(BF16)

    def drain(j, carry):
        x_copy(j).wait_send()
        relay_copy(j).wait_send()
        sp_copy(j).wait_send()
        hp_copy(j).wait_send()
        sx_copy(j).wait_send()
        branch_copy(j).wait_send()
        return carry

    lax.fori_loop(0, blocks, drain, 0)
    att_copy.wait_send()
    if pair:
        for copy in shard_copies:
            copy.wait_send()


def middle(pair, tokens, cotangent, attended, wout_own, wout, wexp, gain, bias, shards, shr_peer):
    rows, model = tokens.shape
    width = attended.shape[1]
    units = wexp.shape[1]
    part_rows = model // 2 if pair else model
    spare = (2, part_rows, units) if pair else (2, 16, 128)
    parts = lax.axis_size("dm")
    if pair:
        grads = [(part_rows, units)] * 2 + [(2, part_rows // parts, units)] * parts
    else:
        grads = [(model, 2 * units)]
    blocks = rows // 256
    shape = jax.ShapeDtypeStruct
    dma = pltpu.SemaphoreType.DMA
    low = pltpu.VMEM((blocks, 128, model), BF16)
    full = pltpu.VMEM((blocks, 128, model), F32)
    return pl.pallas_call(
        functools.partial(middle_kernel, pair, parts),
        out_shape=(
            shape((rows // 2, model), F32),
            shape((rows // 2, model), F32),
            shape((rows, width), BF16),
            shape((rows // 2, model), BF16),
            shape((width, model), BF16),
            shape((8, model), F32),
        )
        + tuple(shape(dims, BF16) for dims in grads),
        in_specs=vmem(13),
        out_specs=tuple(vmem(6 + len(grads))),
        scratch_shapes=[
            pltpu.VMEM((model, units) if pair else (16, 128), BF16),
            pltpu.VMEM((rows, width), BF16),
            pltpu.VMEM((rows, 2 * width), BF16),
            pltpu.VMEM((rows, 2 * width), BF16),
            pltpu.VMEM((rows, model), BF16),
            pltpu.VMEM((rows, units), BF16),
            pltpu.VMEM((rows, units), BF16),
            full, low, low, full, low, low, low, low,
            pltpu.VMEM((rows, model), BF16),
            pltpu.VMEM(spare, BF16),
            dma, dma,
        ]
        + [dma((blocks,))] * 12
        + [dma((4,)), dma((4,))],
        compiler_params=pltpu.CompilerParams(
            vmem_limit_bytes=60 << 20, collective_id=2, has_side_effects=True
        ),
        name="middle",
    )(tokens, cotangent, attended, wout_own, wout, wexp, gain, bias, *shards, shr_peer)


def tail_kernel(
    pair, lengths, dkv, dkvt, dq, summed, k, v, centre, topk, tm, merged, rows_in, counts, ccol, weight,
    fn, sfn, tok_hbm, gain, mgrad, srow, mid, hsum, hsum_x, second_gains,
    sh_keep, sh_given, ex_own, ex_one, ex_two, ex_three,
    result_out, tokens_out, qkv_out, gain_a, gain_b, gain_c, gain_d, expand_out, shrink_out,
    sbuf, cbuf, fgm, to_core, from_core, to_x, from_x, to_right, to_left, from_left,
    from_right, from_fin, pq, pkv, dense, dense_to_core, dense_from_core, dense_to_x, dense_from_x,
    dense_own, first, sfn_tile, grad_all, grad_from_y, grad_back, g_own, g_right, g_left, g_from_left,
    g_from_right, g_total, gain_sum, gain_core, gain_dm, gain_dp, gain_x, shrink_send, shrink_recv, expand_y, tok, tile_sem, mid_sem, hsum_sem, tok_sem,
    ssend, srecv, csend, crecv,
    send_core, recv_core, send_x, recv_x, send_right, recv_left, send_left, recv_right, send_fin,
    recv_fin,
    dsend_core, drecv_core, dsend_x, drecv_x, fsend, frecv, tsend, trecv, osend, orecv,
    ysend, yrecv, gsend_right, grecv_left, gsend_left, grecv_right, asend, arecv,
    gcsend, gcrecv, gmsend, gmrecv, gpsend, gprecv, esend, erecv,
):
    gain_outs = (gain_a, gain_b, gain_c, gain_d)
    rows, width = k.shape
    model = tok.shape[1]
    heads = width // HEAD_DIM
    half_width = model // 2
    half_rows = rows // 2
    blocks = half_rows // 128
    parts = lax.axis_size("dm")
    me, hid, dp = lax.axis_index("dm"), lax.axis_index("hid"), lax.axis_index("dp")
    core, side = lax.rem(hid, 2), hid // 2
    core_peer = {"hid": hid + 1 - 2 * core}
    x_peer = {"hid": hid + 2 - 4 * side}
    y_peer = {"dp": 1 - dp}
    own_start = me * rows
    columns = aligned(side * half_width, half_width)
    other_columns = aligned((1 - side) * half_width, half_width)

    greeted = [{"dm": lax.rem(me + step, parts)} for step in range(1, parts)]
    greeted += [core_peer, x_peer] + ([y_peer] if pair else [])
    barrier = greet(greeted)

    wide = iota((CLP, 256), 1)
    packed = jnp.concatenate([summed[:, width:], jnp.zeros((CLP, 256 - width), F32)], axis=1)
    for h in range(heads):
        packed = jnp.where(wide == width + h, summed[:, h * HEAD_DIM : h * HEAD_DIM + 1], packed)
    sbuf[me] = packed.astype(BF16)
    dense_own[...] = jnp.zeros_like(dense_own)
    mid_copy = pltpu.make_async_copy(mid, dense, mid_sem)
    mid_copy.start()
    hsum_copy = pltpu.make_async_copy(hsum, dense_to_core, hsum_sem)
    hsum_copy.start()
    tok_copy = pltpu.make_async_copy(
        tok_hbm.at[aligned(core * half_rows, half_rows), :], tok, tok_sem
    )
    tok_copy.start()

    @pl.when(me == 0)
    def _():
        from_left[...] = jnp.zeros_like(from_left)
        g_from_left[...] = jnp.zeros_like(g_from_left)

    @pl.when(me == parts - 1)
    def _():
        from_right[...] = jnp.zeros_like(from_right)
        g_from_right[...] = jnp.zeros_like(g_from_right)

    pl.semaphore_wait(barrier, len(greeted))
    sum_copies = small_exchange(sbuf, ssend, srecv, me, parts)
    for copy in sum_copies:
        copy.start()

    def chunk_rows(i, which):
        return aligned(which * HALF + i * CHUNK, CHUNK)

    def block_rows(j, which):
        return aligned(which * half_rows + j * 128, 128)

    def own_rows(j):
        return aligned(j * 128, 128)

    def core_copy(i):
        return remote(to_core.at[i], from_core.at[i], send_core.at[i], recv_core.at[i], core_peer)

    def x_copy(i):
        return remote(to_x.at[i], from_x.at[i], send_x.at[i], recv_x.at[i], x_peer)

    right = {"dm": lax.rem(me + 1, parts)}
    left = {"dm": lax.rem(me + parts - 1, parts)}

    def right_copy(i):
        return remote(to_right.at[i], from_left.at[i], send_right.at[i], recv_left.at[i], right)

    def left_copy(i):
        return remote(to_left.at[i], from_right.at[i], send_left.at[i], recv_right.at[i], left)

    def fin_copy(i):
        return remote(from_x.at[i], from_fin.at[i], send_fin.at[i], recv_fin.at[i], core_peer)

    def dense_core_copy(j):
        return remote(
            dense_to_core.at[j], dense_from_core.at[j], dsend_core.at[j], drecv_core.at[j], core_peer
        )

    def dense_x_copy(j):
        return remote(dense_to_x.at[j], dense_from_x.at[j], dsend_x.at[j], drecv_x.at[j], x_peer)

    def first_copy(j):
        block = first.at[j, :, columns]
        return remote(block, block, fsend.at[j], frecv.at[j], x_peer)

    def tokens_copy(j):
        block = tokens_out.at[block_rows(j, core), :]
        return remote(block, block, tsend.at[j], trecv.at[j], core_peer)

    def result_copy(j):
        block = result_out.at[block_rows(j, core), :]
        return remote(block, block, osend.at[j], orecv.at[j], core_peer)

    def spread_back(start, count):
        other = dot(dkv[aligned((1 - core) * HALF + start * CHUNK, count * CHUNK), :], weight[width:, :])
        other = other.astype(BF16)
        for i in range(count):
            to_core[start + i] = other[i * CHUNK : (i + 1) * CHUNK]
            core_copy(start + i).start()
        mine = dot(dkv[aligned(core * HALF + start * CHUNK, count * CHUNK), :], weight[width:, :])
        mine = mine.astype(BF16)
        for i in range(count):
            fgm[start + i] = mine[i * CHUNK : (i + 1) * CHUNK]

    def chip_sum(i):
        core_copy(i).wait_recv()
        to_x[i] = fgm[i, :, other_columns] + from_core[i, :, other_columns]
        x_copy(i).start()

    def hid_sum(i):
        x_copy(i).wait_recv()
        fgm[i, :, columns] = (
            fgm[i, :, columns].astype(F32)
            + from_core[i, :, columns].astype(F32)
            + from_x[i].astype(F32)
        ).astype(BF16)

    def go_right(i):
        @pl.when(me > 0)
        def _():
            right_copy(i).wait_recv()

        @pl.when(me < parts - 1)
        def _():
            to_right[i] = fgm[i, :, columns] + from_left[i]
            right_copy(i).start()

    def go_left(i):
        @pl.when(me < parts - 1)
        def _():
            left_copy(i).wait_recv()

        @pl.when(me > 0)
        def _():
            to_left[i] = fgm[i, :, columns] + from_right[i]
            left_copy(i).start()

    def finish(i):
        from_x[i] = (
            fgm[i, :, columns].astype(F32) + from_left[i].astype(F32) + from_right[i].astype(F32)
        ).astype(BF16)
        fin_copy(i).start()

    def scatter(i):
        fin_copy(i).wait_recv()
        here = iota((half_rows, CHUNK), 0) + own_start + core * half_rows
        chosen = [
            (srow[:, chunk_rows(i, which)] == here).astype(BF16) for which in (core, 1 - core)
        ]
        picked = jnp.concatenate([from_x[i], from_fin[i]], axis=0)
        dense_own[...] += dot(jnp.concatenate(chosen, axis=1), picked)

    far = jnp.maximum(me, parts - 1 - me)

    def ticks(start, last):
        def tick(t, carry):
            ready = t
            when_in(ready, CHUNKS, hid_sum)
            when_in(ready - LAG * me, CHUNKS, go_right)
            when_in(ready - LAG * (parts - 1 - me), CHUNKS, go_left)
            when_in(ready - LAG * far, CHUNKS, finish)
            when_in(ready - LAG * far - 1, CHUNKS, scatter)
            return carry

        lax.fori_loop(start, last, tick, 0)

    if pair:
        shard = expand_out.shape[0]

        def shard_rows(m):
            return pl.ds(pl.multiple_of(m * shard, 32), shard)

        shrink_copies = []
        for step in range(1, parts):
            target = lax.rem(me + step, parts)
            shrink_send[step] = sh_keep[shard_rows(target), :] + sh_given[shard_rows(target), :]
            shrink_copies.append(
                remote(
                    shrink_send.at[step], shrink_recv.at[step], esend.at[step], erecv.at[step],
                    {"dm": target},
                )
            )
        for copy in shrink_copies:
            copy.start()
        expand_y[0] = (
            ex_own[1 - dp].astype(F32) + ex_one[1 - dp].astype(F32)
            + ex_two[1 - dp].astype(F32) + ex_three[1 - dp].astype(F32)
        ).astype(BF16)
        expand_copy = remote(expand_y.at[0], expand_y.at[1], esend.at[0], erecv.at[0], y_peer)
        expand_copy.start()

    def chip_sums(first, last):
        def one(i, carry):
            chip_sum(i)
            return carry

        lax.fori_loop(first, last, one, 0)

    spread_back(0, 3)
    chip_sums(0, 3)
    spread_back(3, 5)
    chip_sums(3, 8)
    spread_back(8, CHUNKS - 8)
    chip_sums(8, CHUNKS)

    def result_rows(j, carry):
        total = dense_to_core[j].astype(F32) + hsum_x[j].astype(F32)
        result_out[block_rows(j, core), :] = (dense[j] + total).astype(BF16)
        result_copy(j).start()
        return carry

    for copy in sum_copies:
        copy.wait_recv()
    total = sbuf[0].astype(F32)
    for d in range(1, parts):
        total += sbuf[d].astype(F32)
    same = sequence_masks(lengths, topk, rows)
    rest_grad = total[:, :width].astype(BF16)
    product = rest_grad.astype(F32) * rows_in[:, width:]
    score_grads, weights = [], []
    centre_part = jnp.zeros((CLP, width), F32)
    for h in range(heads):
        lanes = head_lanes(width, h)
        top = tm[...].astype(F32)
        zero = jnp.zeros((CLP, width), BF16)
        full = dot_nt(jnp.where(lanes, centre[...], zero), k[...]) * SCALE
        against = dot_nt(jnp.where(lanes, rest_grad, zero), v[...])
        largest, denominator = merged[:, h : h + 1], merged[:, 8 + h : 9 + h]
        mass = merged[:, 16 + h : 17 + h]
        mass_grad = total[:, width + h : width + h + 1]
        probs = jnp.where(same, jnp.exp(full - largest) / denominator, 0.0)
        mean = mass * mass_grad + jnp.sum(jnp.where(lanes, product, 0.0), 1, keepdims=True)
        grad = jnp.where(top > 0.5, mass_grad, against)
        score_grad = (probs * (grad - mean)).astype(BF16)
        centre_part = jnp.where(lanes, dot(score_grad, k[...]), centre_part)
        score_grads.append(score_grad)
        weights.append(jnp.where(top > 0.5, 0.0, probs).astype(BF16))
    cbuf[me] = (centre_part * SCALE).astype(BF16)
    centre_copies = small_exchange(cbuf, csend, crecv, me, parts)
    for copy in centre_copies:
        copy.start()
    score_grad = jnp.concatenate(score_grads, axis=0)
    rest_weight = jnp.concatenate(weights, axis=0)
    pkv[...] = jnp.concatenate(
        [
            (dot_tn(score_grad, block_diagonal(centre[...], heads)) * SCALE).astype(BF16),
            dot_tn(rest_weight, block_diagonal(rest_grad, heads)).astype(BF16),
        ],
        axis=1,
    )
    if pair:
        part = width // 2

        def y_rows(b, d):
            return pl.ds(pl.multiple_of((d * 3 + b) * part, 32), part)

        def y_copy(b):
            return remote(
                grad_all.at[y_rows(b, 1 - dp), :], grad_from_y.at[b], ysend.at[b], yrecv.at[b], y_peer
            )

        def y_back(b):
            return remote(
                grad_all.at[y_rows(b, dp), :], grad_back.at[b], asend.at[b], arecv.at[b], y_peer
            )

        def unit_right(u):
            return remote(g_right.at[u], g_from_left.at[u], gsend_right.at[u], grecv_left.at[u], right)

        def unit_left(u):
            return remote(g_left.at[u], g_from_right.at[u], gsend_left.at[u], grecv_right.at[u], left)

        def y_sum(b):
            y_copy(b).wait_recv()
            both = grad_all[y_rows(b, dp), :] + grad_from_y[b]
            g_own[2 * b] = both[:, :half_width]
            g_own[2 * b + 1] = both[:, half_width:]

        root = parts // 2

        def unit_up(u):
            @pl.when(me < root)
            def _():
                @pl.when(me > 0)
                def _():
                    unit_right(u).wait_recv()

                g_right[u] = g_own[u] + g_from_left[u]
                unit_right(u).start()

            @pl.when(me > root)
            def _():
                @pl.when(me < parts - 1)
                def _():
                    unit_left(u).wait_recv()

                g_left[u] = g_own[u] + g_from_right[u]
                unit_left(u).start()

        def unit_turn(u):
            unit_right(u).wait_recv()

            @pl.when(me < parts - 1)
            def _():
                unit_left(u).wait_recv()

            total = g_own[u] + g_from_left[u] + g_from_right[u]
            g_total[u] = total
            g_left[u] = total
            unit_left(u).start()

            @pl.when(me < parts - 1)
            def _():
                g_right[u] = total
                unit_right(u).start()

        def unit_down(u):
            @pl.when(me < root)
            def _():
                unit_left(u).wait_recv()
                g_total[u] = g_from_right[u]

                @pl.when(me > 0)
                def _():
                    g_left[u] = g_from_right[u]
                    unit_left(u).start()

            @pl.when(me > root)
            def _():
                unit_right(u).wait_recv()
                g_total[u] = g_from_left[u]

                @pl.when(me < parts - 1)
                def _():
                    g_right[u] = g_from_left[u]
                    unit_right(u).start()

        def y_return(b):
            grad_all[y_rows(b, dp), :half_width] = g_total[2 * b]
            grad_all[y_rows(b, dp), half_width:] = g_total[2 * b + 1]
            y_back(b).start()

        def gticks(start, last):
            def tick(t, carry):
                @pl.when(lax.rem(t, 2) == 0)
                def _():
                    when_in(t // 2, 3, y_sum)

                wait = jnp.where(me < root, me, parts - 1 - me)
                up = jnp.where(me == root, -1, t - 1 - LAG * wait)
                when_in(up, UNITS, unit_up)
                away = jnp.where(me < root, root - me, me - root)
                back = t - 1 - LAG * (root + away)

                @pl.when(me == root)
                def _():
                    when_in(back, UNITS, unit_turn)

                @pl.when(me != root)
                def _():
                    when_in(back, UNITS, unit_down)

                @pl.when((back >= 0) & (lax.rem(back + 1, 2) == 0))
                def _():
                    when_in((back - 1) // 2, 3, y_return)

                return carry

            lax.fori_loop(start, last, tick, 0)
    else:

        def gticks(start, last):
            pass

    def slot_tile(c, carry):
        cut = aligned(c * 256, 256)
        fetch = pltpu.make_async_copy(sfn.at[:, cut], sfn_tile, tile_sem)
        fetch.start()
        grad = dot_tn(pkv[...], fn[:, cut])
        fetch.wait()
        grad = (grad + dot(dkvt[...], sfn_tile[...])).astype(BF16)
        grad_all[:width, cut] = grad[:width]
        grad_all[3 * (width // 2) : 3 * (width // 2) + width, cut] = grad[width:]
        return carry

    ticks(0, 1)
    lax.fori_loop(0, model // 256, slot_tile, 0)
    if pair:
        y_copy(0).start()
        y_copy(1).start()
    ticks(1, 2)
    mid_copy.wait()
    hsum_copy.wait()
    lax.fori_loop(0, blocks, result_rows, 0)
    ticks(2, 4)
    for copy in centre_copies:
        copy.wait_recv()
    centre_grad = cbuf[0].astype(F32)
    for d in range(1, parts):
        centre_grad += cbuf[d].astype(F32)
    centre_grad = centre_grad / counts[:, :1]
    high = centre_grad.astype(BF16)
    low = (centre_grad - high.astype(F32)).astype(BF16)

    def queries(i, carry):
        at = aligned(i * 256, 256)
        member = (ccol[at, :] == iota((256, 128), 1)).astype(BF16)
        pq[at, :] = (dq[at, :].astype(F32) + dot(member, high) + dot(member, low)).astype(BF16)
        return carry

    lax.fori_loop(0, rows // 256, queries, 0)
    query_grad = dot_tn(pq[...], fn[...]).astype(BF16)
    grad_all[width : width + width // 2, :] = query_grad[: width // 2]
    grad_all[5 * (width // 2) :, :] = query_grad[width // 2 :]
    if pair:
        y_copy(2).start()
    ticks(4, 5)

    def dense_rows(which):
        at = aligned(which * half_rows, half_rows)
        return dot(pq[at, :], weight[:width, :]) + dot(pkv[at, :], weight[width:, :])

    other_dense = dense_rows(1 - core).astype(BF16)
    for j in range(blocks):
        dense_to_core[j] = other_dense[j * 128 : (j + 1) * 128]
        dense_core_copy(j).start()
    own_dense = dense_rows(core)
    for j in range(blocks):
        dense[j] = own_dense[j * 128 : (j + 1) * 128]
    ticks(5, 6)

    def dense_chip(j, carry):
        dense_core_copy(j).wait_recv()
        dense_to_x[j] = (
            dense[j, :, other_columns] + dense_from_core[j, :, other_columns].astype(F32)
        ).astype(BF16)
        dense_x_copy(j).start()
        return carry

    def dense_hid(j, carry):
        dense_x_copy(j).wait_recv()
        dense_own[own_rows(j), :] += (
            dense[j, :, columns]
            + dense_from_core[j, :, columns].astype(F32)
            + dense_from_x[j].astype(F32)
        )
        return carry

    lax.fori_loop(0, blocks, dense_chip, 0)
    last = CHUNKS + LAG * (parts - 1) + 1

    def joint(t, carry):
        ticks(t, t + 1)
        gticks(t - 6, t - 5)
        return carry

    lax.fori_loop(6, last, joint, 0)
    done = last - 6
    lax.fori_loop(0, blocks, dense_hid, 0)
    mgrad_copy = pltpu.make_async_copy(mgrad, dense, mid_sem)
    mgrad_copy.start()

    gain_sum[...] = jnp.zeros_like(gain_sum)
    tok_copy.wait()

    def first_send(j, carry):
        grad = dense_own[own_rows(j), :].astype(BF16)
        first[j, :, columns] = grad
        first_copy(j).start()
        return carry

    lax.fori_loop(0, blocks, first_send, 0)

    def first_gains(j, carry):
        centred = tok[own_rows(j), :].astype(F32)
        mean = jnp.mean(centred, -1, keepdims=True)
        variance = jnp.mean(jnp.square(centred - mean), -1, keepdims=True)
        normed = (tok[own_rows(j), columns].astype(F32) - mean) * lax.rsqrt(
            variance + EPSILON
        )
        grad = first[j, :, columns].astype(F32)
        gain_sum[0:1, columns] += jnp.sum(grad * normed, 0, keepdims=True)
        gain_sum[1:2, columns] += jnp.sum(grad, 0, keepdims=True)
        return carry

    lax.fori_loop(0, blocks, first_gains, 0)
    gain_sum[2:4, columns] = second_gains[0:2, columns]
    if pair:
        core_gain = remote(gain_sum, gain_core, gcsend, gcrecv, core_peer)
        core_gain.start()
    gticks(done, done + 2)

    def first_back(j, carry):
        first_copy(j).wait_recv()
        at = block_rows(j, core)
        normed, spread = norm_parts(tok[own_rows(j), :].astype(F32))
        inner, _, _ = norm_back(first[j].astype(F32), normed, spread, gain[...][None])
        tokens_out[at, :] = (dense[j] + inner).astype(BF16)
        tokens_copy(j).start()
        return carry

    mgrad_copy.wait()
    if pair:
        core_gain.wait_recv()
        gain_dm[me] = gain_sum[...] + gain_core[...]
        dm_gains = small_exchange(gain_dm, gmsend, gmrecv, me, parts)
        for copy in dm_gains:
            copy.start()
    lax.fori_loop(0, 1, first_back, 0)
    gticks(done + 2, done + 4)
    lax.fori_loop(1, 2, first_back, 0)
    if pair:
        for copy in dm_gains:
            copy.wait_recv()
        line = gain_dm[0]
        for d in range(1, parts):
            line = line + gain_dm[d]
        gain_dp[0] = line
        dp_gain = remote(gain_dp.at[0], gain_dp.at[1], gpsend.at[0], gprecv.at[0], y_peer)
        dp_gain.start()
    lax.fori_loop(2, 4, first_back, 0)
    if pair:
        dp_gain.wait()
        gain_x[0] = gain_dp[0] + gain_dp[1]
        x_gain = remote(gain_x.at[0], gain_x.at[1], gpsend.at[1], gprecv.at[1], x_peer)
        x_gain.start()
    lax.fori_loop(4, blocks, first_back, 0)
    if pair:
        gticks(done + 4, 1 + LAG * 2 * (parts // 2) + UNITS)
        for b in range(3):
            y_copy(b).wait_send()
            y_back(b).wait_recv()
            grad_all[y_rows(b, 1 - dp), :] = grad_back[b]
    small = width // 2
    qkv_out[0, :small] = grad_all[width : width + small, :]
    qkv_out[0, small:] = grad_all[5 * small :, :]
    qkv_out[1] = grad_all[:width, :]
    qkv_out[2] = grad_all[3 * small : 5 * small, :]
    if pair:
        grad = sh_keep[shard_rows(me), :].astype(F32) + sh_given[shard_rows(me), :].astype(F32)
        for step in range(1, parts):
            shrink_copies[step - 1].wait()
            grad = grad + shrink_recv[step].astype(F32)
        shrink_out[...] = grad
        expand_copy.wait()
        grad = expand_y[1].astype(F32)
        for block in (ex_own, ex_one, ex_two, ex_three):
            grad = grad + block[dp].astype(F32)
        expand_out[...] = grad
        x_gain.wait()
        total = gain_x[0] + gain_x[1]
        core_gain.wait_send()
        for copy in dm_gains:
            copy.wait_send()
    else:
        total = gain_sum[...]
    for i, out in enumerate(gain_outs):
        out[...] = total[i]
    if pair:
        for b in range(3):
            y_back(b).wait_send()

        def drain_units(u, carry):
            @pl.when(me < parts - 1)
            def _():
                unit_right(u).wait_send()

            @pl.when(me > 0)
            def _():
                unit_left(u).wait_send()

            return carry

        lax.fori_loop(0, UNITS, drain_units, 0)

    def drain_blocks(j, carry):
        dense_core_copy(j).wait_send()
        dense_x_copy(j).wait_send()
        first_copy(j).wait_send()
        result_copy(j).wait()
        tokens_copy(j).wait()
        return carry

    def drain(i, carry):
        @pl.when(me < parts - 1)
        def _():
            right_copy(i).wait_send()

        @pl.when(me > 0)
        def _():
            left_copy(i).wait_send()

        core_copy(i).wait_send()
        x_copy(i).wait_send()
        fin_copy(i).wait_send()
        return carry

    lax.fori_loop(0, CHUNKS, drain, 0)
    for copy in sum_copies + centre_copies:
        copy.wait_send()
    lax.fori_loop(0, blocks, drain_blocks, 0)


def tail(
    pair, lengths, dkv, dkvt, dq, summed, k, v, centre, topk, tm, merged, rows_in, counts, clusters,
    weight, fn, sfn, tokens, gain, mgrad, srow, mid, hsum, hsum_x, second_gains,
    sh_keep, sh_given, ex_parts, parts,
):
    rows, width = k.shape
    model = tokens.shape[1]
    shape = jax.ShapeDtypeStruct
    dma = pltpu.SemaphoreType.DMA
    blocks = rows // 256
    owned = ex_parts[0].shape[1:]
    chain = pltpu.VMEM((CHUNKS, CHUNK, model // 2), BF16)
    whole = pltpu.VMEM((CHUNKS, CHUNK, model), BF16)
    unit = pltpu.VMEM((UNITS, width // 2, model // 2) if pair else (UNITS, 16, 128), BF16)
    return pl.pallas_call(
        functools.partial(tail_kernel, pair),
        out_shape=(
            shape((rows, model), BF16),
            shape((rows, model), BF16),
            shape((3, width, model), BF16),
            shape((model,), F32),
            shape((model,), F32),
            shape((model,), F32),
            shape((model,), F32),
            shape(owned, F32),
            shape(owned, F32),
        ),
        in_specs=[pl.BlockSpec(memory_space=pltpu.SMEM)]
        + vmem(15)
        + [pl.BlockSpec(memory_space=pl.ANY)] * 2
        + vmem(1)
        + [pl.BlockSpec(memory_space=pl.ANY)]
        + vmem(1)
        + [pl.BlockSpec(memory_space=pl.ANY)] * 2
        + vmem(8),
        out_specs=tuple(vmem(9)),
        scratch_shapes=[
            pltpu.VMEM((parts, CLP, 256), BF16),
            pltpu.VMEM((parts, CLP, width), BF16),
            whole, whole, whole,
            chain, chain, chain, chain, chain, chain,
            chain,
            pltpu.VMEM((rows, width), BF16),
            pltpu.VMEM((rows, 2 * width), BF16),
            pltpu.VMEM((blocks, 128, model), F32),
            pltpu.VMEM((blocks, 128, model), BF16),
            pltpu.VMEM((blocks, 128, model), BF16),
            pltpu.VMEM((blocks, 128, model // 2), BF16),
            pltpu.VMEM((blocks, 128, model // 2), BF16),
            pltpu.VMEM((rows // 2, model // 2), F32),
            pltpu.VMEM((blocks, 128, model), BF16),
            pltpu.VMEM((SLOTS, 256), BF16),
            pltpu.VMEM((3 * width, model), BF16),
            pltpu.VMEM((3, width // 2, model), BF16),
            pltpu.VMEM((3, width // 2, model), BF16),
            unit, unit, unit, unit, unit, unit,
            pltpu.VMEM((8, model), F32),
            pltpu.VMEM((8, model), F32),
            pltpu.VMEM((parts, 8, model), F32),
            pltpu.VMEM((2, 8, model), F32),
            pltpu.VMEM((2, 8, model), F32),
            pltpu.VMEM((parts,) + owned, BF16),
            pltpu.VMEM((parts,) + owned, BF16),
            pltpu.VMEM((2,) + owned, BF16),
            pltpu.VMEM((rows // 2, model), BF16),
            dma, dma, dma, dma,
        ]
        + [dma((parts,))] * 4
        + [dma((CHUNKS,))] * 10
        + [dma((blocks,))] * 10
        + [dma((3,))] * 2
        + [dma((UNITS,))] * 4
        + [dma((3,))] * 2
        + [dma, dma, dma((parts,)), dma((parts,)), dma((2,)), dma((2,)), dma((parts,)), dma((parts,))],
        compiler_params=pltpu.CompilerParams(
            vmem_limit_bytes=58 << 20, collective_id=1, has_side_effects=True
        ),
        name="tail",
    )(
        lengths, dkv, dkvt, dq, summed, k, v, centre, topk, tm, merged, rows_in, counts,
        clusters.reshape(rows, 1), weight.reshape(3 * width, model), fn, sfn, tokens, gain,
        mgrad.reshape(blocks, 128, model), srow, mid.reshape(blocks, 128, model),
        hsum.reshape(blocks, 128, model), hsum_x.reshape(blocks, 128, model), second_gains,
        sh_keep, sh_given, *ex_parts,
    )


def shards(
    tokens,
    clusters,
    top_keys,
    lengths,
    qkv_weight,
    out_weight,
    first_gain,
    first_bias,
    second_gain,
    second_bias,
    expand_weight,
    shrink_weight,
    cotangent,
):
    parts, n_dp = lax.axis_size("dm"), lax.axis_size("dp")
    pair = n_dp == 2
    weight = jnp.swapaxes(qkv_weight, 1, 2)
    topk = jnp.pad(top_keys, ((0, CLP - CL), (0, 0)), constant_values=-1)
    flat = jnp.pad(top_keys.reshape(-1), (0, SLOTS - CL * TOPK), constant_values=-1)
    (
        first_normed, slot_normed, qs, k, v, ks, vs, kst, vst, starts, rcol, rrow, cls, centre, tm, rows_in,
        merged, counts, out_full, expand_full, shrink_peer,
    ) = front(
        pair, lengths, tokens, clusters, weight, first_gain, first_bias,
        flat.reshape(SLOTS, 1), topk, expand_weight, shrink_weight.T, out_weight, parts,
    )
    if pair:
        shrink_shards = [shrink_weight.T]
        source, _ = lax.optimization_barrier((shrink_weight.T, starts))
        for step in range(1, parts):
            shrink_shards.append(
                lax.ppermute(source, "dm", [(i, (i + step) % parts) for i in range(parts)])
            )
    else:
        expand_full = lax.all_gather(expand_weight, ("dp", "dm"), axis=0, tiled=True)
        shrink_full = lax.all_gather(shrink_weight.T, ("dp", "dm"), axis=0, tiled=True)
        shrink_shards = [shrink_full] + [jnp.zeros((16, 128), BF16)] * (parts - 1)
    attended = exact_forward(starts, qs, cls, kst, vs, rows_in, rcol)
    mid, middle_grad, attended_grad, hidden_sum, out_grad_part, second_parts, *grads = middle(
        pair, tokens, cotangent, attended, out_weight, out_full, expand_full,
        second_gain, second_bias, shrink_shards, shrink_peer,
    )
    out_grad = lax.psum(out_grad_part, ("dp", "dm"))
    hidden_sum_x = lax.ppermute(hidden_sum, "hid", [(i, i ^ 2) for i in range(lax.axis_size("hid"))])
    units = expand_weight.shape[1]
    if pair:
        shrink_keep, shrink_give, *expand_parts = grads
        shrink_given = lax.ppermute(shrink_give, "dp", [(0, 1), (1, 0)])
        expand_parts = [expand_parts[0]] + [
            lax.ppermute(expand_parts[step], "dm", [(i, (i + step) % parts) for i in range(parts)])
            for step in range(1, parts)
        ]
    else:
        summed_grads = lax.psum_scatter(grads[0], ("dp", "dm"), scatter_dimension=0, tiled=True)
        shrink_keep = shrink_given = jnp.zeros((16, 128), BF16)
        expand_parts = [jnp.zeros((2, 16, 128), BF16)] * parts
    dq, dkv, dkvt, summed = exact_backward(
        starts, qs, cls, ks, kst, vst, rows_in, rcol, rrow, attended_grad
    )
    result, tokens_grad, qkv_grad, *gains, expand_grad, shrink_grad = tail(
        pair, lengths, dkv, dkvt, dq, summed, k, v, centre, topk, tm, merged, rows_in, counts, clusters,
        weight, first_normed, slot_normed, tokens, first_gain, middle_grad,
        flat.reshape(1, SLOTS), mid, hidden_sum, hidden_sum_x, second_parts,
        shrink_keep, shrink_given, expand_parts, parts,
    )
    out_grad, result = lax.optimization_barrier((out_grad, result))
    if not pair:
        qkv_grad = lax.psum(qkv_grad, ("dp", "dm"))
        gains = lax.psum(jnp.stack(gains), ("dp", "dm", "hid"))
        summed_grads = summed_grads.astype(F32)
        expand_grad, shrink_grad = summed_grads[:, :units], summed_grads[:, units:]
    return (
        result,
        tokens_grad,
        jnp.swapaxes(qkv_grad.astype(F32), 1, 2),
        out_grad.astype(F32),
        gains[0],
        gains[1],
        gains[2],
        gains[3],
        expand_grad,
        shrink_grad.T,
    )


def solution(mesh):
    in_specs = (
        P(("dp", "dm"), None),
        P(("dp", "dm")),
        P("dp", None),
        P("dp"),
        P(None, None, "hid"),
        P("hid", None),
        P(),
        P(),
        P(),
        P(),
        P(("dp", "dm"), "hid"),
        P("hid", ("dp", "dm")),
        P(("dp", "dm"), None),
    )
    out_specs = (
        P(("dp", "dm"), None),
        P(("dp", "dm"), None),
        P(None, None, "hid"),
        P("hid", None),
        P(),
        P(),
        P(),
        P(),
        P(("dp", "dm"), "hid"),
        P("hid", ("dp", "dm")),
    )
    return jax.shard_map(shards, mesh=mesh, in_specs=in_specs, out_specs=out_specs, check_vma=False)
```

```python
import functools

import jax
import jax.numpy as jnp
from jax import lax
from jax.experimental import pallas as pl
from jax.experimental.pallas import tpu as pltpu
from jax.sharding import PartitionSpec as P

HEAD_DIM = 64
CL = 100
TOPK = 32
CLP = 128
SLOTS = 3328
GROUP = 8
GSLOTS = GROUP * TOPK
GROUPS = SLOTS // GSLOTS
WIN = 160
HALF = SLOTS // 2
CHUNK = 128
CHUNKS = HALF // CHUNK
LAG = 2
CENTRE = 6
CENTRE_TICK = 13
GSTART = 7
UNITS = 8
EPSILON = 1e-05
NEGATIVE = -1e30
HIGHEST = lax.Precision.HIGHEST
F32 = jnp.float32
BF16 = jnp.bfloat16
MESH = pl.DeviceIdType.MESH
NT = (((1,), (1,)), ((), ()))
TN = (((0,), (0,)), ((), ()))
SCALE = HEAD_DIM ** (-0.5)


def dot(a, b):
    return jnp.dot(a, b, preferred_element_type=F32)


def dot_nt(a, b):
    return lax.dot_general(a, b, NT, preferred_element_type=F32)


def dot_tn(a, b):
    return lax.dot_general(a, b, TN, preferred_element_type=F32)


def iota(shape, dim):
    return lax.broadcasted_iota(jnp.int32, shape, dim)


def norm_parts(values):
    centred = values - jnp.mean(values, -1, keepdims=True)
    spread = lax.rsqrt(jnp.mean(centred * centred, -1, keepdims=True) + EPSILON)
    return (centred * spread, spread)


def norm_back(upstream, normed, spread, norm_gain):
    through = upstream * norm_gain
    inner = (
        through
        - jnp.mean(through, -1, keepdims=True)
        - normed * jnp.mean(through * normed, -1, keepdims=True)
    )
    return (spread * inner, jnp.sum(upstream * normed, 0), jnp.sum(upstream, 0))


def head_lanes(width, head):
    lane = iota((1, width), 1)
    return lane // HEAD_DIM == head


def block_diagonal(rows, heads):
    width = rows.shape[1]
    zero = jnp.zeros_like(rows)
    return jnp.concatenate(
        [jnp.where(head_lanes(width, h), rows, zero) for h in range(heads)], axis=0
    )


def block_diagonal_turned(turned, heads):
    zero = jnp.zeros((HEAD_DIM, turned.shape[1]), turned.dtype)
    columns = []
    for h in range(heads):
        mine = turned[h * HEAD_DIM : (h + 1) * HEAD_DIM]
        columns.append(jnp.concatenate([mine if i == h else zero for i in range(heads)], axis=0))
    return jnp.concatenate(columns, axis=1)


def diagonal_blocks_turned(full, heads):
    rows, size = full.shape[0] // heads, full.shape[1] // heads
    return jnp.concatenate(
        [full[h * rows : (h + 1) * rows, h * size : (h + 1) * size] for h in range(heads)], axis=0
    )


def diagonal_blocks(full, heads):
    rows, width = full.shape[0] // heads, full.shape[1]
    out = full[:rows]
    for h in range(1, heads):
        out = jnp.where(head_lanes(width, h), full[h * rows : (h + 1) * rows], out)
    return out


def vmem(n):
    return [pl.BlockSpec(memory_space=pltpu.VMEM)] * n


def remote(src, dst, send, recv, device):
    return pltpu.make_async_remote_copy(
        src_ref=src, dst_ref=dst, send_sem=send, recv_sem=recv, device_id=device,
        device_id_type=MESH,
    )


def greet(devices):
    barrier = pltpu.get_barrier_semaphore()
    for device in devices:
        pl.semaphore_signal(barrier, inc=1, device_id=device, device_id_type=MESH)
    return barrier


def small_exchange(buf, sends, recvs, me, parts):
    return [
        remote(
            buf.at[me], buf.at[me], sends.at[step], recvs.at[step],
            {"dm": lax.rem(me + step, parts)},
        )
        for step in range(1, parts)
    ]


def when_in(i, count, work):
    @pl.when((i >= 0) & (i < count))
    def _():
        work(i)


def aligned(start, size):
    return pl.ds(pl.multiple_of(start, 128), size)


def sequence_masks(lengths, topk, rows):
    own_start = lax.axis_index("dm") * rows
    key_second = iota((1, rows), 1) + own_start >= lengths[0]
    centre_second = topk[:, :1] >= lengths[0]
    return key_second == centre_second


def front_kernel(
    pair, lengths, tok, crow, weight, gain, bias, scol, topk, wexp, wshr, wout,
    fn_hbm, sfn_hbm, qs_out, k_out, v_out, ks_out, vs_out, kst_out, vst_out, starts_out, rcol_out, rrow_out,
    cls_out, centre_out, tm_out, rows_out, merged_out, count_out, wall_out, wfull_out, shr_peer_out, ccol,
    fn_out, sfn_out, q_ref, member_ref, csum, rbuf, sbuf, own, to_right, to_left, from_left, from_right,
    rsend, rrecv, ssend, srecv,
    send_right, recv_left, send_left, recv_right, send_x, recv_x, send_core, recv_core,
    send_relay, recv_relay, osend, orecv, wsend, wsend_left, wrecv, ysend, yrecv, psend, precv, local_sems,
):
    rows, model = tok.shape
    width = weight.shape[1]
    heads = width // HEAD_DIM
    half_width = model // 2
    tiles = rows // 128
    parts = lax.axis_size("dm")
    me, hid, dp = lax.axis_index("dm"), lax.axis_index("hid"), lax.axis_index("dp")
    core, side = lax.rem(hid, 2), hid // 2
    core_peer = {"hid": hid + 1 - 2 * core}
    x_peer = {"hid": hid + 2 - 4 * side}
    lane = iota((128, 128), 1)
    columns = aligned(side * half_width, half_width)
    other_columns = aligned((1 - side) * half_width, half_width)
    own_start = me * rows

    greeted = [{"dm": lax.rem(me + step, parts)} for step in range(1, parts)]
    greeted += [core_peer, x_peer]
    if pair:
        greeted.append({"dp": 1 - dp})
    barrier = greet(greeted)

    out_rows = pl.ds(pl.multiple_of(hid * width, 64), width)
    out_own = pltpu.make_async_copy(wout, wall_out.at[out_rows, :], local_sems.at[0])
    out_own.start()
    out_x_rows = pl.ds(pl.multiple_of((hid + 2 - 4 * side) * width, 64), width)
    out_copies = [
        remote(wout, wall_out.at[out_rows, :], osend.at[0], orecv.at[0], core_peer),
        remote(wout, wall_out.at[out_rows, :], osend.at[1], orecv.at[1], x_peer),
        remote(
            wall_out.at[out_x_rows, :], wall_out.at[out_x_rows, :], osend.at[2], orecv.at[2], core_peer
        ),
    ]
    if pair:
        shard = wexp.shape[0]

        def shard_rows(d, m):
            return pl.ds(pl.multiple_of((d * parts + m) * shard, 32), shard)

        mine = shard_rows(dp, me)
        def whole_shard(origin):
            return wfull_out.at[shard_rows(dp, origin), :]

        def hop(origin, source, sends, neighbour):
            return remote(
                source, whole_shard(origin), sends.at[origin], wrecv.at[origin],
                {"dm": lax.rem(neighbour, parts)},
            )

        def across(origin, source):
            return remote(
                source, whole_shard(origin), ysend.at[origin], yrecv.at[origin], {"dp": 1 - dp}
            )

        def pass_on(step):
            @pl.when(me >= step)
            def _():
                origin = me - step
                block = whole_shard(origin)
                hop(origin, block, wsend, me + 1).wait_recv()
                across(origin, block).start()

                @pl.when(me < parts - 1)
                def _():
                    hop(origin, block, wsend, me + 1).start()

            @pl.when(me + step < parts)
            def _():
                origin = me + step
                block = whole_shard(origin)
                hop(origin, block, wsend_left, me + parts - 1).wait_recv()
                across(origin, block).start()

                @pl.when(me > 0)
                def _():
                    hop(origin, block, wsend_left, me + parts - 1).start()

        shard_own = pltpu.make_async_copy(wexp, wfull_out.at[mine, :], local_sems.at[1])
        shard_own.start()
        shrink_peer = remote(wshr, shr_peer_out, psend, precv, {"dp": 1 - dp})

    pl.semaphore_wait(barrier, len(greeted))
    if pair:
        across(me, wexp).start()
        shrink_peer.start()

        @pl.when(me < parts - 1)
        def _():
            hop(me, wexp, wsend, me + 1).start()

        @pl.when(me > 0)
        def _():
            hop(me, wexp, wsend_left, me + parts - 1).start()

    out_copies[0].start()
    out_copies[1].start()

    def first_norm(i, carry):
        at = aligned(i * 256, 256)
        normed, _ = norm_parts(tok[at, :].astype(F32))
        fn_out[at, :] = (normed * gain[...][None] + bias[...][None]).astype(BF16)
        return carry

    lax.fori_loop(0, rows // 256, first_norm, 0)
    fn_copy = pltpu.make_async_copy(fn_out, fn_hbm, local_sems.at[2])
    fn_copy.start()

    @pl.when(me == 0)
    def _():
        from_left[...] = jnp.zeros_like(from_left)

    @pl.when(me == parts - 1)
    def _():
        from_right[...] = jnp.zeros_like(from_right)

    def chunk_rows(i, which):
        return aligned(which * HALF + i * CHUNK, CHUNK)

    def right_copy(i):
        return remote(
            to_right.at[i], from_left.at[i], send_right.at[i], recv_left.at[i],
            {"dm": lax.rem(me + 1, parts)},
        )

    def left_copy(i):
        return remote(
            to_left.at[i], from_right.at[i], send_left.at[i], recv_right.at[i],
            {"dm": lax.rem(me + parts - 1, parts)},
        )

    def x_copy(i):
        block = sfn_out.at[chunk_rows(i, core), columns]
        return remote(block, block, send_x.at[i], recv_x.at[i], x_peer)

    def core_copy(i):
        block = sfn_out.at[chunk_rows(i, core), columns]
        return remote(block, block, send_core.at[i], recv_core.at[i], core_peer)

    def relay_copy(i):
        block = sfn_out.at[chunk_rows(i, core), other_columns]
        return remote(block, block, send_relay.at[i], recv_relay.at[i], core_peer)

    def make_own(first, count):
        at = aligned(core * HALF + first * CHUNK, count * CHUNK)
        chosen = (scol[at, :] == iota((count * CHUNK, rows), 1) + own_start).astype(BF16)
        picked = dot(chosen, fn_out[:, columns]).astype(BF16)
        for i in range(count):
            own[first + i + (first + i >= CENTRE)] = picked[i * CHUNK : (i + 1) * CHUNK]

    def go_right(i):
        @pl.when(me > 0)
        def _():
            right_copy(i).wait_recv()

        @pl.when(me < parts - 1)
        def _():
            to_right[i] = own[i] + from_left[i]
            right_copy(i).start()

    def go_left(i):
        @pl.when(me < parts - 1)
        def _():
            left_copy(i).wait_recv()

        @pl.when(me > 0)
        def _():
            to_left[i] = own[i] + from_right[i]
            left_copy(i).start()

    def slot_chunk(place):
        return jnp.where(place > CENTRE, place - 1, place)

    def finish(place):
        @pl.when(place == CENTRE)
        def _():
            total = own[place].astype(F32) + from_left[place].astype(F32)
            csum[...] = total + from_right[place].astype(F32)

        @pl.when(place != CENTRE)
        def _():
            i = slot_chunk(place)
            sfn_out[chunk_rows(i, core), columns] = (
                own[place] + from_left[place] + from_right[place]
            )
            x_copy(i).start()
            core_copy(i).start()

    def relay(place):
        @pl.when(place != CENTRE)
        def _():
            i = slot_chunk(place)
            x_copy(i).wait_recv()
            relay_copy(i).start()

    far = jnp.maximum(me, parts - 1 - me)

    def ticks(first, last):
        def tick(t, carry):
            when_in(t - LAG * me, CHUNKS + 1, go_right)
            when_in(t - LAG * (parts - 1 - me), CHUNKS + 1, go_left)
            when_in(t - LAG * far, CHUNKS + 1, finish)
            when_in(t - LAG * far - LAG, CHUNKS + 1, relay)
            return carry

        lax.fori_loop(first, last, tick, 0)

    def project(part):
        at = aligned(part * (rows // 2), rows // 2)
        first = fn_out[at, :]
        q_ref[at, :] = dot_nt(first, weight[0]).astype(BF16)
        k_out[at, :] = dot_nt(first, weight[1]).astype(BF16)
        v_out[at, :] = dot_nt(first, weight[2]).astype(BF16)

    lower = (iota((128, 128), 0) > iota((128, 128), 1)).astype(BF16)

    def count_tile(i, running):
        at = aligned(i * 128, 128)
        clusters = jnp.broadcast_to(crow[pl.ds(i, 1), :].astype(F32), (128, 128))
        clusters = jnp.transpose(clusters).astype(jnp.int32)
        ccol[at, :] = clusters[:, :1]
        member = (clusters == lane).astype(F32)
        low = member.astype(BF16)
        member_ref[at, :] = low
        earlier = dot(lower, low) + running
        rcol_out[at, :] = jnp.sum(member * earlier, 1, keepdims=True)
        return running + jnp.sum(member, 0, keepdims=True)

    def place(i, carry):
        at = aligned(i * 256, 256)
        rank_row = rrow_out[:1, :].astype(jnp.int32)
        chosen = (iota((256, rows), 0) + i * 256 == rank_row).astype(BF16)
        qs_out[at, :] = (dot(chosen, q_ref[...]) * SCALE).astype(BF16)
        sorted_member = dot(chosen, member_ref[...])
        cls_out[at, :] = jnp.sum(
            sorted_member * iota((256, 128), 1).astype(F32), 1, keepdims=True
        ).astype(jnp.int32)
        return carry

    make_own(0, 4)
    ticks(0, 1)
    project(0)
    ticks(1, 2)
    make_own(4, 4)
    ticks(2, 4)
    project(1)
    ticks(4, 5)
    if pair:
        pass_on(1)
    counts = lax.fori_loop(0, tiles, count_tile, jnp.zeros((1, 128), F32))
    extended = jnp.concatenate([q_ref[...], jnp.ones((rows, 256 - width), BF16)], axis=1)
    sums = dot_tn(member_ref[...], extended)
    digits = jnp.floor(sums * 0.03125)
    wide = iota((CLP, 256), 1)
    packed = jnp.where(
        wide == width, digits, jnp.where(wide == width + 1, sums - 32.0 * digits, sums)
    )
    own[CENTRE] = jnp.concatenate(
        [packed, jnp.zeros((CLP, half_width - 256), F32)], axis=1
    ).astype(BF16)
    ticks(5, 6)
    make_own(8, CHUNKS - 8)
    ticks(6, 7)
    before = (iota((128, 128), 0) < iota((128, 128), 1)).astype(F32)
    starts = jnp.dot(
        jnp.broadcast_to(counts, (8, 128)), before, precision=HIGHEST, preferred_element_type=F32
    )
    starts_out[...] = starts.astype(jnp.int32)

    def ranks(i, carry):
        at = aligned(i * 128, 128)
        member = member_ref[at, :].astype(F32)
        rank = rcol_out[at, :] + jnp.sum(member * starts[:1], 1, keepdims=True)
        rcol_out[at, :] = rank
        turned = jnp.transpose(jnp.broadcast_to(rank, (128, 128)))
        rrow_out[:, at] = turned[:8]
        return carry

    lax.fori_loop(0, tiles, ranks, 0)
    ticks(7, 8)
    if pair:
        pass_on(2)
    here = iota((CLP, rows), 1) + own_start
    hit = topk[:, :1] == here
    for t in range(1, TOPK):
        hit = hit | (topk[:, t : t + 1] == here)
    tm_out[...] = hit.astype(F32).astype(BF16)
    ticks(8, 9)

    lax.fori_loop(0, rows // 512, place, 0)
    ticks(9, 10)
    lax.fori_loop(rows // 512, rows // 256, place, 0)
    qs_out[rows:, :] = jnp.zeros((WIN, width), BF16)
    cls_out[rows:, :] = jnp.full((WIN, 1), -1, jnp.int32)
    ticks(10, CENTRE_TICK)
    gathered = csum[...]
    count = jnp.maximum(
        32.0 * gathered[:, width : width + 1] + gathered[:, width + 1 : width + 2], 1.0
    )
    count_out[...] = jnp.broadcast_to(count, (CLP, 128))
    centre = (gathered[:, :width] / count).astype(BF16)
    centre_out[...] = centre
    same = sequence_masks(lengths, topk, rows)
    stats = jnp.zeros((CLP, 128), F32)
    rest = jnp.zeros((CLP, width), F32)
    for h in range(heads):
        top = tm_out[...].astype(F32)
        mine_lanes = head_lanes(width, h)
        scores = dot_nt(jnp.where(mine_lanes, centre, jnp.zeros_like(centre)), k_out[...]) * SCALE
        scores = jnp.where(same, scores, NEGATIVE)
        largest = jnp.max(scores, 1, keepdims=True)
        raised = jnp.exp(scores - largest)
        total = jnp.sum(raised, 1, keepdims=True)
        within = raised * top
        mass = jnp.sum(within, 1, keepdims=True)
        rest = jnp.where(mine_lanes, dot((raised - within).astype(BF16), v_out[...]), rest)
        stats = jnp.where(lane == h, largest, stats)
        stats = jnp.where(lane == 8 + h, total, stats)
        stats = jnp.where(lane == 16 + h, mass, stats)
    rbuf[me] = rest.astype(BF16)
    sbuf[me] = jnp.transpose(stats)[:24]
    rest_copies = small_exchange(rbuf, rsend, rrecv, me, parts)
    stat_copies = small_exchange(sbuf, ssend, srecv, me, parts)
    ticks(CENTRE_TICK, CENTRE_TICK + 2)
    out_copies[1].wait_recv()
    out_copies[2].start()
    if pair:
        pass_on(3)
    ticks(CENTRE_TICK + 2, CENTRE_TICK + 3)
    early = CHUNKS // 2
    ticks(CENTRE_TICK + 3, 19)

    def arrive(i, carry):
        core_copy(i).wait_recv()
        relay_copy(i).wait_recv()
        return carry

    def project_slots(first, count):
        for which in range(2):
            at = pl.ds(which * HALF + first * CHUNK, count * CHUNK)
            block = sfn_out[at, :]
            for which_weight, out, turned in ((1, ks_out, kst_out), (2, vs_out, vst_out)):
                product = dot_nt(block, weight[which_weight])
                out[at, :] = product.astype(BF16)
                turned[:, at] = jnp.transpose(product).astype(BF16)

    lax.fori_loop(0, early, arrive, 0)
    project_slots(0, early)
    ticks(19, 20)
    for copy in rest_copies + stat_copies:
        copy.start()
    ticks(20, CHUNKS + 1 + LAG * parts)
    lax.fori_loop(early, CHUNKS, arrive, 0)
    sfn_copy = pltpu.make_async_copy(sfn_out, sfn_hbm, local_sems.at[3])
    sfn_copy.start()
    project_slots(early, CHUNKS - early)
    for copy in rest_copies + stat_copies:
        copy.wait_recv()
    largest = sbuf[0][:8]
    for d in range(1, parts):
        largest = jnp.maximum(largest, sbuf[d][:8])
    total = jnp.zeros((8, 128), F32)
    mass = jnp.zeros((8, 128), F32)
    factors = []
    for d in range(parts):
        factor = jnp.exp(sbuf[d][:8] - largest)
        total += factor * sbuf[d][8:16]
        mass += factor * sbuf[d][16:24]
        factors.append(factor)
    live = iota((8, 128), 0) < heads
    total = jnp.where(live, total, 1.0)
    mass = mass / total
    table = [largest, total, mass] + [factor / total for factor in factors]
    table.append(jnp.zeros((128 - 8 * len(table), 128), F32))
    columns_table = jnp.transpose(jnp.concatenate(table, axis=0))
    merged_out[...] = columns_table
    mass_rows = jnp.zeros((CLP, width), F32)
    rest_rows = jnp.zeros((CLP, width), F32)
    for h in range(heads):
        mine_lanes = head_lanes(width, h)
        mass_rows = jnp.where(mine_lanes, columns_table[:, 16 + h : 17 + h], mass_rows)
        rest = jnp.zeros((CLP, width), F32)
        for d in range(parts):
            lane_at = 24 + 8 * d + h
            rest += columns_table[:, lane_at : lane_at + 1] * rbuf[d].astype(F32)
        rest_rows = jnp.where(mine_lanes, rest, rest_rows)
    rows_out[:, :width] = mass_rows
    rows_out[:, width:] = rest_rows

    def drain(i, carry):
        @pl.when(me < parts - 1)
        def _():
            right_copy(i).wait_send()

        @pl.when(me > 0)
        def _():
            left_copy(i).wait_send()

        return carry

    def drain_slots(i, carry):
        x_copy(i).wait_send()
        core_copy(i).wait_send()
        relay_copy(i).wait_send()
        return carry

    lax.fori_loop(0, CHUNKS + 1, drain, 0)
    lax.fori_loop(0, CHUNKS, drain_slots, 0)
    for copy in rest_copies + stat_copies + out_copies:
        copy.wait_send()
    out_copies[0].wait_recv()
    out_copies[2].wait_recv()
    if pair:
        for origin in range(parts):
            across(origin, wexp).wait()

            @pl.when((me < parts - 1) & (origin <= me))
            def _():
                hop(origin, wexp, wsend, me + 1).wait_send()

            @pl.when((me > 0) & (origin >= me))
            def _():
                hop(origin, wexp, wsend_left, me + parts - 1).wait_send()

        shrink_peer.wait()
        shard_own.wait()
    out_own.wait()
    fn_copy.wait()
    sfn_copy.wait()


def front(pair, lengths, tokens, clusters, weight, gain, bias, scol, topk, wexp, wshr, wout, parts):
    rows, model = tokens.shape
    width = weight.shape[1]
    shape = jax.ShapeDtypeStruct
    dma = pltpu.SemaphoreType.DMA
    chain = pltpu.VMEM((CHUNKS + 1, CHUNK, model // 2), BF16)
    whole = (model, wexp.shape[1]) if pair else (16, 128)
    anywhere = [pl.BlockSpec(memory_space=pl.ANY)]
    return pl.pallas_call(
        functools.partial(front_kernel, pair),
        out_shape=(
            shape(tokens.shape, BF16),
            shape((SLOTS, model), BF16),
            shape((rows + WIN, width), BF16),
            shape((rows, width), BF16),
            shape((rows, width), BF16),
            shape((SLOTS, width), BF16),
            shape((SLOTS, width), BF16),
            shape((width, SLOTS), BF16),
            shape((width, SLOTS), BF16),
            shape((8, 128), jnp.int32),
            shape((rows, 1), F32),
            shape((8, rows), F32),
            shape((rows + WIN, 1), jnp.int32),
            shape((CLP, width), BF16),
            shape((CLP, rows), BF16),
            shape((CLP, 2 * width), F32),
            shape((CLP, 128), F32),
            shape((CLP, 128), F32),
            shape((lax.axis_size("hid") * width, model), BF16),
            shape(whole, BF16),
            shape(wshr.shape, BF16),
            shape((rows, 1), jnp.int32),
        ),
        in_specs=[pl.BlockSpec(memory_space=pltpu.SMEM)] + vmem(7) + anywhere * 3,
        out_specs=tuple(anywhere * 2 + vmem(16) + anywhere * 3 + vmem(1)),
        scratch_shapes=[
            pltpu.VMEM((rows, model), BF16),
            pltpu.VMEM((SLOTS, model), BF16),
            pltpu.VMEM((rows, width), BF16),
            pltpu.VMEM((rows, 128), BF16),
            pltpu.VMEM((CLP, model // 2), F32),
            pltpu.VMEM((parts, CLP, width), BF16),
            pltpu.VMEM((parts, 24, 128), F32),
            chain, chain, chain, chain, chain,
        ]
        + [dma((parts,))] * 4
        + [dma((CHUNKS + 1,))] * 10
        + [dma((3,))] * 2
        + [dma((parts,))] * 5
        + [dma, dma, dma((4,))],
        compiler_params=pltpu.CompilerParams(
            vmem_limit_bytes=56 << 20, collective_id=0, has_side_effects=True
        ),
        name="front",
    )(
        lengths, tokens, clusters.reshape(rows // 128, 128), weight, gain, bias, scol, topk,
        wexp, wshr, wout,
    )


UNROLL = 4
FORWARD_UNROLL = (4, 2)
BACKWARD_UNROLL = (2, 2)
SMALL = 64


def list_windows(starts, rows, lists):
    big_group, big_row, small_group, small_row = lists

    def one_group(g, counts):
        big, small = counts
        first, last = starts[0, g * GROUP], starts[0, g * GROUP + GROUP]
        base = first // 16 * 16
        span = jnp.where(last > first, last - base, 0)
        short = (span > 0) & (span <= SMALL)
        windows = jnp.where(span > SMALL, (span + WIN - 1) // WIN, 0)

        def one(w, carry):
            big_group[big + w] = g
            big_row[big + w] = base + w * WIN
            return carry

        lax.fori_loop(0, windows, one, 0)
        small_group[small] = g
        small_row[small] = base
        return big + windows, small + jnp.where(short, 1, 0)

    big, small = lax.fori_loop(0, GROUPS, one_group, (0, 0))
    for i in range(UNROLL):
        big_group[big + i] = 0
        big_row[big + i] = rows
        small_group[small + i] = 0
        small_row[small + i] = rows
    return big, small


def each_window(starts, rows, lists, window, unroll):
    big, small = list_windows(starts, rows, lists)
    for count, size, group_at, row_at, times in (
        (big, WIN, lists[0], lists[1], unroll[0]),
        (small, SMALL, lists[2], lists[3], unroll[1]),
    ):

        def several(n, carry):
            for i in range(times):
                window(*window_at(starts, group_at, row_at, n * times + i, size))
            return carry

        lax.fori_loop(0, (count + times - 1) // times, several, 0)


def window_probs(scores, mine, inside, h):
    part = jnp.where(mine, scores[:, h * GSLOTS : (h + 1) * GSLOTS], NEGATIVE)
    raised = jnp.exp(part - jnp.max(part, 1, keepdims=True))
    inverse = jnp.where(inside, 1.0 / jnp.sum(raised, 1, keepdims=True), 0.0)
    return raised * inverse


def window_at(starts, group_at, row_at, i, size):
    g = group_at[i]
    row = pl.multiple_of(row_at[i], 16)
    at = pl.ds(pl.multiple_of(g * GSLOTS, GSLOTS), GSLOTS)
    place = iota((size, 1), 0) + row
    inside = (place >= starts[0, g * GROUP]) & (place < starts[0, g * GROUP + GROUP])
    return size, g, pl.ds(row, size), at, inside


def exact_forward_kernel(
    starts, qs, cls, kt_hbm, vs_hbm, both, rcol, att_out, att_s, mix_s, kt, vs, sems, *lists
):
    rows, width = rcol.shape[0], qs.shape[1]
    heads = width // HEAD_DIM
    copies = [
        pltpu.make_async_copy(kt_hbm, kt, sems.at[0]),
        pltpu.make_async_copy(vs_hbm, vs, sems.at[1]),
    ]
    for copy in copies:
        copy.start()
    high = both[...].astype(BF16)
    low = (both[...] - high.astype(F32)).astype(BF16)
    step = (rows + WIN) // 5

    def spread(i, carry):
        at = pl.ds(pl.multiple_of(i * step, 16), step)
        member = (cls[at, :] == iota((step, 128), 1)).astype(BF16)
        mix_s[at, :] = dot(member, high) + dot(member, low)
        return carry

    lax.fori_loop(0, 5, spread, 0)
    for copy in copies:
        copy.wait()

    def window(size, g, here, at, inside):
        keys = block_diagonal_turned(kt[:, at], heads)
        values = block_diagonal(vs[at, :], heads)
        mine = cls[here, :] == iota((size, GSLOTS), 1) // TOPK + g * GROUP
        scores = dot(qs[here, :], keys)
        weights = [window_probs(scores, mine, inside, h).astype(BF16) for h in range(heads)]
        out = dot(jnp.concatenate(weights, axis=1), values)
        mix = mix_s[here, :]
        att_s[here, :] = jnp.where(inside, mix[:, :width] * out + mix[:, width:], att_s[here, :])

    each_window(starts, rows, lists, window, FORWARD_UNROLL)

    def unplace(i, carry):
        at = pl.ds(pl.multiple_of(i * 256, 256), 256)
        chosen = (iota((256, rows), 1) == rcol[at, :].astype(jnp.int32)).astype(BF16)
        att_out[at, :] = dot(chosen, att_s[:rows, :].astype(BF16)).astype(BF16)
        return carry

    lax.fori_loop(0, rows // 256, unplace, 0)


ANYWHERE = pl.BlockSpec(memory_space=pl.ANY)
LISTED = 64


def exact_forward(starts, qs, cls, ks, vs, both, rcol):
    rows, width = rcol.shape[0], qs.shape[1]
    shape = jax.ShapeDtypeStruct
    return pl.pallas_call(
        exact_forward_kernel,
        out_shape=shape((rows, width), BF16),
        in_specs=[pl.BlockSpec(memory_space=pltpu.SMEM)] + vmem(2) + [ANYWHERE] * 2 + vmem(2),
        out_specs=vmem(1)[0],
        scratch_shapes=[
            pltpu.VMEM((rows + WIN, width), F32),
            pltpu.VMEM((rows + WIN, 2 * width), F32),
            pltpu.VMEM((width, SLOTS), BF16),
            pltpu.VMEM((SLOTS, width), BF16),
            pltpu.SemaphoreType.DMA((2,)),
        ]
        + [pltpu.SMEM((LISTED,), jnp.int32)] * 4,
        compiler_params=pltpu.CompilerParams(vmem_limit_bytes=62 << 20),
        name="exact_forward",
    )(starts, qs, cls, ks, vs, both, rcol)


def exact_backward_kernel(
    starts, qs, cls, ks_hbm, kt_hbm, vt_hbm, rows_in, rcol, rrow, grad,
    dq_out, dkvt_out, centre_out,
    grad_s, mass_s, dq_s, part_s, dkv_s, ks, kt, vt, sems, *lists,
):
    rows, width = rcol.shape[0], qs.shape[1]
    heads = width // HEAD_DIM
    copies = [
        pltpu.make_async_copy(ks_hbm, ks, sems.at[0]),
        pltpu.make_async_copy(kt_hbm, kt, sems.at[1]),
        pltpu.make_async_copy(vt_hbm, vt, sems.at[2]),
    ]
    for copy in copies:
        copy.start()
    mass_rows = rows_in[:, :width]
    high = mass_rows.astype(BF16)
    low = (mass_rows - high.astype(F32)).astype(BF16)
    rank_row = rrow[:1, :].astype(jnp.int32)

    def place(i, carry):
        at = pl.ds(pl.multiple_of(i * 256, 256), 256)
        chosen = (iota((256, rows), 0) + i * 256 == rank_row).astype(BF16)
        grad_s[at, :] = dot(chosen, grad[...]).astype(BF16)
        member = (cls[at, :] == iota((256, 128), 1)).astype(BF16)
        mass_s[at, :] = dot(member, high) + dot(member, low)
        return carry

    lax.fori_loop(0, rows // 256, place, 0)
    grad_s[rows:, :] = jnp.zeros((WIN, width), BF16)
    mass_s[rows:, :] = jnp.zeros((WIN, width), F32)
    dkv_s[...] = jnp.zeros_like(dkv_s)
    for copy in copies:
        copy.wait()

    def window(size, g, here, at, inside):
        keys = block_diagonal(ks[at, :], heads)
        mine = cls[here, :] == iota((size, GSLOTS), 1) // TOPK + g * GROUP
        query, upstream = qs[here, :], grad_s[here, :]
        scores = dot(query, block_diagonal_turned(kt[:, at], heads))
        against = dot(upstream, block_diagonal_turned(vt[:, at], heads))
        mass = mass_s[here, :]
        weights, score_grads = [], []
        mass_part = jnp.zeros((size, width), F32)
        for h in range(heads):
            cut = slice(h * GSLOTS, (h + 1) * GSLOTS)
            probs = window_probs(scores, mine, inside, h)
            meeting = jnp.sum(probs * against[:, cut], 1, keepdims=True)
            weighted = probs * mass[:, h * HEAD_DIM : h * HEAD_DIM + 1]
            weights.append(weighted.astype(BF16))
            score_grads.append((weighted * (against[:, cut] - meeting)).astype(BF16))
            mass_part = jnp.where(head_lanes(width, h), meeting, mass_part)
        score_grad = jnp.concatenate(score_grads, axis=1)
        weight = jnp.concatenate(weights, axis=1)
        dq = dot(score_grad, keys) * SCALE
        dq_s[here, :] = jnp.where(inside, dq, dq_s[here, :])
        part_s[here, :] = jnp.where(inside, mass_part, part_s[here, :])
        pair = jnp.concatenate(
            [
                diagonal_blocks_turned(dot_tn(query, score_grad), heads),
                diagonal_blocks_turned(dot_tn(upstream, weight), heads),
            ],
            axis=0,
        )
        dkv_s[:, at] = dkv_s[:, at] + pair

    each_window(starts, rows, lists, window, BACKWARD_UNROLL)
    centre_out[...] = jnp.zeros_like(centre_out)

    def finish_group(g, carry):
        at = pl.ds(pl.multiple_of(g * GSLOTS, GSLOTS), GSLOTS)
        dkvt_out[:, at] = dkv_s[:, at].astype(BF16)
        return carry

    lax.fori_loop(0, GROUPS, finish_group, 0)

    def unplace(i, carry):
        at = pl.ds(pl.multiple_of(i * 256, 256), 256)
        chosen = (iota((256, rows), 1) == rcol[at, :].astype(jnp.int32)).astype(BF16)
        dq_out[at, :] = dot(chosen, dq_s[:rows, :].astype(BF16)).astype(BF16)
        member = (cls[at, :] == iota((256, 128), 1)).astype(BF16)
        pair = jnp.concatenate([part_s[at, :].astype(BF16), grad_s[at, :]], axis=1)
        centre_out[...] += dot_tn(member, pair)
        return carry

    lax.fori_loop(0, rows // 256, unplace, 0)


def exact_backward(starts, qs, cls, ks, kt, vt, rows_in, rcol, rrow, grad):
    rows, width = rcol.shape[0], qs.shape[1]
    shape = jax.ShapeDtypeStruct
    return pl.pallas_call(
        exact_backward_kernel,
        out_shape=(
            shape((rows, width), BF16),
            shape((2 * width, SLOTS), BF16),
            shape((CLP, 2 * width), F32),
        ),
        in_specs=[pl.BlockSpec(memory_space=pltpu.SMEM)] + vmem(2) + [ANYWHERE] * 3 + vmem(4),
        out_specs=tuple(vmem(3)),
        scratch_shapes=[
            pltpu.VMEM((rows + WIN, width), BF16),
            pltpu.VMEM((rows + WIN, width), F32),
            pltpu.VMEM((rows + WIN, width), F32),
            pltpu.VMEM((rows + WIN, width), F32),
            pltpu.VMEM((2 * width, SLOTS), F32),
            pltpu.VMEM((SLOTS, width), BF16),
            pltpu.VMEM((width, SLOTS), BF16),
            pltpu.VMEM((width, SLOTS), BF16),
            pltpu.SemaphoreType.DMA((3,)),
        ]
        + [pltpu.SMEM((LISTED,), jnp.int32)] * 4,
        compiler_params=pltpu.CompilerParams(vmem_limit_bytes=62 << 20),
        name="exact_backward",
    )(starts, qs, cls, ks, kt, vt, rows_in, rcol, rrow, grad)


def gelu_parts(values):
    slope = 0.7978845608028654
    squared = values * values
    turned = jnp.tanh(slope * values * (1.0 + 0.044715 * squared))
    half = 0.5 * (1.0 + turned)
    rise = half + 0.5 * slope * values * (1.0 - turned * turned) * (1.0 + 0.134145 * squared)
    return (values * half, rise)


def middle_kernel(
    pair, parts, tok, cot, att, wout_own, wout, wexp, gain, bias, shr_own, shr_one, shr_two, shr_three, shr_peer,
    mid_out, mgrad_out, agrad_out, hsum_out, wo_out, gains_out, *refs,
):
    grad_outs, refs = refs[: 2 + parts if pair else 1], refs[2 + parts if pair else 1 :]
    middle_body(
        pair, tok, cot, att, wout_own, wout, wexp, gain, bias,
        (shr_own, shr_one, shr_two, shr_three), shr_peer, mid_out, mgrad_out, agrad_out, hsum_out, wo_out, gains_out, grad_outs, *refs,
    )


def middle_body(
    pair, tok, cot, att, wout_own, wout, wexp, gain, bias, shards, shr_peer,
    mid_out, mgrad_out, agrad_out, hsum_out, wo_out, gains_out, grad_outs,
    wshr_ref, att_peer, cat, xcat, sn, act, hg, sp_own, sp_send, sp_recv, hp_own, hp_send, hp_recv,
    sx_send, sx_recv, branch, kept,
    asend, arecv, xsend, xrecv, rsend, rrecv, ssend, srecv, hsend, hrecv, sxs, sxr, bsend, brecv,
    wysend, wyrecv,
):
    rows, width = att.shape
    model = tok.shape[1]
    half_width = 2 * width
    half_rows = rows // 2
    blocks = half_rows // 128
    hid = lax.axis_index("hid")
    core, side = lax.rem(hid, 2), hid // 2
    core_peer = {"hid": hid + 1 - 2 * core}
    x_peer = {"hid": hid + 2 - 4 * side}

    dp = lax.axis_index("dp")
    greeted = [core_peer, x_peer] + ([{"dp": 1 - dp}] if pair else [])
    barrier = greet(greeted)
    gains_out[...] = jnp.zeros_like(gains_out)
    pl.semaphore_wait(barrier, len(greeted))

    units = wexp.shape[1]
    if pair:
        wshr = wshr_ref
        n_dm, my_dm = lax.axis_size("dm"), lax.axis_index("dm")
        shard = model // (2 * n_dm)

        def shard_rows(d, step):
            owner = lax.rem(my_dm + n_dm - step, n_dm)
            return pl.ds(pl.multiple_of((d * n_dm + owner) * shard, 32), shard)

        shard_copies = [
            remote(
                shards[step], wshr.at[shard_rows(dp, step), :], wysend.at[step], wyrecv.at[step],
                {"dp": 1 - dp},
            )
            for step in range(1, n_dm)
        ]
    else:
        wshr = shards[0]

    def block_rows(j, which):
        return pl.ds(pl.multiple_of(which * half_rows + j * 128, 128), 128)

    def own_rows(j):
        return pl.ds(pl.multiple_of(j * 128, 128), 128)

    att_copy = remote(att, att_peer, asend, arecv, core_peer)
    att_copy.start()
    if pair:
        for copy in shard_copies:
            copy.start()
        for step in range(n_dm):
            wshr[shard_rows(dp, step), :] = shards[step][...]
        wshr[shard_rows(1 - dp, 0), :] = shr_peer[...]

    def x_copy(j):
        block = block_rows(j, core)
        return remote(cat.at[block, :], xcat.at[block, :], xsend.at[j], xrecv.at[j], x_peer)

    def relay_copy(j):
        block = xcat.at[block_rows(j, core), :]
        return remote(block, block, rsend.at[j], rrecv.at[j], core_peer)

    def sp_copy(j):
        return remote(sp_send.at[j], sp_recv.at[j], ssend.at[j], srecv.at[j], core_peer)

    def hp_copy(j):
        return remote(hp_send.at[j], hp_recv.at[j], hsend.at[j], hrecv.at[j], core_peer)

    def sx_copy(j):
        return remote(sx_send.at[j], sx_recv.at[j], sxs.at[j], sxr.at[j], x_peer)

    def branch_copy(j):
        block = branch.at[block_rows(j, core), :]
        return remote(block, block, bsend.at[j], brecv.at[j], core_peer)

    def join(at):
        mine, other = att[at, :], att_peer[at, :]
        cat[at, :] = jnp.where(
            core == 0,
            jnp.concatenate([mine, other], axis=1),
            jnp.concatenate([other, mine], axis=1),
        )

    att_copy.wait_recv()

    def spread(j, carry):
        join(block_rows(j, core))
        x_copy(j).start()
        return carry

    lax.fori_loop(0, blocks, spread, 0)

    def join_other(j, carry):
        join(block_rows(j, 1 - core))
        return carry

    lax.fori_loop(0, blocks, join_other, 0)

    def both(ref, j):
        return jnp.concatenate([ref[block_rows(j, core), :], ref[block_rows(j, 1 - core), :]], axis=0)

    def store_both(ref, j, values):
        ref[block_rows(j, core), :] = values[:128]
        ref[block_rows(j, 1 - core), :] = values[128:]

    own_half = pl.ds(pl.multiple_of(side * half_width, 128), half_width)
    other_half = pl.ds(pl.multiple_of((1 - side) * half_width, 128), half_width)

    def forward(j):
        x_copy(j).wait_recv()
        relay_copy(j).start()
        relay_copy(j).wait_recv()
        attention = dot(both(cat, j), wout[own_half, :]) + dot(both(xcat, j), wout[other_half, :])
        middle = both(tok, j).astype(F32) + attention
        mid_out[own_rows(j), :] = middle[:128]
        normed, _ = norm_parts(middle)
        second = (normed * gain[...][None] + bias[...][None]).astype(BF16)
        store_both(sn, j, second)
        hidden = dot(second, wexp[...])
        value, rise = gelu_parts(hidden)
        value = value.astype(BF16)
        store_both(act, j, value)
        if pair:

            @pl.when(j == 0)
            def _():
                for copy in shard_copies:
                    copy.wait_recv()

        grad = (dot(both(cot, j), wshr[...]) * rise).astype(BF16)
        store_both(hg, j, grad)
        part = dot_nt(grad, wexp[...])
        sp_own[j] = part[:128]
        sp_send[j] = part[128:].astype(BF16)
        sp_copy(j).start()
        part = dot_nt(value, wshr[...])
        hp_own[j] = part[:128]
        hp_send[j] = part[128:].astype(BF16)
        hp_copy(j).start()

    def chip_sum(j):
        sp_copy(j).wait_recv()
        total = sp_own[j] + sp_recv[j].astype(F32)
        sx_send[j] = total.astype(BF16)
        sx_copy(j).start()
        hp_copy(j).wait_recv()
        hsum_out[own_rows(j), :] = (hp_own[j] + hp_recv[j].astype(F32)).astype(BF16)

    def norm_grad(j):
        sx_copy(j).wait_recv()
        second_grad = sx_send[j].astype(F32) + sx_recv[j].astype(F32)
        normed, spread_two = norm_parts(mid_out[own_rows(j), :])
        inner, gain_part, bias_part = norm_back(second_grad, normed, spread_two, gain[...][None])
        gains_out[0:1, :] += gain_part[None]
        gains_out[1:2, :] += bias_part[None]
        middle_grad = cot[block_rows(j, core), :].astype(F32) + inner
        mgrad_out[own_rows(j), :] = middle_grad
        branch[block_rows(j, core), :] = middle_grad.astype(BF16)
        branch_copy(j).start()

    def attended_grad(j):
        branch_copy(j).wait_recv()
        for which in range(2):
            at = block_rows(j, which)
            agrad_out[at, :] = dot_nt(branch[at, :], wout_own[...]).astype(BF16)

    def when_block(j, work):
        @pl.when((j >= 0) & (j < blocks))
        def _():
            work(j)

    def ticks(first, last):
        def tick(t, carry):
            when_block(t - 1, chip_sum)
            when_block(t, forward)
            when_block(t - 2, norm_grad)
            when_block(t - 3, attended_grad)
            return carry

        lax.fori_loop(first, last, tick, 0)

    half = model // 2
    part_rows = half if pair else model

    def weight_grad(left, right, which):
        return dot_tn(left[:, aligned(which * half, part_rows)], right[...]).astype(BF16)

    ticks(0, blocks)
    if pair:
        keep_out, give_out = grad_outs[0], grad_outs[1]
        for d in range(2):
            kept[d] = weight_grad(sn, hg, d)
    else:
        grad_outs[0][:, :units] = weight_grad(sn, hg, 0)
    ticks(blocks, blocks + 1)
    if pair:
        parts, me = lax.axis_size("dm"), lax.axis_index("dm")
        shard = half // parts
        for step in range(parts):
            quarter = pl.ds(pl.multiple_of(lax.rem(me + step, parts) * shard, 32), shard)
            for d in range(2):
                grad_outs[2 + step][d] = kept[d, quarter, :]
        give_out[:half, :] = weight_grad(cot, act, 1 - dp)
    else:
        grad_outs[0][:, units:] = weight_grad(cot, act, 0)
    ticks(blocks + 1, blocks + 2)
    if pair:
        keep_out[:half, :] = weight_grad(cot, act, dp)
    ticks(blocks + 2, blocks + 3)
    out_grad = dot_tn(att[...], branch[...]).astype(BF16)
    wo_out[...] = out_grad
    if pair:
        small = width // 2
        keep_out[half:, :] = wo_out[pl.ds(pl.multiple_of(dp * small, 32), small), :]
        give_out[half:, :] = wo_out[pl.ds(pl.multiple_of((1 - dp) * small, 32), small), :]

    def drain(j, carry):
        x_copy(j).wait_send()
        relay_copy(j).wait_send()
        sp_copy(j).wait_send()
        hp_copy(j).wait_send()
        sx_copy(j).wait_send()
        branch_copy(j).wait_send()
        return carry

    lax.fori_loop(0, blocks, drain, 0)
    att_copy.wait_send()
    if pair:
        for copy in shard_copies:
            copy.wait_send()


def middle(pair, tokens, cotangent, attended, wout_own, wout, wexp, gain, bias, shards, shr_peer):
    rows, model = tokens.shape
    width = attended.shape[1]
    units = wexp.shape[1]
    part_rows = model // 2 if pair else model
    spare = (2, part_rows, units) if pair else (2, 16, 128)
    parts = lax.axis_size("dm")
    if pair:
        grads = [(part_rows + width // 2, units)] * 2 + [(2, part_rows // parts, units)] * parts
    else:
        grads = [(model, 2 * units)]
    blocks = rows // 256
    shape = jax.ShapeDtypeStruct
    dma = pltpu.SemaphoreType.DMA
    low = pltpu.VMEM((blocks, 128, model), BF16)
    full = pltpu.VMEM((blocks, 128, model), F32)
    return pl.pallas_call(
        functools.partial(middle_kernel, pair, parts),
        out_shape=(
            shape((rows // 2, model), F32),
            shape((rows // 2, model), F32),
            shape((rows, width), BF16),
            shape((rows // 2, model), BF16),
            shape((width, model), BF16),
            shape((8, model), F32),
        )
        + tuple(shape(dims, BF16) for dims in grads),
        in_specs=vmem(13),
        out_specs=tuple(vmem(6 + len(grads))),
        scratch_shapes=[
            pltpu.VMEM((model, units) if pair else (16, 128), BF16),
            pltpu.VMEM((rows, width), BF16),
            pltpu.VMEM((rows, 2 * width), BF16),
            pltpu.VMEM((rows, 2 * width), BF16),
            pltpu.VMEM((rows, model), BF16),
            pltpu.VMEM((rows, units), BF16),
            pltpu.VMEM((rows, units), BF16),
            full, low, low, full, low, low, low, low,
            pltpu.VMEM((rows, model), BF16),
            pltpu.VMEM(spare, BF16),
            dma, dma,
        ]
        + [dma((blocks,))] * 12
        + [dma((4,)), dma((4,))],
        compiler_params=pltpu.CompilerParams(
            vmem_limit_bytes=60 << 20, collective_id=2, has_side_effects=True
        ),
        name="middle",
    )(tokens, cotangent, attended, wout_own, wout, wexp, gain, bias, *shards, shr_peer)


def tail_kernel(
    pair, lengths, dkvt, dq, summed, k, v, centre, topk, tm, merged, rows_in, counts, ccol, weight,
    fn, sfn, tok_hbm, gain, mgrad, srow, mid, hsum, hsum_x, second_gains,
    sh_keep, sh_given, ex_own, ex_one, ex_two, ex_three,
    result_out, tokens_out, qkv_out, out_out, gain_a, gain_b, gain_c, gain_d, expand_out, shrink_out,
    sbuf, cbuf, fgm, to_core, from_core, to_x, from_x, to_right, to_left, from_left,
    from_right, from_fin, pq, pkv, dense, dense_to_core, dense_from_core, dense_to_x, dense_from_x,
    dense_own, first, sfn_tile, grad_all, grad_from_y, grad_back, g_own, g_right, g_left, g_from_left,
    g_from_right, g_total, gain_sum, gain_core, gain_dm, gain_dp, gain_x, shrink_send, shrink_recv, expand_y, tok, tile_sem, mid_sem, hsum_sem, tok_sem,
    ssend, srecv, csend, crecv,
    send_core, recv_core, send_x, recv_x, send_right, recv_left, send_left, recv_right, send_fin,
    recv_fin,
    dsend_core, drecv_core, dsend_x, drecv_x, fsend, frecv, tsend, trecv, osend, orecv,
    ysend, yrecv, gsend_right, grecv_left, gsend_left, grecv_right, asend, arecv,
    gcsend, gcrecv, gmsend, gmrecv, gpsend, gprecv, esend, erecv,
):
    gain_outs = (gain_a, gain_b, gain_c, gain_d)
    rows, width = k.shape
    model = tok.shape[1]
    heads = width // HEAD_DIM
    half_width = model // 2
    half_rows = rows // 2
    blocks = half_rows // 128
    parts = lax.axis_size("dm")
    me, hid, dp = lax.axis_index("dm"), lax.axis_index("hid"), lax.axis_index("dp")
    core, side = lax.rem(hid, 2), hid // 2
    core_peer = {"hid": hid + 1 - 2 * core}
    x_peer = {"hid": hid + 2 - 4 * side}
    y_peer = {"dp": 1 - dp}
    own_start = me * rows
    columns = aligned(side * half_width, half_width)
    other_columns = aligned((1 - side) * half_width, half_width)

    greeted = [{"dm": lax.rem(me + step, parts)} for step in range(1, parts)]
    greeted += [core_peer, x_peer] + ([y_peer] if pair else [])
    barrier = greet(greeted)

    wide = iota((CLP, 256), 1)
    packed = jnp.concatenate([summed[:, width:], jnp.zeros((CLP, 256 - width), F32)], axis=1)
    for h in range(heads):
        packed = jnp.where(wide == width + h, summed[:, h * HEAD_DIM : h * HEAD_DIM + 1], packed)
    sbuf[me] = packed.astype(BF16)
    dense_own[...] = jnp.zeros_like(dense_own)
    mid_copy = pltpu.make_async_copy(mid, dense, mid_sem)
    mid_copy.start()
    hsum_copy = pltpu.make_async_copy(hsum, dense_to_core, hsum_sem)
    hsum_copy.start()
    tok_copy = pltpu.make_async_copy(
        tok_hbm.at[aligned(core * half_rows, half_rows), :], tok, tok_sem
    )
    tok_copy.start()

    @pl.when(me == 0)
    def _():
        from_left[...] = jnp.zeros_like(from_left)
        g_from_left[...] = jnp.zeros_like(g_from_left)

    @pl.when(me == parts - 1)
    def _():
        from_right[...] = jnp.zeros_like(from_right)
        g_from_right[...] = jnp.zeros_like(g_from_right)

    pl.semaphore_wait(barrier, len(greeted))
    sum_copies = small_exchange(sbuf, ssend, srecv, me, parts)
    for copy in sum_copies:
        copy.start()

    def chunk_rows(i, which):
        return aligned(which * HALF + i * CHUNK, CHUNK)

    def block_rows(j, which):
        return aligned(which * half_rows + j * 128, 128)

    def own_rows(j):
        return aligned(j * 128, 128)

    def core_copy(i):
        return remote(to_core.at[i], from_core.at[i], send_core.at[i], recv_core.at[i], core_peer)

    def x_copy(i):
        return remote(to_x.at[i], from_x.at[i], send_x.at[i], recv_x.at[i], x_peer)

    right = {"dm": lax.rem(me + 1, parts)}
    left = {"dm": lax.rem(me + parts - 1, parts)}

    def right_copy(i):
        return remote(to_right.at[i], from_left.at[i], send_right.at[i], recv_left.at[i], right)

    def left_copy(i):
        return remote(to_left.at[i], from_right.at[i], send_left.at[i], recv_right.at[i], left)

    def fin_copy(i):
        return remote(from_x.at[i], from_fin.at[i], send_fin.at[i], recv_fin.at[i], core_peer)

    def dense_core_copy(j):
        return remote(
            dense_to_core.at[j], dense_from_core.at[j], dsend_core.at[j], drecv_core.at[j], core_peer
        )

    def dense_x_copy(j):
        return remote(dense_to_x.at[j], dense_from_x.at[j], dsend_x.at[j], drecv_x.at[j], x_peer)

    def first_copy(j):
        block = first.at[j, :, columns]
        return remote(block, block, fsend.at[j], frecv.at[j], x_peer)

    def tokens_copy(j):
        block = tokens_out.at[block_rows(j, core), :]
        return remote(block, block, tsend.at[j], trecv.at[j], core_peer)

    def result_copy(j):
        block = result_out.at[block_rows(j, core), :]
        return remote(block, block, osend.at[j], orecv.at[j], core_peer)

    def spread_back(start, count):
        at = aligned((1 - core) * HALF + start * CHUNK, count * CHUNK)
        other = dot_tn(dkvt[:, at], weight[width:, :])
        other = other.astype(BF16)
        for i in range(count):
            to_core[start + i] = other[i * CHUNK : (i + 1) * CHUNK]
            core_copy(start + i).start()
        at = aligned(core * HALF + start * CHUNK, count * CHUNK)
        mine = dot_tn(dkvt[:, at], weight[width:, :])
        mine = mine.astype(BF16)
        for i in range(count):
            fgm[start + i] = mine[i * CHUNK : (i + 1) * CHUNK]

    def chip_sum(i):
        core_copy(i).wait_recv()
        to_x[i] = fgm[i, :, other_columns] + from_core[i, :, other_columns]
        x_copy(i).start()

    def hid_sum(i):
        x_copy(i).wait_recv()
        fgm[i, :, columns] = (
            fgm[i, :, columns].astype(F32)
            + from_core[i, :, columns].astype(F32)
            + from_x[i].astype(F32)
        ).astype(BF16)

    def go_right(i):
        @pl.when(me > 0)
        def _():
            right_copy(i).wait_recv()

        @pl.when(me < parts - 1)
        def _():
            to_right[i] = fgm[i, :, columns] + from_left[i]
            right_copy(i).start()

    def go_left(i):
        @pl.when(me < parts - 1)
        def _():
            left_copy(i).wait_recv()

        @pl.when(me > 0)
        def _():
            to_left[i] = fgm[i, :, columns] + from_right[i]
            left_copy(i).start()

    def finish(i):
        from_x[i] = (
            fgm[i, :, columns].astype(F32) + from_left[i].astype(F32) + from_right[i].astype(F32)
        ).astype(BF16)
        fin_copy(i).start()

    def scatter(i):
        fin_copy(i).wait_recv()
        here = iota((half_rows, CHUNK), 0) + own_start + core * half_rows
        chosen = [
            (srow[:, chunk_rows(i, which)] == here).astype(BF16) for which in (core, 1 - core)
        ]
        picked = jnp.concatenate([from_x[i], from_fin[i]], axis=0)
        dense_own[...] += dot(jnp.concatenate(chosen, axis=1), picked)

    far = jnp.maximum(me, parts - 1 - me)

    def ticks(start, last):
        def tick(t, carry):
            ready = t
            when_in(ready, CHUNKS, hid_sum)
            when_in(ready - LAG * me, CHUNKS, go_right)
            when_in(ready - LAG * (parts - 1 - me), CHUNKS, go_left)
            when_in(ready - LAG * far, CHUNKS, finish)
            when_in(ready - LAG * far - 1, CHUNKS, scatter)
            return carry

        lax.fori_loop(start, last, tick, 0)

    if pair:
        shard = expand_out.shape[0]

        def shard_rows(m):
            return pl.ds(pl.multiple_of(m * shard, 32), shard)

        shrink_copies = []
        for step in range(1, parts):
            target = lax.rem(me + step, parts)
            shrink_send[step] = sh_keep[shard_rows(target), :] + sh_given[shard_rows(target), :]
            shrink_copies.append(
                remote(
                    shrink_send.at[step], shrink_recv.at[step], esend.at[step], erecv.at[step],
                    {"dm": target},
                )
            )
        for copy in shrink_copies:
            copy.start()
        expand_y[0] = (
            ex_own[1 - dp].astype(F32) + ex_one[1 - dp].astype(F32)
            + ex_two[1 - dp].astype(F32) + ex_three[1 - dp].astype(F32)
        ).astype(BF16)
        expand_copy = remote(expand_y.at[0], expand_y.at[1], esend.at[0], erecv.at[0], y_peer)
        expand_copy.start()

    def chip_sums(first, last):
        def one(i, carry):
            chip_sum(i)
            return carry

        lax.fori_loop(first, last, one, 0)

    spread_back(0, 3)
    chip_sums(0, 3)
    spread_back(3, 5)
    chip_sums(3, 8)
    spread_back(8, CHUNKS - 8)
    chip_sums(8, CHUNKS)

    def result_rows(j, carry):
        total = dense_to_core[j].astype(F32) + hsum_x[j].astype(F32)
        result_out[block_rows(j, core), :] = (dense[j] + total).astype(BF16)
        result_copy(j).start()
        return carry

    for copy in sum_copies:
        copy.wait_recv()
    total = sbuf[0].astype(F32)
    for d in range(1, parts):
        total += sbuf[d].astype(F32)
    same = sequence_masks(lengths, topk, rows)
    rest_grad = total[:, :width].astype(BF16)
    product = rest_grad.astype(F32) * rows_in[:, width:]
    score_grads, weights = [], []
    centre_part = jnp.zeros((CLP, width), F32)
    for h in range(heads):
        lanes = head_lanes(width, h)
        top = tm[...].astype(F32)
        zero = jnp.zeros((CLP, width), BF16)
        full = dot_nt(jnp.where(lanes, centre[...], zero), k[...]) * SCALE
        against = dot_nt(jnp.where(lanes, rest_grad, zero), v[...])
        largest, denominator = merged[:, h : h + 1], merged[:, 8 + h : 9 + h]
        mass = merged[:, 16 + h : 17 + h]
        mass_grad = total[:, width + h : width + h + 1]
        probs = jnp.where(same, jnp.exp(full - largest) / denominator, 0.0)
        mean = mass * mass_grad + jnp.sum(jnp.where(lanes, product, 0.0), 1, keepdims=True)
        grad = jnp.where(top > 0.5, mass_grad, against)
        score_grad = (probs * (grad - mean)).astype(BF16)
        centre_part = jnp.where(lanes, dot(score_grad, k[...]), centre_part)
        score_grads.append(score_grad)
        weights.append(jnp.where(top > 0.5, 0.0, probs).astype(BF16))
    cbuf[me] = (centre_part * SCALE).astype(BF16)
    centre_copies = small_exchange(cbuf, csend, crecv, me, parts)
    for copy in centre_copies:
        copy.start()
    score_grad = jnp.concatenate(score_grads, axis=0)
    rest_weight = jnp.concatenate(weights, axis=0)
    pkv[...] = jnp.concatenate(
        [
            (dot_tn(score_grad, block_diagonal(centre[...], heads)) * SCALE).astype(BF16),
            dot_tn(rest_weight, block_diagonal(rest_grad, heads)).astype(BF16),
        ],
        axis=1,
    )
    if pair:
        part = width // 2

        def y_rows(b, d):
            first = jnp.where(b == 3, 6 + d, d * 3 + b)
            return pl.ds(pl.multiple_of(first * part, 32), part)

        def y_copy(b):
            return remote(
                grad_all.at[y_rows(b, 1 - dp), :], grad_from_y.at[b], ysend.at[b], yrecv.at[b], y_peer
            )

        def y_back(b):
            return remote(
                grad_all.at[y_rows(b, dp), :], grad_back.at[b], asend.at[b], arecv.at[b], y_peer
            )

        def unit_right(u):
            return remote(g_right.at[u], g_from_left.at[u], gsend_right.at[u], grecv_left.at[u], right)

        def unit_left(u):
            return remote(g_left.at[u], g_from_right.at[u], gsend_left.at[u], grecv_right.at[u], left)

        def y_sum(turn):
            @pl.when(turn == 0)
            def _():
                both = sh_keep[model // 2 :, :] + sh_given[model // 2 :, :]
                g_own[0] = both[:, :half_width]
                g_own[1] = both[:, half_width:]

            @pl.when(turn > 0)
            def _():
                b = turn - 1
                y_copy(b).wait_recv()
                both = grad_all[y_rows(b, dp), :] + grad_from_y[b]
                g_own[2 * turn] = both[:, :half_width]
                g_own[2 * turn + 1] = both[:, half_width:]

        root = parts // 2

        def unit_up(u):
            @pl.when(me < root)
            def _():
                @pl.when(me > 0)
                def _():
                    unit_right(u).wait_recv()

                g_right[u] = g_own[u] + g_from_left[u]
                unit_right(u).start()

            @pl.when(me > root)
            def _():
                @pl.when(me < parts - 1)
                def _():
                    unit_left(u).wait_recv()

                g_left[u] = g_own[u] + g_from_right[u]
                unit_left(u).start()

        def unit_turn(u):
            unit_right(u).wait_recv()

            @pl.when(me < parts - 1)
            def _():
                unit_left(u).wait_recv()

            total = g_own[u] + g_from_left[u] + g_from_right[u]
            g_total[u] = total
            g_left[u] = total
            unit_left(u).start()

            @pl.when(me < parts - 1)
            def _():
                g_right[u] = total
                unit_right(u).start()

        def unit_down(u):
            @pl.when(me < root)
            def _():
                unit_left(u).wait_recv()
                g_total[u] = g_from_right[u]

                @pl.when(me > 0)
                def _():
                    g_left[u] = g_from_right[u]
                    unit_left(u).start()

            @pl.when(me > root)
            def _():
                unit_right(u).wait_recv()
                g_total[u] = g_from_left[u]

                @pl.when(me < parts - 1)
                def _():
                    g_right[u] = g_from_left[u]
                    unit_right(u).start()

        def y_return(turn):
            b = lax.rem(turn + 3, 4)
            grad_all[y_rows(b, dp), :half_width] = g_total[2 * turn]
            grad_all[y_rows(b, dp), half_width:] = g_total[2 * turn + 1]
            y_back(b).start()

        def gticks(start, last):
            def tick(t, carry):
                @pl.when(lax.rem(t, 2) == 0)
                def _():
                    when_in(t // 2, 4, y_sum)

                wait = jnp.where(me < root, me, parts - 1 - me)
                up = jnp.where(me == root, -1, t - 1 - LAG * wait)
                when_in(up, UNITS, unit_up)
                away = jnp.where(me < root, root - me, me - root)
                back = t - 1 - LAG * (root + away)

                @pl.when(me == root)
                def _():
                    when_in(back, UNITS, unit_turn)

                @pl.when(me != root)
                def _():
                    when_in(back, UNITS, unit_down)

                @pl.when((back >= 0) & (lax.rem(back + 1, 2) == 0))
                def _():
                    when_in((back - 1) // 2, 4, y_return)

                return carry

            lax.fori_loop(start, last, tick, 0)
    else:

        def gticks(start, last):
            pass

    def slot_tile(c, carry):
        cut = aligned(c * 256, 256)
        fetch = pltpu.make_async_copy(sfn.at[:, cut], sfn_tile, tile_sem)
        fetch.start()
        grad = dot_tn(pkv[...], fn[:, cut])
        fetch.wait()
        grad = (grad + dot(dkvt[...], sfn_tile[...])).astype(BF16)
        grad_all[:width, cut] = grad[:width]
        grad_all[3 * (width // 2) : 3 * (width // 2) + width, cut] = grad[width:]
        return carry

    ticks(0, 1)
    lax.fori_loop(0, model // 256, slot_tile, 0)
    if pair:
        y_copy(0).start()
        y_copy(1).start()
    ticks(1, 2)
    mid_copy.wait()
    hsum_copy.wait()
    lax.fori_loop(0, blocks, result_rows, 0)
    ticks(2, 4)
    for copy in centre_copies:
        copy.wait_recv()
    centre_grad = cbuf[0].astype(F32)
    for d in range(1, parts):
        centre_grad += cbuf[d].astype(F32)
    centre_grad = centre_grad / counts[:, :1]
    high = centre_grad.astype(BF16)
    low = (centre_grad - high.astype(F32)).astype(BF16)

    def queries(i, carry):
        at = aligned(i * 256, 256)
        member = (ccol[at, :] == iota((256, 128), 1)).astype(BF16)
        pq[at, :] = (dq[at, :].astype(F32) + dot(member, high) + dot(member, low)).astype(BF16)
        return carry

    lax.fori_loop(0, rows // 256, queries, 0)
    query_grad = dot_tn(pq[...], fn[...]).astype(BF16)
    grad_all[width : width + width // 2, :] = query_grad[: width // 2]
    grad_all[5 * (width // 2) : 3 * width, :] = query_grad[width // 2 :]
    if pair:
        y_copy(2).start()
    ticks(4, 5)

    def dense_rows(which):
        at = aligned(which * half_rows, half_rows)
        return dot(pq[at, :], weight[:width, :]) + dot(pkv[at, :], weight[width:, :])

    other_dense = dense_rows(1 - core).astype(BF16)
    for j in range(blocks):
        dense_to_core[j] = other_dense[j * 128 : (j + 1) * 128]
        dense_core_copy(j).start()
    own_dense = dense_rows(core)
    for j in range(blocks):
        dense[j] = own_dense[j * 128 : (j + 1) * 128]
    ticks(5, 6)

    def dense_chip(j, carry):
        dense_core_copy(j).wait_recv()
        dense_to_x[j] = (
            dense[j, :, other_columns] + dense_from_core[j, :, other_columns].astype(F32)
        ).astype(BF16)
        dense_x_copy(j).start()
        return carry

    def dense_hid(j, carry):
        dense_x_copy(j).wait_recv()
        dense_own[own_rows(j), :] += (
            dense[j, :, columns]
            + dense_from_core[j, :, columns].astype(F32)
            + dense_from_x[j].astype(F32)
        )
        return carry

    lax.fori_loop(0, blocks, dense_chip, 0)
    last = CHUNKS + LAG * (parts - 1) + 1

    def joint(t, carry):
        ticks(t, t + 1)
        gticks(t - GSTART, t - GSTART + 1)
        return carry

    ticks(6, GSTART)
    lax.fori_loop(GSTART, last, joint, 0)
    done = last - GSTART
    lax.fori_loop(0, blocks, dense_hid, 0)
    mgrad_copy = pltpu.make_async_copy(mgrad, dense, mid_sem)
    mgrad_copy.start()

    gain_sum[...] = jnp.zeros_like(gain_sum)
    tok_copy.wait()

    def first_send(j, carry):
        grad = dense_own[own_rows(j), :].astype(BF16)
        first[j, :, columns] = grad
        first_copy(j).start()
        return carry

    lax.fori_loop(0, blocks, first_send, 0)

    def first_gains(j, carry):
        centred = tok[own_rows(j), :].astype(F32)
        mean = jnp.mean(centred, -1, keepdims=True)
        variance = jnp.mean(jnp.square(centred - mean), -1, keepdims=True)
        normed = (tok[own_rows(j), columns].astype(F32) - mean) * lax.rsqrt(
            variance + EPSILON
        )
        grad = first[j, :, columns].astype(F32)
        gain_sum[0:1, columns] += jnp.sum(grad * normed, 0, keepdims=True)
        gain_sum[1:2, columns] += jnp.sum(grad, 0, keepdims=True)
        return carry

    lax.fori_loop(0, blocks, first_gains, 0)
    gain_sum[2:4, columns] = second_gains[0:2, columns]
    if pair:
        core_gain = remote(gain_sum, gain_core, gcsend, gcrecv, core_peer)
        core_gain.start()
    gticks(done, done + 2)

    def first_back(j, carry):
        first_copy(j).wait_recv()
        at = block_rows(j, core)
        normed, spread = norm_parts(tok[own_rows(j), :].astype(F32))
        inner, _, _ = norm_back(first[j].astype(F32), normed, spread, gain[...][None])
        tokens_out[at, :] = (dense[j] + inner).astype(BF16)
        tokens_copy(j).start()
        return carry

    mgrad_copy.wait()
    if pair:
        core_gain.wait_recv()
        gain_dm[me] = gain_sum[...] + gain_core[...]
        dm_gains = small_exchange(gain_dm, gmsend, gmrecv, me, parts)
        for copy in dm_gains:
            copy.start()
    lax.fori_loop(0, 1, first_back, 0)
    gticks(done + 2, done + 4)
    lax.fori_loop(1, 2, first_back, 0)
    if pair:
        for copy in dm_gains:
            copy.wait_recv()
        line = gain_dm[0]
        for d in range(1, parts):
            line = line + gain_dm[d]
        gain_dp[0] = line
        dp_gain = remote(gain_dp.at[0], gain_dp.at[1], gpsend.at[0], gprecv.at[0], y_peer)
        dp_gain.start()
    lax.fori_loop(2, 4, first_back, 0)
    if pair:
        dp_gain.wait()
        gain_x[0] = gain_dp[0] + gain_dp[1]
        x_gain = remote(gain_x.at[0], gain_x.at[1], gpsend.at[1], gprecv.at[1], x_peer)
        x_gain.start()
    lax.fori_loop(4, blocks, first_back, 0)
    if pair:
        gticks(done + 4, 1 + LAG * 2 * (parts // 2) + UNITS)
        for b in range(4):
            if b < 3:
                y_copy(b).wait_send()
            y_back(b).wait_recv()
            grad_all[y_rows(b, 1 - dp), :] = grad_back[b]
    small = width // 2
    qkv_out[0, :small] = grad_all[width : width + small, :]
    qkv_out[0, small:] = grad_all[5 * small : 6 * small, :]
    qkv_out[1] = grad_all[:width, :]
    qkv_out[2] = grad_all[3 * small : 5 * small, :]
    if pair:
        out_out[...] = grad_all[6 * small :, :].astype(F32)
    if pair:
        grad = sh_keep[shard_rows(me), :].astype(F32) + sh_given[shard_rows(me), :].astype(F32)
        for step in range(1, parts):
            shrink_copies[step - 1].wait()
            grad = grad + shrink_recv[step].astype(F32)
        shrink_out[...] = grad
        expand_copy.wait()
        grad = expand_y[1].astype(F32)
        for block in (ex_own, ex_one, ex_two, ex_three):
            grad = grad + block[dp].astype(F32)
        expand_out[...] = grad
        x_gain.wait()
        total = gain_x[0] + gain_x[1]
        core_gain.wait_send()
        for copy in dm_gains:
            copy.wait_send()
    else:
        total = gain_sum[...]
    for i, out in enumerate(gain_outs):
        out[...] = total[i]
    if pair:
        for b in range(4):
            y_back(b).wait_send()

        def drain_units(u, carry):
            @pl.when(me < parts - 1)
            def _():
                unit_right(u).wait_send()

            @pl.when(me > 0)
            def _():
                unit_left(u).wait_send()

            return carry

        lax.fori_loop(0, UNITS, drain_units, 0)

    def drain_blocks(j, carry):
        dense_core_copy(j).wait_send()
        dense_x_copy(j).wait_send()
        first_copy(j).wait_send()
        result_copy(j).wait()
        tokens_copy(j).wait()
        return carry

    def drain(i, carry):
        @pl.when(me < parts - 1)
        def _():
            right_copy(i).wait_send()

        @pl.when(me > 0)
        def _():
            left_copy(i).wait_send()

        core_copy(i).wait_send()
        x_copy(i).wait_send()
        fin_copy(i).wait_send()
        return carry

    lax.fori_loop(0, CHUNKS, drain, 0)
    for copy in sum_copies + centre_copies:
        copy.wait_send()
    lax.fori_loop(0, blocks, drain_blocks, 0)


def tail(
    pair, lengths, dkvt, dq, summed, k, v, centre, topk, tm, merged, rows_in, counts, clusters,
    weight, fn, sfn, tokens, gain, mgrad, srow, mid, hsum, hsum_x, second_gains,
    sh_keep, sh_given, ex_parts, parts,
):
    rows, width = k.shape
    model = tokens.shape[1]
    shape = jax.ShapeDtypeStruct
    dma = pltpu.SemaphoreType.DMA
    blocks = rows // 256
    owned = ex_parts[0].shape[1:]
    chain = pltpu.VMEM((CHUNKS, CHUNK, model // 2), BF16)
    whole = pltpu.VMEM((CHUNKS, CHUNK, model), BF16)
    unit = pltpu.VMEM((UNITS, width // 2, model // 2) if pair else (UNITS, 16, 128), BF16)
    return pl.pallas_call(
        functools.partial(tail_kernel, pair),
        out_shape=(
            shape((rows, model), BF16),
            shape((rows, model), BF16),
            shape((3, width, model), BF16),
            shape((width, model), F32),
            shape((model,), F32),
            shape((model,), F32),
            shape((model,), F32),
            shape((model,), F32),
            shape(owned, F32),
            shape(owned, F32),
        ),
        in_specs=[pl.BlockSpec(memory_space=pltpu.SMEM)]
        + vmem(14)
        + [pl.BlockSpec(memory_space=pl.ANY)] * 2
        + vmem(1)
        + [pl.BlockSpec(memory_space=pl.ANY)]
        + vmem(1)
        + [pl.BlockSpec(memory_space=pl.ANY)] * 2
        + vmem(8),
        out_specs=tuple(vmem(10)),
        scratch_shapes=[
            pltpu.VMEM((parts, CLP, 256), BF16),
            pltpu.VMEM((parts, CLP, width), BF16),
            whole, whole, whole,
            chain, chain, chain, chain, chain, chain,
            chain,
            pltpu.VMEM((rows, width), BF16),
            pltpu.VMEM((rows, 2 * width), BF16),
            pltpu.VMEM((blocks, 128, model), F32),
            pltpu.VMEM((blocks, 128, model), BF16),
            pltpu.VMEM((blocks, 128, model), BF16),
            pltpu.VMEM((blocks, 128, model // 2), BF16),
            pltpu.VMEM((blocks, 128, model // 2), BF16),
            pltpu.VMEM((rows // 2, model // 2), F32),
            pltpu.VMEM((blocks, 128, model), BF16),
            pltpu.VMEM((SLOTS, 256), BF16),
            pltpu.VMEM((4 * width, model), BF16),
            pltpu.VMEM((3, width // 2, model), BF16),
            pltpu.VMEM((4, width // 2, model), BF16),
            unit, unit, unit, unit, unit, unit,
            pltpu.VMEM((8, model), F32),
            pltpu.VMEM((8, model), F32),
            pltpu.VMEM((parts, 8, model), F32),
            pltpu.VMEM((2, 8, model), F32),
            pltpu.VMEM((2, 8, model), F32),
            pltpu.VMEM((parts,) + owned, BF16),
            pltpu.VMEM((parts,) + owned, BF16),
            pltpu.VMEM((2,) + owned, BF16),
            pltpu.VMEM((rows // 2, model), BF16),
            dma, dma, dma, dma,
        ]
        + [dma((parts,))] * 4
        + [dma((CHUNKS,))] * 10
        + [dma((blocks,))] * 10
        + [dma((3,))] * 2
        + [dma((UNITS,))] * 4
        + [dma((4,))] * 2
        + [dma, dma, dma((parts,)), dma((parts,)), dma((2,)), dma((2,)), dma((parts,)), dma((parts,))],
        compiler_params=pltpu.CompilerParams(
            vmem_limit_bytes=58 << 20, collective_id=1, has_side_effects=True
        ),
        name="tail",
    )(
        lengths, dkvt, dq, summed, k, v, centre, topk, tm, merged, rows_in, counts,
        clusters, weight.reshape(3 * width, model), fn, sfn, tokens, gain,
        mgrad.reshape(blocks, 128, model), srow, mid.reshape(blocks, 128, model),
        hsum.reshape(blocks, 128, model), hsum_x.reshape(blocks, 128, model), second_gains,
        sh_keep, sh_given, *ex_parts,
    )


def shards(
    tokens,
    clusters,
    top_keys,
    lengths,
    qkv_weight,
    out_weight,
    first_gain,
    first_bias,
    second_gain,
    second_bias,
    expand_weight,
    shrink_weight,
    cotangent,
):
    parts, n_dp = lax.axis_size("dm"), lax.axis_size("dp")
    pair = n_dp == 2
    weight = jnp.swapaxes(qkv_weight, 1, 2)
    topk = jnp.pad(top_keys, ((0, CLP - CL), (0, 0)), constant_values=-1)
    flat = jnp.pad(top_keys.reshape(-1), (0, SLOTS - CL * TOPK), constant_values=-1)
    (
        first_normed, slot_normed, qs, k, v, ks, vs, kst, vst, starts, rcol, rrow, cls, centre, tm, rows_in,
        merged, counts, out_full, expand_full, shrink_peer, cluster_column,
    ) = front(
        pair, lengths, tokens, clusters, weight, first_gain, first_bias,
        flat.reshape(SLOTS, 1), topk, expand_weight, shrink_weight.T, out_weight, parts,
    )
    if pair:
        shrink_shards = [shrink_weight.T]
        source, _ = lax.optimization_barrier((shrink_weight.T, starts))
        for step in range(1, parts):
            shrink_shards.append(
                lax.ppermute(source, "dm", [(i, (i + step) % parts) for i in range(parts)])
            )
    else:
        expand_full = lax.all_gather(expand_weight, ("dp", "dm"), axis=0, tiled=True)
        shrink_full = lax.all_gather(shrink_weight.T, ("dp", "dm"), axis=0, tiled=True)
        shrink_shards = [shrink_full] + [jnp.zeros((16, 128), BF16)] * (parts - 1)
    attended = exact_forward(starts, qs, cls, kst, vs, rows_in, rcol)
    mid, middle_grad, attended_grad, hidden_sum, out_grad_part, second_parts, *grads = middle(
        pair, tokens, cotangent, attended, out_weight, out_full, expand_full,
        second_gain, second_bias, shrink_shards, shrink_peer,
    )
    hidden_sum_x = lax.ppermute(hidden_sum, "hid", [(i, i ^ 2) for i in range(lax.axis_size("hid"))])
    units = expand_weight.shape[1]
    if pair:
        shrink_keep, shrink_give, *expand_parts = grads
        shrink_given = lax.ppermute(shrink_give, "dp", [(0, 1), (1, 0)])
        expand_parts = [expand_parts[0]] + [
            lax.ppermute(expand_parts[step], "dm", [(i, (i + step) % parts) for i in range(parts)])
            for step in range(1, parts)
        ]
    else:
        summed_grads = lax.psum_scatter(grads[0], ("dp", "dm"), scatter_dimension=0, tiled=True)
        shrink_keep = shrink_given = jnp.zeros((16, 128), BF16)
        expand_parts = [jnp.zeros((2, 16, 128), BF16)] * parts
    dq, dkvt, summed = exact_backward(
        starts, qs, cls, ks, kst, vst, rows_in, rcol, rrow, attended_grad
    )
    result, tokens_grad, qkv_grad, out_grad, *gains, expand_grad, shrink_grad = tail(
        pair, lengths, dkvt, dq, summed, k, v, centre, topk, tm, merged, rows_in, counts, cluster_column,
        weight, first_normed, slot_normed, tokens, first_gain, middle_grad,
        flat.reshape(1, SLOTS), mid, hidden_sum, hidden_sum_x, second_parts,
        shrink_keep, shrink_given, expand_parts, parts,
    )
    if not pair:
        out_grad = lax.psum(out_grad_part, ("dp", "dm")).astype(F32)
        qkv_grad = lax.psum(qkv_grad, ("dp", "dm"))
        gains = lax.psum(jnp.stack(gains), ("dp", "dm", "hid"))
        summed_grads = summed_grads.astype(F32)
        expand_grad, shrink_grad = summed_grads[:, :units], summed_grads[:, units:]
    return (
        result,
        tokens_grad,
        jnp.swapaxes(qkv_grad.astype(F32), 1, 2),
        out_grad,
        gains[0],
        gains[1],
        gains[2],
        gains[3],
        expand_grad,
        shrink_grad.T,
    )


def solution(mesh):
    in_specs = (
        P(("dp", "dm"), None),
        P(("dp", "dm")),
        P("dp", None),
        P("dp"),
        P(None, None, "hid"),
        P("hid", None),
        P(),
        P(),
        P(),
        P(),
        P(("dp", "dm"), "hid"),
        P("hid", ("dp", "dm")),
        P(("dp", "dm"), None),
    )
    out_specs = (
        P(("dp", "dm"), None),
        P(("dp", "dm"), None),
        P(None, None, "hid"),
        P("hid", None),
        P(),
        P(),
        P(),
        P(),
        P(("dp", "dm"), "hid"),
        P("hid", ("dp", "dm")),
    )
    return jax.shard_map(shards, mesh=mesh, in_specs=in_specs, out_specs=out_specs, check_vma=False)
```

```python
import functools

import jax
import jax.numpy as jnp
from jax import lax
from jax.experimental import pallas as pl
from jax.experimental.pallas import tpu as pltpu
from jax.sharding import PartitionSpec as P

HEAD_DIM = 64
CL = 100
TOPK = 32
CLP = 128
SLOTS = 3328
GROUP = 8
GSLOTS = GROUP * TOPK
GROUPS = SLOTS // GSLOTS
WIN = 160
HALF = SLOTS // 2
CHUNK = 128
CHUNKS = HALF // CHUNK
LAG = 2
CENTRE = 6
CENTRE_TICK = 13
GSTART = 8
UNITS = 8
EPSILON = 1e-05
NEGATIVE = -1e30
HIGHEST = lax.Precision.HIGHEST
F32 = jnp.float32
BF16 = jnp.bfloat16
MESH = pl.DeviceIdType.MESH
NT = (((1,), (1,)), ((), ()))
TN = (((0,), (0,)), ((), ()))
SCALE = HEAD_DIM ** (-0.5)


def dot(a, b):
    return jnp.dot(a, b, preferred_element_type=F32)


def dot_nt(a, b):
    return lax.dot_general(a, b, NT, preferred_element_type=F32)


def dot_tn(a, b):
    return lax.dot_general(a, b, TN, preferred_element_type=F32)


def iota(shape, dim):
    return lax.broadcasted_iota(jnp.int32, shape, dim)


def norm_parts(values):
    centred = values - jnp.mean(values, -1, keepdims=True)
    spread = lax.rsqrt(jnp.mean(centred * centred, -1, keepdims=True) + EPSILON)
    return (centred * spread, spread)


def norm_back(upstream, normed, spread, norm_gain):
    through = upstream * norm_gain
    inner = (
        through
        - jnp.mean(through, -1, keepdims=True)
        - normed * jnp.mean(through * normed, -1, keepdims=True)
    )
    return (spread * inner, jnp.sum(upstream * normed, 0), jnp.sum(upstream, 0))


def head_lanes(width, head):
    lane = iota((1, width), 1)
    return lane // HEAD_DIM == head


def block_diagonal(rows, heads):
    width = rows.shape[1]
    zero = jnp.zeros_like(rows)
    return jnp.concatenate(
        [jnp.where(head_lanes(width, h), rows, zero) for h in range(heads)], axis=0
    )


def block_diagonal_turned(turned, heads):
    zero = jnp.zeros((HEAD_DIM, turned.shape[1]), turned.dtype)
    columns = []
    for h in range(heads):
        mine = turned[h * HEAD_DIM : (h + 1) * HEAD_DIM]
        columns.append(jnp.concatenate([mine if i == h else zero for i in range(heads)], axis=0))
    return jnp.concatenate(columns, axis=1)


def diagonal_blocks_turned(full, heads):
    rows, size = full.shape[0] // heads, full.shape[1] // heads
    return jnp.concatenate(
        [full[h * rows : (h + 1) * rows, h * size : (h + 1) * size] for h in range(heads)], axis=0
    )


def diagonal_blocks(full, heads):
    rows, width = full.shape[0] // heads, full.shape[1]
    out = full[:rows]
    for h in range(1, heads):
        out = jnp.where(head_lanes(width, h), full[h * rows : (h + 1) * rows], out)
    return out


def vmem(n):
    return [pl.BlockSpec(memory_space=pltpu.VMEM)] * n


def remote(src, dst, send, recv, device):
    return pltpu.make_async_remote_copy(
        src_ref=src, dst_ref=dst, send_sem=send, recv_sem=recv, device_id=device,
        device_id_type=MESH,
    )


def greet(devices):
    barrier = pltpu.get_barrier_semaphore()
    for device in devices:
        pl.semaphore_signal(barrier, inc=1, device_id=device, device_id_type=MESH)
    return barrier


def small_exchange(buf, sends, recvs, me, parts):
    return [
        remote(
            buf.at[me], buf.at[me], sends.at[step], recvs.at[step],
            {"dm": lax.rem(me + step, parts)},
        )
        for step in range(1, parts)
    ]


def when_in(i, count, work):
    @pl.when((i >= 0) & (i < count))
    def _():
        work(i)


def aligned(start, size):
    return pl.ds(pl.multiple_of(start, 128), size)


def sequence_masks(lengths, topk, rows):
    own_start = lax.axis_index("dm") * rows
    key_second = iota((1, rows), 1) + own_start >= lengths[0]
    centre_second = topk[:, :1] >= lengths[0]
    return key_second == centre_second


def front_kernel(
    pair, lengths, tok, crow, weight, gain, bias, scol, topk, wexp, wshr, wout,
    fn_hbm, sfn_hbm, qs_out, k_out, v_out, ks_out, vs_out, kst_out, vst_out, starts_out, rcol_out, rrow_out,
    cls_out, centre_out, tm_out, rows_out, merged_out, count_out, wall_out, wfull_out, shr_peer_out, ccol,
    fn_out, sfn_out, q_ref, member_ref, csum, rbuf, sbuf, own, to_right, to_left, from_left, from_right,
    rsend, rrecv, ssend, srecv,
    send_right, recv_left, send_left, recv_right, send_x, recv_x, send_core, recv_core,
    send_relay, recv_relay, osend, orecv, wsend, wsend_left, wrecv, ysend, yrecv, psend, precv, local_sems,
):
    rows, model = tok.shape
    width = weight.shape[1]
    heads = width // HEAD_DIM
    half_width = model // 2
    tiles = rows // 128
    parts = lax.axis_size("dm")
    me, hid, dp = lax.axis_index("dm"), lax.axis_index("hid"), lax.axis_index("dp")
    core, side = lax.rem(hid, 2), hid // 2
    core_peer = {"hid": hid + 1 - 2 * core}
    x_peer = {"hid": hid + 2 - 4 * side}
    lane = iota((128, 128), 1)
    columns = aligned(side * half_width, half_width)
    other_columns = aligned((1 - side) * half_width, half_width)
    own_start = me * rows

    greeted = [{"dm": lax.rem(me + step, parts)} for step in range(1, parts)]
    greeted += [core_peer, x_peer]
    if pair:
        greeted.append({"dp": 1 - dp})
    barrier = greet(greeted)

    out_rows = pl.ds(pl.multiple_of(hid * width, 64), width)
    out_own = pltpu.make_async_copy(wout, wall_out.at[out_rows, :], local_sems.at[0])
    out_own.start()
    out_x_rows = pl.ds(pl.multiple_of((hid + 2 - 4 * side) * width, 64), width)
    out_copies = [
        remote(wout, wall_out.at[out_rows, :], osend.at[0], orecv.at[0], core_peer),
        remote(wout, wall_out.at[out_rows, :], osend.at[1], orecv.at[1], x_peer),
        remote(
            wall_out.at[out_x_rows, :], wall_out.at[out_x_rows, :], osend.at[2], orecv.at[2], core_peer
        ),
    ]
    if pair:
        shard = wexp.shape[0]

        def shard_rows(d, m):
            return pl.ds(pl.multiple_of((d * parts + m) * shard, 32), shard)

        mine = shard_rows(dp, me)
        def whole_shard(origin):
            return wfull_out.at[shard_rows(dp, origin), :]

        def hop(origin, source, sends, neighbour):
            return remote(
                source, whole_shard(origin), sends.at[origin], wrecv.at[origin],
                {"dm": lax.rem(neighbour, parts)},
            )

        def across(origin, source):
            return remote(
                source, whole_shard(origin), ysend.at[origin], yrecv.at[origin], {"dp": 1 - dp}
            )

        def pass_on(step):
            @pl.when(me >= step)
            def _():
                origin = me - step
                block = whole_shard(origin)
                hop(origin, block, wsend, me + 1).wait_recv()
                across(origin, block).start()

                @pl.when(me < parts - 1)
                def _():
                    hop(origin, block, wsend, me + 1).start()

            @pl.when(me + step < parts)
            def _():
                origin = me + step
                block = whole_shard(origin)
                hop(origin, block, wsend_left, me + parts - 1).wait_recv()
                across(origin, block).start()

                @pl.when(me > 0)
                def _():
                    hop(origin, block, wsend_left, me + parts - 1).start()

        shard_own = pltpu.make_async_copy(wexp, wfull_out.at[mine, :], local_sems.at[1])
        shard_own.start()
        shrink_peer = remote(wshr, shr_peer_out, psend, precv, {"dp": 1 - dp})

    pl.semaphore_wait(barrier, len(greeted))
    if pair:
        across(me, wexp).start()
        shrink_peer.start()

        @pl.when(me < parts - 1)
        def _():
            hop(me, wexp, wsend, me + 1).start()

        @pl.when(me > 0)
        def _():
            hop(me, wexp, wsend_left, me + parts - 1).start()

    out_copies[0].start()
    out_copies[1].start()

    def first_norm(i, carry):
        at = aligned(i * 256, 256)
        normed, _ = norm_parts(tok[at, :].astype(F32))
        fn_out[at, :] = (normed * gain[...][None] + bias[...][None]).astype(BF16)
        return carry

    lax.fori_loop(0, rows // 256, first_norm, 0)
    fn_copy = pltpu.make_async_copy(fn_out, fn_hbm, local_sems.at[2])
    fn_copy.start()

    @pl.when(me == 0)
    def _():
        from_left[...] = jnp.zeros_like(from_left)

    @pl.when(me == parts - 1)
    def _():
        from_right[...] = jnp.zeros_like(from_right)

    def chunk_rows(i, which):
        return aligned(which * HALF + i * CHUNK, CHUNK)

    def right_copy(i):
        return remote(
            to_right.at[i], from_left.at[i], send_right.at[i], recv_left.at[i],
            {"dm": lax.rem(me + 1, parts)},
        )

    def left_copy(i):
        return remote(
            to_left.at[i], from_right.at[i], send_left.at[i], recv_right.at[i],
            {"dm": lax.rem(me + parts - 1, parts)},
        )

    def x_copy(i):
        block = sfn_out.at[chunk_rows(i, core), columns]
        return remote(block, block, send_x.at[i], recv_x.at[i], x_peer)

    def core_copy(i):
        block = sfn_out.at[chunk_rows(i, core), columns]
        return remote(block, block, send_core.at[i], recv_core.at[i], core_peer)

    def relay_copy(i):
        block = sfn_out.at[chunk_rows(i, core), other_columns]
        return remote(block, block, send_relay.at[i], recv_relay.at[i], core_peer)

    def make_own(first, count):
        at = aligned(core * HALF + first * CHUNK, count * CHUNK)
        chosen = (scol[at, :] == iota((count * CHUNK, rows), 1) + own_start).astype(BF16)
        picked = dot(chosen, fn_out[:, columns]).astype(BF16)
        for i in range(count):
            own[first + i + (first + i >= CENTRE)] = picked[i * CHUNK : (i + 1) * CHUNK]

    def go_right(i):
        @pl.when(me > 0)
        def _():
            right_copy(i).wait_recv()

        @pl.when(me < parts - 1)
        def _():
            to_right[i] = own[i] + from_left[i]
            right_copy(i).start()

    def go_left(i):
        @pl.when(me < parts - 1)
        def _():
            left_copy(i).wait_recv()

        @pl.when(me > 0)
        def _():
            to_left[i] = own[i] + from_right[i]
            left_copy(i).start()

    def slot_chunk(place):
        return jnp.where(place > CENTRE, place - 1, place)

    def finish(place):
        @pl.when(place == CENTRE)
        def _():
            total = own[place].astype(F32) + from_left[place].astype(F32)
            csum[...] = total + from_right[place].astype(F32)

        @pl.when(place != CENTRE)
        def _():
            i = slot_chunk(place)
            sfn_out[chunk_rows(i, core), columns] = (
                own[place] + from_left[place] + from_right[place]
            )
            x_copy(i).start()
            core_copy(i).start()

    def relay(place):
        @pl.when(place != CENTRE)
        def _():
            i = slot_chunk(place)
            x_copy(i).wait_recv()
            relay_copy(i).start()

    far = jnp.maximum(me, parts - 1 - me)

    def ticks(first, last):
        def tick(t, carry):
            when_in(t - LAG * me, CHUNKS + 1, go_right)
            when_in(t - LAG * (parts - 1 - me), CHUNKS + 1, go_left)
            when_in(t - LAG * far, CHUNKS + 1, finish)
            when_in(t - LAG * far - LAG, CHUNKS + 1, relay)
            return carry

        lax.fori_loop(first, last, tick, 0)

    def project(part):
        at = aligned(part * (rows // 2), rows // 2)
        first = fn_out[at, :]
        q_ref[at, :] = dot_nt(first, weight[0]).astype(BF16)
        k_out[at, :] = dot_nt(first, weight[1]).astype(BF16)
        v_out[at, :] = dot_nt(first, weight[2]).astype(BF16)

    lower = (iota((128, 128), 0) > iota((128, 128), 1)).astype(BF16)

    def count_tile(i, running):
        at = aligned(i * 128, 128)
        clusters = jnp.broadcast_to(crow[pl.ds(i, 1), :].astype(F32), (128, 128))
        clusters = jnp.transpose(clusters).astype(jnp.int32)
        ccol[at, :] = clusters[:, :1]
        member = (clusters == lane).astype(F32)
        low = member.astype(BF16)
        member_ref[at, :] = low
        earlier = dot(lower, low) + running
        rcol_out[at, :] = jnp.sum(member * earlier, 1, keepdims=True)
        return running + jnp.sum(member, 0, keepdims=True)

    def place(i, carry):
        at = aligned(i * 256, 256)
        rank_row = rrow_out[:1, :].astype(jnp.int32)
        chosen = (iota((256, rows), 0) + i * 256 == rank_row).astype(BF16)
        qs_out[at, :] = (dot(chosen, q_ref[...]) * SCALE).astype(BF16)
        sorted_member = dot(chosen, member_ref[...])
        cls_out[at, :] = jnp.sum(
            sorted_member * iota((256, 128), 1).astype(F32), 1, keepdims=True
        ).astype(jnp.int32)
        return carry

    make_own(0, 4)
    ticks(0, 1)
    project(0)
    ticks(1, 2)
    make_own(4, 4)
    ticks(2, 4)
    project(1)
    ticks(4, 5)
    if pair:
        pass_on(1)
    counts = lax.fori_loop(0, tiles, count_tile, jnp.zeros((1, 128), F32))
    extended = jnp.concatenate([q_ref[...], jnp.ones((rows, 256 - width), BF16)], axis=1)
    sums = dot_tn(member_ref[...], extended)
    digits = jnp.floor(sums * 0.03125)
    wide = iota((CLP, 256), 1)
    packed = jnp.where(
        wide == width, digits, jnp.where(wide == width + 1, sums - 32.0 * digits, sums)
    )
    own[CENTRE] = jnp.concatenate(
        [packed, jnp.zeros((CLP, half_width - 256), F32)], axis=1
    ).astype(BF16)
    ticks(5, 6)
    make_own(8, CHUNKS - 8)
    ticks(6, 7)
    before = (iota((128, 128), 0) < iota((128, 128), 1)).astype(F32)
    starts = jnp.dot(
        jnp.broadcast_to(counts, (8, 128)), before, precision=HIGHEST, preferred_element_type=F32
    )
    starts_out[...] = starts.astype(jnp.int32)

    def ranks(i, carry):
        at = aligned(i * 128, 128)
        member = member_ref[at, :].astype(F32)
        rank = rcol_out[at, :] + jnp.sum(member * starts[:1], 1, keepdims=True)
        rcol_out[at, :] = rank
        turned = jnp.transpose(jnp.broadcast_to(rank, (128, 128)))
        rrow_out[:, at] = turned[:8]
        return carry

    lax.fori_loop(0, tiles, ranks, 0)
    ticks(7, 8)
    if pair:
        pass_on(2)
    here = iota((CLP, rows), 1) + own_start
    hit = topk[:, :1] == here
    for t in range(1, TOPK):
        hit = hit | (topk[:, t : t + 1] == here)
    tm_out[...] = hit.astype(F32).astype(BF16)
    ticks(8, 9)

    lax.fori_loop(0, rows // 512, place, 0)
    ticks(9, 10)
    lax.fori_loop(rows // 512, rows // 256, place, 0)
    qs_out[rows:, :] = jnp.zeros((WIN, width), BF16)
    cls_out[rows:, :] = jnp.full((WIN, 1), -1, jnp.int32)
    ticks(10, CENTRE_TICK)
    gathered = csum[...]
    count = jnp.maximum(
        32.0 * gathered[:, width : width + 1] + gathered[:, width + 1 : width + 2], 1.0
    )
    count_out[...] = jnp.broadcast_to(count, (CLP, 128))
    centre = (gathered[:, :width] / count).astype(BF16)
    centre_out[...] = centre
    same = sequence_masks(lengths, topk, rows)
    stats = jnp.zeros((CLP, 128), F32)
    rest = jnp.zeros((CLP, width), F32)
    for h in range(heads):
        top = tm_out[...].astype(F32)
        mine_lanes = head_lanes(width, h)
        scores = dot_nt(jnp.where(mine_lanes, centre, jnp.zeros_like(centre)), k_out[...]) * SCALE
        scores = jnp.where(same, scores, NEGATIVE)
        largest = jnp.max(scores, 1, keepdims=True)
        raised = jnp.exp(scores - largest)
        total = jnp.sum(raised, 1, keepdims=True)
        within = raised * top
        mass = jnp.sum(within, 1, keepdims=True)
        rest = jnp.where(mine_lanes, dot((raised - within).astype(BF16), v_out[...]), rest)
        stats = jnp.where(lane == h, largest, stats)
        stats = jnp.where(lane == 8 + h, total, stats)
        stats = jnp.where(lane == 16 + h, mass, stats)
    rbuf[me] = rest.astype(BF16)
    sbuf[me] = jnp.transpose(stats)[:24]
    rest_copies = small_exchange(rbuf, rsend, rrecv, me, parts)
    stat_copies = small_exchange(sbuf, ssend, srecv, me, parts)
    ticks(CENTRE_TICK, CENTRE_TICK + 2)
    out_copies[1].wait_recv()
    out_copies[2].start()
    if pair:
        pass_on(3)
    ticks(CENTRE_TICK + 2, CENTRE_TICK + 3)
    early = CHUNKS // 2
    ticks(CENTRE_TICK + 3, 19)

    def arrive(i, carry):
        core_copy(i).wait_recv()
        relay_copy(i).wait_recv()
        return carry

    def project_slots(first, count):
        for which in range(2):
            at = pl.ds(which * HALF + first * CHUNK, count * CHUNK)
            block = sfn_out[at, :]
            for which_weight, out, turned in ((1, ks_out, kst_out), (2, vs_out, vst_out)):
                product = dot_nt(block, weight[which_weight])
                out[at, :] = product.astype(BF16)
                turned[:, at] = jnp.transpose(product).astype(BF16)

    lax.fori_loop(0, early, arrive, 0)
    project_slots(0, early)
    ticks(19, 20)
    for copy in rest_copies + stat_copies:
        copy.start()
    ticks(20, CHUNKS + 1 + LAG * parts)
    lax.fori_loop(early, CHUNKS, arrive, 0)
    sfn_copy = pltpu.make_async_copy(sfn_out, sfn_hbm, local_sems.at[3])
    sfn_copy.start()
    project_slots(early, CHUNKS - early)
    for copy in rest_copies + stat_copies:
        copy.wait_recv()
    largest = sbuf[0][:8]
    for d in range(1, parts):
        largest = jnp.maximum(largest, sbuf[d][:8])
    total = jnp.zeros((8, 128), F32)
    mass = jnp.zeros((8, 128), F32)
    factors = []
    for d in range(parts):
        factor = jnp.exp(sbuf[d][:8] - largest)
        total += factor * sbuf[d][8:16]
        mass += factor * sbuf[d][16:24]
        factors.append(factor)
    live = iota((8, 128), 0) < heads
    total = jnp.where(live, total, 1.0)
    mass = mass / total
    table = [largest, total, mass] + [factor / total for factor in factors]
    table.append(jnp.zeros((128 - 8 * len(table), 128), F32))
    columns_table = jnp.transpose(jnp.concatenate(table, axis=0))
    merged_out[...] = columns_table
    mass_rows = jnp.zeros((CLP, width), F32)
    rest_rows = jnp.zeros((CLP, width), F32)
    for h in range(heads):
        mine_lanes = head_lanes(width, h)
        mass_rows = jnp.where(mine_lanes, columns_table[:, 16 + h : 17 + h], mass_rows)
        rest = jnp.zeros((CLP, width), F32)
        for d in range(parts):
            lane_at = 24 + 8 * d + h
            rest += columns_table[:, lane_at : lane_at + 1] * rbuf[d].astype(F32)
        rest_rows = jnp.where(mine_lanes, rest, rest_rows)
    rows_out[:, :width] = mass_rows
    rows_out[:, width:] = rest_rows

    def drain(i, carry):
        @pl.when(me < parts - 1)
        def _():
            right_copy(i).wait_send()

        @pl.when(me > 0)
        def _():
            left_copy(i).wait_send()

        return carry

    def drain_slots(i, carry):
        x_copy(i).wait_send()
        core_copy(i).wait_send()
        relay_copy(i).wait_send()
        return carry

    lax.fori_loop(0, CHUNKS + 1, drain, 0)
    lax.fori_loop(0, CHUNKS, drain_slots, 0)
    for copy in rest_copies + stat_copies + out_copies:
        copy.wait_send()
    out_copies[0].wait_recv()
    out_copies[2].wait_recv()
    if pair:
        for origin in range(parts):
            across(origin, wexp).wait()

            @pl.when((me < parts - 1) & (origin <= me))
            def _():
                hop(origin, wexp, wsend, me + 1).wait_send()

            @pl.when((me > 0) & (origin >= me))
            def _():
                hop(origin, wexp, wsend_left, me + parts - 1).wait_send()

        shrink_peer.wait()
        shard_own.wait()
    out_own.wait()
    fn_copy.wait()
    sfn_copy.wait()


def front(pair, lengths, tokens, clusters, weight, gain, bias, scol, topk, wexp, wshr, wout, parts):
    rows, model = tokens.shape
    width = weight.shape[1]
    shape = jax.ShapeDtypeStruct
    dma = pltpu.SemaphoreType.DMA
    chain = pltpu.VMEM((CHUNKS + 1, CHUNK, model // 2), BF16)
    whole = (model, wexp.shape[1]) if pair else (16, 128)
    anywhere = [pl.BlockSpec(memory_space=pl.ANY)]
    return pl.pallas_call(
        functools.partial(front_kernel, pair),
        out_shape=(
            shape(tokens.shape, BF16),
            shape((SLOTS, model), BF16),
            shape((rows + WIN, width), BF16),
            shape((rows, width), BF16),
            shape((rows, width), BF16),
            shape((SLOTS, width), BF16),
            shape((SLOTS, width), BF16),
            shape((width, SLOTS), BF16),
            shape((width, SLOTS), BF16),
            shape((8, 128), jnp.int32),
            shape((rows, 1), F32),
            shape((8, rows), F32),
            shape((rows + WIN, 1), jnp.int32),
            shape((CLP, width), BF16),
            shape((CLP, rows), BF16),
            shape((CLP, 2 * width), F32),
            shape((CLP, 128), F32),
            shape((CLP, 128), F32),
            shape((lax.axis_size("hid") * width, model), BF16),
            shape(whole, BF16),
            shape(wshr.shape, BF16),
            shape((rows, 1), jnp.int32),
        ),
        in_specs=[pl.BlockSpec(memory_space=pltpu.SMEM)] + vmem(7) + anywhere * 3,
        out_specs=tuple(anywhere * 2 + vmem(16) + anywhere * 3 + vmem(1)),
        scratch_shapes=[
            pltpu.VMEM((rows, model), BF16),
            pltpu.VMEM((SLOTS, model), BF16),
            pltpu.VMEM((rows, width), BF16),
            pltpu.VMEM((rows, 128), BF16),
            pltpu.VMEM((CLP, model // 2), F32),
            pltpu.VMEM((parts, CLP, width), BF16),
            pltpu.VMEM((parts, 24, 128), F32),
            chain, chain, chain, chain, chain,
        ]
        + [dma((parts,))] * 4
        + [dma((CHUNKS + 1,))] * 10
        + [dma((3,))] * 2
        + [dma((parts,))] * 5
        + [dma, dma, dma((4,))],
        compiler_params=pltpu.CompilerParams(
            vmem_limit_bytes=56 << 20, collective_id=0, has_side_effects=True
        ),
        name="front",
    )(
        lengths, tokens, clusters.reshape(rows // 128, 128), weight, gain, bias, scol, topk,
        wexp, wshr, wout,
    )


UNROLL = 4
FORWARD_UNROLL = (4, 2)
BACKWARD_UNROLL = (2, 2)
SMALL = 64


def list_windows(starts, rows, lists):
    big_group, big_row, small_group, small_row = lists

    def one_group(g, counts):
        big, small = counts
        first, last = starts[0, g * GROUP], starts[0, g * GROUP + GROUP]
        base = first // 16 * 16
        span = jnp.where(last > first, last - base, 0)
        short = (span > 0) & (span <= SMALL)
        windows = jnp.where(span > SMALL, (span + WIN - 1) // WIN, 0)

        def one(w, carry):
            big_group[big + w] = g
            big_row[big + w] = base + w * WIN
            return carry

        lax.fori_loop(0, windows, one, 0)
        small_group[small] = g
        small_row[small] = base
        return big + windows, small + jnp.where(short, 1, 0)

    big, small = lax.fori_loop(0, GROUPS, one_group, (0, 0))
    for i in range(UNROLL):
        big_group[big + i] = 0
        big_row[big + i] = rows
        small_group[small + i] = 0
        small_row[small + i] = rows
    return big, small


def each_window(starts, rows, lists, window, unroll):
    big, small = list_windows(starts, rows, lists)
    for count, size, group_at, row_at, times in (
        (big, WIN, lists[0], lists[1], unroll[0]),
        (small, SMALL, lists[2], lists[3], unroll[1]),
    ):

        def several(n, carry):
            for i in range(times):
                window(*window_at(starts, group_at, row_at, n * times + i, size))
            return carry

        lax.fori_loop(0, (count + times - 1) // times, several, 0)


def window_probs(scores, mine, inside, h):
    part = jnp.where(mine, scores[:, h * GSLOTS : (h + 1) * GSLOTS], NEGATIVE)
    raised = jnp.exp(part - jnp.max(part, 1, keepdims=True))
    inverse = jnp.where(inside, 1.0 / jnp.sum(raised, 1, keepdims=True), 0.0)
    return raised * inverse


def window_at(starts, group_at, row_at, i, size):
    g = group_at[i]
    row = pl.multiple_of(row_at[i], 16)
    at = pl.ds(pl.multiple_of(g * GSLOTS, GSLOTS), GSLOTS)
    place = iota((size, 1), 0) + row
    inside = (place >= starts[0, g * GROUP]) & (place < starts[0, g * GROUP + GROUP])
    return size, g, pl.ds(row, size), at, inside


def exact_forward_kernel(
    starts, qs, cls, kt_hbm, vs_hbm, both, rcol, att_out, att_s, mix_s, kt, vs, sems, *lists
):
    rows, width = rcol.shape[0], qs.shape[1]
    heads = width // HEAD_DIM
    copies = [
        pltpu.make_async_copy(kt_hbm, kt, sems.at[0]),
        pltpu.make_async_copy(vs_hbm, vs, sems.at[1]),
    ]
    for copy in copies:
        copy.start()
    high = both[...].astype(BF16)
    low = (both[...] - high.astype(F32)).astype(BF16)
    step = (rows + WIN) // 5

    def spread(i, carry):
        at = pl.ds(pl.multiple_of(i * step, 16), step)
        member = (cls[at, :] == iota((step, 128), 1)).astype(BF16)
        mix_s[at, :] = dot(member, high) + dot(member, low)
        return carry

    lax.fori_loop(0, 5, spread, 0)
    for copy in copies:
        copy.wait()

    def window(size, g, here, at, inside):
        keys = block_diagonal_turned(kt[:, at], heads)
        values = block_diagonal(vs[at, :], heads)
        mine = cls[here, :] == iota((size, GSLOTS), 1) // TOPK + g * GROUP
        scores = dot(qs[here, :], keys)
        weights = [window_probs(scores, mine, inside, h).astype(BF16) for h in range(heads)]
        out = dot(jnp.concatenate(weights, axis=1), values)
        mix = mix_s[here, :]
        att_s[here, :] = jnp.where(inside, mix[:, :width] * out + mix[:, width:], att_s[here, :])

    each_window(starts, rows, lists, window, FORWARD_UNROLL)

    def unplace(i, carry):
        at = pl.ds(pl.multiple_of(i * 256, 256), 256)
        chosen = (iota((256, rows), 1) == rcol[at, :].astype(jnp.int32)).astype(BF16)
        att_out[at, :] = dot(chosen, att_s[:rows, :].astype(BF16)).astype(BF16)
        return carry

    lax.fori_loop(0, rows // 256, unplace, 0)


ANYWHERE = pl.BlockSpec(memory_space=pl.ANY)
LISTED = 64


def exact_forward(starts, qs, cls, ks, vs, both, rcol):
    rows, width = rcol.shape[0], qs.shape[1]
    shape = jax.ShapeDtypeStruct
    return pl.pallas_call(
        exact_forward_kernel,
        out_shape=shape((rows, width), BF16),
        in_specs=[pl.BlockSpec(memory_space=pltpu.SMEM)] + vmem(2) + [ANYWHERE] * 2 + vmem(2),
        out_specs=vmem(1)[0],
        scratch_shapes=[
            pltpu.VMEM((rows + WIN, width), F32),
            pltpu.VMEM((rows + WIN, 2 * width), F32),
            pltpu.VMEM((width, SLOTS), BF16),
            pltpu.VMEM((SLOTS, width), BF16),
            pltpu.SemaphoreType.DMA((2,)),
        ]
        + [pltpu.SMEM((LISTED,), jnp.int32)] * 4,
        compiler_params=pltpu.CompilerParams(vmem_limit_bytes=62 << 20),
        name="exact_forward",
    )(starts, qs, cls, ks, vs, both, rcol)


def exact_backward_kernel(
    starts, qs, cls, ks_hbm, kt_hbm, vt_hbm, rows_in, rcol, rrow, grad,
    dq_out, dkvt_out, centre_out,
    grad_s, mass_s, dq_s, part_s, dkv_s, ks, kt, vt, sems, *lists,
):
    rows, width = rcol.shape[0], qs.shape[1]
    heads = width // HEAD_DIM
    copies = [
        pltpu.make_async_copy(ks_hbm, ks, sems.at[0]),
        pltpu.make_async_copy(kt_hbm, kt, sems.at[1]),
        pltpu.make_async_copy(vt_hbm, vt, sems.at[2]),
    ]
    for copy in copies:
        copy.start()
    mass_rows = rows_in[:, :width]
    high = mass_rows.astype(BF16)
    low = (mass_rows - high.astype(F32)).astype(BF16)
    rank_row = rrow[:1, :].astype(jnp.int32)

    def place(i, carry):
        at = pl.ds(pl.multiple_of(i * 256, 256), 256)
        chosen = (iota((256, rows), 0) + i * 256 == rank_row).astype(BF16)
        grad_s[at, :] = dot(chosen, grad[...]).astype(BF16)
        member = (cls[at, :] == iota((256, 128), 1)).astype(BF16)
        mass_s[at, :] = dot(member, high) + dot(member, low)
        return carry

    lax.fori_loop(0, rows // 256, place, 0)
    grad_s[rows:, :] = jnp.zeros((WIN, width), BF16)
    mass_s[rows:, :] = jnp.zeros((WIN, width), F32)
    dkv_s[...] = jnp.zeros_like(dkv_s)
    for copy in copies:
        copy.wait()

    def window(size, g, here, at, inside):
        keys = block_diagonal(ks[at, :], heads)
        mine = cls[here, :] == iota((size, GSLOTS), 1) // TOPK + g * GROUP
        query, upstream = qs[here, :], grad_s[here, :]
        scores = dot(query, block_diagonal_turned(kt[:, at], heads))
        against = dot(upstream, block_diagonal_turned(vt[:, at], heads))
        mass = mass_s[here, :]
        weights, score_grads = [], []
        mass_part = jnp.zeros((size, width), F32)
        for h in range(heads):
            cut = slice(h * GSLOTS, (h + 1) * GSLOTS)
            probs = window_probs(scores, mine, inside, h)
            meeting = jnp.sum(probs * against[:, cut], 1, keepdims=True)
            weighted = probs * mass[:, h * HEAD_DIM : h * HEAD_DIM + 1]
            weights.append(weighted.astype(BF16))
            score_grads.append((weighted * (against[:, cut] - meeting)).astype(BF16))
            mass_part = jnp.where(head_lanes(width, h), meeting, mass_part)
        score_grad = jnp.concatenate(score_grads, axis=1)
        weight = jnp.concatenate(weights, axis=1)
        dq = dot(score_grad, keys) * SCALE
        dq_s[here, :] = jnp.where(inside, dq, dq_s[here, :])
        part_s[here, :] = jnp.where(inside, mass_part, part_s[here, :])
        pair = jnp.concatenate(
            [
                diagonal_blocks_turned(dot_tn(query, score_grad), heads),
                diagonal_blocks_turned(dot_tn(upstream, weight), heads),
            ],
            axis=0,
        )
        dkv_s[:, at] = dkv_s[:, at] + pair

    each_window(starts, rows, lists, window, BACKWARD_UNROLL)
    centre_out[...] = jnp.zeros_like(centre_out)

    def finish_group(g, carry):
        at = pl.ds(pl.multiple_of(g * GSLOTS, GSLOTS), GSLOTS)
        dkvt_out[:, at] = dkv_s[:, at].astype(BF16)
        return carry

    lax.fori_loop(0, GROUPS, finish_group, 0)

    def unplace(i, carry):
        at = pl.ds(pl.multiple_of(i * 256, 256), 256)
        chosen = (iota((256, rows), 1) == rcol[at, :].astype(jnp.int32)).astype(BF16)
        dq_out[at, :] = dot(chosen, dq_s[:rows, :].astype(BF16)).astype(BF16)
        member = (cls[at, :] == iota((256, 128), 1)).astype(BF16)
        pair = jnp.concatenate([part_s[at, :].astype(BF16), grad_s[at, :]], axis=1)
        centre_out[...] += dot_tn(member, pair)
        return carry

    lax.fori_loop(0, rows // 256, unplace, 0)


def exact_backward(starts, qs, cls, ks, kt, vt, rows_in, rcol, rrow, grad):
    rows, width = rcol.shape[0], qs.shape[1]
    shape = jax.ShapeDtypeStruct
    return pl.pallas_call(
        exact_backward_kernel,
        out_shape=(
            shape((rows, width), BF16),
            shape((2 * width, SLOTS), BF16),
            shape((CLP, 2 * width), F32),
        ),
        in_specs=[pl.BlockSpec(memory_space=pltpu.SMEM)] + vmem(2) + [ANYWHERE] * 3 + vmem(4),
        out_specs=tuple(vmem(3)),
        scratch_shapes=[
            pltpu.VMEM((rows + WIN, width), BF16),
            pltpu.VMEM((rows + WIN, width), F32),
            pltpu.VMEM((rows + WIN, width), F32),
            pltpu.VMEM((rows + WIN, width), F32),
            pltpu.VMEM((2 * width, SLOTS), F32),
            pltpu.VMEM((SLOTS, width), BF16),
            pltpu.VMEM((width, SLOTS), BF16),
            pltpu.VMEM((width, SLOTS), BF16),
            pltpu.SemaphoreType.DMA((3,)),
        ]
        + [pltpu.SMEM((LISTED,), jnp.int32)] * 4,
        compiler_params=pltpu.CompilerParams(vmem_limit_bytes=62 << 20),
        name="exact_backward",
    )(starts, qs, cls, ks, kt, vt, rows_in, rcol, rrow, grad)


def gelu_parts(values):
    slope = 0.7978845608028654
    squared = values * values
    turned = jnp.tanh(slope * values * (1.0 + 0.044715 * squared))
    half = 0.5 * (1.0 + turned)
    rise = half + 0.5 * slope * values * (1.0 - turned * turned) * (1.0 + 0.134145 * squared)
    return (values * half, rise)


def middle_kernel(
    pair, parts, tok_hbm, cot_hbm, att, wout_own, wout_hbm, wexp_hbm, gain, bias, shr_own, shr_one, shr_two, shr_three, shr_peer,
    mid_out, mgrad_out, agrad_out, hsum_out, wo_out, gains_out, *refs,
):
    grad_outs, refs = refs[: 2 + parts if pair else 1], refs[2 + parts if pair else 1 :]
    middle_body(
        pair, tok_hbm, cot_hbm, att, wout_own, wout_hbm, wexp_hbm, gain, bias,
        (shr_own, shr_one, shr_two, shr_three), shr_peer, mid_out, mgrad_out, agrad_out, hsum_out, wo_out, gains_out, grad_outs, *refs,
    )


def middle_body(
    pair, tok_hbm, cot_hbm, att, wout_own, wout_hbm, wexp_hbm, gain, bias, shards, shr_peer,
    mid_out, mgrad_out, agrad_out, hsum_out, wo_out, gains_out, grad_outs,
    tok, cot, wout, wexp, fetch_sems, wshr_ref, att_peer, cat, xcat, sn, act, hg, sp_own, sp_send, sp_recv, hp_own, hp_send, hp_recv,
    sx_send, sx_recv, branch, kept,
    asend, arecv, xsend, xrecv, rsend, rrecv, ssend, srecv, hsend, hrecv, sxs, sxr, bsend, brecv,
    wysend, wyrecv,
):
    rows, width = att.shape
    model = tok.shape[1]
    fetches = [
        pltpu.make_async_copy(source, target, fetch_sems.at[i])
        for i, (source, target) in enumerate(
            ((tok_hbm, tok), (wout_hbm, wout), (wexp_hbm, wexp), (cot_hbm, cot))
        )
    ]
    for fetch in fetches:
        fetch.start()
    half_width = 2 * width
    half_rows = rows // 2
    blocks = half_rows // 128
    hid = lax.axis_index("hid")
    core, side = lax.rem(hid, 2), hid // 2
    core_peer = {"hid": hid + 1 - 2 * core}
    x_peer = {"hid": hid + 2 - 4 * side}

    dp = lax.axis_index("dp")
    greeted = [core_peer, x_peer] + ([{"dp": 1 - dp}] if pair else [])
    barrier = greet(greeted)
    gains_out[...] = jnp.zeros_like(gains_out)
    pl.semaphore_wait(barrier, len(greeted))

    units = wexp.shape[1]
    if pair:
        wshr = wshr_ref
        n_dm, my_dm = lax.axis_size("dm"), lax.axis_index("dm")
        shard = model // (2 * n_dm)

        def shard_rows(d, step):
            owner = lax.rem(my_dm + n_dm - step, n_dm)
            return pl.ds(pl.multiple_of((d * n_dm + owner) * shard, 32), shard)

        shard_copies = [
            remote(
                shards[step], wshr.at[shard_rows(dp, step), :], wysend.at[step], wyrecv.at[step],
                {"dp": 1 - dp},
            )
            for step in range(1, n_dm)
        ]
    else:
        wshr = shards[0]

    def block_rows(j, which):
        return pl.ds(pl.multiple_of(which * half_rows + j * 128, 128), 128)

    def own_rows(j):
        return pl.ds(pl.multiple_of(j * 128, 128), 128)

    att_copy = remote(att, att_peer, asend, arecv, core_peer)
    att_copy.start()
    if pair:
        for copy in shard_copies:
            copy.start()
        for step in range(n_dm):
            wshr[shard_rows(dp, step), :] = shards[step][...]
        wshr[shard_rows(1 - dp, 0), :] = shr_peer[...]

    def x_copy(j):
        block = block_rows(j, core)
        return remote(cat.at[block, :], xcat.at[block, :], xsend.at[j], xrecv.at[j], x_peer)

    def relay_copy(j):
        block = xcat.at[block_rows(j, core), :]
        return remote(block, block, rsend.at[j], rrecv.at[j], core_peer)

    def sp_copy(j):
        return remote(sp_send.at[j], sp_recv.at[j], ssend.at[j], srecv.at[j], core_peer)

    def hp_copy(j):
        return remote(hp_send.at[j], hp_recv.at[j], hsend.at[j], hrecv.at[j], core_peer)

    def sx_copy(j):
        return remote(sx_send.at[j], sx_recv.at[j], sxs.at[j], sxr.at[j], x_peer)

    def branch_copy(j):
        block = branch.at[block_rows(j, core), :]
        return remote(block, block, bsend.at[j], brecv.at[j], core_peer)

    def join(at):
        mine, other = att[at, :], att_peer[at, :]
        cat[at, :] = jnp.where(
            core == 0,
            jnp.concatenate([mine, other], axis=1),
            jnp.concatenate([other, mine], axis=1),
        )

    att_copy.wait_recv()

    def spread(j, carry):
        join(block_rows(j, core))
        x_copy(j).start()
        return carry

    lax.fori_loop(0, blocks, spread, 0)

    def join_other(j, carry):
        join(block_rows(j, 1 - core))
        return carry

    lax.fori_loop(0, blocks, join_other, 0)
    for fetch in fetches:
        fetch.wait()

    def both(ref, j):
        return jnp.concatenate([ref[block_rows(j, core), :], ref[block_rows(j, 1 - core), :]], axis=0)

    def store_both(ref, j, values):
        ref[block_rows(j, core), :] = values[:128]
        ref[block_rows(j, 1 - core), :] = values[128:]

    own_half = pl.ds(pl.multiple_of(side * half_width, 128), half_width)
    other_half = pl.ds(pl.multiple_of((1 - side) * half_width, 128), half_width)

    def forward(j):
        x_copy(j).wait_recv()
        relay_copy(j).start()
        relay_copy(j).wait_recv()
        attention = dot(both(cat, j), wout[own_half, :]) + dot(both(xcat, j), wout[other_half, :])
        middle = both(tok, j).astype(F32) + attention
        mid_out[own_rows(j), :] = middle[:128]
        normed, _ = norm_parts(middle)
        second = (normed * gain[...][None] + bias[...][None]).astype(BF16)
        store_both(sn, j, second)
        hidden = dot(second, wexp[...])
        value, rise = gelu_parts(hidden)
        value = value.astype(BF16)
        store_both(act, j, value)
        if pair:

            @pl.when(j == 0)
            def _():
                for copy in shard_copies:
                    copy.wait_recv()

        grad = (dot(both(cot, j), wshr[...]) * rise).astype(BF16)
        store_both(hg, j, grad)
        part = dot_nt(grad, wexp[...])
        sp_own[j] = part[:128]
        sp_send[j] = part[128:].astype(BF16)
        sp_copy(j).start()
        part = dot_nt(value, wshr[...])
        hp_own[j] = part[:128]
        hp_send[j] = part[128:].astype(BF16)
        hp_copy(j).start()

    def chip_sum(j):
        sp_copy(j).wait_recv()
        total = sp_own[j] + sp_recv[j].astype(F32)
        sx_send[j] = total.astype(BF16)
        sx_copy(j).start()
        hp_copy(j).wait_recv()
        hsum_out[own_rows(j), :] = (hp_own[j] + hp_recv[j].astype(F32)).astype(BF16)

    def norm_grad(j):
        sx_copy(j).wait_recv()
        second_grad = sx_send[j].astype(F32) + sx_recv[j].astype(F32)
        normed, spread_two = norm_parts(mid_out[own_rows(j), :])
        inner, gain_part, bias_part = norm_back(second_grad, normed, spread_two, gain[...][None])
        gains_out[0:1, :] += gain_part[None]
        gains_out[1:2, :] += bias_part[None]
        middle_grad = cot[block_rows(j, core), :].astype(F32) + inner
        mgrad_out[own_rows(j), :] = middle_grad
        branch[block_rows(j, core), :] = middle_grad.astype(BF16)
        branch_copy(j).start()

    def attended_grad(j):
        branch_copy(j).wait_recv()
        for which in range(2):
            at = block_rows(j, which)
            agrad_out[at, :] = dot_nt(branch[at, :], wout_own[...]).astype(BF16)

    def when_block(j, work):
        @pl.when((j >= 0) & (j < blocks))
        def _():
            work(j)

    def ticks(first, last):
        def tick(t, carry):
            when_block(t - 1, chip_sum)
            when_block(t, forward)
            when_block(t - 2, norm_grad)
            when_block(t - 3, attended_grad)
            return carry

        lax.fori_loop(first, last, tick, 0)

    half = model // 2
    part_rows = half if pair else model

    def weight_grad(left, right, which):
        return dot_tn(left[:, aligned(which * half, part_rows)], right[...]).astype(BF16)

    ticks(0, blocks)
    if pair:
        keep_out, give_out = grad_outs[0], grad_outs[1]
        for d in range(2):
            kept[d] = weight_grad(sn, hg, d)
    else:
        grad_outs[0][:, :units] = weight_grad(sn, hg, 0)
    ticks(blocks, blocks + 1)
    if pair:
        parts, me = lax.axis_size("dm"), lax.axis_index("dm")
        shard = half // parts
        for step in range(parts):
            quarter = pl.ds(pl.multiple_of(lax.rem(me + step, parts) * shard, 32), shard)
            for d in range(2):
                grad_outs[2 + step][d] = kept[d, quarter, :]
        give_out[:half, :] = weight_grad(cot, act, 1 - dp)
    else:
        grad_outs[0][:, units:] = weight_grad(cot, act, 0)
    ticks(blocks + 1, blocks + 2)
    if pair:
        keep_out[:half, :] = weight_grad(cot, act, dp)
    ticks(blocks + 2, blocks + 3)
    out_grad = dot_tn(att[...], branch[...]).astype(BF16)
    wo_out[...] = out_grad
    if pair:
        small = width // 2
        keep_out[half:, :] = wo_out[pl.ds(pl.multiple_of(dp * small, 32), small), :]
        give_out[half:, :] = wo_out[pl.ds(pl.multiple_of((1 - dp) * small, 32), small), :]

    def drain(j, carry):
        x_copy(j).wait_send()
        relay_copy(j).wait_send()
        sp_copy(j).wait_send()
        hp_copy(j).wait_send()
        sx_copy(j).wait_send()
        branch_copy(j).wait_send()
        return carry

    lax.fori_loop(0, blocks, drain, 0)
    att_copy.wait_send()
    if pair:
        for copy in shard_copies:
            copy.wait_send()


def middle(pair, tokens, cotangent, attended, wout_own, wout, wexp, gain, bias, shards, shr_peer):
    rows, model = tokens.shape
    width = attended.shape[1]
    units = wexp.shape[1]
    part_rows = model // 2 if pair else model
    spare = (2, part_rows, units) if pair else (2, 16, 128)
    parts = lax.axis_size("dm")
    if pair:
        grads = [(part_rows + width // 2, units)] * 2 + [(2, part_rows // parts, units)] * parts
    else:
        grads = [(model, 2 * units)]
    blocks = rows // 256
    shape = jax.ShapeDtypeStruct
    dma = pltpu.SemaphoreType.DMA
    low = pltpu.VMEM((blocks, 128, model), BF16)
    full = pltpu.VMEM((blocks, 128, model), F32)
    return pl.pallas_call(
        functools.partial(middle_kernel, pair, parts),
        out_shape=(
            shape((rows // 2, model), F32),
            shape((rows // 2, model), F32),
            shape((rows, width), BF16),
            shape((rows // 2, model), BF16),
            shape((width, model), BF16),
            shape((8, model), F32),
        )
        + tuple(shape(dims, BF16) for dims in grads),
        in_specs=[ANYWHERE] * 2 + vmem(2) + [ANYWHERE] * 2 + vmem(7),
        out_specs=tuple(vmem(6 + len(grads))),
        scratch_shapes=[
            pltpu.VMEM(tokens.shape, BF16),
            pltpu.VMEM(cotangent.shape, BF16),
            pltpu.VMEM(wout.shape, BF16),
            pltpu.VMEM(wexp.shape, BF16),
            pltpu.SemaphoreType.DMA((4,)),
            pltpu.VMEM((model, units) if pair else (16, 128), BF16),
            pltpu.VMEM((rows, width), BF16),
            pltpu.VMEM((rows, 2 * width), BF16),
            pltpu.VMEM((rows, 2 * width), BF16),
            pltpu.VMEM((rows, model), BF16),
            pltpu.VMEM((rows, units), BF16),
            pltpu.VMEM((rows, units), BF16),
            full, low, low, full, low, low, low, low,
            pltpu.VMEM((rows, model), BF16),
            pltpu.VMEM(spare, BF16),
            dma, dma,
        ]
        + [dma((blocks,))] * 12
        + [dma((4,)), dma((4,))],
        compiler_params=pltpu.CompilerParams(
            vmem_limit_bytes=60 << 20, collective_id=2, has_side_effects=True
        ),
        name="middle",
    )(tokens, cotangent, attended, wout_own, wout, wexp, gain, bias, *shards, shr_peer)


def tail_kernel(
    pair, lengths, dkvt, dq, summed, k, v, centre, topk, tm, merged, rows_in, counts, ccol, weight,
    fn_hbm, sfn, tok_hbm, gain, mgrad, srow, mid, hsum, hsum_x, second_gains,
    sh_keep, sh_given, ex_own, ex_one, ex_two, ex_three,
    result_out, tokens_out, qkv_out, out_out, gain_a, gain_b, gain_c, gain_d, expand_out, shrink_out,
    sbuf, cbuf, fgm, to_core, from_core, to_x, from_x, to_right, to_left, from_left,
    from_right, from_fin, pq, pkv, dense, dense_to_core, dense_from_core, dense_to_x, dense_from_x,
    dense_own, first, sfn_tile, grad_all, grad_from_y, grad_back, g_own, g_right, g_left, g_from_left,
    g_from_right, g_total, gain_sum, gain_core, gain_dm, gain_dp, gain_x, shrink_send, shrink_recv, expand_y, tok, fn, tile_sem, mid_sem, hsum_sem, tok_sem, fn_sem,
    ssend, srecv, csend, crecv,
    send_core, recv_core, send_x, recv_x, send_right, recv_left, send_left, recv_right, send_fin,
    recv_fin,
    dsend_core, drecv_core, dsend_x, drecv_x, fsend, frecv, tsend, trecv, osend, orecv,
    ysend, yrecv, gsend_right, grecv_left, gsend_left, grecv_right, asend, arecv,
    gcsend, gcrecv, gmsend, gmrecv, gpsend, gprecv, esend, erecv,
):
    gain_outs = (gain_a, gain_b, gain_c, gain_d)
    rows, width = k.shape
    model = tok.shape[1]
    heads = width // HEAD_DIM
    half_width = model // 2
    half_rows = rows // 2
    blocks = half_rows // 128
    parts = lax.axis_size("dm")
    me, hid, dp = lax.axis_index("dm"), lax.axis_index("hid"), lax.axis_index("dp")
    core, side = lax.rem(hid, 2), hid // 2
    core_peer = {"hid": hid + 1 - 2 * core}
    x_peer = {"hid": hid + 2 - 4 * side}
    y_peer = {"dp": 1 - dp}
    own_start = me * rows
    columns = aligned(side * half_width, half_width)
    other_columns = aligned((1 - side) * half_width, half_width)

    greeted = [{"dm": lax.rem(me + step, parts)} for step in range(1, parts)]
    greeted += [core_peer, x_peer] + ([y_peer] if pair else [])
    barrier = greet(greeted)

    wide = iota((CLP, 256), 1)
    packed = jnp.concatenate([summed[:, width:], jnp.zeros((CLP, 256 - width), F32)], axis=1)
    for h in range(heads):
        packed = jnp.where(wide == width + h, summed[:, h * HEAD_DIM : h * HEAD_DIM + 1], packed)
    sbuf[me] = packed.astype(BF16)
    dense_own[...] = jnp.zeros_like(dense_own)
    mid_copy = pltpu.make_async_copy(mid, dense, mid_sem)
    mid_copy.start()
    hsum_copy = pltpu.make_async_copy(hsum, dense_to_core, hsum_sem)
    hsum_copy.start()
    tok_copy = pltpu.make_async_copy(
        tok_hbm.at[aligned(core * half_rows, half_rows), :], tok, tok_sem
    )
    tok_copy.start()
    fn_copy = pltpu.make_async_copy(fn_hbm, fn, fn_sem)
    fn_copy.start()

    @pl.when(me == 0)
    def _():
        from_left[...] = jnp.zeros_like(from_left)
        g_from_left[...] = jnp.zeros_like(g_from_left)

    @pl.when(me == parts - 1)
    def _():
        from_right[...] = jnp.zeros_like(from_right)
        g_from_right[...] = jnp.zeros_like(g_from_right)

    pl.semaphore_wait(barrier, len(greeted))
    sum_copies = small_exchange(sbuf, ssend, srecv, me, parts)
    for copy in sum_copies:
        copy.start()

    def chunk_rows(i, which):
        return aligned(which * HALF + i * CHUNK, CHUNK)

    def block_rows(j, which):
        return aligned(which * half_rows + j * 128, 128)

    def own_rows(j):
        return aligned(j * 128, 128)

    def core_copy(i):
        return remote(to_core.at[i], from_core.at[i], send_core.at[i], recv_core.at[i], core_peer)

    def x_copy(i):
        return remote(to_x.at[i], from_x.at[i], send_x.at[i], recv_x.at[i], x_peer)

    right = {"dm": lax.rem(me + 1, parts)}
    left = {"dm": lax.rem(me + parts - 1, parts)}

    def right_copy(i):
        return remote(to_right.at[i], from_left.at[i], send_right.at[i], recv_left.at[i], right)

    def left_copy(i):
        return remote(to_left.at[i], from_right.at[i], send_left.at[i], recv_right.at[i], left)

    def fin_copy(i):
        return remote(from_x.at[i], from_fin.at[i], send_fin.at[i], recv_fin.at[i], core_peer)

    def dense_core_copy(j):
        return remote(
            dense_to_core.at[j], dense_from_core.at[j], dsend_core.at[j], drecv_core.at[j], core_peer
        )

    def dense_x_copy(j):
        return remote(dense_to_x.at[j], dense_from_x.at[j], dsend_x.at[j], drecv_x.at[j], x_peer)

    def first_copy(j):
        block = first.at[j, :, columns]
        return remote(block, block, fsend.at[j], frecv.at[j], x_peer)

    def tokens_copy(j):
        block = tokens_out.at[block_rows(j, core), :]
        return remote(block, block, tsend.at[j], trecv.at[j], core_peer)

    def result_copy(j):
        block = result_out.at[block_rows(j, core), :]
        return remote(block, block, osend.at[j], orecv.at[j], core_peer)

    def spread_back(start, count):
        at = aligned((1 - core) * HALF + start * CHUNK, count * CHUNK)
        other = dot_tn(dkvt[:, at], weight[width:, :])
        other = other.astype(BF16)
        for i in range(count):
            to_core[start + i] = other[i * CHUNK : (i + 1) * CHUNK]
            core_copy(start + i).start()
        at = aligned(core * HALF + start * CHUNK, count * CHUNK)
        mine = dot_tn(dkvt[:, at], weight[width:, :])
        mine = mine.astype(BF16)
        for i in range(count):
            fgm[start + i] = mine[i * CHUNK : (i + 1) * CHUNK]

    def chip_sum(i):
        core_copy(i).wait_recv()
        to_x[i] = fgm[i, :, other_columns] + from_core[i, :, other_columns]
        x_copy(i).start()

    def hid_sum(i):
        x_copy(i).wait_recv()
        fgm[i, :, columns] = (
            fgm[i, :, columns].astype(F32)
            + from_core[i, :, columns].astype(F32)
            + from_x[i].astype(F32)
        ).astype(BF16)

    def go_right(i):
        @pl.when(me > 0)
        def _():
            right_copy(i).wait_recv()

        @pl.when(me < parts - 1)
        def _():
            to_right[i] = fgm[i, :, columns] + from_left[i]
            right_copy(i).start()

    def go_left(i):
        @pl.when(me < parts - 1)
        def _():
            left_copy(i).wait_recv()

        @pl.when(me > 0)
        def _():
            to_left[i] = fgm[i, :, columns] + from_right[i]
            left_copy(i).start()

    def finish(i):
        from_x[i] = (
            fgm[i, :, columns].astype(F32) + from_left[i].astype(F32) + from_right[i].astype(F32)
        ).astype(BF16)
        fin_copy(i).start()

    def scatter(i):
        fin_copy(i).wait_recv()
        here = iota((half_rows, CHUNK), 0) + own_start + core * half_rows
        chosen = [
            (srow[:, chunk_rows(i, which)] == here).astype(BF16) for which in (core, 1 - core)
        ]
        picked = jnp.concatenate([from_x[i], from_fin[i]], axis=0)
        dense_own[...] += dot(jnp.concatenate(chosen, axis=1), picked)

    far = jnp.maximum(me, parts - 1 - me)

    def ticks(start, last):
        def tick(t, carry):
            ready = t
            when_in(ready, CHUNKS, hid_sum)
            when_in(ready - LAG * me, CHUNKS, go_right)
            when_in(ready - LAG * (parts - 1 - me), CHUNKS, go_left)
            when_in(ready - LAG * far, CHUNKS, finish)
            when_in(ready - LAG * far - 1, CHUNKS, scatter)
            return carry

        lax.fori_loop(start, last, tick, 0)

    if pair:
        shard = expand_out.shape[0]

        def shard_rows(m):
            return pl.ds(pl.multiple_of(m * shard, 32), shard)

        shrink_copies = []
        for step in range(1, parts):
            target = lax.rem(me + step, parts)
            shrink_send[step] = sh_keep[shard_rows(target), :] + sh_given[shard_rows(target), :]
            shrink_copies.append(
                remote(
                    shrink_send.at[step], shrink_recv.at[step], esend.at[step], erecv.at[step],
                    {"dm": target},
                )
            )
        for copy in shrink_copies:
            copy.start()
        expand_y[0] = (
            ex_own[1 - dp].astype(F32) + ex_one[1 - dp].astype(F32)
            + ex_two[1 - dp].astype(F32) + ex_three[1 - dp].astype(F32)
        ).astype(BF16)
        expand_copy = remote(expand_y.at[0], expand_y.at[1], esend.at[0], erecv.at[0], y_peer)
        expand_copy.start()

    def chip_sums(first, last):
        def one(i, carry):
            chip_sum(i)
            return carry

        lax.fori_loop(first, last, one, 0)

    spread_back(0, 3)
    chip_sums(0, 3)
    spread_back(3, 5)
    chip_sums(3, 8)
    spread_back(8, CHUNKS - 8)
    chip_sums(8, CHUNKS)

    def result_rows(j, carry):
        total = dense_to_core[j].astype(F32) + hsum_x[j].astype(F32)
        result_out[block_rows(j, core), :] = (dense[j] + total).astype(BF16)
        result_copy(j).start()
        return carry

    for copy in sum_copies:
        copy.wait_recv()
    total = sbuf[0].astype(F32)
    for d in range(1, parts):
        total += sbuf[d].astype(F32)
    same = sequence_masks(lengths, topk, rows)
    rest_grad = total[:, :width].astype(BF16)
    product = rest_grad.astype(F32) * rows_in[:, width:]
    score_grads, weights = [], []
    centre_part = jnp.zeros((CLP, width), F32)
    for h in range(heads):
        lanes = head_lanes(width, h)
        top = tm[...].astype(F32)
        zero = jnp.zeros((CLP, width), BF16)
        full = dot_nt(jnp.where(lanes, centre[...], zero), k[...]) * SCALE
        against = dot_nt(jnp.where(lanes, rest_grad, zero), v[...])
        largest, denominator = merged[:, h : h + 1], merged[:, 8 + h : 9 + h]
        mass = merged[:, 16 + h : 17 + h]
        mass_grad = total[:, width + h : width + h + 1]
        probs = jnp.where(same, jnp.exp(full - largest) / denominator, 0.0)
        mean = mass * mass_grad + jnp.sum(jnp.where(lanes, product, 0.0), 1, keepdims=True)
        grad = jnp.where(top > 0.5, mass_grad, against)
        score_grad = (probs * (grad - mean)).astype(BF16)
        centre_part = jnp.where(lanes, dot(score_grad, k[...]), centre_part)
        score_grads.append(score_grad)
        weights.append(jnp.where(top > 0.5, 0.0, probs).astype(BF16))
    cbuf[me] = (centre_part * SCALE).astype(BF16)
    centre_copies = small_exchange(cbuf, csend, crecv, me, parts)
    for copy in centre_copies:
        copy.start()
    score_grad = jnp.concatenate(score_grads, axis=0)
    rest_weight = jnp.concatenate(weights, axis=0)
    pkv[...] = jnp.concatenate(
        [
            (dot_tn(score_grad, block_diagonal(centre[...], heads)) * SCALE).astype(BF16),
            dot_tn(rest_weight, block_diagonal(rest_grad, heads)).astype(BF16),
        ],
        axis=1,
    )
    if pair:
        part = width // 2

        def y_rows(b, d):
            first = jnp.where(b == 3, 6 + d, d * 3 + b)
            return pl.ds(pl.multiple_of(first * part, 32), part)

        def y_copy(b):
            return remote(
                grad_all.at[y_rows(b, 1 - dp), :], grad_from_y.at[b], ysend.at[b], yrecv.at[b], y_peer
            )

        def y_back(b):
            return remote(
                grad_all.at[y_rows(b, dp), :], grad_back.at[b], asend.at[b], arecv.at[b], y_peer
            )

        def unit_right(u):
            return remote(g_right.at[u], g_from_left.at[u], gsend_right.at[u], grecv_left.at[u], right)

        def unit_left(u):
            return remote(g_left.at[u], g_from_right.at[u], gsend_left.at[u], grecv_right.at[u], left)

        def y_sum(turn):
            @pl.when(turn == 0)
            def _():
                both = sh_keep[model // 2 :, :] + sh_given[model // 2 :, :]
                g_own[0] = both[:, :half_width]
                g_own[1] = both[:, half_width:]

            @pl.when(turn > 0)
            def _():
                b = turn - 1
                y_copy(b).wait_recv()
                both = grad_all[y_rows(b, dp), :] + grad_from_y[b]
                g_own[2 * turn] = both[:, :half_width]
                g_own[2 * turn + 1] = both[:, half_width:]

        root = parts // 2

        def unit_up(u):
            @pl.when(me < root)
            def _():
                @pl.when(me > 0)
                def _():
                    unit_right(u).wait_recv()

                g_right[u] = g_own[u] + g_from_left[u]
                unit_right(u).start()

            @pl.when(me > root)
            def _():
                @pl.when(me < parts - 1)
                def _():
                    unit_left(u).wait_recv()

                g_left[u] = g_own[u] + g_from_right[u]
                unit_left(u).start()

        def unit_turn(u):
            unit_right(u).wait_recv()

            @pl.when(me < parts - 1)
            def _():
                unit_left(u).wait_recv()

            total = g_own[u] + g_from_left[u] + g_from_right[u]
            g_total[u] = total
            g_left[u] = total
            unit_left(u).start()

            @pl.when(me < parts - 1)
            def _():
                g_right[u] = total
                unit_right(u).start()

        def unit_down(u):
            @pl.when(me < root)
            def _():
                unit_left(u).wait_recv()
                g_total[u] = g_from_right[u]

                @pl.when(me > 0)
                def _():
                    g_left[u] = g_from_right[u]
                    unit_left(u).start()

            @pl.when(me > root)
            def _():
                unit_right(u).wait_recv()
                g_total[u] = g_from_left[u]

                @pl.when(me < parts - 1)
                def _():
                    g_right[u] = g_from_left[u]
                    unit_right(u).start()

        def y_return(turn):
            b = lax.rem(turn + 3, 4)
            grad_all[y_rows(b, dp), :half_width] = g_total[2 * turn]
            grad_all[y_rows(b, dp), half_width:] = g_total[2 * turn + 1]
            y_back(b).start()

        def gticks(start, last):
            def tick(t, carry):
                @pl.when(lax.rem(t, 2) == 0)
                def _():
                    when_in(t // 2, 4, y_sum)

                wait = jnp.where(me < root, me, parts - 1 - me)
                up = jnp.where(me == root, -1, t - 1 - LAG * wait)
                when_in(up, UNITS, unit_up)
                away = jnp.where(me < root, root - me, me - root)
                back = t - 1 - LAG * (root + away)

                @pl.when(me == root)
                def _():
                    when_in(back, UNITS, unit_turn)

                @pl.when(me != root)
                def _():
                    when_in(back, UNITS, unit_down)

                @pl.when((back >= 0) & (lax.rem(back + 1, 2) == 0))
                def _():
                    when_in((back - 1) // 2, 4, y_return)

                return carry

            lax.fori_loop(start, last, tick, 0)
    else:

        def gticks(start, last):
            pass

    def slot_tile(c, carry):
        cut = aligned(c * 256, 256)
        fetch = pltpu.make_async_copy(sfn.at[:, cut], sfn_tile, tile_sem)
        fetch.start()
        grad = dot_tn(pkv[...], fn[:, cut])
        fetch.wait()
        grad = (grad + dot(dkvt[...], sfn_tile[...])).astype(BF16)
        grad_all[:width, cut] = grad[:width]
        grad_all[3 * (width // 2) : 3 * (width // 2) + width, cut] = grad[width:]
        return carry

    ticks(0, 1)
    fn_copy.wait()
    lax.fori_loop(0, model // 256, slot_tile, 0)
    if pair:
        y_copy(0).start()
        y_copy(1).start()
    ticks(1, 2)
    mid_copy.wait()
    hsum_copy.wait()
    lax.fori_loop(0, blocks, result_rows, 0)
    ticks(2, 4)
    for copy in centre_copies:
        copy.wait_recv()
    centre_grad = cbuf[0].astype(F32)
    for d in range(1, parts):
        centre_grad += cbuf[d].astype(F32)
    centre_grad = centre_grad / counts[:, :1]
    high = centre_grad.astype(BF16)
    low = (centre_grad - high.astype(F32)).astype(BF16)

    def queries(i, carry):
        at = aligned(i * 256, 256)
        member = (ccol[at, :] == iota((256, 128), 1)).astype(BF16)
        pq[at, :] = (dq[at, :].astype(F32) + dot(member, high) + dot(member, low)).astype(BF16)
        return carry

    lax.fori_loop(0, rows // 256, queries, 0)
    query_grad = dot_tn(pq[...], fn[...]).astype(BF16)
    grad_all[width : width + width // 2, :] = query_grad[: width // 2]
    grad_all[5 * (width // 2) : 3 * width, :] = query_grad[width // 2 :]
    if pair:
        y_copy(2).start()
    ticks(4, 5)

    def dense_rows(which):
        at = aligned(which * half_rows, half_rows)
        return dot(pq[at, :], weight[:width, :]) + dot(pkv[at, :], weight[width:, :])

    other_dense = dense_rows(1 - core).astype(BF16)
    for j in range(blocks):
        dense_to_core[j] = other_dense[j * 128 : (j + 1) * 128]
        dense_core_copy(j).start()
    own_dense = dense_rows(core)
    for j in range(blocks):
        dense[j] = own_dense[j * 128 : (j + 1) * 128]
    ticks(5, 6)

    def dense_chip(j, carry):
        dense_core_copy(j).wait_recv()
        dense_to_x[j] = (
            dense[j, :, other_columns] + dense_from_core[j, :, other_columns].astype(F32)
        ).astype(BF16)
        dense_x_copy(j).start()
        return carry

    def dense_hid(j, carry):
        dense_x_copy(j).wait_recv()
        dense_own[own_rows(j), :] += (
            dense[j, :, columns]
            + dense_from_core[j, :, columns].astype(F32)
            + dense_from_x[j].astype(F32)
        )
        return carry

    lax.fori_loop(0, blocks, dense_chip, 0)
    last = CHUNKS + LAG * (parts - 1) + 1

    def joint(t, carry):
        ticks(t, t + 1)
        gticks(t - GSTART, t - GSTART + 1)
        return carry

    ticks(6, GSTART)
    lax.fori_loop(GSTART, last, joint, 0)
    done = last - GSTART
    lax.fori_loop(0, blocks, dense_hid, 0)
    mgrad_copy = pltpu.make_async_copy(mgrad, dense, mid_sem)
    mgrad_copy.start()

    gain_sum[...] = jnp.zeros_like(gain_sum)
    tok_copy.wait()

    def first_send(j, carry):
        grad = dense_own[own_rows(j), :].astype(BF16)
        first[j, :, columns] = grad
        first_copy(j).start()
        return carry

    lax.fori_loop(0, blocks, first_send, 0)

    def first_gains(j, carry):
        centred = tok[own_rows(j), :].astype(F32)
        mean = jnp.mean(centred, -1, keepdims=True)
        variance = jnp.mean(jnp.square(centred - mean), -1, keepdims=True)
        normed = (tok[own_rows(j), columns].astype(F32) - mean) * lax.rsqrt(
            variance + EPSILON
        )
        grad = first[j, :, columns].astype(F32)
        gain_sum[0:1, columns] += jnp.sum(grad * normed, 0, keepdims=True)
        gain_sum[1:2, columns] += jnp.sum(grad, 0, keepdims=True)
        return carry

    lax.fori_loop(0, blocks, first_gains, 0)
    gain_sum[2:4, columns] = second_gains[0:2, columns]
    if pair:
        core_gain = remote(gain_sum, gain_core, gcsend, gcrecv, core_peer)
        core_gain.start()
    gticks(done, done + 2)

    def first_back(j, carry):
        first_copy(j).wait_recv()
        at = block_rows(j, core)
        normed, spread = norm_parts(tok[own_rows(j), :].astype(F32))
        inner, _, _ = norm_back(first[j].astype(F32), normed, spread, gain[...][None])
        tokens_out[at, :] = (dense[j] + inner).astype(BF16)
        tokens_copy(j).start()
        return carry

    mgrad_copy.wait()
    if pair:
        core_gain.wait_recv()
        gain_dm[me] = gain_sum[...] + gain_core[...]
        dm_gains = small_exchange(gain_dm, gmsend, gmrecv, me, parts)
        for copy in dm_gains:
            copy.start()
    lax.fori_loop(0, 1, first_back, 0)
    gticks(done + 2, done + 4)
    lax.fori_loop(1, 2, first_back, 0)
    if pair:
        for copy in dm_gains:
            copy.wait_recv()
        line = gain_dm[0]
        for d in range(1, parts):
            line = line + gain_dm[d]
        gain_dp[0] = line
        dp_gain = remote(gain_dp.at[0], gain_dp.at[1], gpsend.at[0], gprecv.at[0], y_peer)
        dp_gain.start()
    lax.fori_loop(2, 4, first_back, 0)
    if pair:
        dp_gain.wait()
        gain_x[0] = gain_dp[0] + gain_dp[1]
        x_gain = remote(gain_x.at[0], gain_x.at[1], gpsend.at[1], gprecv.at[1], x_peer)
        x_gain.start()
    lax.fori_loop(4, blocks, first_back, 0)
    if pair:
        gticks(done + 4, 1 + LAG * 2 * (parts // 2) + UNITS)
        for b in range(4):
            if b < 3:
                y_copy(b).wait_send()
            y_back(b).wait_recv()
            grad_all[y_rows(b, 1 - dp), :] = grad_back[b]
    small = width // 2
    qkv_out[0, :small] = grad_all[width : width + small, :]
    qkv_out[0, small:] = grad_all[5 * small : 6 * small, :]
    qkv_out[1] = grad_all[:width, :]
    qkv_out[2] = grad_all[3 * small : 5 * small, :]
    if pair:
        out_out[...] = grad_all[6 * small :, :].astype(F32)
    if pair:
        grad = sh_keep[shard_rows(me), :].astype(F32) + sh_given[shard_rows(me), :].astype(F32)
        for step in range(1, parts):
            shrink_copies[step - 1].wait()
            grad = grad + shrink_recv[step].astype(F32)
        shrink_out[...] = grad
        expand_copy.wait()
        grad = expand_y[1].astype(F32)
        for block in (ex_own, ex_one, ex_two, ex_three):
            grad = grad + block[dp].astype(F32)
        expand_out[...] = grad
        x_gain.wait()
        total = gain_x[0] + gain_x[1]
        core_gain.wait_send()
        for copy in dm_gains:
            copy.wait_send()
    else:
        total = gain_sum[...]
    for i, out in enumerate(gain_outs):
        out[...] = total[i]
    if pair:
        for b in range(4):
            y_back(b).wait_send()

        def drain_units(u, carry):
            @pl.when(me < parts - 1)
            def _():
                unit_right(u).wait_send()

            @pl.when(me > 0)
            def _():
                unit_left(u).wait_send()

            return carry

        lax.fori_loop(0, UNITS, drain_units, 0)

    def drain_blocks(j, carry):
        dense_core_copy(j).wait_send()
        dense_x_copy(j).wait_send()
        first_copy(j).wait_send()
        result_copy(j).wait()
        tokens_copy(j).wait()
        return carry

    def drain(i, carry):
        @pl.when(me < parts - 1)
        def _():
            right_copy(i).wait_send()

        @pl.when(me > 0)
        def _():
            left_copy(i).wait_send()

        core_copy(i).wait_send()
        x_copy(i).wait_send()
        fin_copy(i).wait_send()
        return carry

    lax.fori_loop(0, CHUNKS, drain, 0)
    for copy in sum_copies + centre_copies:
        copy.wait_send()
    lax.fori_loop(0, blocks, drain_blocks, 0)


def tail(
    pair, lengths, dkvt, dq, summed, k, v, centre, topk, tm, merged, rows_in, counts, clusters,
    weight, fn, sfn, tokens, gain, mgrad, srow, mid, hsum, hsum_x, second_gains,
    sh_keep, sh_given, ex_parts, parts,
):
    rows, width = k.shape
    model = tokens.shape[1]
    shape = jax.ShapeDtypeStruct
    dma = pltpu.SemaphoreType.DMA
    blocks = rows // 256
    owned = ex_parts[0].shape[1:]
    chain = pltpu.VMEM((CHUNKS, CHUNK, model // 2), BF16)
    whole = pltpu.VMEM((CHUNKS, CHUNK, model), BF16)
    unit = pltpu.VMEM((UNITS, width // 2, model // 2) if pair else (UNITS, 16, 128), BF16)
    return pl.pallas_call(
        functools.partial(tail_kernel, pair),
        out_shape=(
            shape((rows, model), BF16),
            shape((rows, model), BF16),
            shape((3, width, model), BF16),
            shape((width, model), F32),
            shape((model,), F32),
            shape((model,), F32),
            shape((model,), F32),
            shape((model,), F32),
            shape(owned, F32),
            shape(owned, F32),
        ),
        in_specs=[pl.BlockSpec(memory_space=pltpu.SMEM)]
        + vmem(13)
        + [pl.BlockSpec(memory_space=pl.ANY)] * 3
        + vmem(1)
        + [pl.BlockSpec(memory_space=pl.ANY)]
        + vmem(1)
        + [pl.BlockSpec(memory_space=pl.ANY)] * 2
        + vmem(8),
        out_specs=tuple(vmem(10)),
        scratch_shapes=[
            pltpu.VMEM((parts, CLP, 256), BF16),
            pltpu.VMEM((parts, CLP, width), BF16),
            whole, whole, whole,
            chain, chain, chain, chain, chain, chain,
            chain,
            pltpu.VMEM((rows, width), BF16),
            pltpu.VMEM((rows, 2 * width), BF16),
            pltpu.VMEM((blocks, 128, model), F32),
            pltpu.VMEM((blocks, 128, model), BF16),
            pltpu.VMEM((blocks, 128, model), BF16),
            pltpu.VMEM((blocks, 128, model // 2), BF16),
            pltpu.VMEM((blocks, 128, model // 2), BF16),
            pltpu.VMEM((rows // 2, model // 2), F32),
            pltpu.VMEM((blocks, 128, model), BF16),
            pltpu.VMEM((SLOTS, 256), BF16),
            pltpu.VMEM((4 * width, model), BF16),
            pltpu.VMEM((3, width // 2, model), BF16),
            pltpu.VMEM((4, width // 2, model), BF16),
            unit, unit, unit, unit, unit, unit,
            pltpu.VMEM((8, model), F32),
            pltpu.VMEM((8, model), F32),
            pltpu.VMEM((parts, 8, model), F32),
            pltpu.VMEM((2, 8, model), F32),
            pltpu.VMEM((2, 8, model), F32),
            pltpu.VMEM((parts,) + owned, BF16),
            pltpu.VMEM((parts,) + owned, BF16),
            pltpu.VMEM((2,) + owned, BF16),
            pltpu.VMEM((rows // 2, model), BF16),
            pltpu.VMEM((rows, model), BF16),
            dma, dma, dma, dma, dma,
        ]
        + [dma((parts,))] * 4
        + [dma((CHUNKS,))] * 10
        + [dma((blocks,))] * 10
        + [dma((3,))] * 2
        + [dma((UNITS,))] * 4
        + [dma((4,))] * 2
        + [dma, dma, dma((parts,)), dma((parts,)), dma((2,)), dma((2,)), dma((parts,)), dma((parts,))],
        compiler_params=pltpu.CompilerParams(
            vmem_limit_bytes=58 << 20, collective_id=1, has_side_effects=True
        ),
        name="tail",
    )(
        lengths, dkvt, dq, summed, k, v, centre, topk, tm, merged, rows_in, counts,
        clusters, weight.reshape(3 * width, model), fn, sfn, tokens, gain,
        mgrad.reshape(blocks, 128, model), srow, mid.reshape(blocks, 128, model),
        hsum.reshape(blocks, 128, model), hsum_x.reshape(blocks, 128, model), second_gains,
        sh_keep, sh_given, *ex_parts,
    )


def deliver_kernel(count, qkv, *refs):
    sources, qkv_out, targets = refs[:count], refs[count], refs[count + 1 :]
    for part in range(qkv.shape[0]):
        qkv_out[part] = qkv[part].astype(F32)
    for source, target in zip(sources, targets):
        target[...] = source[...]


def deliver(qkv, *arrays):
    shape = jax.ShapeDtypeStruct
    count = len(arrays)
    return pl.pallas_call(
        functools.partial(deliver_kernel, count),
        out_shape=(shape(qkv.shape, F32),) + tuple(shape(a.shape, a.dtype) for a in arrays),
        in_specs=vmem(count + 1),
        out_specs=tuple(vmem(count + 1)),
        compiler_params=pltpu.CompilerParams(vmem_limit_bytes=62 << 20),
        name="deliver",
    )(qkv, *arrays)


def shards(
    tokens,
    clusters,
    top_keys,
    lengths,
    qkv_weight,
    out_weight,
    first_gain,
    first_bias,
    second_gain,
    second_bias,
    expand_weight,
    shrink_weight,
    cotangent,
):
    parts, n_dp = lax.axis_size("dm"), lax.axis_size("dp")
    pair = n_dp == 2
    weight = jnp.swapaxes(qkv_weight, 1, 2)
    topk = jnp.pad(top_keys, ((0, CLP - CL), (0, 0)), constant_values=-1)
    flat = jnp.pad(top_keys.reshape(-1), (0, SLOTS - CL * TOPK), constant_values=-1)
    (
        first_normed, slot_normed, qs, k, v, ks, vs, kst, vst, starts, rcol, rrow, cls, centre, tm, rows_in,
        merged, counts, out_full, expand_full, shrink_peer, cluster_column,
    ) = front(
        pair, lengths, tokens, clusters, weight, first_gain, first_bias,
        flat.reshape(SLOTS, 1), topk, expand_weight, shrink_weight.T, out_weight, parts,
    )
    if pair:
        shrink_shards = [shrink_weight.T]
        source, _ = lax.optimization_barrier((shrink_weight.T, starts))
        for step in range(1, parts):
            shrink_shards.append(
                lax.ppermute(source, "dm", [(i, (i + step) % parts) for i in range(parts)])
            )
    else:
        expand_full = lax.all_gather(expand_weight, ("dp", "dm"), axis=0, tiled=True)
        shrink_full = lax.all_gather(shrink_weight.T, ("dp", "dm"), axis=0, tiled=True)
        shrink_shards = [shrink_full] + [jnp.zeros((16, 128), BF16)] * (parts - 1)
    attended = exact_forward(starts, qs, cls, kst, vs, rows_in, rcol)
    mid, middle_grad, attended_grad, hidden_sum, out_grad_part, second_parts, *grads = middle(
        pair, tokens, cotangent, attended, out_weight, out_full, expand_full,
        second_gain, second_bias, shrink_shards, shrink_peer,
    )
    hidden_sum_x = lax.ppermute(hidden_sum, "hid", [(i, i ^ 2) for i in range(lax.axis_size("hid"))])
    units = expand_weight.shape[1]
    if pair:
        shrink_keep, shrink_give, *expand_parts = grads
        shrink_given = lax.ppermute(shrink_give, "dp", [(0, 1), (1, 0)])
        expand_parts = [expand_parts[0]] + [
            lax.ppermute(expand_parts[step], "dm", [(i, (i + step) % parts) for i in range(parts)])
            for step in range(1, parts)
        ]
    else:
        summed_grads = lax.psum_scatter(grads[0], ("dp", "dm"), scatter_dimension=0, tiled=True)
        shrink_keep = shrink_given = jnp.zeros((16, 128), BF16)
        expand_parts = [jnp.zeros((2, 16, 128), BF16)] * parts
    dq, dkvt, summed = exact_backward(
        starts, qs, cls, ks, kst, vst, rows_in, rcol, rrow, attended_grad
    )
    result, tokens_grad, qkv_grad, out_grad, *gains, expand_grad, shrink_grad = tail(
        pair, lengths, dkvt, dq, summed, k, v, centre, topk, tm, merged, rows_in, counts, cluster_column,
        weight, first_normed, slot_normed, tokens, first_gain, middle_grad,
        flat.reshape(1, SLOTS), mid, hidden_sum, hidden_sum_x, second_parts,
        shrink_keep, shrink_given, expand_parts, parts,
    )
    if pair:
        qkv_grad, result, tokens_grad, out_grad, expand_grad, shrink_grad, *gains = deliver(
            qkv_grad, result, tokens_grad, out_grad, expand_grad, shrink_grad, *gains
        )
    else:
        out_grad = lax.psum(out_grad_part, ("dp", "dm")).astype(F32)
        qkv_grad = lax.psum(qkv_grad, ("dp", "dm"))
        gains = lax.psum(jnp.stack(gains), ("dp", "dm", "hid"))
        summed_grads = summed_grads.astype(F32)
        expand_grad, shrink_grad = summed_grads[:, :units], summed_grads[:, units:]
    return (
        result,
        tokens_grad,
        jnp.swapaxes(qkv_grad.astype(F32), 1, 2),
        out_grad,
        gains[0],
        gains[1],
        gains[2],
        gains[3],
        expand_grad,
        shrink_grad.T,
    )


def solution(mesh):
    in_specs = (
        P(("dp", "dm"), None),
        P(("dp", "dm")),
        P("dp", None),
        P("dp"),
        P(None, None, "hid"),
        P("hid", None),
        P(),
        P(),
        P(),
        P(),
        P(("dp", "dm"), "hid"),
        P("hid", ("dp", "dm")),
        P(("dp", "dm"), None),
    )
    out_specs = (
        P(("dp", "dm"), None),
        P(("dp", "dm"), None),
        P(None, None, "hid"),
        P("hid", None),
        P(),
        P(),
        P(),
        P(),
        P(("dp", "dm"), "hid"),
        P("hid", ("dp", "dm")),
    )
    return jax.shard_map(shards, mesh=mesh, in_specs=in_specs, out_specs=out_specs, check_vma=False)
```

```python
import functools

import jax
import jax.numpy as jnp
from jax import lax
from jax.experimental import pallas as pl
from jax.experimental.pallas import tpu as pltpu
from jax.sharding import PartitionSpec as P

HEAD_DIM = 64
CL = 100
TOPK = 32
CLP = 128
SLOTS = 3328
GROUP = 8
GSLOTS = GROUP * TOPK
GROUPS = SLOTS // GSLOTS
WIN = 160
HALF = SLOTS // 2
CHUNK = 128
CHUNKS = HALF // CHUNK
LAG = 2
CENTRE = 6
CENTRE_TICK = 14
GSTART = 10
UNITS = 8
EPSILON = 1e-05
NEGATIVE = -1e30
HIGHEST = lax.Precision.HIGHEST
F32 = jnp.float32
BF16 = jnp.bfloat16
MESH = pl.DeviceIdType.MESH
NT = (((1,), (1,)), ((), ()))
TN = (((0,), (0,)), ((), ()))
SCALE = HEAD_DIM ** (-0.5)


def dot(a, b):
    return jnp.dot(a, b, preferred_element_type=F32)


def dot_nt(a, b):
    return lax.dot_general(a, b, NT, preferred_element_type=F32)


def dot_tn(a, b):
    return lax.dot_general(a, b, TN, preferred_element_type=F32)


def iota(shape, dim):
    return lax.broadcasted_iota(jnp.int32, shape, dim)


def norm_parts(values):
    centred = values - jnp.mean(values, -1, keepdims=True)
    spread = lax.rsqrt(jnp.mean(centred * centred, -1, keepdims=True) + EPSILON)
    return (centred * spread, spread)


def norm_back(upstream, normed, spread, norm_gain):
    through = upstream * norm_gain
    inner = (
        through
        - jnp.mean(through, -1, keepdims=True)
        - normed * jnp.mean(through * normed, -1, keepdims=True)
    )
    return (spread * inner, jnp.sum(upstream * normed, 0), jnp.sum(upstream, 0))


def head_lanes(width, head):
    lane = iota((1, width), 1)
    return lane // HEAD_DIM == head


def block_diagonal(rows, heads):
    width = rows.shape[1]
    zero = jnp.zeros_like(rows)
    return jnp.concatenate(
        [jnp.where(head_lanes(width, h), rows, zero) for h in range(heads)], axis=0
    )


def block_diagonal_turned(turned, heads):
    zero = jnp.zeros((HEAD_DIM, turned.shape[1]), turned.dtype)
    columns = []
    for h in range(heads):
        mine = turned[h * HEAD_DIM : (h + 1) * HEAD_DIM]
        columns.append(jnp.concatenate([mine if i == h else zero for i in range(heads)], axis=0))
    return jnp.concatenate(columns, axis=1)


def diagonal_blocks_turned(full, heads):
    rows, size = full.shape[0] // heads, full.shape[1] // heads
    return jnp.concatenate(
        [full[h * rows : (h + 1) * rows, h * size : (h + 1) * size] for h in range(heads)], axis=0
    )


def diagonal_blocks(full, heads):
    rows, width = full.shape[0] // heads, full.shape[1]
    out = full[:rows]
    for h in range(1, heads):
        out = jnp.where(head_lanes(width, h), full[h * rows : (h + 1) * rows], out)
    return out


def vmem(n):
    return [pl.BlockSpec(memory_space=pltpu.VMEM)] * n


def remote(src, dst, send, recv, device):
    return pltpu.make_async_remote_copy(
        src_ref=src, dst_ref=dst, send_sem=send, recv_sem=recv, device_id=device,
        device_id_type=MESH,
    )


def greet(devices):
    barrier = pltpu.get_barrier_semaphore()
    for device in devices:
        pl.semaphore_signal(barrier, inc=1, device_id=device, device_id_type=MESH)
    return barrier


def small_exchange(buf, sends, recvs, me, parts):
    return [
        remote(
            buf.at[me], buf.at[me], sends.at[step], recvs.at[step],
            {"dm": lax.rem(me + step, parts)},
        )
        for step in range(1, parts)
    ]


def when_in(i, count, work):
    @pl.when((i >= 0) & (i < count))
    def _():
        work(i)


def aligned(start, size):
    return pl.ds(pl.multiple_of(start, 128), size)


def sequence_masks(lengths, topk, rows):
    own_start = lax.axis_index("dm") * rows
    key_second = iota((1, rows), 1) + own_start >= lengths[0]
    centre_second = topk[:, :1] >= lengths[0]
    return key_second == centre_second


def front_kernel(
    pair, lengths, tok, crow, weight, gain, bias, scol, topk, wexp, wshr, wout,
    fn_hbm, sfn_hbm, qs_out, k_out, v_out, ks_out, vs_out, kst_out, vst_out, starts_out, rcol_out, rrow_out,
    cls_out, centre_out, tm_out, rows_out, merged_out, count_out, wall_out, wfull_out, shr_peer_out, ccol,
    fn_out, sfn_out, q_ref, member_ref, csum, rbuf, sbuf, own, to_right, to_left, from_left, from_right,
    rsend, rrecv, ssend, srecv,
    send_right, recv_left, send_left, recv_right, send_x, recv_x, send_core, recv_core,
    send_relay, recv_relay, osend, orecv, wsend, wsend_left, wrecv, ysend, yrecv, psend, precv, local_sems,
):
    rows, model = tok.shape
    width = weight.shape[1]
    heads = width // HEAD_DIM
    half_width = model // 2
    tiles = rows // 128
    parts = lax.axis_size("dm")
    me, hid, dp = lax.axis_index("dm"), lax.axis_index("hid"), lax.axis_index("dp")
    core, side = lax.rem(hid, 2), hid // 2
    core_peer = {"hid": hid + 1 - 2 * core}
    x_peer = {"hid": hid + 2 - 4 * side}
    lane = iota((128, 128), 1)
    columns = aligned(side * half_width, half_width)
    other_columns = aligned((1 - side) * half_width, half_width)
    own_start = me * rows

    greeted = [{"dm": lax.rem(me + step, parts)} for step in range(1, parts)]
    greeted += [core_peer, x_peer]
    if pair:
        greeted.append({"dp": 1 - dp})
    barrier = greet(greeted)

    out_rows = pl.ds(pl.multiple_of(hid * width, 64), width)
    out_own = pltpu.make_async_copy(wout, wall_out.at[out_rows, :], local_sems.at[0])
    out_own.start()
    out_x_rows = pl.ds(pl.multiple_of((hid + 2 - 4 * side) * width, 64), width)
    out_copies = [
        remote(wout, wall_out.at[out_rows, :], osend.at[0], orecv.at[0], core_peer),
        remote(wout, wall_out.at[out_rows, :], osend.at[1], orecv.at[1], x_peer),
        remote(
            wall_out.at[out_x_rows, :], wall_out.at[out_x_rows, :], osend.at[2], orecv.at[2], core_peer
        ),
    ]
    if pair:
        shard = wexp.shape[0]

        def shard_rows(d, m):
            return pl.ds(pl.multiple_of((d * parts + m) * shard, 32), shard)

        mine = shard_rows(dp, me)
        def whole_shard(origin):
            return wfull_out.at[shard_rows(dp, origin), :]

        def hop(origin, source, sends, neighbour):
            return remote(
                source, whole_shard(origin), sends.at[origin], wrecv.at[origin],
                {"dm": lax.rem(neighbour, parts)},
            )

        def across(origin, source):
            return remote(
                source, whole_shard(origin), ysend.at[origin], yrecv.at[origin], {"dp": 1 - dp}
            )

        def pass_on(step):
            @pl.when(me >= step)
            def _():
                origin = me - step
                block = whole_shard(origin)
                hop(origin, block, wsend, me + 1).wait_recv()
                across(origin, block).start()

                @pl.when(me < parts - 1)
                def _():
                    hop(origin, block, wsend, me + 1).start()

            @pl.when(me + step < parts)
            def _():
                origin = me + step
                block = whole_shard(origin)
                hop(origin, block, wsend_left, me + parts - 1).wait_recv()
                across(origin, block).start()

                @pl.when(me > 0)
                def _():
                    hop(origin, block, wsend_left, me + parts - 1).start()

        shard_own = pltpu.make_async_copy(wexp, wfull_out.at[mine, :], local_sems.at[1])
        shard_own.start()
        shrink_peer = remote(wshr, shr_peer_out, psend, precv, {"dp": 1 - dp})

    pl.semaphore_wait(barrier, len(greeted))
    if pair:
        across(me, wexp).start()
        shrink_peer.start()

        @pl.when(me < parts - 1)
        def _():
            hop(me, wexp, wsend, me + 1).start()

        @pl.when(me > 0)
        def _():
            hop(me, wexp, wsend_left, me + parts - 1).start()

    out_copies[0].start()
    out_copies[1].start()

    def first_norm(i, carry):
        at = aligned(i * 256, 256)
        normed, _ = norm_parts(tok[at, :].astype(F32))
        fn_out[at, :] = (normed * gain[...][None] + bias[...][None]).astype(BF16)
        return carry

    lax.fori_loop(0, rows // 256, first_norm, 0)
    fn_copy = pltpu.make_async_copy(fn_out, fn_hbm, local_sems.at[2])
    fn_copy.start()

    @pl.when(me == 0)
    def _():
        from_left[...] = jnp.zeros_like(from_left)

    @pl.when(me == parts - 1)
    def _():
        from_right[...] = jnp.zeros_like(from_right)

    def chunk_rows(i, which):
        return aligned(which * HALF + i * CHUNK, CHUNK)

    def right_copy(i):
        return remote(
            to_right.at[i], from_left.at[i], send_right.at[i], recv_left.at[i],
            {"dm": lax.rem(me + 1, parts)},
        )

    def left_copy(i):
        return remote(
            to_left.at[i], from_right.at[i], send_left.at[i], recv_right.at[i],
            {"dm": lax.rem(me + parts - 1, parts)},
        )

    def x_copy(i):
        block = sfn_out.at[chunk_rows(i, core), columns]
        return remote(block, block, send_x.at[i], recv_x.at[i], x_peer)

    def core_copy(i):
        block = sfn_out.at[chunk_rows(i, core), columns]
        return remote(block, block, send_core.at[i], recv_core.at[i], core_peer)

    def relay_copy(i):
        block = sfn_out.at[chunk_rows(i, core), other_columns]
        return remote(block, block, send_relay.at[i], recv_relay.at[i], core_peer)

    def make_own(first, count):
        at = aligned(core * HALF + first * CHUNK, count * CHUNK)
        chosen = (scol[at, :] == iota((count * CHUNK, rows), 1) + own_start).astype(BF16)
        picked = dot(chosen, fn_out[:, columns]).astype(BF16)
        for i in range(count):
            own[first + i + (first + i >= CENTRE)] = picked[i * CHUNK : (i + 1) * CHUNK]

    def go_right(i):
        @pl.when(me > 0)
        def _():
            right_copy(i).wait_recv()

        @pl.when(me < parts - 1)
        def _():
            to_right[i] = own[i] + from_left[i]
            right_copy(i).start()

    def go_left(i):
        @pl.when(me < parts - 1)
        def _():
            left_copy(i).wait_recv()

        @pl.when(me > 0)
        def _():
            to_left[i] = own[i] + from_right[i]
            left_copy(i).start()

    def slot_chunk(place):
        return jnp.where(place > CENTRE, place - 1, place)

    def finish(place):
        @pl.when(place == CENTRE)
        def _():
            total = own[place].astype(F32) + from_left[place].astype(F32)
            csum[...] = total + from_right[place].astype(F32)

        @pl.when(place != CENTRE)
        def _():
            i = slot_chunk(place)
            sfn_out[chunk_rows(i, core), columns] = (
                own[place] + from_left[place] + from_right[place]
            )
            x_copy(i).start()
            core_copy(i).start()

    def relay(place):
        @pl.when(place != CENTRE)
        def _():
            i = slot_chunk(place)
            x_copy(i).wait_recv()
            relay_copy(i).start()

    far = jnp.maximum(me, parts - 1 - me)

    def ticks(first, last):
        def tick(t, carry):
            when_in(t - LAG * me, CHUNKS + 1, go_right)
            when_in(t - LAG * (parts - 1 - me), CHUNKS + 1, go_left)
            when_in(t - LAG * far, CHUNKS + 1, finish)
            when_in(t - LAG * far - LAG, CHUNKS + 1, relay)
            return carry

        lax.fori_loop(first, last, tick, 0)

    def project(part):
        at = aligned(part * (rows // 2), rows // 2)
        first = fn_out[at, :]
        q_ref[at, :] = dot_nt(first, weight[0]).astype(BF16)
        k_out[at, :] = dot_nt(first, weight[1]).astype(BF16)
        v_out[at, :] = dot_nt(first, weight[2]).astype(BF16)

    lower = (iota((128, 128), 0) > iota((128, 128), 1)).astype(BF16)

    def count_tile(i, running):
        at = aligned(i * 128, 128)
        clusters = jnp.broadcast_to(crow[pl.ds(i, 1), :].astype(F32), (128, 128))
        clusters = jnp.transpose(clusters).astype(jnp.int32)
        ccol[at, :] = clusters[:, :1]
        member = (clusters == lane).astype(F32)
        low = member.astype(BF16)
        member_ref[at, :] = low
        earlier = dot(lower, low) + running
        rcol_out[at, :] = jnp.sum(member * earlier, 1, keepdims=True)
        return running + jnp.sum(member, 0, keepdims=True)

    def place(i, carry):
        at = aligned(i * 256, 256)
        rank_row = rrow_out[:1, :].astype(jnp.int32)
        chosen = (iota((256, rows), 0) + i * 256 == rank_row).astype(BF16)
        qs_out[at, :] = (dot(chosen, q_ref[...]) * SCALE).astype(BF16)
        sorted_member = dot(chosen, member_ref[...])
        cls_out[at, :] = jnp.sum(
            sorted_member * iota((256, 128), 1).astype(F32), 1, keepdims=True
        ).astype(jnp.int32)
        return carry

    make_own(0, 4)
    ticks(0, 1)
    project(0)
    ticks(1, 2)
    make_own(4, 4)
    ticks(2, 4)
    project(1)
    ticks(4, 5)
    if pair:
        pass_on(1)
    counts = lax.fori_loop(0, tiles, count_tile, jnp.zeros((1, 128), F32))
    extended = jnp.concatenate([q_ref[...], jnp.ones((rows, 256 - width), BF16)], axis=1)
    sums = dot_tn(member_ref[...], extended)
    digits = jnp.floor(sums * 0.03125)
    wide = iota((CLP, 256), 1)
    packed = jnp.where(
        wide == width, digits, jnp.where(wide == width + 1, sums - 32.0 * digits, sums)
    )
    own[CENTRE] = jnp.concatenate(
        [packed, jnp.zeros((CLP, half_width - 256), F32)], axis=1
    ).astype(BF16)
    ticks(5, 6)
    make_own(8, CHUNKS - 8)
    ticks(6, 7)
    before = (iota((128, 128), 0) < iota((128, 128), 1)).astype(F32)
    starts = jnp.dot(
        jnp.broadcast_to(counts, (8, 128)), before, precision=HIGHEST, preferred_element_type=F32
    )
    starts_out[...] = starts.astype(jnp.int32)

    def ranks(i, carry):
        at = aligned(i * 128, 128)
        member = member_ref[at, :].astype(F32)
        rank = rcol_out[at, :] + jnp.sum(member * starts[:1], 1, keepdims=True)
        rcol_out[at, :] = rank
        turned = jnp.transpose(jnp.broadcast_to(rank, (128, 128)))
        rrow_out[:, at] = turned[:8]
        return carry

    lax.fori_loop(0, tiles, ranks, 0)
    ticks(7, 8)
    if pair:
        pass_on(2)
    here = iota((CLP, rows), 1) + own_start
    hit = topk[:, :1] == here
    for t in range(1, TOPK):
        hit = hit | (topk[:, t : t + 1] == here)
    tm_out[...] = hit.astype(F32).astype(BF16)
    ticks(8, 9)

    lax.fori_loop(0, rows // 512, place, 0)
    ticks(9, 10)
    lax.fori_loop(rows // 512, rows // 256, place, 0)
    qs_out[rows:, :] = jnp.zeros((WIN, width), BF16)
    cls_out[rows:, :] = jnp.full((WIN, 1), -1, jnp.int32)
    ticks(10, CENTRE_TICK)
    gathered = csum[...]
    count = jnp.maximum(
        32.0 * gathered[:, width : width + 1] + gathered[:, width + 1 : width + 2], 1.0
    )
    count_out[...] = jnp.broadcast_to(count, (CLP, 128))
    centre = (gathered[:, :width] / count).astype(BF16)
    centre_out[...] = centre
    same = sequence_masks(lengths, topk, rows)
    stats = jnp.zeros((CLP, 128), F32)
    rest = jnp.zeros((CLP, width), F32)
    for h in range(heads):
        top = tm_out[...].astype(F32)
        mine_lanes = head_lanes(width, h)
        scores = dot_nt(jnp.where(mine_lanes, centre, jnp.zeros_like(centre)), k_out[...]) * SCALE
        scores = jnp.where(same, scores, NEGATIVE)
        largest = jnp.max(scores, 1, keepdims=True)
        raised = jnp.exp(scores - largest)
        total = jnp.sum(raised, 1, keepdims=True)
        within = raised * top
        mass = jnp.sum(within, 1, keepdims=True)
        rest = jnp.where(mine_lanes, dot((raised - within).astype(BF16), v_out[...]), rest)
        stats = jnp.where(lane == h, largest, stats)
        stats = jnp.where(lane == 8 + h, total, stats)
        stats = jnp.where(lane == 16 + h, mass, stats)
    rbuf[me] = rest.astype(BF16)
    sbuf[me] = jnp.transpose(stats)[:24]
    rest_copies = small_exchange(rbuf, rsend, rrecv, me, parts)
    stat_copies = small_exchange(sbuf, ssend, srecv, me, parts)
    ticks(CENTRE_TICK, CENTRE_TICK + 2)
    out_copies[1].wait_recv()
    out_copies[2].start()
    if pair:
        pass_on(3)
    ticks(CENTRE_TICK + 2, CENTRE_TICK + 3)
    early = CHUNKS // 2
    ticks(CENTRE_TICK + 3, 19)

    def arrive(i, carry):
        core_copy(i).wait_recv()
        relay_copy(i).wait_recv()
        return carry

    def project_slots(first, count):
        for which in range(2):
            at = pl.ds(which * HALF + first * CHUNK, count * CHUNK)
            block = sfn_out[at, :]
            for which_weight, out, turned in ((1, ks_out, kst_out), (2, vs_out, vst_out)):
                product = dot_nt(block, weight[which_weight])
                out[at, :] = product.astype(BF16)
                turned[:, at] = jnp.transpose(product).astype(BF16)

    lax.fori_loop(0, early, arrive, 0)
    project_slots(0, early)
    ticks(19, 20)
    for copy in rest_copies + stat_copies:
        copy.start()
    ticks(20, CHUNKS + 1 + LAG * parts)
    lax.fori_loop(early, CHUNKS, arrive, 0)
    sfn_copy = pltpu.make_async_copy(sfn_out, sfn_hbm, local_sems.at[3])
    sfn_copy.start()
    project_slots(early, CHUNKS - early)
    for copy in rest_copies + stat_copies:
        copy.wait_recv()
    largest = sbuf[0][:8]
    for d in range(1, parts):
        largest = jnp.maximum(largest, sbuf[d][:8])
    total = jnp.zeros((8, 128), F32)
    mass = jnp.zeros((8, 128), F32)
    factors = []
    for d in range(parts):
        factor = jnp.exp(sbuf[d][:8] - largest)
        total += factor * sbuf[d][8:16]
        mass += factor * sbuf[d][16:24]
        factors.append(factor)
    live = iota((8, 128), 0) < heads
    total = jnp.where(live, total, 1.0)
    mass = mass / total
    table = [largest, total, mass] + [factor / total for factor in factors]
    table.append(jnp.zeros((128 - 8 * len(table), 128), F32))
    columns_table = jnp.transpose(jnp.concatenate(table, axis=0))
    merged_out[...] = columns_table
    mass_rows = jnp.zeros((CLP, width), F32)
    rest_rows = jnp.zeros((CLP, width), F32)
    for h in range(heads):
        mine_lanes = head_lanes(width, h)
        mass_rows = jnp.where(mine_lanes, columns_table[:, 16 + h : 17 + h], mass_rows)
        rest = jnp.zeros((CLP, width), F32)
        for d in range(parts):
            lane_at = 24 + 8 * d + h
            rest += columns_table[:, lane_at : lane_at + 1] * rbuf[d].astype(F32)
        rest_rows = jnp.where(mine_lanes, rest, rest_rows)
    rows_out[:, :width] = mass_rows
    rows_out[:, width:] = rest_rows

    def drain(i, carry):
        @pl.when(me < parts - 1)
        def _():
            right_copy(i).wait_send()

        @pl.when(me > 0)
        def _():
            left_copy(i).wait_send()

        return carry

    def drain_slots(i, carry):
        x_copy(i).wait_send()
        core_copy(i).wait_send()
        relay_copy(i).wait_send()
        return carry

    lax.fori_loop(0, CHUNKS + 1, drain, 0)
    lax.fori_loop(0, CHUNKS, drain_slots, 0)
    for copy in rest_copies + stat_copies + out_copies:
        copy.wait_send()
    out_copies[0].wait_recv()
    out_copies[2].wait_recv()
    if pair:
        for origin in range(parts):
            across(origin, wexp).wait()

            @pl.when((me < parts - 1) & (origin <= me))
            def _():
                hop(origin, wexp, wsend, me + 1).wait_send()

            @pl.when((me > 0) & (origin >= me))
            def _():
                hop(origin, wexp, wsend_left, me + parts - 1).wait_send()

        shrink_peer.wait()
        shard_own.wait()
    out_own.wait()
    fn_copy.wait()
    sfn_copy.wait()


def front(pair, lengths, tokens, clusters, weight, gain, bias, scol, topk, wexp, wshr, wout, parts):
    rows, model = tokens.shape
    width = weight.shape[1]
    shape = jax.ShapeDtypeStruct
    dma = pltpu.SemaphoreType.DMA
    chain = pltpu.VMEM((CHUNKS + 1, CHUNK, model // 2), BF16)
    whole = (model, wexp.shape[1]) if pair else (16, 128)
    anywhere = [pl.BlockSpec(memory_space=pl.ANY)]
    return pl.pallas_call(
        functools.partial(front_kernel, pair),
        out_shape=(
            shape(tokens.shape, BF16),
            shape((SLOTS, model), BF16),
            shape((rows + WIN, width), BF16),
            shape((rows, width), BF16),
            shape((rows, width), BF16),
            shape((SLOTS, width), BF16),
            shape((SLOTS, width), BF16),
            shape((width, SLOTS), BF16),
            shape((width, SLOTS), BF16),
            shape((8, 128), jnp.int32),
            shape((rows, 1), F32),
            shape((8, rows), F32),
            shape((rows + WIN, 1), jnp.int32),
            shape((CLP, width), BF16),
            shape((CLP, rows), BF16),
            shape((CLP, 2 * width), F32),
            shape((CLP, 128), F32),
            shape((CLP, 128), F32),
            shape((lax.axis_size("hid") * width, model), BF16),
            shape(whole, BF16),
            shape(wshr.shape, BF16),
            shape((rows, 1), jnp.int32),
        ),
        in_specs=[pl.BlockSpec(memory_space=pltpu.SMEM)] + vmem(7) + anywhere * 3,
        out_specs=tuple(anywhere * 2 + vmem(16) + anywhere * 3 + vmem(1)),
        scratch_shapes=[
            pltpu.VMEM((rows, model), BF16),
            pltpu.VMEM((SLOTS, model), BF16),
            pltpu.VMEM((rows, width), BF16),
            pltpu.VMEM((rows, 128), BF16),
            pltpu.VMEM((CLP, model // 2), F32),
            pltpu.VMEM((parts, CLP, width), BF16),
            pltpu.VMEM((parts, 24, 128), F32),
            chain, chain, chain, chain, chain,
        ]
        + [dma((parts,))] * 4
        + [dma((CHUNKS + 1,))] * 10
        + [dma((3,))] * 2
        + [dma((parts,))] * 5
        + [dma, dma, dma((4,))],
        compiler_params=pltpu.CompilerParams(
            vmem_limit_bytes=56 << 20, collective_id=0, has_side_effects=True
        ),
        name="front",
    )(
        lengths, tokens, clusters.reshape(rows // 128, 128), weight, gain, bias, scol, topk,
        wexp, wshr, wout,
    )


UNROLL = 4
FORWARD_UNROLL = (4, 2)
BACKWARD_UNROLL = (2, 2)
SMALL = 64


def list_windows(starts, rows, lists):
    big_group, big_row, small_group, small_row = lists

    def one_group(g, counts):
        big, small = counts
        first, last = starts[0, g * GROUP], starts[0, g * GROUP + GROUP]
        base = first // 16 * 16
        span = jnp.where(last > first, last - base, 0)
        short = (span > 0) & (span <= SMALL)
        windows = jnp.where(span > SMALL, (span + WIN - 1) // WIN, 0)

        def one(w, carry):
            big_group[big + w] = g
            big_row[big + w] = base + w * WIN
            return carry

        lax.fori_loop(0, windows, one, 0)
        small_group[small] = g
        small_row[small] = base
        return big + windows, small + jnp.where(short, 1, 0)

    big, small = lax.fori_loop(0, GROUPS, one_group, (0, 0))
    for i in range(UNROLL):
        big_group[big + i] = 0
        big_row[big + i] = rows
        small_group[small + i] = 0
        small_row[small + i] = rows
    return big, small


def each_window(starts, rows, lists, window, unroll):
    big, small = list_windows(starts, rows, lists)
    for count, size, group_at, row_at, times in (
        (big, WIN, lists[0], lists[1], unroll[0]),
        (small, SMALL, lists[2], lists[3], unroll[1]),
    ):

        def several(n, carry):
            for i in range(times):
                window(*window_at(starts, group_at, row_at, n * times + i, size))
            return carry

        lax.fori_loop(0, (count + times - 1) // times, several, 0)


def window_probs(scores, mine, inside, h):
    part = jnp.where(mine, scores[:, h * GSLOTS : (h + 1) * GSLOTS], NEGATIVE)
    raised = jnp.exp(part - jnp.max(part, 1, keepdims=True))
    inverse = jnp.where(inside, 1.0 / jnp.sum(raised, 1, keepdims=True), 0.0)
    return raised * inverse


def window_at(starts, group_at, row_at, i, size):
    g = group_at[i]
    row = pl.multiple_of(row_at[i], 16)
    at = pl.ds(pl.multiple_of(g * GSLOTS, GSLOTS), GSLOTS)
    place = iota((size, 1), 0) + row
    inside = (place >= starts[0, g * GROUP]) & (place < starts[0, g * GROUP + GROUP])
    return size, g, pl.ds(row, size), at, inside


def exact_forward_kernel(
    starts, qs, cls, kt_hbm, vs_hbm, both, rcol, att_out, att_s, mix_s, kt, vs, sems, *lists
):
    rows, width = rcol.shape[0], qs.shape[1]
    heads = width // HEAD_DIM
    copies = [
        pltpu.make_async_copy(kt_hbm, kt, sems.at[0]),
        pltpu.make_async_copy(vs_hbm, vs, sems.at[1]),
    ]
    for copy in copies:
        copy.start()
    high = both[...].astype(BF16)
    low = (both[...] - high.astype(F32)).astype(BF16)
    step = (rows + WIN) // 5

    def spread(i, carry):
        at = pl.ds(pl.multiple_of(i * step, 16), step)
        member = (cls[at, :] == iota((step, 128), 1)).astype(BF16)
        mix_s[at, :] = dot(member, high) + dot(member, low)
        return carry

    lax.fori_loop(0, 5, spread, 0)
    for copy in copies:
        copy.wait()

    def window(size, g, here, at, inside):
        keys = block_diagonal_turned(kt[:, at], heads)
        values = block_diagonal(vs[at, :], heads)
        mine = cls[here, :] == iota((size, GSLOTS), 1) // TOPK + g * GROUP
        scores = dot(qs[here, :], keys)
        weights = [window_probs(scores, mine, inside, h).astype(BF16) for h in range(heads)]
        out = dot(jnp.concatenate(weights, axis=1), values)
        mix = mix_s[here, :]
        att_s[here, :] = jnp.where(inside, mix[:, :width] * out + mix[:, width:], att_s[here, :])

    each_window(starts, rows, lists, window, FORWARD_UNROLL)

    def unplace(i, carry):
        at = pl.ds(pl.multiple_of(i * 256, 256), 256)
        chosen = (iota((256, rows), 1) == rcol[at, :].astype(jnp.int32)).astype(BF16)
        att_out[at, :] = dot(chosen, att_s[:rows, :].astype(BF16)).astype(BF16)
        return carry

    lax.fori_loop(0, rows // 256, unplace, 0)


ANYWHERE = pl.BlockSpec(memory_space=pl.ANY)
LISTED = 64


def exact_forward(starts, qs, cls, ks, vs, both, rcol):
    rows, width = rcol.shape[0], qs.shape[1]
    shape = jax.ShapeDtypeStruct
    return pl.pallas_call(
        exact_forward_kernel,
        out_shape=shape((rows, width), BF16),
        in_specs=[pl.BlockSpec(memory_space=pltpu.SMEM)] + vmem(2) + [ANYWHERE] * 2 + vmem(2),
        out_specs=vmem(1)[0],
        scratch_shapes=[
            pltpu.VMEM((rows + WIN, width), F32),
            pltpu.VMEM((rows + WIN, 2 * width), F32),
            pltpu.VMEM((width, SLOTS), BF16),
            pltpu.VMEM((SLOTS, width), BF16),
            pltpu.SemaphoreType.DMA((2,)),
        ]
        + [pltpu.SMEM((LISTED,), jnp.int32)] * 4,
        compiler_params=pltpu.CompilerParams(vmem_limit_bytes=62 << 20),
        name="exact_forward",
    )(starts, qs, cls, ks, vs, both, rcol)


def exact_backward_kernel(
    starts, qs, cls, ks_hbm, kt_hbm, vt_hbm, rows_in, rcol, rrow, grad,
    dq_out, dkvt_out, centre_out,
    grad_s, mass_s, dq_s, part_s, dkv_s, ks, kt, vt, sems, *lists,
):
    rows, width = rcol.shape[0], qs.shape[1]
    heads = width // HEAD_DIM
    copies = [
        pltpu.make_async_copy(ks_hbm, ks, sems.at[0]),
        pltpu.make_async_copy(kt_hbm, kt, sems.at[1]),
        pltpu.make_async_copy(vt_hbm, vt, sems.at[2]),
    ]
    for copy in copies:
        copy.start()
    mass_rows = rows_in[:, :width]
    high = mass_rows.astype(BF16)
    low = (mass_rows - high.astype(F32)).astype(BF16)
    rank_row = rrow[:1, :].astype(jnp.int32)

    def place(i, carry):
        at = pl.ds(pl.multiple_of(i * 256, 256), 256)
        chosen = (iota((256, rows), 0) + i * 256 == rank_row).astype(BF16)
        grad_s[at, :] = dot(chosen, grad[...]).astype(BF16)
        member = (cls[at, :] == iota((256, 128), 1)).astype(BF16)
        mass_s[at, :] = dot(member, high) + dot(member, low)
        return carry

    lax.fori_loop(0, rows // 256, place, 0)
    grad_s[rows:, :] = jnp.zeros((WIN, width), BF16)
    mass_s[rows:, :] = jnp.zeros((WIN, width), F32)
    dkv_s[...] = jnp.zeros_like(dkv_s)
    for copy in copies:
        copy.wait()

    def window(size, g, here, at, inside):
        keys = block_diagonal(ks[at, :], heads)
        mine = cls[here, :] == iota((size, GSLOTS), 1) // TOPK + g * GROUP
        query, upstream = qs[here, :], grad_s[here, :]
        scores = dot(query, block_diagonal_turned(kt[:, at], heads))
        against = dot(upstream, block_diagonal_turned(vt[:, at], heads))
        mass = mass_s[here, :]
        weights, score_grads = [], []
        mass_part = jnp.zeros((size, width), F32)
        for h in range(heads):
            cut = slice(h * GSLOTS, (h + 1) * GSLOTS)
            probs = window_probs(scores, mine, inside, h)
            meeting = jnp.sum(probs * against[:, cut], 1, keepdims=True)
            weighted = probs * mass[:, h * HEAD_DIM : h * HEAD_DIM + 1]
            weights.append(weighted.astype(BF16))
            score_grads.append((weighted * (against[:, cut] - meeting)).astype(BF16))
            mass_part = jnp.where(head_lanes(width, h), meeting, mass_part)
        score_grad = jnp.concatenate(score_grads, axis=1)
        weight = jnp.concatenate(weights, axis=1)
        dq = dot(score_grad, keys) * SCALE
        dq_s[here, :] = jnp.where(inside, dq, dq_s[here, :])
        part_s[here, :] = jnp.where(inside, mass_part, part_s[here, :])
        pair = jnp.concatenate(
            [
                diagonal_blocks_turned(dot_tn(query, score_grad), heads),
                diagonal_blocks_turned(dot_tn(upstream, weight), heads),
            ],
            axis=0,
        )
        dkv_s[:, at] = dkv_s[:, at] + pair

    each_window(starts, rows, lists, window, BACKWARD_UNROLL)
    centre_out[...] = jnp.zeros_like(centre_out)

    def finish_group(g, carry):
        at = pl.ds(pl.multiple_of(g * GSLOTS, GSLOTS), GSLOTS)
        dkvt_out[:, at] = dkv_s[:, at].astype(BF16)
        return carry

    lax.fori_loop(0, GROUPS, finish_group, 0)

    def unplace(i, carry):
        at = pl.ds(pl.multiple_of(i * 256, 256), 256)
        chosen = (iota((256, rows), 1) == rcol[at, :].astype(jnp.int32)).astype(BF16)
        dq_out[at, :] = dot(chosen, dq_s[:rows, :].astype(BF16)).astype(BF16)
        member = (cls[at, :] == iota((256, 128), 1)).astype(BF16)
        pair = jnp.concatenate([part_s[at, :].astype(BF16), grad_s[at, :]], axis=1)
        centre_out[...] += dot_tn(member, pair)
        return carry

    lax.fori_loop(0, rows // 256, unplace, 0)


def exact_backward(starts, qs, cls, ks, kt, vt, rows_in, rcol, rrow, grad):
    rows, width = rcol.shape[0], qs.shape[1]
    shape = jax.ShapeDtypeStruct
    return pl.pallas_call(
        exact_backward_kernel,
        out_shape=(
            shape((rows, width), BF16),
            shape((2 * width, SLOTS), BF16),
            shape((CLP, 2 * width), F32),
        ),
        in_specs=[pl.BlockSpec(memory_space=pltpu.SMEM)] + vmem(2) + [ANYWHERE] * 3 + vmem(4),
        out_specs=tuple(vmem(3)),
        scratch_shapes=[
            pltpu.VMEM((rows + WIN, width), BF16),
            pltpu.VMEM((rows + WIN, width), F32),
            pltpu.VMEM((rows + WIN, width), F32),
            pltpu.VMEM((rows + WIN, width), F32),
            pltpu.VMEM((2 * width, SLOTS), F32),
            pltpu.VMEM((SLOTS, width), BF16),
            pltpu.VMEM((width, SLOTS), BF16),
            pltpu.VMEM((width, SLOTS), BF16),
            pltpu.SemaphoreType.DMA((3,)),
        ]
        + [pltpu.SMEM((LISTED,), jnp.int32)] * 4,
        compiler_params=pltpu.CompilerParams(vmem_limit_bytes=62 << 20),
        name="exact_backward",
    )(starts, qs, cls, ks, kt, vt, rows_in, rcol, rrow, grad)


def gelu_parts(values):
    slope = 0.7978845608028654
    squared = values * values
    turned = jnp.tanh(slope * values * (1.0 + 0.044715 * squared))
    half = 0.5 * (1.0 + turned)
    rise = half + 0.5 * slope * values * (1.0 - turned * turned) * (1.0 + 0.134145 * squared)
    return (values * half, rise)


def middle_kernel(
    pair, parts, tok_hbm, cot_hbm, att, wout_own, wout_hbm, wexp_hbm, gain, bias, shr_own, shr_one, shr_two, shr_three, shr_peer,
    mid_out, mgrad_out, agrad_out, hsum_out, wo_out, gains_out, *refs,
):
    grad_outs, refs = refs[: 2 + parts if pair else 1], refs[2 + parts if pair else 1 :]
    middle_body(
        pair, tok_hbm, cot_hbm, att, wout_own, wout_hbm, wexp_hbm, gain, bias,
        (shr_own, shr_one, shr_two, shr_three), shr_peer, mid_out, mgrad_out, agrad_out, hsum_out, wo_out, gains_out, grad_outs, *refs,
    )


def middle_body(
    pair, tok_hbm, cot_hbm, att, wout_own, wout_hbm, wexp_hbm, gain, bias, shards, shr_peer,
    mid_out, mgrad_out, agrad_out, hsum_out, wo_out, gains_out, grad_outs,
    tok, cot, wout, wexp, fetch_sems, wshr_ref, att_peer, cat, xcat, sn, act, hg, sp_own, sp_send, sp_recv, hp_own, hp_send, hp_recv,
    sx_send, sx_recv, branch, kept,
    asend, arecv, xsend, xrecv, rsend, rrecv, ssend, srecv, hsend, hrecv, sxs, sxr, bsend, brecv,
    wysend, wyrecv,
):
    rows, width = att.shape
    model = tok.shape[1]
    fetches = [
        pltpu.make_async_copy(source, target, fetch_sems.at[i])
        for i, (source, target) in enumerate(
            ((tok_hbm, tok), (wout_hbm, wout), (wexp_hbm, wexp), (cot_hbm, cot))
        )
    ]
    for fetch in fetches:
        fetch.start()
    half_width = 2 * width
    half_rows = rows // 2
    blocks = half_rows // 128
    hid = lax.axis_index("hid")
    core, side = lax.rem(hid, 2), hid // 2
    core_peer = {"hid": hid + 1 - 2 * core}
    x_peer = {"hid": hid + 2 - 4 * side}

    dp = lax.axis_index("dp")
    greeted = [core_peer, x_peer] + ([{"dp": 1 - dp}] if pair else [])
    barrier = greet(greeted)
    gains_out[...] = jnp.zeros_like(gains_out)
    pl.semaphore_wait(barrier, len(greeted))

    units = wexp.shape[1]
    if pair:
        wshr = wshr_ref
        n_dm, my_dm = lax.axis_size("dm"), lax.axis_index("dm")
        shard = model // (2 * n_dm)

        def shard_rows(d, step):
            owner = lax.rem(my_dm + n_dm - step, n_dm)
            return pl.ds(pl.multiple_of((d * n_dm + owner) * shard, 32), shard)

        shard_copies = [
            remote(
                shards[step], wshr.at[shard_rows(dp, step), :], wysend.at[step], wyrecv.at[step],
                {"dp": 1 - dp},
            )
            for step in range(1, n_dm)
        ]
    else:
        wshr = shards[0]

    def block_rows(j, which):
        return pl.ds(pl.multiple_of(which * half_rows + j * 128, 128), 128)

    def own_rows(j):
        return pl.ds(pl.multiple_of(j * 128, 128), 128)

    att_copy = remote(att, att_peer, asend, arecv, core_peer)
    att_copy.start()
    if pair:
        for copy in shard_copies:
            copy.start()
        for step in range(n_dm):
            wshr[shard_rows(dp, step), :] = shards[step][...]
        wshr[shard_rows(1 - dp, 0), :] = shr_peer[...]

    def x_copy(j):
        block = block_rows(j, core)
        return remote(cat.at[block, :], xcat.at[block, :], xsend.at[j], xrecv.at[j], x_peer)

    def relay_copy(j):
        block = xcat.at[block_rows(j, core), :]
        return remote(block, block, rsend.at[j], rrecv.at[j], core_peer)

    def sp_copy(j):
        return remote(sp_send.at[j], sp_recv.at[j], ssend.at[j], srecv.at[j], core_peer)

    def hp_copy(j):
        return remote(hp_send.at[j], hp_recv.at[j], hsend.at[j], hrecv.at[j], core_peer)

    def sx_copy(j):
        return remote(sx_send.at[j], sx_recv.at[j], sxs.at[j], sxr.at[j], x_peer)

    def branch_copy(j):
        block = branch.at[block_rows(j, core), :]
        return remote(block, block, bsend.at[j], brecv.at[j], core_peer)

    def join(at):
        mine, other = att[at, :], att_peer[at, :]
        cat[at, :] = jnp.where(
            core == 0,
            jnp.concatenate([mine, other], axis=1),
            jnp.concatenate([other, mine], axis=1),
        )

    att_copy.wait_recv()

    def spread(j, carry):
        join(block_rows(j, core))
        x_copy(j).start()
        return carry

    lax.fori_loop(0, blocks, spread, 0)

    def join_other(j, carry):
        join(block_rows(j, 1 - core))
        return carry

    lax.fori_loop(0, blocks, join_other, 0)
    for fetch in fetches:
        fetch.wait()

    def both(ref, j):
        return jnp.concatenate([ref[block_rows(j, core), :], ref[block_rows(j, 1 - core), :]], axis=0)

    def store_both(ref, j, values):
        ref[block_rows(j, core), :] = values[:128]
        ref[block_rows(j, 1 - core), :] = values[128:]

    own_half = pl.ds(pl.multiple_of(side * half_width, 128), half_width)
    other_half = pl.ds(pl.multiple_of((1 - side) * half_width, 128), half_width)

    def forward(j):
        x_copy(j).wait_recv()
        relay_copy(j).start()
        relay_copy(j).wait_recv()
        attention = dot(both(cat, j), wout[own_half, :]) + dot(both(xcat, j), wout[other_half, :])
        middle = both(tok, j).astype(F32) + attention
        mid_out[own_rows(j), :] = middle[:128]
        normed, _ = norm_parts(middle)
        second = (normed * gain[...][None] + bias[...][None]).astype(BF16)
        store_both(sn, j, second)
        hidden = dot(second, wexp[...])
        value, rise = gelu_parts(hidden)
        value = value.astype(BF16)
        store_both(act, j, value)
        if pair:

            @pl.when(j == 0)
            def _():
                for copy in shard_copies:
                    copy.wait_recv()

        grad = (dot(both(cot, j), wshr[...]) * rise).astype(BF16)
        store_both(hg, j, grad)
        part = dot_nt(grad, wexp[...])
        sp_own[j] = part[:128]
        sp_send[j] = part[128:].astype(BF16)
        sp_copy(j).start()
        part = dot_nt(value, wshr[...])
        hp_own[j] = part[:128]
        hp_send[j] = part[128:].astype(BF16)
        hp_copy(j).start()

    def chip_sum(j):
        sp_copy(j).wait_recv()
        total = sp_own[j] + sp_recv[j].astype(F32)
        sx_send[j] = total.astype(BF16)
        sx_copy(j).start()
        hp_copy(j).wait_recv()
        hsum_out[own_rows(j), :] = (hp_own[j] + hp_recv[j].astype(F32)).astype(BF16)

    def norm_grad(j):
        sx_copy(j).wait_recv()
        second_grad = sx_send[j].astype(F32) + sx_recv[j].astype(F32)
        normed, spread_two = norm_parts(mid_out[own_rows(j), :])
        inner, gain_part, bias_part = norm_back(second_grad, normed, spread_two, gain[...][None])
        gains_out[0:1, :] += gain_part[None]
        gains_out[1:2, :] += bias_part[None]
        middle_grad = cot[block_rows(j, core), :].astype(F32) + inner
        mgrad_out[own_rows(j), :] = middle_grad
        branch[block_rows(j, core), :] = middle_grad.astype(BF16)
        branch_copy(j).start()

    def attended_grad(j):
        branch_copy(j).wait_recv()
        for which in range(2):
            at = block_rows(j, which)
            agrad_out[at, :] = dot_nt(branch[at, :], wout_own[...]).astype(BF16)

    def when_block(j, work):
        @pl.when((j >= 0) & (j < blocks))
        def _():
            work(j)

    def ticks(first, last):
        def tick(t, carry):
            when_block(t - 1, chip_sum)
            when_block(t, forward)
            when_block(t - 2, norm_grad)
            when_block(t - 3, attended_grad)
            return carry

        lax.fori_loop(first, last, tick, 0)

    half = model // 2
    part_rows = half if pair else model

    def weight_grad(left, right, which):
        return dot_tn(left[:, aligned(which * half, part_rows)], right[...]).astype(BF16)

    ticks(0, blocks)
    if pair:
        keep_out, give_out = grad_outs[0], grad_outs[1]
        for d in range(2):
            kept[d] = weight_grad(sn, hg, d)
    else:
        grad_outs[0][:, :units] = weight_grad(sn, hg, 0)
    ticks(blocks, blocks + 1)
    if pair:
        parts, me = lax.axis_size("dm"), lax.axis_index("dm")
        shard = half // parts
        for step in range(parts):
            quarter = pl.ds(pl.multiple_of(lax.rem(me + step, parts) * shard, 32), shard)
            for d in range(2):
                grad_outs[2 + step][d] = kept[d, quarter, :]
        give_out[:half, :] = weight_grad(cot, act, 1 - dp)
    else:
        grad_outs[0][:, units:] = weight_grad(cot, act, 0)
    ticks(blocks + 1, blocks + 2)
    if pair:
        keep_out[:half, :] = weight_grad(cot, act, dp)
    ticks(blocks + 2, blocks + 3)
    out_grad = dot_tn(att[...], branch[...]).astype(BF16)
    wo_out[...] = out_grad
    if pair:
        small = width // 2
        keep_out[half:, :] = wo_out[pl.ds(pl.multiple_of(dp * small, 32), small), :]
        give_out[half:, :] = wo_out[pl.ds(pl.multiple_of((1 - dp) * small, 32), small), :]

    def drain(j, carry):
        x_copy(j).wait_send()
        relay_copy(j).wait_send()
        sp_copy(j).wait_send()
        hp_copy(j).wait_send()
        sx_copy(j).wait_send()
        branch_copy(j).wait_send()
        return carry

    lax.fori_loop(0, blocks, drain, 0)
    att_copy.wait_send()
    if pair:
        for copy in shard_copies:
            copy.wait_send()


def middle(pair, tokens, cotangent, attended, wout_own, wout, wexp, gain, bias, shards, shr_peer):
    rows, model = tokens.shape
    width = attended.shape[1]
    units = wexp.shape[1]
    part_rows = model // 2 if pair else model
    spare = (2, part_rows, units) if pair else (2, 16, 128)
    parts = lax.axis_size("dm")
    if pair:
        grads = [(part_rows + width // 2, units)] * 2 + [(2, part_rows // parts, units)] * parts
    else:
        grads = [(model, 2 * units)]
    blocks = rows // 256
    shape = jax.ShapeDtypeStruct
    dma = pltpu.SemaphoreType.DMA
    low = pltpu.VMEM((blocks, 128, model), BF16)
    full = pltpu.VMEM((blocks, 128, model), F32)
    return pl.pallas_call(
        functools.partial(middle_kernel, pair, parts),
        out_shape=(
            shape((rows // 2, model), F32),
            shape((rows // 2, model), F32),
            shape((rows, width), BF16),
            shape((rows // 2, model), BF16),
            shape((width, model), BF16),
            shape((8, model), F32),
        )
        + tuple(shape(dims, BF16) for dims in grads),
        in_specs=[ANYWHERE] * 2 + vmem(2) + [ANYWHERE] * 2 + vmem(7),
        out_specs=tuple(vmem(6 + len(grads))),
        scratch_shapes=[
            pltpu.VMEM(tokens.shape, BF16),
            pltpu.VMEM(cotangent.shape, BF16),
            pltpu.VMEM(wout.shape, BF16),
            pltpu.VMEM(wexp.shape, BF16),
            pltpu.SemaphoreType.DMA((4,)),
            pltpu.VMEM((model, units) if pair else (16, 128), BF16),
            pltpu.VMEM((rows, width), BF16),
            pltpu.VMEM((rows, 2 * width), BF16),
            pltpu.VMEM((rows, 2 * width), BF16),
            pltpu.VMEM((rows, model), BF16),
            pltpu.VMEM((rows, units), BF16),
            pltpu.VMEM((rows, units), BF16),
            full, low, low, full, low, low, low, low,
            pltpu.VMEM((rows, model), BF16),
            pltpu.VMEM(spare, BF16),
            dma, dma,
        ]
        + [dma((blocks,))] * 12
        + [dma((4,)), dma((4,))],
        compiler_params=pltpu.CompilerParams(
            vmem_limit_bytes=60 << 20, collective_id=2, has_side_effects=True
        ),
        name="middle",
    )(tokens, cotangent, attended, wout_own, wout, wexp, gain, bias, *shards, shr_peer)


def tail_kernel(
    pair, lengths, dkvt, dq, summed, k, v, centre, topk, tm, merged, rows_in, counts, ccol, weight,
    fn_hbm, sfn, tok_hbm, gain, mgrad, srow, mid, hsum, hsum_x, second_gains,
    sh_keep, sh_given, ex_own, ex_one, ex_two, ex_three,
    result_out, tokens_out, qkv_out, out_out, gain_a, gain_b, gain_c, gain_d, expand_out, shrink_out,
    sbuf, cbuf, fgm, to_core, from_core, to_x, from_x, to_right, to_left, from_left,
    from_right, from_fin, pq, pkv, dense, dense_to_core, dense_from_core, dense_to_x, dense_from_x,
    dense_own, first, sfn_tile, grad_all, grad_from_y, grad_back, g_own, g_right, g_left, g_from_left,
    g_from_right, g_total, gain_sum, gain_core, gain_dm, gain_dp, gain_x, shrink_send, shrink_recv, expand_y, tok, fn, tile_sem, mid_sem, hsum_sem, tok_sem, fn_sem,
    ssend, srecv, csend, crecv,
    send_core, recv_core, send_x, recv_x, send_right, recv_left, send_left, recv_right, send_fin,
    recv_fin,
    dsend_core, drecv_core, dsend_x, drecv_x, fsend, frecv, tsend, trecv, osend, orecv,
    ysend, yrecv, gsend_right, grecv_left, gsend_left, grecv_right, asend, arecv,
    gcsend, gcrecv, gmsend, gmrecv, gpsend, gprecv, esend, erecv,
):
    gain_outs = (gain_a, gain_b, gain_c, gain_d)
    rows, width = k.shape
    model = tok.shape[1]
    heads = width // HEAD_DIM
    half_width = model // 2
    half_rows = rows // 2
    blocks = half_rows // 128
    parts = lax.axis_size("dm")
    me, hid, dp = lax.axis_index("dm"), lax.axis_index("hid"), lax.axis_index("dp")
    core, side = lax.rem(hid, 2), hid // 2
    core_peer = {"hid": hid + 1 - 2 * core}
    x_peer = {"hid": hid + 2 - 4 * side}
    y_peer = {"dp": 1 - dp}
    own_start = me * rows
    columns = aligned(side * half_width, half_width)
    other_columns = aligned((1 - side) * half_width, half_width)

    greeted = [{"dm": lax.rem(me + step, parts)} for step in range(1, parts)]
    greeted += [core_peer, x_peer] + ([y_peer] if pair else [])
    barrier = greet(greeted)

    wide = iota((CLP, 256), 1)
    packed = jnp.concatenate([summed[:, width:], jnp.zeros((CLP, 256 - width), F32)], axis=1)
    for h in range(heads):
        packed = jnp.where(wide == width + h, summed[:, h * HEAD_DIM : h * HEAD_DIM + 1], packed)
    sbuf[me] = packed.astype(BF16)
    dense_own[...] = jnp.zeros_like(dense_own)
    mid_copy = pltpu.make_async_copy(mid, dense, mid_sem)
    mid_copy.start()
    hsum_copy = pltpu.make_async_copy(hsum, dense_to_core, hsum_sem)
    hsum_copy.start()
    tok_copy = pltpu.make_async_copy(
        tok_hbm.at[aligned(core * half_rows, half_rows), :], tok, tok_sem
    )
    tok_copy.start()
    fn_copy = pltpu.make_async_copy(fn_hbm, fn, fn_sem)
    fn_copy.start()

    @pl.when(me == 0)
    def _():
        from_left[...] = jnp.zeros_like(from_left)
        g_from_left[...] = jnp.zeros_like(g_from_left)

    @pl.when(me == parts - 1)
    def _():
        from_right[...] = jnp.zeros_like(from_right)
        g_from_right[...] = jnp.zeros_like(g_from_right)

    pl.semaphore_wait(barrier, len(greeted))
    sum_copies = small_exchange(sbuf, ssend, srecv, me, parts)
    for copy in sum_copies:
        copy.start()

    def chunk_rows(i, which):
        return aligned(which * HALF + i * CHUNK, CHUNK)

    def block_rows(j, which):
        return aligned(which * half_rows + j * 128, 128)

    def own_rows(j):
        return aligned(j * 128, 128)

    def core_copy(i):
        return remote(to_core.at[i], from_core.at[i], send_core.at[i], recv_core.at[i], core_peer)

    def x_copy(i):
        return remote(to_x.at[i], from_x.at[i], send_x.at[i], recv_x.at[i], x_peer)

    right = {"dm": lax.rem(me + 1, parts)}
    left = {"dm": lax.rem(me + parts - 1, parts)}

    def right_copy(i):
        return remote(to_right.at[i], from_left.at[i], send_right.at[i], recv_left.at[i], right)

    def left_copy(i):
        return remote(to_left.at[i], from_right.at[i], send_left.at[i], recv_right.at[i], left)

    def fin_copy(i):
        return remote(from_x.at[i], from_fin.at[i], send_fin.at[i], recv_fin.at[i], core_peer)

    def dense_core_copy(j):
        return remote(
            dense_to_core.at[j], dense_from_core.at[j], dsend_core.at[j], drecv_core.at[j], core_peer
        )

    def dense_x_copy(j):
        return remote(dense_to_x.at[j], dense_from_x.at[j], dsend_x.at[j], drecv_x.at[j], x_peer)

    def first_copy(j):
        block = first.at[j, :, columns]
        return remote(block, block, fsend.at[j], frecv.at[j], x_peer)

    def tokens_copy(j):
        block = tokens_out.at[block_rows(j, core), :]
        return remote(block, block, tsend.at[j], trecv.at[j], core_peer)

    def result_copy(j):
        block = result_out.at[block_rows(j, core), :]
        return remote(block, block, osend.at[j], orecv.at[j], core_peer)

    def spread_back(start, count):
        at = aligned((1 - core) * HALF + start * CHUNK, count * CHUNK)
        other = dot_tn(dkvt[:, at], weight[width:, :])
        other = other.astype(BF16)
        for i in range(count):
            to_core[start + i] = other[i * CHUNK : (i + 1) * CHUNK]
            core_copy(start + i).start()
        at = aligned(core * HALF + start * CHUNK, count * CHUNK)
        mine = dot_tn(dkvt[:, at], weight[width:, :])
        mine = mine.astype(BF16)
        for i in range(count):
            fgm[start + i] = mine[i * CHUNK : (i + 1) * CHUNK]

    def chip_sum(i):
        core_copy(i).wait_recv()
        to_x[i] = fgm[i, :, other_columns] + from_core[i, :, other_columns]
        x_copy(i).start()

    def hid_sum(i):
        x_copy(i).wait_recv()
        fgm[i, :, columns] = (
            fgm[i, :, columns].astype(F32)
            + from_core[i, :, columns].astype(F32)
            + from_x[i].astype(F32)
        ).astype(BF16)

    def go_right(i):
        @pl.when(me > 0)
        def _():
            right_copy(i).wait_recv()

        @pl.when(me < parts - 1)
        def _():
            to_right[i] = fgm[i, :, columns] + from_left[i]
            right_copy(i).start()

    def go_left(i):
        @pl.when(me < parts - 1)
        def _():
            left_copy(i).wait_recv()

        @pl.when(me > 0)
        def _():
            to_left[i] = fgm[i, :, columns] + from_right[i]
            left_copy(i).start()

    def finish(i):
        from_x[i] = (
            fgm[i, :, columns].astype(F32) + from_left[i].astype(F32) + from_right[i].astype(F32)
        ).astype(BF16)
        fin_copy(i).start()

    def scatter(i):
        fin_copy(i).wait_recv()
        here = iota((half_rows, CHUNK), 0) + own_start + core * half_rows
        chosen = [
            (srow[:, chunk_rows(i, which)] == here).astype(BF16) for which in (core, 1 - core)
        ]
        picked = jnp.concatenate([from_x[i], from_fin[i]], axis=0)
        dense_own[...] += dot(jnp.concatenate(chosen, axis=1), picked)

    far = jnp.maximum(me, parts - 1 - me)

    def ticks(start, last):
        def tick(t, carry):
            ready = t
            when_in(ready, CHUNKS, hid_sum)
            when_in(ready - LAG * me, CHUNKS, go_right)
            when_in(ready - LAG * (parts - 1 - me), CHUNKS, go_left)
            when_in(ready - LAG * far, CHUNKS, finish)
            when_in(ready - LAG * far - 1, CHUNKS, scatter)
            return carry

        lax.fori_loop(start, last, tick, 0)

    if pair:
        shard = expand_out.shape[0]

        def shard_rows(m):
            return pl.ds(pl.multiple_of(m * shard, 32), shard)

        shrink_copies = []
        for step in range(1, parts):
            target = lax.rem(me + step, parts)
            shrink_send[step] = sh_keep[shard_rows(target), :] + sh_given[shard_rows(target), :]
            shrink_copies.append(
                remote(
                    shrink_send.at[step], shrink_recv.at[step], esend.at[step], erecv.at[step],
                    {"dm": target},
                )
            )
        for copy in shrink_copies:
            copy.start()
        expand_y[0] = (
            ex_own[1 - dp].astype(F32) + ex_one[1 - dp].astype(F32)
            + ex_two[1 - dp].astype(F32) + ex_three[1 - dp].astype(F32)
        ).astype(BF16)
        expand_copy = remote(expand_y.at[0], expand_y.at[1], esend.at[0], erecv.at[0], y_peer)
        expand_copy.start()

    def chip_sums(first, last):
        def one(i, carry):
            chip_sum(i)
            return carry

        lax.fori_loop(first, last, one, 0)

    spread_back(0, 3)
    chip_sums(0, 3)
    spread_back(3, 5)
    chip_sums(3, 8)
    spread_back(8, CHUNKS - 8)
    chip_sums(8, CHUNKS)

    def result_rows(j, carry):
        total = dense_to_core[j].astype(F32) + hsum_x[j].astype(F32)
        result_out[block_rows(j, core), :] = (dense[j] + total).astype(BF16)
        result_copy(j).start()
        return carry

    for copy in sum_copies:
        copy.wait_recv()
    total = sbuf[0].astype(F32)
    for d in range(1, parts):
        total += sbuf[d].astype(F32)
    same = sequence_masks(lengths, topk, rows)
    rest_grad = total[:, :width].astype(BF16)
    product = rest_grad.astype(F32) * rows_in[:, width:]
    score_grads, weights = [], []
    centre_part = jnp.zeros((CLP, width), F32)
    for h in range(heads):
        lanes = head_lanes(width, h)
        top = tm[...].astype(F32)
        zero = jnp.zeros((CLP, width), BF16)
        full = dot_nt(jnp.where(lanes, centre[...], zero), k[...]) * SCALE
        against = dot_nt(jnp.where(lanes, rest_grad, zero), v[...])
        largest, denominator = merged[:, h : h + 1], merged[:, 8 + h : 9 + h]
        mass = merged[:, 16 + h : 17 + h]
        mass_grad = total[:, width + h : width + h + 1]
        probs = jnp.where(same, jnp.exp(full - largest) / denominator, 0.0)
        mean = mass * mass_grad + jnp.sum(jnp.where(lanes, product, 0.0), 1, keepdims=True)
        grad = jnp.where(top > 0.5, mass_grad, against)
        score_grad = (probs * (grad - mean)).astype(BF16)
        centre_part = jnp.where(lanes, dot(score_grad, k[...]), centre_part)
        score_grads.append(score_grad)
        weights.append(jnp.where(top > 0.5, 0.0, probs).astype(BF16))
    cbuf[me] = (centre_part * SCALE).astype(BF16)
    centre_copies = small_exchange(cbuf, csend, crecv, me, parts)
    for copy in centre_copies:
        copy.start()
    score_grad = jnp.concatenate(score_grads, axis=0)
    rest_weight = jnp.concatenate(weights, axis=0)
    pkv[...] = jnp.concatenate(
        [
            (dot_tn(score_grad, block_diagonal(centre[...], heads)) * SCALE).astype(BF16),
            dot_tn(rest_weight, block_diagonal(rest_grad, heads)).astype(BF16),
        ],
        axis=1,
    )
    if pair:
        part = width // 2

        def y_rows(b, d):
            first = jnp.where(b == 3, 6 + d, d * 3 + b)
            return pl.ds(pl.multiple_of(first * part, 32), part)

        def y_copy(b):
            return remote(
                grad_all.at[y_rows(b, 1 - dp), :], grad_from_y.at[b], ysend.at[b], yrecv.at[b], y_peer
            )

        def y_back(b):
            return remote(
                grad_all.at[y_rows(b, dp), :], grad_back.at[b], asend.at[b], arecv.at[b], y_peer
            )

        def unit_right(u):
            return remote(g_right.at[u], g_from_left.at[u], gsend_right.at[u], grecv_left.at[u], right)

        def unit_left(u):
            return remote(g_left.at[u], g_from_right.at[u], gsend_left.at[u], grecv_right.at[u], left)

        def y_sum(turn):
            @pl.when(turn == 0)
            def _():
                both = sh_keep[model // 2 :, :] + sh_given[model // 2 :, :]
                g_own[0] = both[:, :half_width]
                g_own[1] = both[:, half_width:]

            @pl.when(turn > 0)
            def _():
                b = turn - 1
                y_copy(b).wait_recv()
                both = grad_all[y_rows(b, dp), :] + grad_from_y[b]
                g_own[2 * turn] = both[:, :half_width]
                g_own[2 * turn + 1] = both[:, half_width:]

        root = parts // 2

        def unit_up(u):
            @pl.when(me < root)
            def _():
                @pl.when(me > 0)
                def _():
                    unit_right(u).wait_recv()

                g_right[u] = g_own[u] + g_from_left[u]
                unit_right(u).start()

            @pl.when(me > root)
            def _():
                @pl.when(me < parts - 1)
                def _():
                    unit_left(u).wait_recv()

                g_left[u] = g_own[u] + g_from_right[u]
                unit_left(u).start()

        def unit_turn(u):
            unit_right(u).wait_recv()

            @pl.when(me < parts - 1)
            def _():
                unit_left(u).wait_recv()

            total = g_own[u] + g_from_left[u] + g_from_right[u]
            g_total[u] = total
            g_left[u] = total
            unit_left(u).start()

            @pl.when(me < parts - 1)
            def _():
                g_right[u] = total
                unit_right(u).start()

        def unit_down(u):
            @pl.when(me < root)
            def _():
                unit_left(u).wait_recv()
                g_total[u] = g_from_right[u]

                @pl.when(me > 0)
                def _():
                    g_left[u] = g_from_right[u]
                    unit_left(u).start()

            @pl.when(me > root)
            def _():
                unit_right(u).wait_recv()
                g_total[u] = g_from_left[u]

                @pl.when(me < parts - 1)
                def _():
                    g_right[u] = g_from_left[u]
                    unit_right(u).start()

        def y_return(turn):
            b = lax.rem(turn + 3, 4)
            grad_all[y_rows(b, dp), :half_width] = g_total[2 * turn]
            grad_all[y_rows(b, dp), half_width:] = g_total[2 * turn + 1]
            y_back(b).start()

        def gticks(start, last):
            def tick(t, carry):
                @pl.when(lax.rem(t, 2) == 0)
                def _():
                    when_in(t // 2, 4, y_sum)

                wait = jnp.where(me < root, me, parts - 1 - me)
                up = jnp.where(me == root, -1, t - 1 - LAG * wait)
                when_in(up, UNITS, unit_up)
                away = jnp.where(me < root, root - me, me - root)
                back = t - 1 - LAG * (root + away)

                @pl.when(me == root)
                def _():
                    when_in(back, UNITS, unit_turn)

                @pl.when(me != root)
                def _():
                    when_in(back, UNITS, unit_down)

                @pl.when((back >= 0) & (lax.rem(back + 1, 2) == 0))
                def _():
                    when_in((back - 1) // 2, 4, y_return)

                return carry

            lax.fori_loop(start, last, tick, 0)
    else:

        def gticks(start, last):
            pass

    def slot_tile(c, carry):
        cut = aligned(c * 256, 256)
        fetch = pltpu.make_async_copy(sfn.at[:, cut], sfn_tile, tile_sem)
        fetch.start()
        grad = dot_tn(pkv[...], fn[:, cut])
        fetch.wait()
        grad = (grad + dot(dkvt[...], sfn_tile[...])).astype(BF16)
        grad_all[:width, cut] = grad[:width]
        grad_all[3 * (width // 2) : 3 * (width // 2) + width, cut] = grad[width:]
        return carry

    ticks(0, 1)
    fn_copy.wait()
    lax.fori_loop(0, model // 256, slot_tile, 0)
    if pair:
        y_copy(0).start()
        y_copy(1).start()
    ticks(1, 2)
    mid_copy.wait()
    hsum_copy.wait()
    lax.fori_loop(0, blocks, result_rows, 0)
    ticks(2, 4)
    for copy in centre_copies:
        copy.wait_recv()
    centre_grad = cbuf[0].astype(F32)
    for d in range(1, parts):
        centre_grad += cbuf[d].astype(F32)
    centre_grad = centre_grad / counts[:, :1]
    high = centre_grad.astype(BF16)
    low = (centre_grad - high.astype(F32)).astype(BF16)

    def queries(i, carry):
        at = aligned(i * 256, 256)
        member = (ccol[at, :] == iota((256, 128), 1)).astype(BF16)
        pq[at, :] = (dq[at, :].astype(F32) + dot(member, high) + dot(member, low)).astype(BF16)
        return carry

    lax.fori_loop(0, rows // 256, queries, 0)
    query_grad = dot_tn(pq[...], fn[...]).astype(BF16)
    grad_all[width : width + width // 2, :] = query_grad[: width // 2]
    grad_all[5 * (width // 2) : 3 * width, :] = query_grad[width // 2 :]
    if pair:
        y_copy(2).start()
    ticks(4, 5)

    def dense_rows(which):
        at = aligned(which * half_rows, half_rows)
        return dot(pq[at, :], weight[:width, :]) + dot(pkv[at, :], weight[width:, :])

    other_dense = dense_rows(1 - core).astype(BF16)
    for j in range(blocks):
        dense_to_core[j] = other_dense[j * 128 : (j + 1) * 128]
        dense_core_copy(j).start()
    own_dense = dense_rows(core)
    for j in range(blocks):
        dense[j] = own_dense[j * 128 : (j + 1) * 128]
    ticks(5, 6)

    def dense_chip(j, carry):
        dense_core_copy(j).wait_recv()
        dense_to_x[j] = (
            dense[j, :, other_columns] + dense_from_core[j, :, other_columns].astype(F32)
        ).astype(BF16)
        dense_x_copy(j).start()
        return carry

    def dense_hid(j, carry):
        dense_x_copy(j).wait_recv()
        dense_own[own_rows(j), :] += (
            dense[j, :, columns]
            + dense_from_core[j, :, columns].astype(F32)
            + dense_from_x[j].astype(F32)
        )
        return carry

    lax.fori_loop(0, blocks, dense_chip, 0)
    last = CHUNKS + LAG * (parts - 1) + 1

    def joint(t, carry):
        ticks(t, t + 1)
        gticks(t - GSTART, t - GSTART + 1)
        return carry

    ticks(6, GSTART)
    lax.fori_loop(GSTART, last, joint, 0)
    done = last - GSTART
    lax.fori_loop(0, blocks, dense_hid, 0)
    mgrad_copy = pltpu.make_async_copy(mgrad, dense, mid_sem)
    mgrad_copy.start()

    gain_sum[...] = jnp.zeros_like(gain_sum)
    tok_copy.wait()

    def first_send(j, carry):
        grad = dense_own[own_rows(j), :].astype(BF16)
        first[j, :, columns] = grad
        first_copy(j).start()
        return carry

    lax.fori_loop(0, blocks, first_send, 0)

    def first_gains(j, carry):
        centred = tok[own_rows(j), :].astype(F32)
        mean = jnp.mean(centred, -1, keepdims=True)
        variance = jnp.mean(jnp.square(centred - mean), -1, keepdims=True)
        normed = (tok[own_rows(j), columns].astype(F32) - mean) * lax.rsqrt(
            variance + EPSILON
        )
        grad = first[j, :, columns].astype(F32)
        gain_sum[0:1, columns] += jnp.sum(grad * normed, 0, keepdims=True)
        gain_sum[1:2, columns] += jnp.sum(grad, 0, keepdims=True)
        return carry

    lax.fori_loop(0, blocks, first_gains, 0)
    gain_sum[2:4, columns] = second_gains[0:2, columns]
    if pair:
        core_gain = remote(gain_sum, gain_core, gcsend, gcrecv, core_peer)
        core_gain.start()
    gticks(done, done + 2)

    def first_back(j, carry):
        first_copy(j).wait_recv()
        at = block_rows(j, core)
        normed, spread = norm_parts(tok[own_rows(j), :].astype(F32))
        inner, _, _ = norm_back(first[j].astype(F32), normed, spread, gain[...][None])
        tokens_out[at, :] = (dense[j] + inner).astype(BF16)
        tokens_copy(j).start()
        return carry

    mgrad_copy.wait()
    if pair:
        core_gain.wait_recv()
        gain_dm[me] = gain_sum[...] + gain_core[...]
        dm_gains = small_exchange(gain_dm, gmsend, gmrecv, me, parts)
        for copy in dm_gains:
            copy.start()
    lax.fori_loop(0, 1, first_back, 0)
    gticks(done + 2, done + 4)
    lax.fori_loop(1, 2, first_back, 0)
    if pair:
        for copy in dm_gains:
            copy.wait_recv()
        line = gain_dm[0]
        for d in range(1, parts):
            line = line + gain_dm[d]
        gain_dp[0] = line
        dp_gain = remote(gain_dp.at[0], gain_dp.at[1], gpsend.at[0], gprecv.at[0], y_peer)
        dp_gain.start()
    lax.fori_loop(2, 4, first_back, 0)
    if pair:
        dp_gain.wait()
        gain_x[0] = gain_dp[0] + gain_dp[1]
        x_gain = remote(gain_x.at[0], gain_x.at[1], gpsend.at[1], gprecv.at[1], x_peer)
        x_gain.start()
    lax.fori_loop(4, blocks, first_back, 0)
    if pair:
        gticks(done + 4, 1 + LAG * 2 * (parts // 2) + UNITS)
        for b in range(4):
            if b < 3:
                y_copy(b).wait_send()
            y_back(b).wait_recv()
            grad_all[y_rows(b, 1 - dp), :] = grad_back[b]
    small = width // 2
    qkv_out[0, :small] = grad_all[width : width + small, :]
    qkv_out[0, small:] = grad_all[5 * small : 6 * small, :]
    qkv_out[1] = grad_all[:width, :]
    qkv_out[2] = grad_all[3 * small : 5 * small, :]
    if pair:
        out_out[...] = grad_all[6 * small :, :].astype(F32)
    if pair:
        grad = sh_keep[shard_rows(me), :].astype(F32) + sh_given[shard_rows(me), :].astype(F32)
        for step in range(1, parts):
            shrink_copies[step - 1].wait()
            grad = grad + shrink_recv[step].astype(F32)
        shrink_out[...] = grad
        expand_copy.wait()
        grad = expand_y[1].astype(F32)
        for block in (ex_own, ex_one, ex_two, ex_three):
            grad = grad + block[dp].astype(F32)
        expand_out[...] = grad
        x_gain.wait()
        total = gain_x[0] + gain_x[1]
        core_gain.wait_send()
        for copy in dm_gains:
            copy.wait_send()
    else:
        total = gain_sum[...]
    for i, out in enumerate(gain_outs):
        out[...] = total[i]
    if pair:
        for b in range(4):
            y_back(b).wait_send()

        def drain_units(u, carry):
            @pl.when(me < parts - 1)
            def _():
                unit_right(u).wait_send()

            @pl.when(me > 0)
            def _():
                unit_left(u).wait_send()

            return carry

        lax.fori_loop(0, UNITS, drain_units, 0)

    def drain_blocks(j, carry):
        dense_core_copy(j).wait_send()
        dense_x_copy(j).wait_send()
        first_copy(j).wait_send()
        result_copy(j).wait()
        tokens_copy(j).wait()
        return carry

    def drain(i, carry):
        @pl.when(me < parts - 1)
        def _():
            right_copy(i).wait_send()

        @pl.when(me > 0)
        def _():
            left_copy(i).wait_send()

        core_copy(i).wait_send()
        x_copy(i).wait_send()
        fin_copy(i).wait_send()
        return carry

    lax.fori_loop(0, CHUNKS, drain, 0)
    for copy in sum_copies + centre_copies:
        copy.wait_send()
    lax.fori_loop(0, blocks, drain_blocks, 0)


def tail(
    pair, lengths, dkvt, dq, summed, k, v, centre, topk, tm, merged, rows_in, counts, clusters,
    weight, fn, sfn, tokens, gain, mgrad, srow, mid, hsum, hsum_x, second_gains,
    sh_keep, sh_given, ex_parts, parts,
):
    rows, width = k.shape
    model = tokens.shape[1]
    shape = jax.ShapeDtypeStruct
    dma = pltpu.SemaphoreType.DMA
    blocks = rows // 256
    owned = ex_parts[0].shape[1:]
    chain = pltpu.VMEM((CHUNKS, CHUNK, model // 2), BF16)
    whole = pltpu.VMEM((CHUNKS, CHUNK, model), BF16)
    unit = pltpu.VMEM((UNITS, width // 2, model // 2) if pair else (UNITS, 16, 128), BF16)
    return pl.pallas_call(
        functools.partial(tail_kernel, pair),
        out_shape=(
            shape((rows, model), BF16),
            shape((rows, model), BF16),
            shape((3, width, model), BF16),
            shape((width, model), F32),
            shape((model,), F32),
            shape((model,), F32),
            shape((model,), F32),
            shape((model,), F32),
            shape(owned, F32),
            shape(owned, F32),
        ),
        in_specs=[pl.BlockSpec(memory_space=pltpu.SMEM)]
        + vmem(13)
        + [pl.BlockSpec(memory_space=pl.ANY)] * 3
        + vmem(1)
        + [pl.BlockSpec(memory_space=pl.ANY)]
        + vmem(1)
        + [pl.BlockSpec(memory_space=pl.ANY)] * 2
        + vmem(8),
        out_specs=tuple(vmem(10)),
        scratch_shapes=[
            pltpu.VMEM((parts, CLP, 256), BF16),
            pltpu.VMEM((parts, CLP, width), BF16),
            whole, whole, whole,
            chain, chain, chain, chain, chain, chain,
            chain,
            pltpu.VMEM((rows, width), BF16),
            pltpu.VMEM((rows, 2 * width), BF16),
            pltpu.VMEM((blocks, 128, model), F32),
            pltpu.VMEM((blocks, 128, model), BF16),
            pltpu.VMEM((blocks, 128, model), BF16),
            pltpu.VMEM((blocks, 128, model // 2), BF16),
            pltpu.VMEM((blocks, 128, model // 2), BF16),
            pltpu.VMEM((rows // 2, model // 2), F32),
            pltpu.VMEM((blocks, 128, model), BF16),
            pltpu.VMEM((SLOTS, 256), BF16),
            pltpu.VMEM((4 * width, model), BF16),
            pltpu.VMEM((3, width // 2, model), BF16),
            pltpu.VMEM((4, width // 2, model), BF16),
            unit, unit, unit, unit, unit, unit,
            pltpu.VMEM((8, model), F32),
            pltpu.VMEM((8, model), F32),
            pltpu.VMEM((parts, 8, model), F32),
            pltpu.VMEM((2, 8, model), F32),
            pltpu.VMEM((2, 8, model), F32),
            pltpu.VMEM((parts,) + owned, BF16),
            pltpu.VMEM((parts,) + owned, BF16),
            pltpu.VMEM((2,) + owned, BF16),
            pltpu.VMEM((rows // 2, model), BF16),
            pltpu.VMEM((rows, model), BF16),
            dma, dma, dma, dma, dma,
        ]
        + [dma((parts,))] * 4
        + [dma((CHUNKS,))] * 10
        + [dma((blocks,))] * 10
        + [dma((3,))] * 2
        + [dma((UNITS,))] * 4
        + [dma((4,))] * 2
        + [dma, dma, dma((parts,)), dma((parts,)), dma((2,)), dma((2,)), dma((parts,)), dma((parts,))],
        compiler_params=pltpu.CompilerParams(
            vmem_limit_bytes=58 << 20, collective_id=1, has_side_effects=True
        ),
        name="tail",
    )(
        lengths, dkvt, dq, summed, k, v, centre, topk, tm, merged, rows_in, counts,
        clusters, weight.reshape(3 * width, model), fn, sfn, tokens, gain,
        mgrad.reshape(blocks, 128, model), srow, mid.reshape(blocks, 128, model),
        hsum.reshape(blocks, 128, model), hsum_x.reshape(blocks, 128, model), second_gains,
        sh_keep, sh_given, *ex_parts,
    )


def deliver_kernel(count, qkv, *refs):
    sources, qkv_out, targets = refs[:count], refs[count], refs[count + 1 :]
    for part in range(qkv.shape[0]):
        qkv_out[part] = qkv[part].astype(F32)
    for source, target in zip(sources, targets):
        target[...] = source[...]


def deliver(qkv, *arrays):
    shape = jax.ShapeDtypeStruct
    count = len(arrays)
    return pl.pallas_call(
        functools.partial(deliver_kernel, count),
        out_shape=(shape(qkv.shape, F32),) + tuple(shape(a.shape, a.dtype) for a in arrays),
        in_specs=vmem(count + 1),
        out_specs=tuple(vmem(count + 1)),
        compiler_params=pltpu.CompilerParams(vmem_limit_bytes=62 << 20),
        name="deliver",
    )(qkv, *arrays)


def shards(
    tokens,
    clusters,
    top_keys,
    lengths,
    qkv_weight,
    out_weight,
    first_gain,
    first_bias,
    second_gain,
    second_bias,
    expand_weight,
    shrink_weight,
    cotangent,
):
    parts, n_dp = lax.axis_size("dm"), lax.axis_size("dp")
    pair = n_dp == 2
    weight = jnp.swapaxes(qkv_weight, 1, 2)
    topk = jnp.pad(top_keys, ((0, CLP - CL), (0, 0)), constant_values=-1)
    flat = jnp.pad(top_keys.reshape(-1), (0, SLOTS - CL * TOPK), constant_values=-1)
    (
        first_normed, slot_normed, qs, k, v, ks, vs, kst, vst, starts, rcol, rrow, cls, centre, tm, rows_in,
        merged, counts, out_full, expand_full, shrink_peer, cluster_column,
    ) = front(
        pair, lengths, tokens, clusters, weight, first_gain, first_bias,
        flat.reshape(SLOTS, 1), topk, expand_weight, shrink_weight.T, out_weight, parts,
    )
    if pair:
        shrink_shards = [shrink_weight.T]
        source, _ = lax.optimization_barrier((shrink_weight.T, starts))
        for step in range(1, parts):
            shrink_shards.append(
                lax.ppermute(source, "dm", [(i, (i + step) % parts) for i in range(parts)])
            )
    else:
        expand_full = lax.all_gather(expand_weight, ("dp", "dm"), axis=0, tiled=True)
        shrink_full = lax.all_gather(shrink_weight.T, ("dp", "dm"), axis=0, tiled=True)
        shrink_shards = [shrink_full] + [jnp.zeros((16, 128), BF16)] * (parts - 1)
    attended = exact_forward(starts, qs, cls, kst, vs, rows_in, rcol)
    mid, middle_grad, attended_grad, hidden_sum, out_grad_part, second_parts, *grads = middle(
        pair, tokens, cotangent, attended, out_weight, out_full, expand_full,
        second_gain, second_bias, shrink_shards, shrink_peer,
    )
    hidden_sum_x = lax.ppermute(hidden_sum, "hid", [(i, i ^ 2) for i in range(lax.axis_size("hid"))])
    units = expand_weight.shape[1]
    if pair:
        shrink_keep, shrink_give, *expand_parts = grads
        shrink_given = lax.ppermute(shrink_give, "dp", [(0, 1), (1, 0)])
        expand_parts = [expand_parts[0]] + [
            lax.ppermute(expand_parts[step], "dm", [(i, (i + step) % parts) for i in range(parts)])
            for step in range(1, parts)
        ]
    else:
        summed_grads = lax.psum_scatter(grads[0], ("dp", "dm"), scatter_dimension=0, tiled=True)
        shrink_keep = shrink_given = jnp.zeros((16, 128), BF16)
        expand_parts = [jnp.zeros((2, 16, 128), BF16)] * parts
    dq, dkvt, summed = exact_backward(
        starts, qs, cls, ks, kst, vst, rows_in, rcol, rrow, attended_grad
    )
    result, tokens_grad, qkv_grad, out_grad, *gains, expand_grad, shrink_grad = tail(
        pair, lengths, dkvt, dq, summed, k, v, centre, topk, tm, merged, rows_in, counts, cluster_column,
        weight, first_normed, slot_normed, tokens, first_gain, middle_grad,
        flat.reshape(1, SLOTS), mid, hidden_sum, hidden_sum_x, second_parts,
        shrink_keep, shrink_given, expand_parts, parts,
    )
    if pair:
        qkv_grad, result, tokens_grad, out_grad, expand_grad, shrink_grad, *gains = deliver(
            qkv_grad, result, tokens_grad, out_grad, expand_grad, shrink_grad, *gains
        )
    else:
        out_grad = lax.psum(out_grad_part, ("dp", "dm")).astype(F32)
        qkv_grad = lax.psum(qkv_grad, ("dp", "dm"))
        gains = lax.psum(jnp.stack(gains), ("dp", "dm", "hid"))
        summed_grads = summed_grads.astype(F32)
        expand_grad, shrink_grad = summed_grads[:, :units], summed_grads[:, units:]
    return (
        result,
        tokens_grad,
        jnp.swapaxes(qkv_grad.astype(F32), 1, 2),
        out_grad,
        gains[0],
        gains[1],
        gains[2],
        gains[3],
        expand_grad,
        shrink_grad.T,
    )


def solution(mesh):
    in_specs = (
        P(("dp", "dm"), None),
        P(("dp", "dm")),
        P("dp", None),
        P("dp"),
        P(None, None, "hid"),
        P("hid", None),
        P(),
        P(),
        P(),
        P(),
        P(("dp", "dm"), "hid"),
        P("hid", ("dp", "dm")),
        P(("dp", "dm"), None),
    )
    out_specs = (
        P(("dp", "dm"), None),
        P(("dp", "dm"), None),
        P(None, None, "hid"),
        P("hid", None),
        P(),
        P(),
        P(),
        P(),
        P(("dp", "dm"), "hid"),
        P("hid", ("dp", "dm")),
    )
    return jax.shard_map(shards, mesh=mesh, in_specs=in_specs, out_specs=out_specs, check_vma=False)
```
